32 devices in a mesh: fsdp: 4 (over z), ctx: 8 (over y, x, core).
Axes of the slice: x: 2, y: 2, z: 4, core: 2. Of those that a mesh axis runs over, the one named last changes fastest.
Arguments:
- tokens: bfloat16 [8, 1024, 1088], P('fsdp', 'ctx'), may hold values from -6 to 6
- lengths: int32 [8], P('fsdp'), may hold values from 256 to 1024, as said below
- cotangent: bfloat16 [8, 1024, 1088], P('fsdp', 'ctx'), may hold values from -6 to 6
- ln_gain: bfloat16 [2, 2, 1088], P(None, None, 'fsdp'), may hold values from 0.25 to 1.75
- ln_bias: bfloat16 [2, 2, 1088], P(None, None, 'fsdp'), may hold values from -1.5 to 1.5
- w_qkv: bfloat16 [2, 1088, 3264], P(None, 'fsdp'), may hold values from -0.1875 to 0.1875
- b_qv: bfloat16 [2, 2, 1088], P(None, None, 'fsdp'), may hold values from -2.5 to 2.5
- w_out: bfloat16 [2, 1088, 1088], P(None, 'fsdp'), may hold values from -3 to 3
- b_out: bfloat16 [2, 1088], P(None, 'fsdp'), may hold values from -1.5 to 1.5
- w_up: bfloat16 [2, 1088, 4352], P(None, 'fsdp'), may hold values from -0.1875 to 0.1875
- b_up: bfloat16 [2, 4352], P(None, 'fsdp'), may hold values from -2.5 to 2.5
- w_down: bfloat16 [2, 4352, 1088], P(None, 'fsdp'), may hold values from -0.09375 to 0.09375
- b_down: bfloat16 [2, 1088], P(None, 'fsdp'), may hold values from -1.5 to 1.5
Outputs:
- activations: bfloat16 [8, 1024, 1088], P('fsdp', 'ctx')
- input_grad: float32 [8, 1024, 1088], P('fsdp', 'ctx')
- ln_gain_grad: float32 [2, 2, 1088], P(None, None, 'fsdp')
- ln_bias_grad: float32 [2, 2, 1088], P(None, None, 'fsdp')
- w_qkv_grad: float32 [2, 1088, 3264], P(None, 'fsdp')
- b_qv_grad: float32 [2, 2, 1088], P(None, None, 'fsdp')
- w_out_grad: float32 [2, 1088, 1088], P(None, 'fsdp')
- b_out_grad: float32 [2, 1088], P(None, 'fsdp')
- w_up_grad: float32 [2, 1088, 4352], P(None, 'fsdp')
- b_up_grad: float32 [2, 4352], P(None, 'fsdp')
- w_down_grad: float32 [2, 4352, 1088], P(None, 'fsdp')
- b_down_grad: float32 [2, 1088], P(None, 'fsdp')
The draws below stay inside these ranges and needn't reach their ends.
Inputs may be any that keep to these rules, and one draw needn't show every extreme that they name: `lengths`: in each aligned group of 2 sequences (those of one index of fsdp), one sequence has all 1024 slots valid.
All inputs are finite; a program needn't handle non-finite values.
Results may differ from the reference program's by a relative error of at most 0.022.
Values may be sent and summed in bfloat16 or wider, within the bound.
A program may use at most 320 MiB of HBM per device.

```python
import jax
import jax.numpy as jnp
from jax import lax

HEADS = 17
HEAD_DIM = 64
D = 1088
FF = 4352
LAYERS = 2
SEQS = 2
SLOTS = 1024
SEQUENCES = 8


def draw_lengths(key, part):
    key = jax.random.fold_in(key, 7)
    first_key, second_key = jax.random.split(key)
    group_total = SEQUENCES // SEQS
    drawn = jax.random.randint(first_key, (group_total, SEQS), SLOTS // 4, SLOTS + 1, dtype=jnp.int32)
    chosen = jax.random.randint(second_key, (group_total, 1), 0, SEQS, dtype=jnp.int32)
    picked = jnp.arange(SEQS, dtype=jnp.int32)[None, :] == chosen
    return jnp.where(picked, SLOTS, drawn).reshape(SEQUENCES).astype(jnp.int32)


def block_scale(key, dims, shards, low, largest):
    gain, own = 1.0, jax.random.fold_in(key, 6)
    for dim, parts in shards:
        draws = jnp.exp(jax.random.uniform(jax.random.fold_in(own, dim), (parts,), jnp.float32, low / len(shards), largest / len(shards)))
        gain = gain * jnp.repeat(draws, dims[dim] // parts).reshape([-1 if axis == dim else 1 for axis in range(len(dims))])
    return gain


def noise(key, extent, width, bound, cuts=(), kind=jnp.bfloat16):
    factor_of = block_scale(key, extent, cuts, -0.22, 0.18) if cuts else 1.0
    array = jax.random.normal(key, extent, jnp.float32) * width * factor_of
    return jnp.minimum(jnp.maximum(array, -bound), bound).astype(kind)


def setup_inputs(seed: int = 0) -> dict:
    arg_keys = jax.random.split(jax.random.key(seed), 14)
    return {
        "tokens": noise(arg_keys[0], (SEQUENCES, SLOTS, D), 1.0, 6.0, ((0, 4), (1, 8))),
        "lengths": draw_lengths(jax.random.fold_in(arg_keys[13], 71), 0),
        "cotangent": noise(arg_keys[2], (SEQUENCES, SLOTS, D), 1.0, 6.0, ((0, 4), (1, 8))),
        "ln_gain": jnp.clip(1.0 + 0.15 * jax.random.normal(arg_keys[3], (LAYERS, 2, D), jnp.float32), 0.25, 1.75).astype(jnp.bfloat16),
        "ln_bias": noise(arg_keys[4], (LAYERS, 2, D), 0.3, 1.5, ((2, 4),)),
        "w_qkv": noise(arg_keys[5], (LAYERS, D, 3 * D), D ** -0.5, 0.1875, ((1, 4),)),
        "b_qv": noise(arg_keys[6], (LAYERS, 2, D), 0.5, 2.5, ((2, 4),)),
        "w_out": noise(arg_keys[7], (LAYERS, D, D), (max(1, D // 256)) ** -0.5, 3.0, ((1, 4),)),
        "b_out": noise(arg_keys[8], (LAYERS, D), 0.3, 1.5, ((1, 4),)),
        "w_up": noise(arg_keys[9], (LAYERS, D, FF), D ** -0.5, 0.1875, ((1, 4),)),
        "b_up": noise(arg_keys[10], (LAYERS, FF), 0.5, 2.5, ((1, 4),)),
        "w_down": noise(arg_keys[11], (LAYERS, FF, D), FF ** -0.5, 0.09375, ((1, 4),)),
        "b_down": noise(arg_keys[12], (LAYERS, D), 0.3, 1.5, ((1, 4),)),
    }


@jax.custom_vjp
def low(v):
    return lax.optimization_barrier(v.astype(jnp.bfloat16)).astype(jnp.float32)

@jax.custom_vjp
def low_back(v):
    return v

def low_keep(v):
    return (low(v), None)

def low_pass(kept, grad):
    return (grad,)

def back_keep(v):
    return (v, None)

def back_low(kept, grad):
    return (low(grad),)
low.defvjp(low_keep, low_pass)
low_back.defvjp(back_keep, back_low)

def layer_norm(values, scales, shifts):
    average = lax.optimization_barrier(jnp.mean(values, axis=-1, keepdims=True))
    centred = values - average
    variance = lax.optimization_barrier(jnp.mean(centred * centred, axis=-1, keepdims=True))
    return centred * lax.rsqrt(variance + 1e-05) * scales + shifts

def attend_one(queries, key_rows, value_rows, length_one):
    slot_count = key_rows.shape[0]
    scores = jnp.einsum('qhe,khe->hqk', queries, key_rows, precision=lax.Precision.HIGHEST) * HEAD_DIM ** (-0.5)
    scores = low_back(scores)
    places = jnp.arange(slot_count, dtype=jnp.int32)
    allowed = (places[None, :] <= places[:, None]) & (places[None, :] < length_one)
    scores = jnp.where(allowed[None], scores, -1e+30)
    weights = jax.nn.softmax(scores, axis=-1)
    return jnp.einsum('hqk,khe->qhe', low(weights), value_rows, precision=lax.Precision.HIGHEST)

def attend_item(item_tuple):
    return attend_one(item_tuple[0], item_tuple[1], item_tuple[2], item_tuple[3])

def block_layer(hidden, lengths, params):
    gain_rows, shift_rows, mix_weight, mix_bias, out_weight, out_bias, up_weight, up_bias, down_weight, down_bias = params
    group_count, slot_count = (hidden.shape[0], hidden.shape[1])
    normed = low(layer_norm(hidden, gain_rows[0], shift_rows[0]))
    mixed_rows = jnp.einsum('gtd,df->gtf', normed, mix_weight, precision=lax.Precision.HIGHEST)
    queries = low_back(low(mixed_rows[..., :D] + mix_bias[0]))
    key_rows = low_back(low(mixed_rows[..., D:2 * D]))
    value_rows = low_back(low(mixed_rows[..., 2 * D:] + mix_bias[1]))
    split_shape = (group_count, slot_count, HEADS, HEAD_DIM)
    attended = lax.map(jax.checkpoint(attend_item), (queries.reshape(split_shape), key_rows.reshape(split_shape), value_rows.reshape(split_shape), lengths))
    attended = low_back(low(attended.reshape(hidden.shape)))
    branch_out = low_back(jnp.einsum('gtd,de->gte', attended, out_weight, precision=lax.Precision.HIGHEST) + out_bias)
    middle = hidden + branch_out
    normed_second = low(layer_norm(middle, gain_rows[1], shift_rows[1]))
    upper_pre = low_back(jnp.einsum('gtd,df->gtf', normed_second, up_weight, precision=lax.Precision.HIGHEST) + up_bias)
    active = low(jax.nn.gelu(upper_pre))
    branch_mlp = low_back(jnp.einsum('gtf,fd->gtd', active, down_weight, precision=lax.Precision.HIGHEST) + down_bias)
    return middle + branch_mlp

def forward(tokens_block, lengths_block, params):
    hidden = tokens_block
    for layer_index in range(LAYERS):
        hidden = block_layer(hidden, lengths_block, tuple((item[layer_index] for item in params)))
    places = jnp.arange(SLOTS, dtype=jnp.int32)
    valid_rows = (places[None, :] < lengths_block[:, None]).astype(hidden.dtype)
    return hidden * valid_rows[:, :, None]

def reference(tokens, lengths, cotangent, ln_gain, ln_bias, w_qkv, b_qv, w_out, b_out, w_up, b_up, w_down, b_down):
    params = tuple((item.astype(jnp.float32) for item in (ln_gain, ln_bias, w_qkv, b_qv, w_out, b_out, w_up, b_up, w_down, b_down)))
    group_total = SEQUENCES // SEQS
    token_groups = tokens.astype(jnp.float32).reshape(group_total, SEQS, SLOTS, D)
    length_groups = lengths.reshape(group_total, SEQS)
    cot_groups = cotangent.astype(jnp.float32).reshape(group_total, SEQS, SLOTS, D)

    def one_group(totals, item_tuple):
        token_block, length_block, cot_block = item_tuple

        def apply_block(inputs_now, params_now):
            return forward(inputs_now, length_block, params_now)
        outputs, pull_back = jax.vjp(apply_block, token_block, params)
        token_grad, param_grads = pull_back(cot_block)
        totals = tuple((first_sum + second_sum for first_sum, second_sum in zip(totals, param_grads)))
        return (totals, (outputs, token_grad))
    start_sums = tuple((jnp.zeros(item.shape, jnp.float32) for item in params))
    totals, (outputs, token_grads) = lax.scan(one_group, start_sums, (token_groups, length_groups, cot_groups))
    activations = outputs.reshape(SEQUENCES, SLOTS, D).astype(jnp.bfloat16)
    input_grad = token_grads.reshape(SEQUENCES, SLOTS, D)
    return (activations, input_grad, totals[0], totals[1], totals[2], totals[3], totals[4], totals[5], totals[6], totals[7], totals[8], totals[9])
```

```python
import functools

import jax
import jax.numpy as jnp
from jax import lax
from jax.experimental import pallas as pl
from jax.experimental.pallas import tpu as pltpu
from jax.sharding import PartitionSpec as P

MESH = pl.DeviceIdType.MESH


class Place:
    def __init__(self):
        self.depth = lax.axis_size("fsdp")
        self.z = lax.axis_index("fsdp")
        self.c8 = lax.axis_index("ctx")
        self.core = lax.rem(self.c8, 2)
        self.p = self.c8 // 2
        self.px = lax.rem(self.p, 2)
        self.py = self.p // 2
        self.sib = {"ctx": self.c8 + 1 - 2 * self.core}
        self.x_dev = {"ctx": self.c8 + 2 - 4 * self.px}
        self.y_dev = {"ctx": self.c8 + 4 - 8 * self.py}
        self.p_x = self.p + 1 - 2 * self.px
        self.p_y = self.p + 2 - 4 * self.py
        self.p_d = 3 - self.p
        self.relay_from = self.p + (1 - self.core) * (1 - 2 * self.px) + self.core * (2 - 4 * self.py)
        self.relay_dev = {
            "ctx": self.c8 + (1 - self.core) * (4 - 8 * self.py) + self.core * (2 - 4 * self.px)
        }

    def up(self):
        return {"fsdp": self.z + 1}

    def down(self):
        return {"fsdp": self.z - 1}

    def greet(self):
        barrier = pltpu.get_barrier_semaphore()
        for device in (self.sib, self.x_dev, self.y_dev):
            pl.semaphore_signal(barrier, inc=1, device_id=device, device_id_type=MESH)

        @pl.when(self.z > 0)
        def _():
            pl.semaphore_signal(barrier, inc=1, device_id=self.down(), device_id_type=MESH)

        @pl.when(self.z < self.depth - 1)
        def _():
            pl.semaphore_signal(barrier, inc=1, device_id=self.up(), device_id_type=MESH)

        below = jnp.where(self.z > 0, 1, 0)
        above = jnp.where(self.z < self.depth - 1, 1, 0)
        pl.semaphore_wait(barrier, 3 + below + above)


def remote(src, dst, send_sem, recv_sem, device):
    return pltpu.make_async_remote_copy(
        src_ref=src, dst_ref=dst, send_sem=send_sem, recv_sem=recv_sem, device_id=device, device_id_type=MESH
    )


class Gather:
    def __init__(self, at, own, whole, left_core, send, recv):
        self.at, self.own, self.whole = at, own, whole
        self.send, self.recv = send, recv
        rows = own.shape[0]
        unit = rows // 17
        self.t1 = 2 * unit
        self.block = 8 * unit
        self.rest = pl.ds(16 * unit, unit)
        self.has_rest = at.core == left_core

    def t1_rows(self, p, core=None):
        core = self.at.core if core is None else core
        return pl.ds(pl.multiple_of(core * self.block + p * self.t1, 16), self.t1)

    def block_rows(self, core):
        return pl.ds(pl.multiple_of(core * self.block, 16), self.block)

    def copy(self, kind, shard, rows, device, src=None, second=False):
        depth = self.at.depth
        slot = kind * depth + shard
        src = self.whole.at[shard, rows] if src is None else src
        send = self.send.at[(8 * depth + kind) if second else slot]
        return remote(src, self.whole.at[shard, rows], send, self.recv.at[slot], device)

    def start(self):
        at = self.at
        mine = self.t1_rows(at.p)

        @pl.when(at.z < at.depth - 1)
        def _():
            self.copy(0, at.z, mine, at.up(), self.own.at[mine]).start()

            @pl.when(self.has_rest)
            def _():
                self.copy(1, at.z, self.rest, at.up(), self.own.at[self.rest]).start()

        @pl.when(at.z > 0)
        def _():
            self.copy(0, at.z, mine, at.down(), self.own.at[mine], True).start()

            @pl.when(self.has_rest)
            def _():
                self.copy(1, at.z, self.rest, at.down(), self.own.at[self.rest], True).start()

    def cases(self, step, do):
        at = self.at

        @pl.when(at.z - 1 - step >= 0)
        def _():
            do(at.z - 1 - step, at.z < at.depth - 1, at.up())

        @pl.when(at.z + 1 + step < at.depth)
        def _():
            do(at.z + 1 + step, at.z > 0, at.down())

    def arrive(self, step):
        at = self.at
        mine = self.t1_rows(at.p)

        def do(shard, onward, device):
            self.copy(0, shard, mine, at.sib).wait_recv()

            @pl.when(onward)
            def _():
                self.copy(0, shard, mine, device).start()

            self.copy(2, shard, mine, at.x_dev).start()
            self.copy(3, shard, mine, at.y_dev).start()

            @pl.when(self.has_rest)
            def _():
                self.copy(1, shard, self.rest, at.sib).wait_recv()

                @pl.when(onward)
                def _():
                    self.copy(1, shard, self.rest, device).start()

                self.copy(5, shard, self.rest, at.sib).start()

        self.cases(step, do)

    def plane(self, step):
        at = self.at

        def do(shard, onward, device):
            self.copy(2, shard, self.t1_rows(at.p_x), at.sib).wait_recv()
            self.copy(3, shard, self.t1_rows(at.p_y), at.sib).wait_recv()
            self.copy(4, shard, self.t1_rows(at.relay_from), at.relay_dev).start()

        self.cases(step, do)

    def share(self, step):
        at = self.at

        def do(shard, onward, device):
            self.copy(4, shard, self.t1_rows(at.p_d), at.sib).wait_recv()
            self.copy(6, shard, self.block_rows(at.core), at.sib).start()

        self.cases(step, do)

    def finish(self):
        at = self.at
        mine = self.t1_rows(at.p)

        def do(shard, onward, device):
            self.copy(6, shard, self.block_rows(1 - at.core), at.sib).wait_recv()

            @pl.when(jnp.logical_not(self.has_rest))
            def _():
                self.copy(5, shard, self.rest, at.sib).wait_recv()

        for step in range(at.depth - 1):
            self.cases(step, do)

    def drain(self):
        at = self.at
        mine = self.t1_rows(at.p)

        @pl.when(at.z < at.depth - 1)
        def _():
            self.copy(0, at.z, mine, at.up(), self.own.at[mine]).wait_send()

            @pl.when(self.has_rest)
            def _():
                self.copy(1, at.z, self.rest, at.up(), self.own.at[self.rest]).wait_send()

        @pl.when(at.z > 0)
        def _():
            self.copy(0, at.z, mine, at.down(), self.own.at[mine], True).wait_send()

            @pl.when(self.has_rest)
            def _():
                self.copy(1, at.z, self.rest, at.down(), self.own.at[self.rest], True).wait_send()

        def do(shard, onward, device):
            @pl.when(onward)
            def _():
                self.copy(0, shard, mine, device).wait_send()

                @pl.when(self.has_rest)
                def _():
                    self.copy(1, shard, self.rest, device).wait_send()

            self.copy(2, shard, mine, at.x_dev).wait_send()
            self.copy(3, shard, mine, at.y_dev).wait_send()
            self.copy(4, shard, self.t1_rows(at.relay_from), at.relay_dev).wait_send()
            self.copy(6, shard, self.block_rows(at.core), at.sib).wait_send()

            @pl.when(self.has_rest)
            def _():
                self.copy(5, shard, self.rest, at.sib).wait_send()

        for step in range(at.depth - 1):
            self.cases(step, do)


def gather_kernel(count, *refs):
    owns, small = refs[:count], refs[count]
    wholes, small_all = refs[count + 1 : 2 * count + 1], refs[2 * count + 1]
    send, recv, own_sem, small_send, small_recv = refs[2 * count + 2 : 2 * count + 7]
    stages = refs[2 * count + 7 :]
    at = Place()
    depth = at.depth
    at.greet()
    items = [
        Gather(at, owns[k], wholes[k], k % 2, send.at[k], recv.at[k]) for k in range(count)
    ]
    loads = [pltpu.make_async_copy(owns[k], stages[k], own_sem.at[0, k]) for k in range(count)]
    loads.append(pltpu.make_async_copy(small, stages[count], own_sem.at[0, count]))
    stores = [
        pltpu.make_async_copy(stages[k], wholes[k].at[at.z], own_sem.at[1, k]) for k in range(count)
    ]
    stores.append(pltpu.make_async_copy(stages[count], small_all.at[at.z], own_sem.at[1, count]))

    def small_copy(shard, device, src=None, second=False):
        return remote(
            small_all.at[shard] if src is None else src,
            small_all.at[shard],
            small_send.at[depth if second else shard],
            small_recv.at[shard],
            device,
        )

    @pl.when(at.z < depth - 1)
    def _():
        small_copy(at.z, at.up(), small).start()

    @pl.when(at.z > 0)
    def _():
        small_copy(at.z, at.down(), small, True).start()

    steps = depth - 1
    items[0].start()
    for copy in loads:
        copy.start()

    def small_do(shard, onward, device):
        small_copy(shard, at.sib).wait_recv()

        @pl.when(onward)
        def _():
            small_copy(shard, device).start()

    for k in range(count):
        if k == 0:
            for step in range(steps):
                items[0].arrive(step)
            for load, store in zip(loads, stores):
                load.wait()
                store.start()
        if k == 0:
            for step in range(steps):
                items[0].cases(step, small_do)
        if k + 1 < count:
            items[k + 1].start()
        for step in range(steps):
            items[k].plane(step)
            if k + 1 < count:
                items[k + 1].arrive(step)
            items[k].share(step)
    for item in items:
        item.finish()
    for copy in stores:
        copy.wait()
    for item in items:
        item.drain()

    @pl.when(at.z < depth - 1)
    def _():
        small_copy(at.z, at.up(), small).wait_send()

    @pl.when(at.z > 0)
    def _():
        small_copy(at.z, at.down(), small, True).wait_send()

    def small_end(shard, onward, device):
        @pl.when(onward)
        def _():
            small_copy(shard, device).wait_send()

    for step in range(steps):
        items[0].cases(step, small_end)


def gather_weights(owns, small):
    depth = lax.axis_size("fsdp")
    count = len(owns)
    any_spec = pl.BlockSpec(memory_space=pl.ANY)
    shapes = [jax.ShapeDtypeStruct((depth,) + item.shape, item.dtype) for item in list(owns) + [small]]
    return pl.pallas_call(
        functools.partial(gather_kernel, count),
        out_shape=shapes,
        in_specs=[any_spec] * (count + 1),
        out_specs=[any_spec] * (count + 1),
        scratch_shapes=[
            pltpu.SemaphoreType.DMA((count, 8 * depth + 8)),
            pltpu.SemaphoreType.DMA((count, 8 * depth)),
            pltpu.SemaphoreType.DMA((2, count + 1)),
            pltpu.SemaphoreType.DMA((depth + 1,)),
            pltpu.SemaphoreType.DMA((depth,)),
        ]
        + [pltpu.VMEM(item.shape, item.dtype) for item in list(owns) + [small]],
        compiler_params=pltpu.CompilerParams(
            collective_id=0, has_side_effects=True, vmem_limit_bytes=40 * 1024 * 1024
        ),
    )(*owns, small)


def both(*conds):
    conds = [c for c in conds if c is not None]
    if not conds:
        return None
    total = conds[0]
    for c in conds[1:]:
        total = jnp.logical_and(total, c)
    return total


def under(cond, do):
    if cond is None:
        do()
    else:
        pl.when(cond)(do)


def add_rows(acc, extra, rows):
    def step(i, carry):
        piece = pl.ds(pl.multiple_of(i * 16, 16), 16)
        acc[piece, :] = acc[piece, :] + extra[piece, :]
        return carry

    lax.fori_loop(0, rows // 16, step, 0)


def add_rows_two(acc, one, two, rows):
    def step(i, carry):
        piece = pl.ds(pl.multiple_of(i * 16, 16), 16)
        total = acc[piece, :].astype(jnp.float32) + one[piece, :].astype(jnp.float32)
        acc[piece, :] = (total + two[piece, :].astype(jnp.float32)).astype(jnp.bfloat16)
        return carry

    lax.fori_loop(0, rows // 16, step, 0)


class Geometry:
    def __init__(self, rows, cols, line_part):
        self.rows, self.cols = rows, cols
        unit = rows // 17
        self.unit = unit
        self.block = 8 * unit
        self.t2 = line_part
        self.t1 = 2 * unit - line_part

    def scratch(self, depth):
        cols = self.cols
        vm = lambda *shape: pltpu.VMEM(shape + (cols,), jnp.bfloat16)
        out = [
            vm(depth, self.block),
            vm(depth, self.block),
            vm(3, depth, self.t1),
            vm(depth + 1, self.t1),
            vm(depth, self.unit),
            vm(depth + 1, self.unit),
            vm(depth, self.unit),
            vm(2, self.unit),
        ]
        if self.t2:
            out += [vm(depth + 1, 4 * self.t2), vm(3, self.t2)]
        return out


SLOTS = 48


class Reduce:
    def __init__(self, at, geo, part, out, left_core, bufs, send, recv, local):
        self.at, self.geo, self.part, self.out = at, geo, part, out
        self.acc, self.sib_in, self.plane_in, self.z_in, self.racc, self.rz_in, self.rsib_in, self.rplane_in = bufs[:8]
        if geo.t2:
            self.z2_in, self.plane2_in = bufs[8:]
        self.send, self.recv, self.local = send, recv, local
        self.has_rest = at.core == left_core
        self.no_rest = at.core != left_core
        self.rest = pl.ds(16 * geo.unit, geo.unit)
        self.names, self.posts = {}, []
        core, p = at.core, at.p
        self.direct_p = p + (1 - core) * (2 - 4 * at.py) + core * (1 - 2 * at.px)
        self.owner_dev = {
            "ctx": at.c8 + (1 - core) * (2 - 4 * at.px) + core * (4 - 8 * at.py)
        }

    def slot(self, name):
        return self.names.setdefault(name, len(self.names))

    def make(self, name, src, dst, device):
        i = self.slot(name)
        return remote(src, dst, self.send.at[i], self.recv.at[i], device)

    def post(self, name, src, dst, device, cond=None):
        under(cond, lambda: self.make(name, src, dst, device).start())
        self.posts.append((name, src, dst, device, cond))

    def take(self, name, dst, cond=None):
        under(cond, lambda: self.make(name, dst, dst, self.at.sib).wait_recv())

    def c1(self, p):
        return pl.ds(pl.multiple_of(p * self.geo.t1, 16), self.geo.t1)

    def c2(self, p):
        return pl.ds(pl.multiple_of(4 * self.geo.t1 + p * self.geo.t2, 16), self.geo.t2)

    def o1(self, p, core):
        return pl.ds(pl.multiple_of(core * self.geo.block + p * self.geo.t1, 16), self.geo.t1)

    def o2(self, p, core):
        return pl.ds(
            pl.multiple_of(core * self.geo.block + 4 * self.geo.t1 + p * self.geo.t2, 16), self.geo.t2
        )

    def begin(self):
        at, geo = self.at, self.geo
        mine = pl.ds(pl.multiple_of(at.core * geo.block, 16), geo.block)
        other = pl.ds(pl.multiple_of((1 - at.core) * geo.block, 16), geo.block)
        self.post("sib", self.part.at[:, other], self.sib_in, at.sib)
        self.post("rsib", self.part.at[:, self.rest], self.rsib_in, at.sib, self.no_rest)
        self.load = pltpu.make_async_copy(self.part.at[:, mine], self.acc, self.local.at[0])
        self.load.start()
        self.rload = pltpu.make_async_copy(self.part.at[:, self.rest], self.racc, self.local.at[1])
        pl.when(self.has_rest)(lambda: self.rload.start())

    def cores(self):
        at, geo = self.at, self.geo
        self.load.wait()
        self.take("sib", self.sib_in)
        for t in range(at.depth):
            add_rows(self.acc.at[t], self.sib_in.at[t], geo.block)
        self.post("diag", self.acc.at[:, self.c1(at.p_d)], self.plane_in.at[0], at.relay_dev)
        self.post("near", self.acc.at[:, self.c1(self.direct_p)], self.plane_in.at[1], at.relay_dev)

        def rest():
            self.rload.wait()
            self.make("rsib", self.rsib_in, self.rsib_in, at.sib).wait_recv()
            for t in range(at.depth):
                add_rows(self.racc.at[t], self.rsib_in.at[t], geo.unit)

        pl.when(self.has_rest)(rest)

    def line(self, step, name, acc, landing, rows, cond=None):
        at = self.at
        last = at.depth - 1
        right, left = last - step, step

        def go_right():
            @pl.when(at.z > 0)
            def _():
                self.make(f"{name}{right}", landing.at[right], landing.at[right], at.sib).wait_recv()
                add_rows(acc(right), landing.at[right], rows)

        def go_left():
            @pl.when(at.z < last)
            def _():
                self.make(f"{name}{left}", landing.at[left], landing.at[left], at.sib).wait_recv()
                add_rows(acc(left), landing.at[left], rows)

        is_right, is_left = both(at.z < right, cond), both(at.z > left, cond)
        under(is_right, go_right)
        self.post(f"{name}{right}", acc(right), landing.at[right], at.up(), is_right)
        under(is_left, go_left)
        self.post(f"{name}{left}", acc(left), landing.at[left], at.down(), both(at.z > left + 1, cond))
        self.post(f"{name}end{left}", acc(left), landing.at[at.depth], at.down(), both(at.z == left + 1, cond))

    def line_end(self, name, acc, landing, rows, cond=None):
        at = self.at
        last = at.depth - 1
        for t in range(at.depth):
            def from_below():
                self.make(f"{name}{t}", landing.at[t], landing.at[t], at.sib).wait_recv()
                add_rows(acc(t), landing.at[t], rows)

            def from_above():
                self.make(f"{name}end{t}", landing.at[at.depth], landing.at[at.depth], at.sib).wait_recv()
                add_rows(acc(t), landing.at[at.depth], rows)

            if t > 0:
                under(both(at.z == t, cond), from_below)
            if t < last:
                under(both(at.z == t, cond), from_above)

    def relay(self):
        at, geo = self.at, self.geo
        self.take("diag", self.plane_in.at[0])
        mine = self.c1(at.relay_from)
        for t in range(at.depth):
            add_rows(self.acc.at[t, mine], self.plane_in.at[0, t], geo.t1)
        self.post("relay", self.acc.at[:, mine], self.plane_in.at[2], self.owner_dev)

    def combine(self):
        at, geo = self.at, self.geo
        self.take("near", self.plane_in.at[1])
        self.take("relay", self.plane_in.at[2])
        mine = self.c1(at.p)
        for t in range(at.depth):
            add_rows_two(self.acc.at[t, mine], self.plane_in.at[1, t], self.plane_in.at[2, t], geo.t1)

    def line1(self, step):
        mine = self.c1(self.at.p)
        self.line(step, "z", lambda t: self.acc.at[t, mine], self.z_in, self.geo.t1)

    def line1_end(self):
        at, geo = self.at, self.geo
        mine = self.c1(at.p)
        self.line_end("z", lambda t: self.acc.at[t, mine], self.z_in, geo.t1)
        self.spread("a", self.acc.at[at.z, mine], self.o1)

    def line2(self, step):
        at, geo = self.at, self.geo
        if geo.t2:
            span = pl.ds(4 * geo.t1, 4 * geo.t2)
            self.line(step, "w", lambda t: self.acc.at[t, span], self.z2_in, 4 * geo.t2)
        self.line(step, "r", lambda t: self.racc.at[t], self.rz_in, geo.unit, self.has_rest)

    def line2_end(self):
        at, geo = self.at, self.geo
        self.line_end("r", lambda t: self.racc.at[t], self.rz_in, geo.unit, self.has_rest)
        self.post("rx", self.racc.at[at.z], self.rplane_in.at[0], at.x_dev, self.has_rest)
        if geo.t2:
            span = pl.ds(4 * geo.t1, 4 * geo.t2)
            self.line_end("w", lambda t: self.acc.at[t, span], self.z2_in, 4 * geo.t2)
            self.post("diag2", self.acc.at[at.z, self.c2(at.p_d)], self.plane2_in.at[0], at.relay_dev)
            self.post("near2", self.acc.at[at.z, self.c2(self.direct_p)], self.plane2_in.at[1], at.relay_dev)

    def relay2(self):
        at, geo = self.at, self.geo
        if geo.t2:
            self.take("diag2", self.plane2_in.at[0])
            mine = self.c2(at.relay_from)
            add_rows(self.acc.at[at.z, mine], self.plane2_in.at[0], geo.t2)
            self.post("relay2", self.acc.at[at.z, mine], self.plane2_in.at[2], self.owner_dev)

    def rest_x(self):
        at, geo = self.at, self.geo

        def rest():
            self.make("rx", self.rplane_in.at[0], self.rplane_in.at[0], at.sib).wait_recv()
            self.make("rx", self.racc.at[at.z], self.rplane_in.at[0], at.x_dev).wait_send()
            add_rows(self.racc.at[at.z], self.rplane_in.at[0], geo.unit)

        pl.when(self.has_rest)(rest)
        self.posts = [item for item in self.posts if item[0] != "rx"]
        self.post("ry", self.racc.at[at.z], self.rplane_in.at[1], at.y_dev, self.has_rest)

    def rest_y(self):
        at, geo = self.at, self.geo

        def rest():
            self.make("ry", self.rplane_in.at[1], self.rplane_in.at[1], at.sib).wait_recv()
            self.make("ry", self.racc.at[at.z], self.rplane_in.at[1], at.y_dev).wait_send()
            add_rows(self.racc.at[at.z], self.rplane_in.at[1], geo.unit)
            pltpu.make_async_copy(self.racc.at[at.z], self.out.at[self.rest], self.local.at[2]).start()

        pl.when(self.has_rest)(rest)
        self.posts = [item for item in self.posts if item[0] != "ry"]
        self.post("rout", self.racc.at[at.z], self.out.at[self.rest], at.sib, self.has_rest)

    def combine2(self):
        at, geo = self.at, self.geo
        if geo.t2:
            self.take("near2", self.plane2_in.at[1])
            self.take("relay2", self.plane2_in.at[2])
            mine = self.c2(at.p)
            add_rows_two(self.acc.at[at.z, mine], self.plane2_in.at[1], self.plane2_in.at[2], geo.t2)
            self.spread("b", self.acc.at[at.z, mine], self.o2)

    def spread(self, name, src, rows):
        at = self.at
        mine = rows(at.p, at.core)
        index = 3 if name == "a" else 4
        pltpu.make_async_copy(src, self.out.at[mine], self.local.at[index]).start()
        self.post(name + "x", src, self.out.at[mine], at.x_dev)
        self.post(name + "y", src, self.out.at[mine], at.y_dev)
        self.post(name + "s", src, self.out.at[mine], at.sib)

    def spread_relay(self, name, rows):
        at = self.at
        for far, place in ((name + "x", at.p_x), (name + "y", at.p_y)):
            here = self.out.at[rows(place, at.core)]
            self.take(far, here)
            self.post(far + "s", here, here, at.sib)
        here = self.out.at[rows(at.relay_from, at.core)]
        self.post(name + "d", here, here, at.relay_dev)

    def spread_last(self, name, rows):
        at = self.at
        here = self.out.at[rows(at.p_d, at.core)]
        self.take(name + "d", here)
        self.post(name + "ds", here, here, at.sib)

    def spread_end(self, name, src, rows):
        at = self.at
        for suffix, place in (("s", at.p), ("xs", at.p_x), ("ys", at.p_y), ("ds", at.p_d)):
            self.take(name + suffix, self.out.at[rows(place, 1 - at.core)])
        index = 3 if name == "a" else 4
        pltpu.make_async_copy(src, self.out.at[rows(at.p, at.core)], self.local.at[index]).wait()

    def finish(self):
        at = self.at
        self.spread_end("a", self.acc.at[at.z, self.c1(at.p)], self.o1)
        if self.geo.t2:
            self.spread_end("b", self.acc.at[at.z, self.c2(at.p)], self.o2)
        pl.when(self.has_rest)(
            lambda: pltpu.make_async_copy(self.racc.at[at.z], self.out.at[self.rest], self.local.at[2]).wait()
        )
        self.take("rout", self.out.at[self.rest], self.no_rest)

    def drain(self):
        for name, src, dst, device, cond in self.posts:
            under(cond, lambda: self.make(name, src, dst, device).wait_send())

    def stages(self):
        steps = range(self.at.depth - 1)
        has2 = bool(self.geo.t2)
        return [
            [self.cores],
            [functools.partial(self.line2, i) for i in steps[:1]] + [self.relay],
            [functools.partial(self.line2, i) for i in steps[1:]] + [self.combine],
            [self.line2_end] + [functools.partial(self.line1, i) for i in steps[:1]],
            [self.relay2, self.rest_x] + [functools.partial(self.line1, i) for i in steps[1:2]],
            [self.combine2, self.rest_y] + [functools.partial(self.line1, i) for i in steps[2:]],
            [self.line1_end] + ([functools.partial(self.spread_relay, "b", self.o2)] if has2 else []),
            [functools.partial(self.spread_relay, "a", self.o1)]
            + ([functools.partial(self.spread_last, "b", self.o2)] if has2 else []),
            [functools.partial(self.spread_last, "a", self.o1)],
            [self.finish],
        ]


def reduce_kernel(geos, lag, *refs):
    count = len(geos)
    parts, outs = refs[:count], refs[count : 2 * count]
    send, recv, local = refs[2 * count : 2 * count + 3]
    rest = list(refs[2 * count + 3 :])
    at = Place()
    at.greet()
    items = []
    for k, geo in enumerate(geos):
        size = 10 if geo.t2 else 8
        bufs, rest = rest[:size], rest[size:]
        items.append(
            Reduce(at, geo, parts[k], outs[k], k % 2, bufs, send.at[k], recv.at[k], local.at[k])
        )
    for item in items:
        item.begin()
    plan = []
    for k, item in enumerate(items):
        for s, todo in enumerate(item.stages()):
            plan.append((s + lag * k, k, todo))
    for _, _, todo in sorted(plan, key=lambda entry: entry[:2]):
        for do in todo:
            do()
    for item in items:
        item.drain()


def reduce_grads(parts, line_parts, collective_id, lag=2):
    depth = lax.axis_size("fsdp")
    geos = [Geometry(item.shape[1], item.shape[2], b) for item, b in zip(parts, line_parts)]
    any_spec = pl.BlockSpec(memory_space=pl.ANY)
    count = len(parts)
    scratch = [
        pltpu.SemaphoreType.DMA((count, SLOTS)),
        pltpu.SemaphoreType.DMA((count, SLOTS)),
        pltpu.SemaphoreType.DMA((count, 5)),
    ]
    for geo in geos:
        scratch += geo.scratch(depth)
    return pl.pallas_call(
        functools.partial(reduce_kernel, geos, lag),
        out_shape=[jax.ShapeDtypeStruct(item.shape[1:], item.dtype) for item in parts],
        in_specs=[any_spec] * count,
        out_specs=[any_spec] * count,
        scratch_shapes=scratch,
        compiler_params=pltpu.CompilerParams(
            collective_id=collective_id, has_side_effects=True, vmem_limit_bytes=60 * 1024 * 1024
        ),
    )(*parts)
HEAD_DIM = 64


def normalize(values, scales, shifts):
    average = jnp.mean(values, axis=-1, keepdims=True)
    centred = values - average
    variance = jnp.mean(centred * centred, axis=-1, keepdims=True)
    return centred * lax.rsqrt(variance + 1e-05) * scales + shifts


def outer_sum(left_rows, right_rows):
    return lax.dot_general(
        left_rows, right_rows, (((0,), (0,)), ((), ())), preferred_element_type=jnp.float32
    )


def times_transpose(left_rows, weight_rows):
    return lax.dot_general(
        left_rows, weight_rows, (((1,), (1,)), ((), ())), preferred_element_type=jnp.float32
    )


def allowed_mask(positions, key_places, lengths):
    causal = (key_places[None, :] <= positions[:, None]) & (key_places[None, :] >= 0)
    inside = key_places[None, :] < lengths[:, None]
    return causal[None, None, :, :] & inside[:, None, None, :]


def attend_forward(queries, key_part, value_part, positions, lengths, score_scale):
    seq_count, row_count, head_count, head_width = queries.shape
    lowest = jnp.full((seq_count, head_count, row_count), -1e30, jnp.float32)
    key_places = jnp.arange(key_part.shape[1], dtype=jnp.int32)
    allowed = allowed_mask(positions, key_places, lengths)
    scores = (
        jnp.einsum("sqhe,skhe->shqk", queries, key_part, preferred_element_type=jnp.float32)
        * score_scale
    )
    scores = jnp.where(allowed, scores, -1e30)
    new_top = jnp.maximum(lowest, jnp.max(scores, axis=-1))
    exp_weights = jnp.where(allowed, jnp.exp(scores - new_top[..., None]), 0.0)
    running_total = jnp.sum(exp_weights, axis=-1)
    running_sum = jnp.einsum(
        "shqk,skhe->shqe",
        exp_weights.astype(jnp.bfloat16),
        value_part,
        preferred_element_type=jnp.float32,
    )
    output = jnp.transpose(running_sum / running_total[..., None], (0, 2, 1, 3))
    return (output, new_top + jnp.log(running_total))


def block_terms(
    queries,
    grad_out,
    log_total,
    delta_row,
    key_part,
    value_part,
    first_key,
    positions,
    lengths,
    score_scale,
):
    key_places = first_key + jnp.arange(key_part.shape[1], dtype=jnp.int32)
    allowed = allowed_mask(positions, key_places, lengths)
    scores = (
        jnp.einsum("sqhe,skhe->shqk", queries, key_part, preferred_element_type=jnp.float32)
        * score_scale
    )
    scores = jnp.where(allowed, scores, -1e30)
    probability = jnp.where(allowed, jnp.exp(scores - log_total[..., None]), 0.0)
    grad_probs = jnp.einsum(
        "sqhe,skhe->shqk", grad_out, value_part, preferred_element_type=jnp.float32
    )
    grad_scores = (probability * (grad_probs - delta_row[..., None])).astype(jnp.bfloat16)
    query_add = (
        jnp.einsum("shqk,skhe->sqhe", grad_scores, key_part, preferred_element_type=jnp.float32)
        * score_scale
    )
    key_add = (
        jnp.einsum("shqk,sqhe->skhe", grad_scores, queries, preferred_element_type=jnp.float32)
        * score_scale
    )
    value_add = jnp.einsum(
        "shqk,sqhe->skhe",
        probability.astype(jnp.bfloat16),
        grad_out,
        preferred_element_type=jnp.float32,
    )
    return (query_add, key_add, value_add)


def pack_small(ln_gain, ln_bias, b_qv, b_out, b_up, b_down):
    layers, _, part = ln_gain.shape
    return jnp.concatenate(
        [
            ln_gain.reshape(layers, 2, part),
            ln_bias.reshape(layers, 2, part),
            b_qv.reshape(layers, 2, part),
            b_out.reshape(layers, 1, part),
            b_down.reshape(layers, 1, part),
            b_up.reshape(layers, 4, part),
        ],
        axis=1,
    )


def unpack_small(whole):
    depth, _, part = whole.shape
    flat = jnp.transpose(whole[:, :8], (1, 0, 2)).reshape(8, depth * part)
    up_bias = whole[:, 8:].reshape(depth * 4 * part)
    return flat[0:2], flat[2:4], flat[4:6], flat[6], flat[7], up_bias


def small_rows(gains, shifts, mix_bias, out_bias, down_bias, up_bias, depth):
    width = gains.shape[-1]
    flat = jnp.concatenate([gains, shifts, mix_bias, out_bias[None], down_bias[None]], axis=0)
    flat = jnp.transpose(flat.reshape(8, depth, width // depth), (1, 0, 2))
    return jnp.concatenate([flat, up_bias.reshape(depth, 4, width // depth)], axis=1)


def fast_mesh(rows):
    return lax.axis_size("ctx") == 8 and rows % 272 == 0


def gather_all(weights, small):
    flat = [item for layer in weights for item in layer]
    layers = len(weights)
    if fast_mesh(flat[0].shape[0]):
        packed = small.reshape(layers * small.shape[1], small.shape[2])
        *wholes, small_all = gather_weights(flat, packed)
        small_all = small_all.reshape(-1, layers, small.shape[1], small.shape[2])
        wholes = [item.reshape(-1, item.shape[2]) for item in wholes]
    else:
        wholes = [lax.all_gather(item, "fsdp", axis=0, tiled=True) for item in flat]
        small_all = lax.all_gather(small, "fsdp", axis=0)
    return [wholes[4 * i : 4 * i + 4] for i in range(layers)], [small_all[:, i] for i in range(layers)]


def reduce_layer(grads, collective_id):
    depth = lax.axis_size("fsdp")
    if fast_mesh(grads[0].shape[0] // depth):
        parts = [item.reshape(depth, item.shape[0] // depth, item.shape[1]) for item in grads]
        return reduce_grads(parts, [0] * len(parts), collective_id, lag=1)
    shards_now = [
        lax.psum_scatter(item, "fsdp", scatter_dimension=0, tiled=True) for item in grads
    ]
    return [lax.psum(item, "ctx") for item in shards_now]


def shards(
    tokens,
    lengths,
    cotangent,
    ln_gain,
    ln_bias,
    w_qkv,
    b_qv,
    w_out,
    b_out,
    w_up,
    b_up,
    w_down,
    b_down,
):
    seq_count, row_count, model_width = tokens.shape
    head_width = HEAD_DIM
    head_count = model_width // head_width
    score_scale = head_width ** (-0.5)
    ctx_index = lax.axis_index("ctx")
    depth = lax.axis_size("fsdp")
    positions = ctx_index * row_count + jnp.arange(row_count, dtype=jnp.int32)
    valid_rows = (positions[None, :] < lengths[:, None]).astype(jnp.float32)[..., None]
    flat_rows = seq_count * row_count
    split_shape = (seq_count, row_count, head_count, head_width)
    layer_total = ln_gain.shape[0]
    hidden = tokens.astype(jnp.float32).reshape(flat_rows, model_width)
    small = pack_small(ln_gain, ln_bias, b_qv, b_out, b_up, b_down)
    weights, smalls = gather_all(
        [(w_qkv[i], w_out[i], w_up[i], w_down[i]) for i in range(layer_total)], small
    )
    kept_layers = []
    for layer_index in range(layer_total):
        mix_weight, out_weight, up_weight, down_weight = weights[layer_index]
        gain_rows, shift_rows, mix_bias, out_bias, down_bias, up_bias = unpack_small(
            smalls[layer_index].astype(jnp.float32)
        )
        normed_first = normalize(hidden, gain_rows[0], shift_rows[0]).astype(jnp.bfloat16)
        mixed_rows = jnp.dot(normed_first, mix_weight, preferred_element_type=jnp.float32)
        queries = (
            (mixed_rows[:, :model_width] + mix_bias[0]).astype(jnp.bfloat16).reshape(split_shape)
        )
        key_rows = (
            mixed_rows[:, model_width : 2 * model_width].astype(jnp.bfloat16).reshape(split_shape)
        )
        value_rows = (
            (mixed_rows[:, 2 * model_width :] + mix_bias[1])
            .astype(jnp.bfloat16)
            .reshape(split_shape)
        )
        key_part = lax.all_gather(key_rows, "ctx", axis=1, tiled=True)
        value_part = lax.all_gather(value_rows, "ctx", axis=1, tiled=True)
        output, log_total = attend_forward(
            queries, key_part, value_part, positions, lengths, score_scale
        )
        output = output.reshape(flat_rows, model_width)
        attended = output.astype(jnp.bfloat16)
        middle = (
            hidden + jnp.dot(attended, out_weight, preferred_element_type=jnp.float32) + out_bias
        )
        normed_second = normalize(middle, gain_rows[1], shift_rows[1]).astype(jnp.bfloat16)
        upper_pre = (
            jnp.dot(normed_second, up_weight, preferred_element_type=jnp.float32) + up_bias
        )
        active = jax.nn.gelu(upper_pre).astype(jnp.bfloat16)
        kept_layers.append(
            (
                hidden,
                normed_first,
                queries,
                key_part,
                value_part,
                output,
                log_total,
                attended,
                middle,
                normed_second,
                upper_pre,
                active,
                gain_rows,
                shift_rows,
            )
        )
        hidden = (
            middle + jnp.dot(active, down_weight, preferred_element_type=jnp.float32) + down_bias
        )
    activations = (valid_rows * hidden.reshape(seq_count, row_count, model_width)).astype(
        jnp.bfloat16
    )
    grad_hidden = (cotangent.astype(jnp.float32) * valid_rows).reshape(flat_rows, model_width)
    big_grads = [None] * layer_total
    small_grads = [None] * layer_total
    for layer_index in reversed(range(layer_total)):
        (
            hidden_in,
            normed_first,
            queries,
            key_part,
            value_part,
            output,
            log_total,
            attended,
            middle,
            normed_second,
            upper_pre,
            active,
            gain_rows,
            shift_rows,
        ) = kept_layers[layer_index]
        mix_weight, out_weight, up_weight, down_weight = weights[layer_index]
        grad_branch = grad_hidden.astype(jnp.bfloat16)
        down_bias_grad = jnp.sum(grad_branch.astype(jnp.float32), axis=0)
        down_grad = outer_sum(active, grad_branch)
        grad_active = times_transpose(grad_branch, down_weight)
        unused_gelu, gelu_pull = jax.vjp(jax.nn.gelu, upper_pre)
        grad_upper = gelu_pull(grad_active)[0].astype(jnp.bfloat16)
        up_bias_grad = jnp.sum(grad_upper.astype(jnp.float32), axis=0)
        up_grad = outer_sum(normed_second, grad_upper)
        grad_normed = times_transpose(grad_upper, up_weight)
        unused_norm, norm_pull = jax.vjp(normalize, middle, gain_rows[1], shift_rows[1])
        grad_middle, gain_second, shift_second = norm_pull(grad_normed)
        grad_middle = grad_middle + grad_hidden
        grad_attn = grad_middle.astype(jnp.bfloat16)
        out_bias_grad = jnp.sum(grad_attn.astype(jnp.float32), axis=0)
        out_grad = outer_sum(attended, grad_attn)
        grad_output = times_transpose(grad_attn, out_weight).astype(jnp.bfloat16)
        delta_row = jnp.transpose(
            jnp.sum((grad_output.astype(jnp.float32) * output).reshape(split_shape), axis=-1),
            (0, 2, 1),
        )
        grad_heads = grad_output.reshape(split_shape)
        query_grad, key_add, value_add = block_terms(
            queries,
            grad_heads,
            log_total,
            delta_row,
            key_part,
            value_part,
            0,
            positions,
            lengths,
            score_scale,
        )
        key_low = lax.psum_scatter(
            key_add.astype(jnp.bfloat16), "ctx", scatter_dimension=1, tiled=True
        ).reshape(flat_rows, model_width)
        value_low = lax.psum_scatter(
            value_add.astype(jnp.bfloat16), "ctx", scatter_dimension=1, tiled=True
        ).reshape(flat_rows, model_width)
        query_low = query_grad.reshape(flat_rows, model_width).astype(jnp.bfloat16)
        grad_mixed = jnp.concatenate([query_low, key_low, value_low], axis=1)
        mix_bias_grad = jnp.stack(
            [
                jnp.sum(query_low.astype(jnp.float32), axis=0),
                jnp.sum(value_low.astype(jnp.float32), axis=0),
            ]
        )
        mix_grad = outer_sum(normed_first, grad_mixed)
        grad_normed_first = times_transpose(grad_mixed, mix_weight)
        unused_first, first_pull = jax.vjp(normalize, hidden_in, gain_rows[0], shift_rows[0])
        grad_input, gain_first, shift_first = first_pull(grad_normed_first)
        grad_hidden = grad_input + grad_middle
        big_grads[layer_index] = reduce_layer(
            [item.astype(jnp.bfloat16) for item in (up_grad, down_grad, mix_grad, out_grad)],
            1 + layer_index,
        )
        small_grads[layer_index] = small_rows(
            jnp.stack([gain_first, gain_second]),
            jnp.stack([shift_first, shift_second]),
            mix_bias_grad,
            out_bias_grad,
            down_bias_grad,
            up_bias_grad,
            depth,
        )
    input_grad = grad_hidden.reshape(seq_count, row_count, model_width)
    packed = jnp.stack(small_grads).astype(jnp.bfloat16)
    total = lax.psum(packed, ("fsdp", "ctx"))
    own = lax.dynamic_index_in_dim(total, lax.axis_index("fsdp"), 1, keepdims=False)
    own = own.astype(jnp.float32)

    def whole(member):
        return jnp.stack([big_grads[i][member].astype(jnp.float32) for i in range(layer_total)])

    return (
        activations,
        input_grad,
        own[:, 0:2],
        own[:, 2:4],
        whole(2),
        own[:, 4:6],
        whole(3),
        own[:, 6],
        whole(0),
        own[:, 8:].reshape(layer_total, -1),
        whole(1),
        own[:, 7],
    )


def solution(mesh):
    placed = (
        P("fsdp", "ctx", None),
        P("fsdp"),
        P("fsdp", "ctx", None),
        P(None, None, "fsdp"),
        P(None, None, "fsdp"),
        P(None, "fsdp", None),
        P(None, None, "fsdp"),
        P(None, "fsdp", None),
        P(None, "fsdp"),
        P(None, "fsdp", None),
        P(None, "fsdp"),
        P(None, "fsdp", None),
        P(None, "fsdp"),
    )
    return jax.shard_map(
        shards,
        mesh=mesh,
        in_specs=placed,
        out_specs=(
            P("fsdp", "ctx", None),
            P("fsdp", "ctx", None),
            P(None, None, "fsdp"),
            P(None, None, "fsdp"),
            P(None, "fsdp", None),
            P(None, None, "fsdp"),
            P(None, "fsdp", None),
            P(None, "fsdp"),
            P(None, "fsdp", None),
            P(None, "fsdp"),
            P(None, "fsdp", None),
            P(None, "fsdp"),
        ),
        check_vma=False,
    )
```

```python
import functools

import jax
import jax.numpy as jnp
from jax import lax
from jax.experimental import pallas as pl
from jax.experimental.pallas import tpu as pltpu
from jax.sharding import PartitionSpec as P

MESH = pl.DeviceIdType.MESH


class Place:
    def __init__(self):
        self.depth = lax.axis_size("fsdp")
        self.z = lax.axis_index("fsdp")
        self.c8 = lax.axis_index("ctx")
        self.core = lax.rem(self.c8, 2)
        self.p = self.c8 // 2
        self.px = lax.rem(self.p, 2)
        self.py = self.p // 2
        self.sib = {"ctx": self.c8 + 1 - 2 * self.core}
        self.x_dev = {"ctx": self.c8 + 2 - 4 * self.px}
        self.y_dev = {"ctx": self.c8 + 4 - 8 * self.py}
        self.p_x = self.p + 1 - 2 * self.px
        self.p_y = self.p + 2 - 4 * self.py
        self.p_d = 3 - self.p
        self.relay_from = self.p + (1 - self.core) * (1 - 2 * self.px) + self.core * (2 - 4 * self.py)
        self.relay_dev = {
            "ctx": self.c8 + (1 - self.core) * (4 - 8 * self.py) + self.core * (2 - 4 * self.px)
        }

    def up(self):
        return {"fsdp": self.z + 1}

    def down(self):
        return {"fsdp": self.z - 1}

    def greet(self):
        barrier = pltpu.get_barrier_semaphore()
        for device in (self.sib, self.x_dev, self.y_dev):
            pl.semaphore_signal(barrier, inc=1, device_id=device, device_id_type=MESH)

        @pl.when(self.z > 0)
        def _():
            pl.semaphore_signal(barrier, inc=1, device_id=self.down(), device_id_type=MESH)

        @pl.when(self.z < self.depth - 1)
        def _():
            pl.semaphore_signal(barrier, inc=1, device_id=self.up(), device_id_type=MESH)

        below = jnp.where(self.z > 0, 1, 0)
        above = jnp.where(self.z < self.depth - 1, 1, 0)
        pl.semaphore_wait(barrier, 3 + below + above)


def remote(src, dst, send_sem, recv_sem, device):
    return pltpu.make_async_remote_copy(
        src_ref=src, dst_ref=dst, send_sem=send_sem, recv_sem=recv_sem, device_id=device, device_id_type=MESH
    )


class Gather:
    def __init__(self, at, own, whole, left_core, send, recv):
        self.at, self.own, self.whole = at, own, whole
        self.send, self.recv = send, recv
        rows = own.shape[0]
        self.rows = rows
        unit = rows // 17
        self.t1 = 2 * unit
        self.block = 8 * unit
        self.rest = pl.ds(16 * unit, unit)
        self.has_rest = at.core == left_core

    def t1_rows(self, p, core=None):
        core = self.at.core if core is None else core
        return pl.ds(pl.multiple_of(core * self.block + p * self.t1, 16), self.t1)

    def block_rows(self, core):
        return pl.ds(pl.multiple_of(core * self.block, 16), self.block)

    def copy(self, kind, shard, rows, device, src=None, second=False):
        depth = self.at.depth
        slot = kind * depth + shard
        place = self.place(shard, rows)
        src = place if src is None else src
        send = self.send.at[(8 * depth + kind) if second else slot]
        return remote(src, place, send, self.recv.at[slot], device)

    def place(self, shard, rows):
        first = pl.multiple_of(shard * self.rows + rows.start, 16)
        return self.whole.at[pl.ds(first, rows.size)]

    def start(self):
        at = self.at
        mine = self.t1_rows(at.p)

        @pl.when(at.z < at.depth - 1)
        def _():
            self.copy(0, at.z, mine, at.up(), self.own.at[mine]).start()

            @pl.when(self.has_rest)
            def _():
                self.copy(1, at.z, self.rest, at.up(), self.own.at[self.rest]).start()

        @pl.when(at.z > 0)
        def _():
            self.copy(0, at.z, mine, at.down(), self.own.at[mine], True).start()

            @pl.when(self.has_rest)
            def _():
                self.copy(1, at.z, self.rest, at.down(), self.own.at[self.rest], True).start()

    def cases(self, step, do):
        at = self.at

        @pl.when(at.z - 1 - step >= 0)
        def _():
            do(at.z - 1 - step, at.z < at.depth - 1, at.up())

        @pl.when(at.z + 1 + step < at.depth)
        def _():
            do(at.z + 1 + step, at.z > 0, at.down())

    def arrive(self, step):
        at = self.at
        mine = self.t1_rows(at.p)

        def do(shard, onward, device):
            self.copy(0, shard, mine, at.sib).wait_recv()

            @pl.when(onward)
            def _():
                self.copy(0, shard, mine, device).start()

            self.copy(2, shard, mine, at.x_dev).start()
            self.copy(3, shard, mine, at.y_dev).start()

            @pl.when(self.has_rest)
            def _():
                self.copy(1, shard, self.rest, at.sib).wait_recv()

                @pl.when(onward)
                def _():
                    self.copy(1, shard, self.rest, device).start()

                self.copy(5, shard, self.rest, at.sib).start()

        self.cases(step, do)

    def plane(self, step):
        at = self.at

        def do(shard, onward, device):
            self.copy(2, shard, self.t1_rows(at.p_x), at.sib).wait_recv()
            self.copy(3, shard, self.t1_rows(at.p_y), at.sib).wait_recv()
            self.copy(4, shard, self.t1_rows(at.relay_from), at.relay_dev).start()

        self.cases(step, do)

    def share(self, step):
        at = self.at

        def do(shard, onward, device):
            self.copy(4, shard, self.t1_rows(at.p_d), at.sib).wait_recv()
            self.copy(6, shard, self.block_rows(at.core), at.sib).start()

        self.cases(step, do)

    def finish(self):
        at = self.at
        mine = self.t1_rows(at.p)

        def do(shard, onward, device):
            self.copy(6, shard, self.block_rows(1 - at.core), at.sib).wait_recv()

            @pl.when(jnp.logical_not(self.has_rest))
            def _():
                self.copy(5, shard, self.rest, at.sib).wait_recv()

        for step in range(at.depth - 1):
            self.cases(step, do)

    def drain(self):
        at = self.at
        mine = self.t1_rows(at.p)

        @pl.when(at.z < at.depth - 1)
        def _():
            self.copy(0, at.z, mine, at.up(), self.own.at[mine]).wait_send()

            @pl.when(self.has_rest)
            def _():
                self.copy(1, at.z, self.rest, at.up(), self.own.at[self.rest]).wait_send()

        @pl.when(at.z > 0)
        def _():
            self.copy(0, at.z, mine, at.down(), self.own.at[mine], True).wait_send()

            @pl.when(self.has_rest)
            def _():
                self.copy(1, at.z, self.rest, at.down(), self.own.at[self.rest], True).wait_send()

        def do(shard, onward, device):
            @pl.when(onward)
            def _():
                self.copy(0, shard, mine, device).wait_send()

                @pl.when(self.has_rest)
                def _():
                    self.copy(1, shard, self.rest, device).wait_send()

            self.copy(2, shard, mine, at.x_dev).wait_send()
            self.copy(3, shard, mine, at.y_dev).wait_send()
            self.copy(4, shard, self.t1_rows(at.relay_from), at.relay_dev).wait_send()
            self.copy(6, shard, self.block_rows(at.core), at.sib).wait_send()

            @pl.when(self.has_rest)
            def _():
                self.copy(5, shard, self.rest, at.sib).wait_send()

        for step in range(at.depth - 1):
            self.cases(step, do)


def both(*conds):
    conds = [c for c in conds if c is not None]
    if not conds:
        return None
    total = conds[0]
    for c in conds[1:]:
        total = jnp.logical_and(total, c)
    return total


def under(cond, do):
    if cond is None:
        do()
    else:
        pl.when(cond)(do)


def add_rows(acc, extra, rows):
    def step(i, carry):
        piece = pl.ds(pl.multiple_of(i * 16, 16), 16)
        acc[piece, :] = acc[piece, :] + extra[piece, :]
        return carry

    lax.fori_loop(0, rows // 16, step, 0)


def add_rows_two(acc, one, two, rows):
    def step(i, carry):
        piece = pl.ds(pl.multiple_of(i * 16, 16), 16)
        total = acc[piece, :].astype(jnp.float32) + one[piece, :].astype(jnp.float32)
        acc[piece, :] = (total + two[piece, :].astype(jnp.float32)).astype(jnp.bfloat16)
        return carry

    lax.fori_loop(0, rows // 16, step, 0)


class Geometry:
    def __init__(self, rows, cols, line_part):
        self.rows, self.cols = rows, cols
        unit = rows // 17
        self.unit = unit
        self.block = 8 * unit
        self.t2 = line_part
        self.t1 = 2 * unit - line_part

    def scratch(self, depth):
        cols = self.cols
        vm = lambda *shape: pltpu.VMEM(shape + (cols,), jnp.bfloat16)
        out = [
            vm(depth, self.block),
            vm(depth, self.block),
            vm(3, depth, self.t1),
            vm(depth + 1, self.t1),
            vm(depth, self.unit),
            vm(depth + 1, self.unit),
            vm(depth, self.unit),
            vm(2, self.unit),
        ]
        if self.t2:
            out += [vm(depth + 1, 4 * self.t2), vm(3, self.t2)]
        return out


SLOTS = 48


class Reduce:
    def __init__(self, at, geo, part, out, left_core, bufs, send, recv, local):
        self.at, self.geo, self.part, self.out = at, geo, part, out
        self.acc, self.sib_in, self.plane_in, self.z_in, self.racc, self.rz_in, self.rsib_in, self.rplane_in = bufs[:8]
        if geo.t2:
            self.z2_in, self.plane2_in = bufs[8:]
        self.send, self.recv, self.local = send, recv, local
        self.has_rest = at.core == left_core
        self.no_rest = at.core != left_core
        self.rest = pl.ds(16 * geo.unit, geo.unit)
        self.names, self.posts = {}, []
        core, p = at.core, at.p
        self.direct_p = p + (1 - core) * (2 - 4 * at.py) + core * (1 - 2 * at.px)
        self.owner_dev = {
            "ctx": at.c8 + (1 - core) * (2 - 4 * at.px) + core * (4 - 8 * at.py)
        }

    def slot(self, name):
        return self.names.setdefault(name, len(self.names))

    def make(self, name, src, dst, device):
        i = self.slot(name)
        return remote(src, dst, self.send.at[i], self.recv.at[i], device)

    def post(self, name, src, dst, device, cond=None):
        under(cond, lambda: self.make(name, src, dst, device).start())
        self.posts.append((name, src, dst, device, cond))

    def take(self, name, dst, cond=None):
        under(cond, lambda: self.make(name, dst, dst, self.at.sib).wait_recv())

    def c1(self, p):
        return pl.ds(pl.multiple_of(p * self.geo.t1, 16), self.geo.t1)

    def c2(self, p):
        return pl.ds(pl.multiple_of(4 * self.geo.t1 + p * self.geo.t2, 16), self.geo.t2)

    def o1(self, p, core):
        return pl.ds(pl.multiple_of(core * self.geo.block + p * self.geo.t1, 16), self.geo.t1)

    def o2(self, p, core):
        return pl.ds(
            pl.multiple_of(core * self.geo.block + 4 * self.geo.t1 + p * self.geo.t2, 16), self.geo.t2
        )

    def begin(self):
        at, geo = self.at, self.geo
        mine = pl.ds(pl.multiple_of(at.core * geo.block, 16), geo.block)
        other = pl.ds(pl.multiple_of((1 - at.core) * geo.block, 16), geo.block)
        self.post("sib", self.part.at[:, other], self.sib_in, at.sib)
        self.post("rsib", self.part.at[:, self.rest], self.rsib_in, at.sib, self.no_rest)
        self.load = pltpu.make_async_copy(self.part.at[:, mine], self.acc, self.local.at[0])
        self.load.start()
        self.rload = pltpu.make_async_copy(self.part.at[:, self.rest], self.racc, self.local.at[1])
        pl.when(self.has_rest)(lambda: self.rload.start())

    def cores(self):
        at, geo = self.at, self.geo
        self.load.wait()
        self.take("sib", self.sib_in)
        for t in range(at.depth):
            add_rows(self.acc.at[t], self.sib_in.at[t], geo.block)
        self.post("diag", self.acc.at[:, self.c1(at.p_d)], self.plane_in.at[0], at.relay_dev)
        self.post("near", self.acc.at[:, self.c1(self.direct_p)], self.plane_in.at[1], at.relay_dev)

        def rest():
            self.rload.wait()
            self.make("rsib", self.rsib_in, self.rsib_in, at.sib).wait_recv()
            for t in range(at.depth):
                add_rows(self.racc.at[t], self.rsib_in.at[t], geo.unit)

        pl.when(self.has_rest)(rest)

    def line(self, step, name, acc, landing, rows, cond=None):
        at = self.at
        last = at.depth - 1
        right, left = last - step, step

        def go_right():
            @pl.when(at.z > 0)
            def _():
                self.make(f"{name}{right}", landing.at[right], landing.at[right], at.sib).wait_recv()
                add_rows(acc(right), landing.at[right], rows)

        def go_left():
            @pl.when(at.z < last)
            def _():
                self.make(f"{name}{left}", landing.at[left], landing.at[left], at.sib).wait_recv()
                add_rows(acc(left), landing.at[left], rows)

        is_right, is_left = both(at.z < right, cond), both(at.z > left, cond)
        under(is_right, go_right)
        self.post(f"{name}{right}", acc(right), landing.at[right], at.up(), is_right)
        under(is_left, go_left)
        self.post(f"{name}{left}", acc(left), landing.at[left], at.down(), both(at.z > left + 1, cond))
        self.post(f"{name}end{left}", acc(left), landing.at[at.depth], at.down(), both(at.z == left + 1, cond))

    def line_end(self, name, acc, landing, rows, cond=None):
        at = self.at
        last = at.depth - 1
        for t in range(at.depth):
            def from_below():
                self.make(f"{name}{t}", landing.at[t], landing.at[t], at.sib).wait_recv()
                add_rows(acc(t), landing.at[t], rows)

            def from_above():
                self.make(f"{name}end{t}", landing.at[at.depth], landing.at[at.depth], at.sib).wait_recv()
                add_rows(acc(t), landing.at[at.depth], rows)

            if t > 0:
                under(both(at.z == t, cond), from_below)
            if t < last:
                under(both(at.z == t, cond), from_above)

    def relay(self):
        at, geo = self.at, self.geo
        self.take("diag", self.plane_in.at[0])
        mine = self.c1(at.relay_from)
        for t in range(at.depth):
            add_rows(self.acc.at[t, mine], self.plane_in.at[0, t], geo.t1)
        self.post("relay", self.acc.at[:, mine], self.plane_in.at[2], self.owner_dev)

    def combine(self):
        at, geo = self.at, self.geo
        self.take("near", self.plane_in.at[1])
        self.take("relay", self.plane_in.at[2])
        mine = self.c1(at.p)
        for t in range(at.depth):
            add_rows_two(self.acc.at[t, mine], self.plane_in.at[1, t], self.plane_in.at[2, t], geo.t1)

    def line1(self, step):
        mine = self.c1(self.at.p)
        self.line(step, "z", lambda t: self.acc.at[t, mine], self.z_in, self.geo.t1)

    def line1_end(self):
        at, geo = self.at, self.geo
        mine = self.c1(at.p)
        self.line_end("z", lambda t: self.acc.at[t, mine], self.z_in, geo.t1)
        self.spread("a", self.acc.at[at.z, mine], self.o1)

    def line2(self, step):
        at, geo = self.at, self.geo
        if geo.t2:
            span = pl.ds(4 * geo.t1, 4 * geo.t2)
            self.line(step, "w", lambda t: self.acc.at[t, span], self.z2_in, 4 * geo.t2)
        self.line(step, "r", lambda t: self.racc.at[t], self.rz_in, geo.unit, self.has_rest)

    def line2_end(self):
        at, geo = self.at, self.geo
        self.line_end("r", lambda t: self.racc.at[t], self.rz_in, geo.unit, self.has_rest)
        self.post("rx", self.racc.at[at.z], self.rplane_in.at[0], at.x_dev, self.has_rest)
        if geo.t2:
            span = pl.ds(4 * geo.t1, 4 * geo.t2)
            self.line_end("w", lambda t: self.acc.at[t, span], self.z2_in, 4 * geo.t2)
            self.post("diag2", self.acc.at[at.z, self.c2(at.p_d)], self.plane2_in.at[0], at.relay_dev)
            self.post("near2", self.acc.at[at.z, self.c2(self.direct_p)], self.plane2_in.at[1], at.relay_dev)

    def relay2(self):
        at, geo = self.at, self.geo
        if geo.t2:
            self.take("diag2", self.plane2_in.at[0])
            mine = self.c2(at.relay_from)
            add_rows(self.acc.at[at.z, mine], self.plane2_in.at[0], geo.t2)
            self.post("relay2", self.acc.at[at.z, mine], self.plane2_in.at[2], self.owner_dev)

    def rest_x(self):
        at, geo = self.at, self.geo

        def rest():
            self.make("rx", self.rplane_in.at[0], self.rplane_in.at[0], at.sib).wait_recv()
            self.make("rx", self.racc.at[at.z], self.rplane_in.at[0], at.x_dev).wait_send()
            add_rows(self.racc.at[at.z], self.rplane_in.at[0], geo.unit)

        pl.when(self.has_rest)(rest)
        self.posts = [item for item in self.posts if item[0] != "rx"]
        self.post("ry", self.racc.at[at.z], self.rplane_in.at[1], at.y_dev, self.has_rest)

    def rest_y(self):
        at, geo = self.at, self.geo

        def rest():
            self.make("ry", self.rplane_in.at[1], self.rplane_in.at[1], at.sib).wait_recv()
            self.make("ry", self.racc.at[at.z], self.rplane_in.at[1], at.y_dev).wait_send()
            add_rows(self.racc.at[at.z], self.rplane_in.at[1], geo.unit)
            pltpu.make_async_copy(self.racc.at[at.z], self.out.at[self.rest], self.local.at[2]).start()

        pl.when(self.has_rest)(rest)
        self.posts = [item for item in self.posts if item[0] != "ry"]
        self.post("rout", self.racc.at[at.z], self.out.at[self.rest], at.sib, self.has_rest)

    def combine2(self):
        at, geo = self.at, self.geo
        if geo.t2:
            self.take("near2", self.plane2_in.at[1])
            self.take("relay2", self.plane2_in.at[2])
            mine = self.c2(at.p)
            add_rows_two(self.acc.at[at.z, mine], self.plane2_in.at[1], self.plane2_in.at[2], geo.t2)
            self.spread("b", self.acc.at[at.z, mine], self.o2)

    def spread(self, name, src, rows):
        at = self.at
        mine = rows(at.p, at.core)
        index = 3 if name == "a" else 4
        pltpu.make_async_copy(src, self.out.at[mine], self.local.at[index]).start()
        self.post(name + "x", src, self.out.at[mine], at.x_dev)
        self.post(name + "y", src, self.out.at[mine], at.y_dev)
        self.post(name + "s", src, self.out.at[mine], at.sib)

    def spread_relay(self, name, rows):
        at = self.at
        for far, place in ((name + "x", at.p_x), (name + "y", at.p_y)):
            here = self.out.at[rows(place, at.core)]
            self.take(far, here)
            self.post(far + "s", here, here, at.sib)
        here = self.out.at[rows(at.relay_from, at.core)]
        self.post(name + "d", here, here, at.relay_dev)

    def spread_last(self, name, rows):
        at = self.at
        here = self.out.at[rows(at.p_d, at.core)]
        self.take(name + "d", here)
        self.post(name + "ds", here, here, at.sib)

    def spread_end(self, name, src, rows):
        at = self.at
        for suffix, place in (("s", at.p), ("xs", at.p_x), ("ys", at.p_y), ("ds", at.p_d)):
            self.take(name + suffix, self.out.at[rows(place, 1 - at.core)])
        index = 3 if name == "a" else 4
        pltpu.make_async_copy(src, self.out.at[rows(at.p, at.core)], self.local.at[index]).wait()

    def finish(self):
        at = self.at
        self.spread_end("a", self.acc.at[at.z, self.c1(at.p)], self.o1)
        if self.geo.t2:
            self.spread_end("b", self.acc.at[at.z, self.c2(at.p)], self.o2)
        pl.when(self.has_rest)(
            lambda: pltpu.make_async_copy(self.racc.at[at.z], self.out.at[self.rest], self.local.at[2]).wait()
        )
        self.take("rout", self.out.at[self.rest], self.no_rest)

    def drain(self):
        for name, src, dst, device, cond in self.posts:
            under(cond, lambda: self.make(name, src, dst, device).wait_send())

    def stages(self):
        steps = range(self.at.depth - 1)
        has2 = bool(self.geo.t2)
        return [
            [self.cores],
            [functools.partial(self.line2, i) for i in steps[:1]] + [self.relay],
            [functools.partial(self.line2, i) for i in steps[1:]] + [self.combine],
            [self.line2_end] + [functools.partial(self.line1, i) for i in steps[:1]],
            [self.relay2, self.rest_x] + [functools.partial(self.line1, i) for i in steps[1:2]],
            [self.combine2, self.rest_y] + [functools.partial(self.line1, i) for i in steps[2:]],
            [self.line1_end] + ([functools.partial(self.spread_relay, "b", self.o2)] if has2 else []),
            [functools.partial(self.spread_relay, "a", self.o1)]
            + ([functools.partial(self.spread_last, "b", self.o2)] if has2 else []),
            [functools.partial(self.spread_last, "a", self.o1)],
            [self.finish],
        ]


def reduce_kernel(geos, lag, *refs):
    count = len(geos)
    parts, outs = refs[:count], refs[count : 2 * count]
    send, recv, local = refs[2 * count : 2 * count + 3]
    rest = list(refs[2 * count + 3 :])
    at = Place()
    at.greet()
    items = []
    for k, geo in enumerate(geos):
        size = 10 if geo.t2 else 8
        bufs, rest = rest[:size], rest[size:]
        items.append(
            Reduce(at, geo, parts[k], outs[k], k % 2, bufs, send.at[k], recv.at[k], local.at[k])
        )
    for item in items:
        item.begin()
    plan = []
    for k, item in enumerate(items):
        for s, todo in enumerate(item.stages()):
            plan.append((s + lag * k, k, todo))
    for _, _, todo in sorted(plan, key=lambda entry: entry[:2]):
        for do in todo:
            do()
    for item in items:
        item.drain()


def reduce_grads(parts, line_parts, collective_id, lag=2):
    depth = lax.axis_size("fsdp")
    geos = [Geometry(item.shape[1], item.shape[2], b) for item, b in zip(parts, line_parts)]
    any_spec = pl.BlockSpec(memory_space=pl.ANY)
    count = len(parts)
    scratch = [
        pltpu.SemaphoreType.DMA((count, SLOTS)),
        pltpu.SemaphoreType.DMA((count, SLOTS)),
        pltpu.SemaphoreType.DMA((count, 5)),
    ]
    for geo in geos:
        scratch += geo.scratch(depth)
    return pl.pallas_call(
        functools.partial(reduce_kernel, geos, lag),
        out_shape=[jax.ShapeDtypeStruct(item.shape[1:], item.dtype) for item in parts],
        in_specs=[any_spec] * count,
        out_specs=[any_spec] * count,
        scratch_shapes=scratch,
        compiler_params=pltpu.CompilerParams(
            collective_id=collective_id, has_side_effects=True, vmem_limit_bytes=60 * 1024 * 1024
        ),
    )(*parts)


HEAD_DIM = 64

LANES = 128
F32, BF16 = jnp.float32, jnp.bfloat16


def pad_lanes(n):
    return (n + LANES - 1) // LANES * LANES


def by_tiles(total, tile, do):
    count = total // tile

    def step(i, carry):
        do(pl.multiple_of(i * tile, tile), tile)
        return carry

    if count:
        lax.fori_loop(0, count, step, 0)
    if total % tile:
        do(count * tile, total % tile)


def row_norm(values):
    average = jnp.mean(values, axis=-1, keepdims=True)
    centred = values - average
    variance = jnp.mean(centred * centred, axis=-1, keepdims=True)
    scale = lax.rsqrt(variance + 1e-05)
    return centred * scale, scale


GELU_A = 0.7978845608028654
GELU_B = 0.044715


def gelu_of(u):
    return 0.5 * u * (1.0 + jnp.tanh(GELU_A * (u + GELU_B * u * u * u)))


class Context:
    def __init__(self, at, own, whole, rows, send, recv, local):
        self.at, self.own, self.whole, self.rows = at, own, whole, rows
        self.send, self.recv, self.local = send, recv, local
        core, p = at.core, at.p
        self.names, self.posts = {}, []

    def place(self, p, core):
        return self.whole.at[:, pl.ds(pl.multiple_of((2 * p + core) * self.rows, 16), self.rows)]

    def make(self, name, src, dst, device):
        i = self.names.setdefault(name, len(self.names))
        return remote(src, dst, self.send.at[i], self.recv.at[i], device)

    def post(self, name, src, dst, device):
        self.make(name, src, dst, device).start()
        self.posts.append((name, src, dst, device))

    def take(self, name, dst):
        self.make(name, dst, dst, self.at.sib).wait_recv()

    def start(self):
        at = self.at
        here = self.place(at.p, at.core)
        self.post("x", self.own, here, at.x_dev)
        self.post("y", self.own, here, at.y_dev)
        self.post("s", self.own, here, at.sib)
        self.keep = pltpu.make_async_copy(self.own, here, self.local)
        self.keep.start()

    def relay(self):
        at = self.at
        for name, p in (("x", at.p_x), ("y", at.p_y)):
            self.take(name, self.place(p, at.core))
        here = self.place(at.relay_from, at.core)
        self.post("d", here, here, at.relay_dev)
        for name, p in (("x", at.p_x), ("y", at.p_y)):
            here = self.place(p, at.core)
            self.post(name + "s", here, here, at.sib)

    def last(self):
        at = self.at
        here = self.place(at.p_d, at.core)
        self.take("d", here)
        self.post("ds", here, here, at.sib)

    def finish(self):
        at = self.at
        for name, p in (("s", at.p), ("xs", at.p_x), ("ys", at.p_y), ("ds", at.p_d)):
            self.take(name, self.place(p, 1 - at.core))
        self.keep.wait()

    def drain(self, own):
        for name, src, dst, device in self.posts:
            if (name in ("x", "y", "s")) == own:
                self.make(name, src, dst, device).wait_send()


KEPT = ("h", "a", "q", "kv", "o", "lse", "h1", "c", "u")


def kept_shapes(seqs, slots, rows, width, ff):
    wide = pad_lanes(width)
    flat = seqs * rows
    return {
        "h": ((flat, width), F32),
        "a": ((flat, width), BF16),
        "q": ((flat, wide), BF16),
        "kv": ((seqs, slots, 2 * wide), BF16),
        "o": ((flat, wide), BF16),
        "lse": ((flat * 2, LANES), F32),
        "h1": ((flat, width), F32),
        "c": ((flat, width), BF16),
        "u": ((flat, ff), F32),
    }


def key_bias(out, seqs, rows, slots, lengths, ctx):
    for s in range(seqs):
        key = lax.broadcasted_iota(jnp.int32, (rows, slots), 1)
        row = ctx * rows + lax.broadcasted_iota(jnp.int32, (rows, slots), 0)
        seen = jnp.logical_and(key <= row, key < lengths[s])
        out[s] = jnp.where(seen, 0.0, -1e30)


def two_heads(block):
    lane = lax.broadcasted_iota(jnp.int32, block.shape, 1)
    zero = jnp.zeros_like(block)
    return jnp.concatenate(
        [jnp.where(lane < HEAD_DIM, block, zero), jnp.where(lane < HEAD_DIM, zero, block)], axis=0
    )


def one_pair(stacked, rows):
    lane = lax.broadcasted_iota(jnp.int32, (rows, LANES), 1)
    return jnp.where(lane < HEAD_DIM, stacked[:rows], stacked[rows:])


def across(a, b):
    return lax.dot_general(a, b, (((1,), (1,)), ((), ())), preferred_element_type=F32)


def attend(s, first, count, q_ref, kv_ref, bias_ref, o_ref, lse_ref, rows, pairs, wide):
    def step(i, carry):
        j = first + i
        col = pl.ds(pl.multiple_of(j * LANES, LANES), LANES)
        q2 = two_heads(q_ref[pl.ds(s * rows, rows), col])
        keys = kv_ref[s, :, col]
        values = kv_ref[s, :, pl.ds(pl.multiple_of(wide + j * LANES, LANES), LANES)]
        bias = bias_ref[s]
        scores = across(q2, keys) * (HEAD_DIM ** (-0.5))
        scores = scores + jnp.concatenate([bias, bias], axis=0)
        top = jnp.max(scores, axis=-1, keepdims=True)
        weights = jnp.exp(scores - top)
        total = jnp.sum(weights, axis=-1, keepdims=True)
        out = jnp.dot(weights.astype(BF16), values, preferred_element_type=F32) / total
        o_ref[pl.ds(s * rows, rows), col] = one_pair(out, rows).astype(BF16)
        mine = s * pairs + j
        here = pl.ds(s * 2 * rows, 2 * rows)
        lane = lax.broadcasted_iota(jnp.int32, (2 * rows, LANES), 1)
        lse_ref[here, :] = jnp.where(lane == mine, top + jnp.log(total), lse_ref[here, :])
        return carry

    lax.fori_loop(0, count, step, 0)


def forward_kernel(dims, *refs):
    layers, seqs, rows, slots, width, ff, depth = dims
    flat, wide = seqs * rows, pad_lanes(width)
    pairs = wide // LANES
    refs = list(refs)

    def grab(n):
        out = refs[:n]
        del refs[:n]
        return out

    tokens, lengths, w_qkv, w_out, w_up, w_down, small = grab(7)
    acts, vecs = grab(2)
    wholes = grab(4 * layers)
    kept = [dict(zip(KEPT, grab(len(KEPT)))) for _ in range(layers)]
    (send, recv, small_send, small_recv, kv_send, kv_recv, load_sem, keep_sem, stage_sem) = grab(9)
    (small_all, vec, up_bias, h, a, q, own_kv, kv, bias, o, lse, h1, c, u, z) = grab(15)
    w_bufs = grab(4)
    at = Place()
    at.greet()

    owns = [ref.at[l] for l in range(layers) for ref in (w_qkv, w_out, w_up, w_down)]
    items = [Gather(at, owns[k], wholes[k], k % 2, send.at[k], recv.at[k]) for k in range(4 * layers)]
    contexts = [
        Context(at, own_kv, kept[l]["kv"], rows, kv_send.at[l], kv_recv.at[l], keep_sem.at[l, len(KEPT)])
        for l in range(layers)
    ]
    pending = {}

    def keep(l, name, src):
        copy = pltpu.make_async_copy(src, kept[l][name], keep_sem.at[l, KEPT.index(name)])
        copy.start()
        pending[(l, name)] = copy

    def free(l, name):
        copy = pending.pop((l, name), None)
        if copy is not None:
            copy.wait()

    def buffer(k):
        return w_bufs[k % 4]

    def own_copy(k, load):
        r = owns[k].shape[0]
        shard = lax.rem(at.z + k // 4, depth)
        place = buffer(k).at[pl.ds(pl.multiple_of(shard * r, 16), r)]
        if load:
            return pltpu.make_async_copy(owns[k], place, stage_sem.at[0, k])
        return pltpu.make_async_copy(place, items[k].place(at.z, pl.ds(0, r)), stage_sem.at[1, k])

    def own_load(k):
        own_copy(k, True).start()

    def own_store(k):
        own_copy(k, True).wait()
        own_copy(k, False).start()

    def own_done(k):
        own_copy(k, False).wait()

    def fetch(k):
        pltpu.make_async_copy(wholes[k], buffer(k), load_sem.at[k]).start()

    def ready(k):
        pltpu.make_async_copy(wholes[k], buffer(k), load_sem.at[k]).wait()

    def small_copy(shard, device, src=None, second=False):
        return remote(
            small_all.at[shard] if src is None else src,
            small_all.at[shard],
            small_send.at[depth if second else shard],
            small_recv.at[shard],
            device,
        )

    def small_start():
        @pl.when(at.z < depth - 1)
        def _():
            small_copy(at.z, at.up(), small).start()

        @pl.when(at.z > 0)
        def _():
            small_copy(at.z, at.down(), small, True).start()

        pltpu.make_async_copy(small, small_all.at[at.z], stage_sem.at[2, 0]).start()

    def small_take():
        def do(shard, onward, device):
            small_copy(shard, at.sib).wait_recv()
            pl.when(onward)(lambda: small_copy(shard, device).start())

        for step in range(depth - 1):
            items[0].cases(step, do)
        pltpu.make_async_copy(small, small_all.at[at.z], stage_sem.at[2, 0]).wait()

    def small_drain():
        @pl.when(at.z < depth - 1)
        def _():
            small_copy(at.z, at.up(), small).wait_send()

        @pl.when(at.z > 0)
        def _():
            small_copy(at.z, at.down(), small, True).wait_send()

        def do(shard, onward, device):
            pl.when(onward)(lambda: small_copy(shard, device).wait_send())

        for step in range(depth - 1):
            items[0].cases(step, do)

    def small_spread():
        part = width // depth
        per_layer = small_all.shape[1] // layers
        total = jnp.zeros((small_all.shape[1], wide), F32)
        room = jnp.zeros((small_all.shape[1], wide - small_all.shape[2]), F32)
        pieces = [small_all[i].astype(F32) for i in range(depth)]
        for i in range(depth):
            piece = jnp.concatenate([pieces[i], room], axis=1)
            total = total + (pltpu.roll(piece, i * part, 1) if i else piece)
        for l in range(layers):
            vec[l] = total[l * per_layer : l * per_layer + 8]
            vecs[l] = total[l * per_layer : l * per_layer + 8]
            wide_up = jnp.zeros((1, ff), F32)
            up_room = jnp.zeros((1, ff - small_all.shape[2]), F32)
            for i in range(depth):
                for r in range(4):
                    at_row = l * per_layer + 8 + r
                    piece = jnp.concatenate([pieces[i][at_row : at_row + 1], up_room], axis=1)
                    shift = (i * 4 + r) * part
                    wide_up = wide_up + (pltpu.roll(piece, shift, 1) if shift else piece)
            up_bias[l] = jnp.broadcast_to(wide_up, (8, ff))

    def row(l, i):
        return vec[l, pl.ds(i, 1), pl.ds(0, width)]

    def norm(l, i, src, dst):
        def do(first, size):
            here = pl.ds(first, size)
            unit, _ = row_norm(src[here, :])
            dst[here, :] = (unit * row(l, i) + row(l, 2 + i)).astype(BF16)

        by_tiles(flat, 32, do)

    def load_tokens():
        def do(first, size):
            here = pl.ds(first, size)
            h[here, :] = tokens[here, :].astype(F32)

        by_tiles(flat, 32, do)

    def mix(l):
        def do(first, size):
            cols = pl.ds(first, size)
            u[:, cols] = jnp.dot(a[...], w_bufs[0][:, cols], preferred_element_type=F32)

        by_tiles(3 * width, 256, do)

        for s in range(seqs):

            def split(first, size):
                here, there = pl.ds(s * rows + first, size), pl.ds(first, size)
                queries = u[here, pl.ds(0, width)] + row(l, 4)
                keys = u[here, pl.ds(width, width)]
                values = u[here, pl.ds(2 * width, width)] + row(l, 5)
                q[here, pl.ds(0, width)] = queries.astype(BF16)
                own_kv[s, there, pl.ds(0, width)] = keys.astype(BF16)
                own_kv[s, there, pl.ds(wide, width)] = values.astype(BF16)

            by_tiles(rows, 32, split)

    def project(l):
        def do(first, size):
            cols = pl.ds(first, size)
            bias_row = vec[l, pl.ds(6, 1), cols]
            h1[:, cols] = (
                h[:, cols]
                + jnp.dot(o[:, pl.ds(0, width)], w_bufs[1][:, cols], preferred_element_type=F32)
                + bias_row
            )

        by_tiles(width, 256, do)

    def rise(l):
        def do(first, size):
            cols = pl.ds(first, size)
            pre = jnp.dot(c[...], w_bufs[2][:, cols], preferred_element_type=F32) + up_bias[l, pl.ds(0, 1), cols]
            u[:, cols] = pre
            z[:, cols] = gelu_of(pre).astype(BF16)

        by_tiles(ff, 256, do)

    def fall(l):
        def do(first, size):
            cols = pl.ds(first, size)
            h[:, cols] = (
                h1[:, cols]
                + jnp.dot(z[...], w_bufs[3][:, cols], preferred_element_type=F32)
                + vec[l, pl.ds(7, 1), cols]
            )

        by_tiles(width, 256, do)

    def finish_tokens():
        for s in range(seqs):
            def do(first, size):
                here = pl.ds(s * rows + first, size)
                place = at.c8 * rows + first + lax.broadcasted_iota(jnp.int32, (size, width), 0)
                acts[here, :] = jnp.where(place < lengths[s], h[here, :], 0.0).astype(BF16)

            by_tiles(rows, 32, do)

    steps = depth - 1
    ticks = []
    for k in range(4 * layers):
        if k == 0:
            ticks += [functools.partial(items[0].arrive, i) for i in range(steps)]
        if k + 2 < 4 * layers:
            ticks.append(items[k + 2].start)
        for i in range(steps):
            ticks.append(functools.partial(items[k].plane, i))
            if k + 1 < 4 * layers:
                ticks.append(functools.partial(items[k + 1].arrive, i))
            ticks.append(functools.partial(items[k].share, i))
        ticks.append(("end", k))

    def tick(n):
        for _ in range(n):
            if not ticks:
                return
            item = ticks.pop(0)
            if isinstance(item, tuple) and item[0] == "end":
                items[item[1]].finish()
            else:
                item()

    def reach(k):
        while ("end", k) in ticks:
            tick(1)

    small_start()
    items[0].start()
    items[1].start()
    for k in range(4 * layers):
        own_load(k)
    load_tokens()
    q[...] = jnp.zeros_like(q)
    o[...] = jnp.zeros_like(o)
    own_kv[...] = jnp.zeros_like(own_kv)
    lse[...] = jnp.zeros_like(lse)
    key_bias(bias, seqs, rows, slots, lengths, at.c8)
    for k in range(4 * layers):
        own_store(k)
    tick(steps)
    small_take()
    small_spread()
    for k in range(4 * layers):
        own_done(k)
    for l in range(layers):
        k = 4 * l
        free(l - 1, "a")
        norm(l, 0, h, a)
        keep(l, "h", h)
        keep(l, "a", a)
        reach(k)
        fetch(k)
        free(l - 1, "u")
        free(l - 1, "q")
        if l:
            contexts[l - 1].drain(True)
        ready(k)
        mix(l)
        contexts[l].start()
        keep(l, "q", q)
        tick(8)
        contexts[l].relay()
        reach(k + 1)
        fetch(k + 1)
        tick(4)
        contexts[l].last()
        tick(3)
        contexts[l].finish()
        seen = pltpu.make_async_copy(kept[l]["kv"], kv, load_sem.at[4 * layers])
        seen.start()
        free(l - 1, "o")
        free(l - 1, "lse")
        seen.wait()
        half = pairs // 2
        for s in range(seqs):
            attend(s, 0, half, q, kv, bias, o, lse, rows, pairs, wide)
            tick(2)
            attend(s, half, pairs - half, q, kv, bias, o, lse, rows, pairs, wide)
            tick(2)
        keep(l, "o", o)
        keep(l, "lse", lse)
        ready(k + 1)
        free(l - 1, "h1")
        project(l)
        keep(l, "h1", h1)
        free(l - 1, "c")
        norm(l, 1, h1, c)
        keep(l, "c", c)
        reach(k + 2)
        fetch(k + 2)
        ready(k + 2)
        rise(l)
        keep(l, "u", u)
        reach(k + 3)
        fetch(k + 3)
        free(l, "h")
        ready(k + 3)
        fall(l)
    tick(len(ticks))
    finish_tokens()
    for key in list(pending):
        free(*key)
    small_drain()
    for item in items:
        item.drain()
    contexts[-1].drain(True)
    for context in contexts:
        context.drain(False)


def forward(tokens, lengths, w_qkv, w_out, w_up, w_down, small):
    seqs, rows, width = tokens.shape
    layers, part, _ = w_qkv.shape
    depth = lax.axis_size("fsdp")
    slots = rows * lax.axis_size("ctx")
    ff = w_up.shape[2]
    flat, wide = seqs * rows, pad_lanes(width)
    dims = (layers, seqs, rows, slots, width, ff, depth)
    any_spec = pl.BlockSpec(memory_space=pl.ANY)
    vmem = pl.BlockSpec(memory_space=pltpu.VMEM)
    struct = lambda shape, kind: jax.ShapeDtypeStruct(shape, kind)
    shapes = kept_shapes(seqs, slots, rows, width, ff)
    out_shape = [struct((flat, width), BF16), struct((layers, 8, wide), F32)]
    for l in range(layers):
        for ref in (w_qkv, w_out, w_up, w_down):
            out_shape.append(struct((depth * ref.shape[1], ref.shape[2]), BF16))
    for l in range(layers):
        out_shape += [struct(*shapes[name]) for name in KEPT]
    count = 4 * layers
    dma = pltpu.SemaphoreType.DMA
    scratch = [
        dma((count, 8 * depth + 8)),
        dma((count, 8 * depth)),
        dma((depth + 1,)),
        dma((depth,)),
        dma((layers, 8)),
        dma((layers, 8)),
        dma((count + 1,)),
        dma((layers, len(KEPT) + 1)),
        dma((3, count)),
        pltpu.VMEM((depth,) + small.shape, BF16),
        pltpu.VMEM((layers, 8, wide), F32),
        pltpu.VMEM((layers, 8, ff), F32),
        pltpu.VMEM((flat, width), F32),
        pltpu.VMEM((flat, width), BF16),
        pltpu.VMEM((flat, wide), BF16),
        pltpu.VMEM((seqs, rows, 2 * wide), BF16),
        pltpu.VMEM((seqs, slots, 2 * wide), BF16),
        pltpu.VMEM((seqs, rows, slots), F32),
        pltpu.VMEM((flat, wide), BF16),
        pltpu.VMEM((2 * flat, LANES), F32),
        pltpu.VMEM((flat, width), F32),
        pltpu.VMEM((flat, width), BF16),
        pltpu.VMEM((flat, ff), F32),
        pltpu.VMEM((flat, ff), BF16),
    ] + [pltpu.VMEM((depth * ref.shape[1], ref.shape[2]), BF16) for ref in (w_qkv, w_out, w_up, w_down)]
    outs = pl.pallas_call(
        functools.partial(forward_kernel, dims),
        out_shape=out_shape,
        in_specs=[vmem, pl.BlockSpec(memory_space=pltpu.SMEM)] + [any_spec] * 5,
        out_specs=[vmem, vmem] + [any_spec] * (len(out_shape) - 2),
        scratch_shapes=scratch,
        compiler_params=pltpu.CompilerParams(
            collective_id=0, has_side_effects=True, vmem_limit_bytes=63 * 1024 * 1024
        ),
    )(tokens.reshape(flat, width), lengths, w_qkv, w_out, w_up, w_down, small)
    acts, vecs = outs[:2]
    wholes = outs[2 : 2 + count]
    rest = outs[2 + count :]
    kept = [dict(zip(KEPT, rest[l * len(KEPT) : (l + 1) * len(KEPT)])) for l in range(layers)]
    return acts, vecs, [wholes[4 * l : 4 * l + 4] for l in range(layers)], kept


def normalize(values, scales, shifts):
    average = jnp.mean(values, axis=-1, keepdims=True)
    centred = values - average
    variance = jnp.mean(centred * centred, axis=-1, keepdims=True)
    return centred * lax.rsqrt(variance + 1e-05) * scales + shifts


def outer_sum(left_rows, right_rows):
    return lax.dot_general(
        left_rows, right_rows, (((0,), (0,)), ((), ())), preferred_element_type=jnp.float32
    )


def times_transpose(left_rows, weight_rows):
    return lax.dot_general(
        left_rows, weight_rows, (((1,), (1,)), ((), ())), preferred_element_type=jnp.float32
    )


def allowed_mask(positions, key_places, lengths):
    causal = (key_places[None, :] <= positions[:, None]) & (key_places[None, :] >= 0)
    inside = key_places[None, :] < lengths[:, None]
    return causal[None, None, :, :] & inside[:, None, None, :]


def attend_forward(queries, key_part, value_part, positions, lengths, score_scale):
    seq_count, row_count, head_count, head_width = queries.shape
    lowest = jnp.full((seq_count, head_count, row_count), -1e30, jnp.float32)
    key_places = jnp.arange(key_part.shape[1], dtype=jnp.int32)
    allowed = allowed_mask(positions, key_places, lengths)
    scores = (
        jnp.einsum("sqhe,skhe->shqk", queries, key_part, preferred_element_type=jnp.float32)
        * score_scale
    )
    scores = jnp.where(allowed, scores, -1e30)
    new_top = jnp.maximum(lowest, jnp.max(scores, axis=-1))
    exp_weights = jnp.where(allowed, jnp.exp(scores - new_top[..., None]), 0.0)
    running_total = jnp.sum(exp_weights, axis=-1)
    running_sum = jnp.einsum(
        "shqk,skhe->shqe",
        exp_weights.astype(jnp.bfloat16),
        value_part,
        preferred_element_type=jnp.float32,
    )
    output = jnp.transpose(running_sum / running_total[..., None], (0, 2, 1, 3))
    return (output, new_top + jnp.log(running_total))


def block_terms(
    queries,
    grad_out,
    log_total,
    delta_row,
    key_part,
    value_part,
    first_key,
    positions,
    lengths,
    score_scale,
):
    key_places = first_key + jnp.arange(key_part.shape[1], dtype=jnp.int32)
    allowed = allowed_mask(positions, key_places, lengths)
    scores = (
        jnp.einsum("sqhe,skhe->shqk", queries, key_part, preferred_element_type=jnp.float32)
        * score_scale
    )
    scores = jnp.where(allowed, scores, -1e30)
    probability = jnp.where(allowed, jnp.exp(scores - log_total[..., None]), 0.0)
    grad_probs = jnp.einsum(
        "sqhe,skhe->shqk", grad_out, value_part, preferred_element_type=jnp.float32
    )
    grad_scores = (probability * (grad_probs - delta_row[..., None])).astype(jnp.bfloat16)
    query_add = (
        jnp.einsum("shqk,skhe->sqhe", grad_scores, key_part, preferred_element_type=jnp.float32)
        * score_scale
    )
    key_add = (
        jnp.einsum("shqk,sqhe->skhe", grad_scores, queries, preferred_element_type=jnp.float32)
        * score_scale
    )
    value_add = jnp.einsum(
        "shqk,sqhe->skhe",
        probability.astype(jnp.bfloat16),
        grad_out,
        preferred_element_type=jnp.float32,
    )
    return (query_add, key_add, value_add)


def pack_small(ln_gain, ln_bias, b_qv, b_out, b_up, b_down):
    layers, _, part = ln_gain.shape
    return jnp.concatenate(
        [ln_gain, ln_bias, b_qv, b_out[:, None], b_down[:, None], b_up.reshape(layers, 4, part)],
        axis=1,
    )


def unpack_small(whole):
    depth, _, part = whole.shape
    flat = jnp.transpose(whole[:, :8], (1, 0, 2)).reshape(8, depth * part)
    up_bias = whole[:, 8:].reshape(depth * 4 * part)
    return flat[0:2], flat[2:4], flat[4:6], flat[6], flat[7], up_bias


def small_rows(gains, shifts, mix_bias, out_bias, down_bias, up_bias, depth):
    width = gains.shape[-1]
    flat = jnp.concatenate([gains, shifts, mix_bias, out_bias[None], down_bias[None]], axis=0)
    flat = jnp.transpose(flat.reshape(8, depth, width // depth), (1, 0, 2))
    return jnp.concatenate([flat, up_bias.reshape(depth, 4, width // depth)], axis=1)


def fast_mesh(rows):
    return lax.axis_size("ctx") == 8 and rows % 272 == 0


def gather_all(weights, small):
    flat = [item for layer in weights for item in layer]
    layers = len(weights)
    wholes = [lax.all_gather(item, "fsdp", axis=0, tiled=True) for item in flat]
    small_all = lax.all_gather(small, "fsdp", axis=0)
    return [wholes[4 * i : 4 * i + 4] for i in range(layers)], [small_all[:, i] for i in range(layers)]


def reduce_layer(grads, collective_id):
    depth = lax.axis_size("fsdp")
    if fast_mesh(grads[0].shape[0] // depth):
        parts = [item.reshape(depth, item.shape[0] // depth, item.shape[1]) for item in grads]
        return reduce_grads(parts, [0] * len(parts), collective_id, lag=1)
    shards_now = [
        lax.psum_scatter(item, "fsdp", scatter_dimension=0, tiled=True) for item in grads
    ]
    return [lax.psum(item, "ctx") for item in shards_now]


def shards(
    tokens,
    lengths,
    cotangent,
    ln_gain,
    ln_bias,
    w_qkv,
    b_qv,
    w_out,
    b_out,
    w_up,
    b_up,
    w_down,
    b_down,
):
    seq_count, row_count, model_width = tokens.shape
    head_width = HEAD_DIM
    head_count = model_width // head_width
    score_scale = head_width ** (-0.5)
    ctx_index = lax.axis_index("ctx")
    depth = lax.axis_size("fsdp")
    positions = ctx_index * row_count + jnp.arange(row_count, dtype=jnp.int32)
    valid_rows = (positions[None, :] < lengths[:, None]).astype(jnp.float32)[..., None]
    flat_rows = seq_count * row_count
    split_shape = (seq_count, row_count, head_count, head_width)
    layer_total = ln_gain.shape[0]
    hidden = tokens.astype(jnp.float32).reshape(flat_rows, model_width)
    small = pack_small(ln_gain, ln_bias, b_qv, b_out, b_up, b_down)
    if fast_mesh(w_qkv.shape[1]):
        part = small.shape[2]
        padded = jnp.pad(small, ((0, 0), (0, 4), (0, pad_lanes(part) - part)))
        activations, vectors, weights, kept = forward(
            tokens, lengths, w_qkv, w_out, w_up, w_down, padded.reshape(layer_total * 16, -1)
        )
        activations = activations.reshape(tokens.shape)
        kept_layers = []
        for layer_index in range(layer_total):
            one = kept[layer_index]
            wide = one["q"].shape[1]
            cut = lambda array: array[..., :model_width]
            heads = cut(one["q"]).reshape(split_shape)
            kv_shape = (seq_count, -1, head_count, head_width)
            attended = cut(one["o"])
            lse = one["lse"].reshape(seq_count, 2, row_count, -1)
            pairs = wide // LANES
            log_total = jnp.stack(
                [
                    jnp.stack([lse[s, n % 2, :, s * pairs + n // 2] for n in range(head_count)])
                    for s in range(seq_count)
                ]
            )
            kept_layers.append(
                (
                    one["h"],
                    one["a"],
                    heads,
                    cut(one["kv"]).reshape(kv_shape),
                    cut(one["kv"][..., wide:]).reshape(kv_shape),
                    attended.astype(jnp.float32),
                    log_total,
                    attended,
                    one["h1"],
                    one["c"],
                    one["u"],
                    jax.nn.gelu(one["u"]).astype(jnp.bfloat16),
                    cut(vectors[layer_index, 0:2]),
                    cut(vectors[layer_index, 2:4]),
                )
            )
    else:
        weights, smalls = gather_all(
            [(w_qkv[i], w_out[i], w_up[i], w_down[i]) for i in range(layer_total)], small
        )
        kept_layers = []
        for layer_index in range(layer_total):
            mix_weight, out_weight, up_weight, down_weight = weights[layer_index]
            gain_rows, shift_rows, mix_bias, out_bias, down_bias, up_bias = unpack_small(
                smalls[layer_index].astype(jnp.float32)
            )
            normed_first = normalize(hidden, gain_rows[0], shift_rows[0]).astype(jnp.bfloat16)
            mixed_rows = jnp.dot(normed_first, mix_weight, preferred_element_type=jnp.float32)
            queries = (
                (mixed_rows[:, :model_width] + mix_bias[0]).astype(jnp.bfloat16).reshape(split_shape)
            )
            key_rows = (
                mixed_rows[:, model_width : 2 * model_width].astype(jnp.bfloat16).reshape(split_shape)
            )
            value_rows = (
                (mixed_rows[:, 2 * model_width :] + mix_bias[1])
                .astype(jnp.bfloat16)
                .reshape(split_shape)
            )
            key_part = lax.all_gather(key_rows, "ctx", axis=1, tiled=True)
            value_part = lax.all_gather(value_rows, "ctx", axis=1, tiled=True)
            output, log_total = attend_forward(
                queries, key_part, value_part, positions, lengths, score_scale
            )
            output = output.reshape(flat_rows, model_width)
            attended = output.astype(jnp.bfloat16)
            middle = (
                hidden + jnp.dot(attended, out_weight, preferred_element_type=jnp.float32) + out_bias
            )
            normed_second = normalize(middle, gain_rows[1], shift_rows[1]).astype(jnp.bfloat16)
            upper_pre = (
                jnp.dot(normed_second, up_weight, preferred_element_type=jnp.float32) + up_bias
            )
            active = jax.nn.gelu(upper_pre).astype(jnp.bfloat16)
            kept_layers.append(
                (
                    hidden,
                    normed_first,
                    queries,
                    key_part,
                    value_part,
                    output,
                    log_total,
                    attended,
                    middle,
                    normed_second,
                    upper_pre,
                    active,
                    gain_rows,
                    shift_rows,
                )
            )
            hidden = (
                middle + jnp.dot(active, down_weight, preferred_element_type=jnp.float32) + down_bias
            )
        activations = (valid_rows * hidden.reshape(seq_count, row_count, model_width)).astype(
            jnp.bfloat16
        )
    grad_hidden = (cotangent.astype(jnp.float32) * valid_rows).reshape(flat_rows, model_width)
    big_grads = [None] * layer_total
    small_grads = [None] * layer_total
    for layer_index in reversed(range(layer_total)):
        (
            hidden_in,
            normed_first,
            queries,
            key_part,
            value_part,
            output,
            log_total,
            attended,
            middle,
            normed_second,
            upper_pre,
            active,
            gain_rows,
            shift_rows,
        ) = kept_layers[layer_index]
        mix_weight, out_weight, up_weight, down_weight = weights[layer_index]
        grad_branch = grad_hidden.astype(jnp.bfloat16)
        down_bias_grad = jnp.sum(grad_branch.astype(jnp.float32), axis=0)
        down_grad = outer_sum(active, grad_branch)
        grad_active = times_transpose(grad_branch, down_weight)
        unused_gelu, gelu_pull = jax.vjp(jax.nn.gelu, upper_pre)
        grad_upper = gelu_pull(grad_active)[0].astype(jnp.bfloat16)
        up_bias_grad = jnp.sum(grad_upper.astype(jnp.float32), axis=0)
        up_grad = outer_sum(normed_second, grad_upper)
        grad_normed = times_transpose(grad_upper, up_weight)
        unused_norm, norm_pull = jax.vjp(normalize, middle, gain_rows[1], shift_rows[1])
        grad_middle, gain_second, shift_second = norm_pull(grad_normed)
        grad_middle = grad_middle + grad_hidden
        grad_attn = grad_middle.astype(jnp.bfloat16)
        out_bias_grad = jnp.sum(grad_attn.astype(jnp.float32), axis=0)
        out_grad = outer_sum(attended, grad_attn)
        grad_output = times_transpose(grad_attn, out_weight).astype(jnp.bfloat16)
        delta_row = jnp.transpose(
            jnp.sum((grad_output.astype(jnp.float32) * output).reshape(split_shape), axis=-1),
            (0, 2, 1),
        )
        grad_heads = grad_output.reshape(split_shape)
        query_grad, key_add, value_add = block_terms(
            queries,
            grad_heads,
            log_total,
            delta_row,
            key_part,
            value_part,
            0,
            positions,
            lengths,
            score_scale,
        )
        key_low = lax.psum_scatter(
            key_add.astype(jnp.bfloat16), "ctx", scatter_dimension=1, tiled=True
        ).reshape(flat_rows, model_width)
        value_low = lax.psum_scatter(
            value_add.astype(jnp.bfloat16), "ctx", scatter_dimension=1, tiled=True
        ).reshape(flat_rows, model_width)
        query_low = query_grad.reshape(flat_rows, model_width).astype(jnp.bfloat16)
        grad_mixed = jnp.concatenate([query_low, key_low, value_low], axis=1)
        mix_bias_grad = jnp.stack(
            [
                jnp.sum(query_low.astype(jnp.float32), axis=0),
                jnp.sum(value_low.astype(jnp.float32), axis=0),
            ]
        )
        mix_grad = outer_sum(normed_first, grad_mixed)
        grad_normed_first = times_transpose(grad_mixed, mix_weight)
        unused_first, first_pull = jax.vjp(normalize, hidden_in, gain_rows[0], shift_rows[0])
        grad_input, gain_first, shift_first = first_pull(grad_normed_first)
        grad_hidden = grad_input + grad_middle
        big_grads[layer_index] = reduce_layer(
            [item.astype(jnp.bfloat16) for item in (up_grad, down_grad, mix_grad, out_grad)],
            1 + layer_index,
        )
        small_grads[layer_index] = small_rows(
            jnp.stack([gain_first, gain_second]),
            jnp.stack([shift_first, shift_second]),
            mix_bias_grad,
            out_bias_grad,
            down_bias_grad,
            up_bias_grad,
            depth,
        )
    input_grad = grad_hidden.reshape(seq_count, row_count, model_width)
    packed = jnp.stack(small_grads).astype(jnp.bfloat16)
    total = lax.psum(packed, ("fsdp", "ctx"))
    own = lax.dynamic_index_in_dim(total, lax.axis_index("fsdp"), 1, keepdims=False)
    own = own.astype(jnp.float32)

    def whole(member):
        return jnp.stack([big_grads[i][member].astype(jnp.float32) for i in range(layer_total)])

    return (
        activations,
        input_grad,
        own[:, 0:2],
        own[:, 2:4],
        whole(2),
        own[:, 4:6],
        whole(3),
        own[:, 6],
        whole(0),
        own[:, 8:].reshape(layer_total, -1),
        whole(1),
        own[:, 7],
    )


def solution(mesh):
    placed = (
        P("fsdp", "ctx", None),
        P("fsdp"),
        P("fsdp", "ctx", None),
        P(None, None, "fsdp"),
        P(None, None, "fsdp"),
        P(None, "fsdp", None),
        P(None, None, "fsdp"),
        P(None, "fsdp", None),
        P(None, "fsdp"),
        P(None, "fsdp", None),
        P(None, "fsdp"),
        P(None, "fsdp", None),
        P(None, "fsdp"),
    )
    return jax.shard_map(
        shards,
        mesh=mesh,
        in_specs=placed,
        out_specs=(
            P("fsdp", "ctx", None),
            P("fsdp", "ctx", None),
            P(None, None, "fsdp"),
            P(None, None, "fsdp"),
            P(None, "fsdp", None),
            P(None, None, "fsdp"),
            P(None, "fsdp", None),
            P(None, "fsdp"),
            P(None, "fsdp", None),
            P(None, "fsdp"),
            P(None, "fsdp", None),
            P(None, "fsdp"),
        ),
        check_vma=False,
    )
```

```python
import functools

import jax
import jax.numpy as jnp
from jax import lax
from jax.experimental import pallas as pl
from jax.experimental.pallas import tpu as pltpu
from jax.sharding import PartitionSpec as P

MESH = pl.DeviceIdType.MESH


class Place:
    def __init__(self):
        self.depth = lax.axis_size("fsdp")
        self.z = lax.axis_index("fsdp")
        self.c8 = lax.axis_index("ctx")
        self.core = lax.rem(self.c8, 2)
        self.p = self.c8 // 2
        self.px = lax.rem(self.p, 2)
        self.py = self.p // 2
        self.sib = {"ctx": self.c8 + 1 - 2 * self.core}
        self.x_dev = {"ctx": self.c8 + 2 - 4 * self.px}
        self.y_dev = {"ctx": self.c8 + 4 - 8 * self.py}
        self.p_x = self.p + 1 - 2 * self.px
        self.p_y = self.p + 2 - 4 * self.py
        self.p_d = 3 - self.p
        self.relay_from = self.p + (1 - self.core) * (1 - 2 * self.px) + self.core * (2 - 4 * self.py)
        self.relay_dev = {
            "ctx": self.c8 + (1 - self.core) * (4 - 8 * self.py) + self.core * (2 - 4 * self.px)
        }

    def up(self):
        return {"fsdp": self.z + 1}

    def down(self):
        return {"fsdp": self.z - 1}

    def greet(self):
        barrier = pltpu.get_barrier_semaphore()
        for device in (self.sib, self.x_dev, self.y_dev):
            pl.semaphore_signal(barrier, inc=1, device_id=device, device_id_type=MESH)

        @pl.when(self.z > 0)
        def _():
            pl.semaphore_signal(barrier, inc=1, device_id=self.down(), device_id_type=MESH)

        @pl.when(self.z < self.depth - 1)
        def _():
            pl.semaphore_signal(barrier, inc=1, device_id=self.up(), device_id_type=MESH)

        below = jnp.where(self.z > 0, 1, 0)
        above = jnp.where(self.z < self.depth - 1, 1, 0)
        pl.semaphore_wait(barrier, 3 + below + above)


def remote(src, dst, send_sem, recv_sem, device):
    return pltpu.make_async_remote_copy(
        src_ref=src, dst_ref=dst, send_sem=send_sem, recv_sem=recv_sem, device_id=device, device_id_type=MESH
    )


class Gather:
    def __init__(self, at, own, whole, left_core, send, recv):
        self.at, self.own, self.whole = at, own, whole
        self.send, self.recv = send, recv
        rows = own.shape[0]
        self.rows = rows
        unit = rows // 17
        self.t1 = 2 * unit
        self.block = 8 * unit
        self.rest = pl.ds(16 * unit, unit)
        self.has_rest = at.core == left_core

    def t1_rows(self, p, core=None):
        core = self.at.core if core is None else core
        return pl.ds(pl.multiple_of(core * self.block + p * self.t1, 16), self.t1)

    def block_rows(self, core):
        return pl.ds(pl.multiple_of(core * self.block, 16), self.block)

    def copy(self, kind, shard, rows, device, src=None, second=False):
        depth = self.at.depth
        slot = kind * depth + shard
        place = self.place(shard, rows)
        src = place if src is None else src
        send = self.send.at[(8 * depth + kind) if second else slot]
        return remote(src, place, send, self.recv.at[slot], device)

    def place(self, shard, rows):
        first = pl.multiple_of(shard * self.rows + rows.start, 16)
        return self.whole.at[pl.ds(first, rows.size)]

    def start(self):
        at = self.at
        mine = self.t1_rows(at.p)

        @pl.when(at.z < at.depth - 1)
        def _():
            self.copy(0, at.z, mine, at.up(), self.own.at[mine]).start()

            @pl.when(self.has_rest)
            def _():
                self.copy(1, at.z, self.rest, at.up(), self.own.at[self.rest]).start()

        @pl.when(at.z > 0)
        def _():
            self.copy(0, at.z, mine, at.down(), self.own.at[mine], True).start()

            @pl.when(self.has_rest)
            def _():
                self.copy(1, at.z, self.rest, at.down(), self.own.at[self.rest], True).start()

    def cases(self, step, do):
        at = self.at

        @pl.when(at.z - 1 - step >= 0)
        def _():
            do(at.z - 1 - step, at.z < at.depth - 1, at.up())

        @pl.when(at.z + 1 + step < at.depth)
        def _():
            do(at.z + 1 + step, at.z > 0, at.down())

    def arrive(self, step):
        at = self.at
        mine = self.t1_rows(at.p)

        def do(shard, onward, device):
            self.copy(0, shard, mine, at.sib).wait_recv()

            @pl.when(onward)
            def _():
                self.copy(0, shard, mine, device).start()

            self.copy(2, shard, mine, at.x_dev).start()
            self.copy(3, shard, mine, at.y_dev).start()

            @pl.when(self.has_rest)
            def _():
                self.copy(1, shard, self.rest, at.sib).wait_recv()

                @pl.when(onward)
                def _():
                    self.copy(1, shard, self.rest, device).start()

                self.copy(5, shard, self.rest, at.sib).start()

        self.cases(step, do)

    def plane(self, step):
        at = self.at

        def do(shard, onward, device):
            self.copy(2, shard, self.t1_rows(at.p_x), at.sib).wait_recv()
            self.copy(3, shard, self.t1_rows(at.p_y), at.sib).wait_recv()
            self.copy(4, shard, self.t1_rows(at.relay_from), at.relay_dev).start()

        self.cases(step, do)

    def share(self, step):
        at = self.at

        def do(shard, onward, device):
            self.copy(4, shard, self.t1_rows(at.p_d), at.sib).wait_recv()
            self.copy(6, shard, self.block_rows(at.core), at.sib).start()

        self.cases(step, do)

    def finish(self):
        at = self.at
        mine = self.t1_rows(at.p)

        def do(shard, onward, device):
            self.copy(6, shard, self.block_rows(1 - at.core), at.sib).wait_recv()

            @pl.when(jnp.logical_not(self.has_rest))
            def _():
                self.copy(5, shard, self.rest, at.sib).wait_recv()

        for step in range(at.depth - 1):
            self.cases(step, do)

    def drain(self):
        at = self.at
        mine = self.t1_rows(at.p)

        @pl.when(at.z < at.depth - 1)
        def _():
            self.copy(0, at.z, mine, at.up(), self.own.at[mine]).wait_send()

            @pl.when(self.has_rest)
            def _():
                self.copy(1, at.z, self.rest, at.up(), self.own.at[self.rest]).wait_send()

        @pl.when(at.z > 0)
        def _():
            self.copy(0, at.z, mine, at.down(), self.own.at[mine], True).wait_send()

            @pl.when(self.has_rest)
            def _():
                self.copy(1, at.z, self.rest, at.down(), self.own.at[self.rest], True).wait_send()

        def do(shard, onward, device):
            @pl.when(onward)
            def _():
                self.copy(0, shard, mine, device).wait_send()

                @pl.when(self.has_rest)
                def _():
                    self.copy(1, shard, self.rest, device).wait_send()

            self.copy(2, shard, mine, at.x_dev).wait_send()
            self.copy(3, shard, mine, at.y_dev).wait_send()
            self.copy(4, shard, self.t1_rows(at.relay_from), at.relay_dev).wait_send()
            self.copy(6, shard, self.block_rows(at.core), at.sib).wait_send()

            @pl.when(self.has_rest)
            def _():
                self.copy(5, shard, self.rest, at.sib).wait_send()

        for step in range(at.depth - 1):
            self.cases(step, do)


def both(*conds):
    conds = [c for c in conds if c is not None]
    if not conds:
        return None
    total = conds[0]
    for c in conds[1:]:
        total = jnp.logical_and(total, c)
    return total


def under(cond, do):
    if cond is None:
        do()
    else:
        pl.when(cond)(do)


def add_rows(acc, extra, rows):
    def step(i, carry):
        piece = pl.ds(pl.multiple_of(i * 16, 16), 16)
        acc[piece, :] = acc[piece, :] + extra[piece, :]
        return carry

    lax.fori_loop(0, rows // 16, step, 0)


def add_rows_two(acc, one, two, rows):
    def step(i, carry):
        piece = pl.ds(pl.multiple_of(i * 16, 16), 16)
        total = acc[piece, :].astype(jnp.float32) + one[piece, :].astype(jnp.float32)
        acc[piece, :] = (total + two[piece, :].astype(jnp.float32)).astype(jnp.bfloat16)
        return carry

    lax.fori_loop(0, rows // 16, step, 0)


HEAD_DIM = 64
LANES = 128
F32, BF16 = jnp.float32, jnp.bfloat16


def pad_lanes(n):
    return (n + LANES - 1) // LANES * LANES


def by_tiles(total, tile, do):
    count = total // tile

    def step(i, carry):
        do(pl.multiple_of(i * tile, tile), tile)
        return carry

    if count:
        lax.fori_loop(0, count, step, 0)
    if total % tile:
        do(count * tile, total % tile)


def row_norm(values):
    average = jnp.mean(values, axis=-1, keepdims=True)
    centred = values - average
    variance = jnp.mean(centred * centred, axis=-1, keepdims=True)
    scale = lax.rsqrt(variance + 1e-05)
    return centred * scale, scale


GELU_A = 0.7978845608028654
GELU_B = 0.044715


def gelu_both(u):
    square = u * u
    bent = jnp.tanh(GELU_A * (u + GELU_B * u * square))
    half = 0.5 * (1.0 + bent)
    slope = half + 0.5 * u * (1.0 - bent * bent) * (GELU_A * (1.0 + 3.0 * GELU_B * square))
    return u * half, slope


def cut_pieces(src, dst, part, first):
    depth = 4

    def do(off, size):
        here = pl.ds(off, size)
        left = []
        for t in range(depth):
            start = (first + t * (src.shape[1] // part // depth)) * part
            block = src[here, pl.ds(start, part)]
            for core in range(2):
                dst[core, here, pl.ds(t * LANES, LANES)] = block[:, core * LANES : (core + 1) * LANES]
            left.append(block[:, 2 * LANES :])
        rest = jnp.concatenate(left + [jnp.zeros_like(left[0])] * 4, axis=1)
        for core in range(2):
            dst[core, here, pl.ds(depth * LANES, LANES)] = rest

    by_tiles(src.shape[0], 64, do)


class Context:
    def __init__(self, at, own, whole, rows, send, recv, local):
        self.at, self.own, self.whole, self.rows = at, own, whole, rows
        self.send, self.recv, self.local = send, recv, local
        core, p = at.core, at.p
        self.names, self.posts = {}, []

    def place(self, p, core):
        return self.whole.at[:, pl.ds(pl.multiple_of((2 * p + core) * self.rows, 16), self.rows)]

    def make(self, name, src, dst, device):
        i = self.names.setdefault(name, len(self.names))
        return remote(src, dst, self.send.at[i], self.recv.at[i], device)

    def post(self, name, src, dst, device):
        self.make(name, src, dst, device).start()
        self.posts.append((name, src, dst, device))

    def take(self, name, dst):
        self.make(name, dst, dst, self.at.sib).wait_recv()

    def start(self):
        at = self.at
        here = self.place(at.p, at.core)
        self.post("x", self.own, here, at.x_dev)
        self.post("y", self.own, here, at.y_dev)
        self.post("s", self.own, here, at.sib)
        self.keep = pltpu.make_async_copy(self.own, here, self.local)
        self.keep.start()

    def relay(self):
        at = self.at
        for name, p in (("x", at.p_x), ("y", at.p_y)):
            self.take(name, self.place(p, at.core))
        here = self.place(at.relay_from, at.core)
        self.post("d", here, here, at.relay_dev)
        for name, p in (("x", at.p_x), ("y", at.p_y)):
            here = self.place(p, at.core)
            self.post(name + "s", here, here, at.sib)

    def last(self):
        at = self.at
        here = self.place(at.p_d, at.core)
        self.take("d", here)
        self.post("ds", here, here, at.sib)

    def finish(self):
        at = self.at
        for name, p in (("s", at.p), ("xs", at.p_x), ("ys", at.p_y), ("ds", at.p_d)):
            self.take(name, self.place(p, 1 - at.core))
        self.keep.wait()

    def drain(self, own):
        for name, src, dst, device in self.posts:
            if (name in ("x", "y", "s")) == own:
                self.make(name, src, dst, device).wait_send()


KEPT = ("h", "pa", "q", "kv", "o", "po", "lse", "h1", "pc", "pz", "dg")
PIECE = 5 * LANES


def kept_shapes(seqs, slots, rows, width, ff):
    wide = pad_lanes(width)
    flat = seqs * rows
    return {
        "h": ((flat, width), F32),
        "pa": ((2, flat, PIECE), BF16),
        "q": ((flat, wide), BF16),
        "kv": ((seqs, slots, 2 * wide), BF16),
        "o": ((flat, wide), BF16),
        "po": ((2, flat, PIECE), BF16),
        "lse": ((flat * 2, LANES), F32),
        "h1": ((flat, width), F32),
        "pc": ((2, flat, PIECE), BF16),
        "pz": ((2, 4, flat, PIECE), BF16),
        "dg": ((flat, ff), BF16),
    }


def key_bias(out, seqs, rows, slots, lengths, ctx):
    for s in range(seqs):
        key = lax.broadcasted_iota(jnp.int32, (rows, slots), 1)
        row = ctx * rows + lax.broadcasted_iota(jnp.int32, (rows, slots), 0)
        seen = jnp.logical_and(key <= row, key < lengths[s])
        out[s] = jnp.where(seen, 0.0, -1e30)


def two_heads(block):
    lane = lax.broadcasted_iota(jnp.int32, block.shape, 1)
    zero = jnp.zeros_like(block)
    return jnp.concatenate(
        [jnp.where(lane < HEAD_DIM, block, zero), jnp.where(lane < HEAD_DIM, zero, block)], axis=0
    )


def one_pair(stacked, rows):
    lane = lax.broadcasted_iota(jnp.int32, (rows, LANES), 1)
    return jnp.where(lane < HEAD_DIM, stacked[:rows], stacked[rows:])


def across(a, b):
    return lax.dot_general(a, b, (((1,), (1,)), ((), ())), preferred_element_type=F32)


def attend(s, first, count, q_ref, kv_ref, bias_ref, o_ref, lse_ref, rows, pairs, wide):
    def step(i, carry):
        j = first + i
        col = pl.ds(pl.multiple_of(j * LANES, LANES), LANES)
        q2 = two_heads(q_ref[pl.ds(s * rows, rows), col])
        keys = kv_ref[s, :, col]
        values = kv_ref[s, :, pl.ds(pl.multiple_of(wide + j * LANES, LANES), LANES)]
        bias = bias_ref[s]
        scores = across(q2, keys) * (HEAD_DIM ** (-0.5))
        scores = scores + jnp.concatenate([bias, bias], axis=0)
        top = jnp.max(scores, axis=-1, keepdims=True)
        weights = jnp.exp(scores - top)
        total = jnp.sum(weights, axis=-1, keepdims=True)
        out = jnp.dot(weights.astype(BF16), values, preferred_element_type=F32) / total
        o_ref[pl.ds(s * rows, rows), col] = one_pair(out, rows).astype(BF16)
        mine = s * pairs + j
        here = pl.ds(s * 2 * rows, 2 * rows)
        lane = lax.broadcasted_iota(jnp.int32, (2 * rows, LANES), 1)
        lse_ref[here, :] = jnp.where(lane == mine, top + jnp.log(total), lse_ref[here, :])
        return carry

    lax.fori_loop(0, count, step, 0)


def forward_kernel(dims, *refs):
    layers, seqs, rows, slots, width, ff, depth = dims
    flat, wide = seqs * rows, pad_lanes(width)
    pairs = wide // LANES
    part = width // depth
    refs = list(refs)

    def grab(n):
        out = refs[:n]
        del refs[:n]
        return out

    tokens, lengths, w_qkv, w_out, w_up, w_down, small = grab(7)
    acts, vecs = grab(2)
    wholes = grab(4 * layers)
    kept = [dict(zip(KEPT, grab(len(KEPT)))) for _ in range(layers)]
    (send, recv, small_send, small_recv, kv_send, kv_recv, load_sem, keep_sem, stage_sem) = grab(9)
    (small_all, vec, up_bias, h, a, q, own_kv, kv, bias, o, lse, h1, c, u, z, dg, pa, pc, po, pz) = grab(20)
    w_bufs = grab(4)
    at = Place()
    at.greet()

    owns = [ref.at[l] for l in range(layers) for ref in (w_qkv, w_out, w_up, w_down)]
    items = [Gather(at, owns[k], wholes[k], k % 2, send.at[k], recv.at[k]) for k in range(4 * layers)]
    contexts = [
        Context(at, own_kv, kept[l]["kv"], rows, kv_send.at[l], kv_recv.at[l], keep_sem.at[l, len(KEPT)])
        for l in range(layers)
    ]
    pending = {}

    def keep(l, name, src):
        copy = pltpu.make_async_copy(src, kept[l][name], keep_sem.at[l, KEPT.index(name)])
        copy.start()
        pending[(l, name)] = copy

    def free(l, name):
        copy = pending.pop((l, name), None)
        if copy is not None:
            copy.wait()

    def buffer(k):
        return w_bufs[k % 4]

    def own_copy(k, load):
        r = owns[k].shape[0]
        shard = lax.rem(at.z + k // 4, depth)
        place = buffer(k).at[pl.ds(pl.multiple_of(shard * r, 16), r)]
        if load:
            return pltpu.make_async_copy(owns[k], place, stage_sem.at[0, k])
        return pltpu.make_async_copy(place, items[k].place(at.z, pl.ds(0, r)), stage_sem.at[1, k])

    def own_load(k):
        own_copy(k, True).start()

    def own_store(k):
        own_copy(k, True).wait()
        own_copy(k, False).start()

    def own_done(k):
        own_copy(k, False).wait()

    def fetch(k):
        pltpu.make_async_copy(wholes[k], buffer(k), load_sem.at[k]).start()

    def ready(k):
        pltpu.make_async_copy(wholes[k], buffer(k), load_sem.at[k]).wait()

    def small_copy(shard, device, src=None, second=False):
        return remote(
            small_all.at[shard] if src is None else src,
            small_all.at[shard],
            small_send.at[depth if second else shard],
            small_recv.at[shard],
            device,
        )

    def small_start():
        @pl.when(at.z < depth - 1)
        def _():
            small_copy(at.z, at.up(), small).start()

        @pl.when(at.z > 0)
        def _():
            small_copy(at.z, at.down(), small, True).start()

        pltpu.make_async_copy(small, small_all.at[at.z], stage_sem.at[2, 0]).start()

    def small_take():
        def do(shard, onward, device):
            small_copy(shard, at.sib).wait_recv()
            pl.when(onward)(lambda: small_copy(shard, device).start())

        for step in range(depth - 1):
            items[0].cases(step, do)
        pltpu.make_async_copy(small, small_all.at[at.z], stage_sem.at[2, 0]).wait()

    def small_drain():
        @pl.when(at.z < depth - 1)
        def _():
            small_copy(at.z, at.up(), small).wait_send()

        @pl.when(at.z > 0)
        def _():
            small_copy(at.z, at.down(), small, True).wait_send()

        def do(shard, onward, device):
            pl.when(onward)(lambda: small_copy(shard, device).wait_send())

        for step in range(depth - 1):
            items[0].cases(step, do)

    def small_spread():
        part = width // depth
        per_layer = small_all.shape[1] // layers
        total = jnp.zeros((small_all.shape[1], wide), F32)
        room = jnp.zeros((small_all.shape[1], wide - small_all.shape[2]), F32)
        pieces = [small_all[i].astype(F32) for i in range(depth)]
        for i in range(depth):
            piece = jnp.concatenate([pieces[i], room], axis=1)
            total = total + (pltpu.roll(piece, i * part, 1) if i else piece)
        for l in range(layers):
            vec[l] = total[l * per_layer : l * per_layer + 8]
            vecs[l] = total[l * per_layer : l * per_layer + 8]
            wide_up = jnp.zeros((1, ff), F32)
            up_room = jnp.zeros((1, ff - small_all.shape[2]), F32)
            for i in range(depth):
                for r in range(4):
                    at_row = l * per_layer + 8 + r
                    piece = jnp.concatenate([pieces[i][at_row : at_row + 1], up_room], axis=1)
                    shift = (i * 4 + r) * part
                    wide_up = wide_up + (pltpu.roll(piece, shift, 1) if shift else piece)
            up_bias[l] = jnp.broadcast_to(wide_up, (8, ff))

    def row(l, i):
        return vec[l, pl.ds(i, 1), pl.ds(0, width)]

    def norm(l, i, src, dst):
        def do(first, size):
            here = pl.ds(first, size)
            unit, _ = row_norm(src[here, :])
            dst[here, :] = (unit * row(l, i) + row(l, 2 + i)).astype(BF16)

        by_tiles(flat, 32, do)

    def load_tokens():
        def do(first, size):
            here = pl.ds(first, size)
            h[here, :] = tokens[here, :].astype(F32)

        by_tiles(flat, 32, do)

    def mix(l):
        def do(first, size):
            cols = pl.ds(first, size)
            u[:, cols] = jnp.dot(a[...], w_bufs[0][:, cols], preferred_element_type=F32)

        by_tiles(3 * width, 256, do)

        for s in range(seqs):

            def split(first, size):
                here, there = pl.ds(s * rows + first, size), pl.ds(first, size)
                queries = u[here, pl.ds(0, width)] + row(l, 4)
                keys = u[here, pl.ds(width, width)]
                values = u[here, pl.ds(2 * width, width)] + row(l, 5)
                q[here, pl.ds(0, width)] = queries.astype(BF16)
                own_kv[s, there, pl.ds(0, width)] = keys.astype(BF16)
                own_kv[s, there, pl.ds(wide, width)] = values.astype(BF16)

            by_tiles(rows, 32, split)

    def project(l):
        def do(first, size):
            cols = pl.ds(first, size)
            bias_row = vec[l, pl.ds(6, 1), cols]
            h1[:, cols] = (
                h[:, cols]
                + jnp.dot(o[:, pl.ds(0, width)], w_bufs[1][:, cols], preferred_element_type=F32)
                + bias_row
            )

        by_tiles(width, 256, do)

    def rise(l):
        def do(first, size):
            cols = pl.ds(first, size)
            pre = jnp.dot(c[...], w_bufs[2][:, cols], preferred_element_type=F32) + up_bias[l, pl.ds(0, 1), cols]
            value, slope = gelu_both(pre)
            z[:, cols] = value.astype(BF16)
            dg[:, cols] = slope.astype(BF16)

        by_tiles(ff, 256, do)

    def fall(l):
        def do(first, size):
            cols = pl.ds(first, size)
            h[:, cols] = (
                h1[:, cols]
                + jnp.dot(z[...], w_bufs[3][:, cols], preferred_element_type=F32)
                + vec[l, pl.ds(7, 1), cols]
            )

        by_tiles(width, 256, do)

    def finish_tokens():
        for s in range(seqs):
            def do(first, size):
                here = pl.ds(s * rows + first, size)
                place = at.c8 * rows + first + lax.broadcasted_iota(jnp.int32, (size, width), 0)
                acts[here, :] = jnp.where(place < lengths[s], h[here, :], 0.0).astype(BF16)

            by_tiles(rows, 32, do)

    steps = depth - 1
    ticks = []
    for k in range(4 * layers):
        if k == 0:
            ticks += [functools.partial(items[0].arrive, i) for i in range(steps)]
        if k + 2 < 4 * layers:
            ticks.append(items[k + 2].start)
        for i in range(steps):
            ticks.append(functools.partial(items[k].plane, i))
            if k + 1 < 4 * layers:
                ticks.append(functools.partial(items[k + 1].arrive, i))
            ticks.append(functools.partial(items[k].share, i))
        ticks.append(("end", k))

    def tick(n):
        for _ in range(n):
            if not ticks:
                return
            item = ticks.pop(0)
            if isinstance(item, tuple) and item[0] == "end":
                items[item[1]].finish()
            else:
                item()

    def reach(k):
        while ("end", k) in ticks:
            tick(1)

    small_start()
    items[0].start()
    items[1].start()
    for k in range(4 * layers):
        own_load(k)
    load_tokens()
    q[...] = jnp.zeros_like(q)
    o[...] = jnp.zeros_like(o)
    own_kv[...] = jnp.zeros_like(own_kv)
    lse[...] = jnp.zeros_like(lse)
    key_bias(bias, seqs, rows, slots, lengths, at.c8)
    for k in range(4 * layers):
        own_store(k)
    tick(steps)
    small_take()
    small_spread()
    for k in range(4 * layers):
        own_done(k)
    for l in range(layers):
        k = 4 * l
        norm(l, 0, h, a)
        keep(l, "h", h)
        free(l - 1, "pa")
        cut_pieces(a, pa, part, 0)
        keep(l, "pa", pa)
        reach(k)
        fetch(k)
        free(l - 1, "q")
        if l:
            contexts[l - 1].drain(True)
        ready(k)
        mix(l)
        contexts[l].start()
        keep(l, "q", q)
        tick(8)
        contexts[l].relay()
        reach(k + 1)
        fetch(k + 1)
        tick(4)
        contexts[l].last()
        tick(3)
        contexts[l].finish()
        seen = pltpu.make_async_copy(kept[l]["kv"], kv, load_sem.at[4 * layers])
        seen.start()
        free(l - 1, "o")
        free(l - 1, "lse")
        seen.wait()
        half = pairs // 2
        for s in range(seqs):
            attend(s, 0, half, q, kv, bias, o, lse, rows, pairs, wide)
            tick(2)
            attend(s, half, pairs - half, q, kv, bias, o, lse, rows, pairs, wide)
            tick(2)
        keep(l, "o", o)
        keep(l, "lse", lse)
        free(l - 1, "po")
        cut_pieces(o.at[:, pl.ds(0, wide)], po, part, 0)
        keep(l, "po", po)
        ready(k + 1)
        free(l - 1, "h1")
        project(l)
        keep(l, "h1", h1)
        norm(l, 1, h1, c)
        free(l - 1, "pc")
        cut_pieces(c, pc, part, 0)
        keep(l, "pc", pc)
        reach(k + 2)
        fetch(k + 2)
        ready(k + 2)
        free(l - 1, "dg")
        rise(l)
        keep(l, "dg", dg)
        free(l - 1, "pz")
        for i in range(4):
            cut_pieces(z, pz.at[:, i], part, i)
        keep(l, "pz", pz)
        reach(k + 3)
        fetch(k + 3)
        free(l, "h")
        ready(k + 3)
        fall(l)
    tick(len(ticks))
    finish_tokens()
    for key in list(pending):
        free(*key)
    small_drain()
    for item in items:
        item.drain()
    contexts[-1].drain(True)
    for context in contexts:
        context.drain(False)


def forward(tokens, lengths, w_qkv, w_out, w_up, w_down, small):
    seqs, rows, width = tokens.shape
    layers, part, _ = w_qkv.shape
    depth = lax.axis_size("fsdp")
    slots = rows * lax.axis_size("ctx")
    ff = w_up.shape[2]
    flat, wide = seqs * rows, pad_lanes(width)
    dims = (layers, seqs, rows, slots, width, ff, depth)
    any_spec = pl.BlockSpec(memory_space=pl.ANY)
    vmem = pl.BlockSpec(memory_space=pltpu.VMEM)
    struct = lambda shape, kind: jax.ShapeDtypeStruct(shape, kind)
    shapes = kept_shapes(seqs, slots, rows, width, ff)
    out_shape = [struct((flat, width), BF16), struct((layers, 8, wide), F32)]
    for l in range(layers):
        for ref in (w_qkv, w_out, w_up, w_down):
            out_shape.append(struct((depth * ref.shape[1], ref.shape[2]), BF16))
    for l in range(layers):
        out_shape += [struct(*shapes[name]) for name in KEPT]
    count = 4 * layers
    dma = pltpu.SemaphoreType.DMA
    scratch = [
        dma((count, 8 * depth + 8)),
        dma((count, 8 * depth)),
        dma((depth + 1,)),
        dma((depth,)),
        dma((layers, 8)),
        dma((layers, 8)),
        dma((count + 1,)),
        dma((layers, len(KEPT) + 1)),
        dma((3, count)),
        pltpu.VMEM((depth,) + small.shape, BF16),
        pltpu.VMEM((layers, 8, wide), F32),
        pltpu.VMEM((layers, 8, ff), F32),
        pltpu.VMEM((flat, width), F32),
        pltpu.VMEM((flat, width), BF16),
        pltpu.VMEM((flat, wide), BF16),
        pltpu.VMEM((seqs, rows, 2 * wide), BF16),
        pltpu.VMEM((seqs, slots, 2 * wide), BF16),
        pltpu.VMEM((seqs, rows, slots), F32),
        pltpu.VMEM((flat, wide), BF16),
        pltpu.VMEM((2 * flat, LANES), F32),
        pltpu.VMEM((flat, width), F32),
        pltpu.VMEM((flat, width), BF16),
        pltpu.VMEM((flat, 3 * width), F32),
        pltpu.VMEM((flat, ff), BF16),
        pltpu.VMEM((flat, ff), BF16),
        pltpu.VMEM((2, flat, PIECE), BF16),
        pltpu.VMEM((2, flat, PIECE), BF16),
        pltpu.VMEM((2, flat, PIECE), BF16),
        pltpu.VMEM((2, 4, flat, PIECE), BF16),
    ] + [pltpu.VMEM((depth * ref.shape[1], ref.shape[2]), BF16) for ref in (w_qkv, w_out, w_up, w_down)]
    outs = pl.pallas_call(
        functools.partial(forward_kernel, dims),
        out_shape=out_shape,
        in_specs=[vmem, pl.BlockSpec(memory_space=pltpu.SMEM)] + [any_spec] * 5,
        out_specs=[vmem, vmem] + [any_spec] * (len(out_shape) - 2),
        scratch_shapes=scratch,
        compiler_params=pltpu.CompilerParams(
            collective_id=0, has_side_effects=True, vmem_limit_bytes=63 * 1024 * 1024
        ),
    )(tokens.reshape(flat, width), lengths, w_qkv, w_out, w_up, w_down, small)
    acts, vecs = outs[:2]
    wholes = outs[2 : 2 + count]
    rest = outs[2 + count :]
    kept = [dict(zip(KEPT, rest[l * len(KEPT) : (l + 1) * len(KEPT)])) for l in range(layers)]
    return acts, vecs, [wholes[4 * l : 4 * l + 4] for l in range(layers)], kept


SETS = 4
KINDS = ("down", "up", "out", "mix")


def over_rows(a, b):
    return lax.dot_general(a, b, (((0,), (0,)), ((), ())), preferred_element_type=F32)


class Granule:
    def __init__(self, at, index, acc, plane_in, z_in, fin, out, send, recv, local, credit, wait_credit, give_credit):
        self.at, self.index, self.acc, self.plane_in, self.z_in = at, index, acc, plane_in, z_in
        self.fin, self.out, self.send, self.recv, self.local = fin, out, send, recv, local
        self.credit, self.wait_credit, self.give_credit = credit, wait_credit, give_credit
        self.t1 = acc.shape[1] // 4
        self.names, self.posts = {}, []
        core, p = at.core, at.p
        self.direct_p = p + (1 - core) * (2 - 4 * at.py) + core * (1 - 2 * at.px)
        self.owner_dev = {"ctx": at.c8 + (1 - core) * (2 - 4 * at.px) + core * (4 - 8 * at.py)}

    def make(self, name, src, dst, device):
        i = self.names.setdefault(name, len(self.names))
        return remote(src, dst, self.send.at[i], self.recv.at[i], device)

    def post(self, name, src, dst, device, cond=None):
        under(cond, lambda: self.make(name, src, dst, device).start())
        self.posts.append((name, src, dst, device, cond))

    def take(self, name, dst):
        self.make(name, dst, dst, self.at.sib).wait_recv()

    def chunk(self, p):
        return pl.ds(pl.multiple_of(p * self.t1, 16), self.t1)

    def place(self, p, core):
        return self.out.at[pl.ds(pl.multiple_of(core * 4 * self.t1 + p * self.t1, 16), self.t1)]

    def begin(self):
        at = self.at
        if self.wait_credit is not None:
            below = jnp.where(at.z > 0, 1, 0)
            above = jnp.where(at.z < at.depth - 1, 1, 0)
            pl.semaphore_wait(self.wait_credit, 2 + below + above)
        self.post("diag", self.acc.at[:, self.chunk(at.p_d)], self.plane_in.at[0], at.relay_dev)
        self.post("near", self.acc.at[:, self.chunk(self.direct_p)], self.plane_in.at[1], at.relay_dev)

    def relay(self):
        at = self.at
        self.take("diag", self.plane_in.at[0])
        mine = self.chunk(at.relay_from)
        for t in range(at.depth):
            add_rows(self.acc.at[t, mine], self.plane_in.at[0, t], self.t1)
        self.post("relay", self.acc.at[:, mine], self.plane_in.at[2], self.owner_dev)

    def combine(self):
        at = self.at
        self.take("near", self.plane_in.at[1])
        self.take("relay", self.plane_in.at[2])
        mine = self.chunk(at.p)
        for t in range(at.depth):
            add_rows_two(self.acc.at[t, mine], self.plane_in.at[1, t], self.plane_in.at[2, t], self.t1)

    def line(self, step):
        at = self.at
        last = at.depth - 1
        right, left = last - step, step
        mine = self.chunk(at.p)
        acc = lambda t: self.acc.at[t, mine]

        def go(t, here):
            @pl.when(here)
            def _():
                self.take(f"z{t}", self.z_in.at[t])
                add_rows(acc(t), self.z_in.at[t], self.t1)

        is_right, is_left = at.z < right, at.z > left
        under(is_right, lambda: go(right, at.z > 0))
        self.post(f"z{right}", acc(right), self.z_in.at[right], at.up(), is_right)
        under(is_left, lambda: go(left, at.z < last))
        self.post(f"z{left}", acc(left), self.z_in.at[left], at.down(), at.z > left + 1)
        self.post(f"e{left}", acc(left), self.z_in.at[at.depth], at.down(), at.z == left + 1)

    def end(self):
        at = self.at
        last = at.depth - 1
        mine = self.chunk(at.p)
        for t in range(at.depth):
            def below():
                self.take(f"z{t}", self.z_in.at[t])
                add_rows(self.acc.at[t, mine], self.z_in.at[t], self.t1)

            def above():
                self.take(f"e{t}", self.z_in.at[at.depth])
                add_rows(self.acc.at[t, mine], self.z_in.at[at.depth], self.t1)

            if t > 0:
                under(at.z == t, below)
            if t < last:
                under(at.z == t, above)
        if self.give_credit:
            for device in (at.x_dev, at.y_dev):
                pl.semaphore_signal(self.credit, inc=1, device_id=device, device_id_type=MESH)
            under(
                at.z > 0,
                lambda: pl.semaphore_signal(self.credit, inc=1, device_id=at.down(), device_id_type=MESH),
            )
            under(
                at.z < last,
                lambda: pl.semaphore_signal(self.credit, inc=1, device_id=at.up(), device_id_type=MESH),
            )
        self.fin[...] = self.acc[at.z, mine]
        here = self.place(at.p, at.core)
        pltpu.make_async_copy(self.fin, here, self.local).start()
        self.post("sx", self.fin, here, at.x_dev)
        self.post("sy", self.fin, here, at.y_dev)
        self.post("ss", self.fin, here, at.sib)

    def release(self):
        keep = []
        for name, src, dst, device, cond in self.posts:
            if name[0] == "s":
                keep.append((name, src, dst, device, cond))
            else:
                under(cond, lambda: self.make(name, src, dst, device).wait_send())
        self.posts = keep

    def spread_relay(self):
        at = self.at
        for far, p in (("sx", at.p_x), ("sy", at.p_y)):
            here = self.place(p, at.core)
            self.take(far, here)
            self.post(far + "s", here, here, at.sib)
        here = self.place(at.relay_from, at.core)
        self.post("sd", here, here, at.relay_dev)

    def spread_last(self):
        at = self.at
        here = self.place(at.p_d, at.core)
        self.take("sd", here)
        self.post("sds", here, here, at.sib)

    def finish(self):
        at = self.at
        for name, p in (("ss", at.p), ("sxs", at.p_x), ("sys", at.p_y), ("sds", at.p_d)):
            self.take(name, self.place(p, 1 - at.core))
        pltpu.make_async_copy(self.fin, self.place(at.p, at.core), self.local).wait()

    def drain(self):
        for name, src, dst, device, cond in self.posts:
            under(cond, lambda: self.make(name, src, dst, device).wait_send())

    def stages(self):
        steps = range(self.at.depth - 1)
        out = [[self.relay], [self.combine, functools.partial(self.line, 0)]]
        out += [[functools.partial(self.line, i)] for i in steps[1:]]
        out += [[self.end], [self.release, self.spread_relay], [self.spread_last], [self.finish]]
        return out


class KeyGrads:
    def __init__(self, at, parts, sib_in, stage, plane_in, send, recv, local, credit, layer):
        self.at, self.parts, self.sib_in, self.stage, self.plane_in = at, parts, sib_in, stage, plane_in
        self.send, self.recv, self.local, self.credit, self.layer = send, recv, local, credit, layer
        self.names, self.posts = {}, []
        core, p = at.core, at.p
        self.direct_p = p + (1 - core) * (2 - 4 * at.py) + core * (1 - 2 * at.px)
        self.owner_dev = {"ctx": at.c8 + (1 - core) * (2 - 4 * at.px) + core * (4 - 8 * at.py)}
        self.order = [at.p_d, self.direct_p, at.relay_from, at.p]

    def make(self, name, src, dst, device):
        i = self.names.setdefault(name, len(self.names))
        return remote(src, dst, self.send.at[i], self.recv.at[i], device)

    def post(self, name, src, dst, device):
        self.make(name, src, dst, device).start()
        self.posts.append((name, src, dst, device))

    def take(self, name, dst):
        self.make(name, dst, dst, self.at.sib).wait_recv()

    def start(self):
        for i, p in enumerate(self.other_order()):
            self.post(f"s{i}", self.parts.at[1, p], self.sib_in.at[p], self.at.sib)

    def other_order(self):
        at = self.at
        core = 1 - at.core
        direct = at.p + (1 - core) * (2 - 4 * at.py) + core * (1 - 2 * at.px)
        relay = at.p + (1 - core) * (1 - 2 * at.px) + core * (2 - 4 * at.py)
        return [at.p_d, direct, relay, at.p]

    def add(self, p, extra):
        seqs, rows = self.parts.shape[2], self.parts.shape[3]
        for s in range(seqs):
            add_rows(self.parts.at[0, p, s], extra.at[s], rows)

    def core_sum(self, i):
        p = self.order[i]
        self.take(f"s{i}", self.sib_in.at[p])
        copy = pltpu.make_async_copy(self.sib_in.at[p], self.stage, self.local)
        copy.start()
        copy.wait()
        self.add(p, self.stage)

    def first(self):
        at = self.at
        self.core_sum(0)
        if self.layer is not None:
            pl.semaphore_wait(self.credit, 2)
        self.post("diag", self.parts.at[0, at.p_d], self.plane_in.at[0], at.relay_dev)
        self.core_sum(1)
        self.post("near", self.parts.at[0, self.direct_p], self.plane_in.at[1], at.relay_dev)
        self.core_sum(2)
        self.core_sum(3)

    def relay(self):
        at = self.at
        self.take("diag", self.plane_in.at[0])
        self.add(at.relay_from, self.plane_in.at[0])
        self.post("relay", self.parts.at[0, at.relay_from], self.plane_in.at[2], self.owner_dev)

    def combine(self, give_credit):
        at = self.at
        seqs, rows = self.parts.shape[2], self.parts.shape[3]
        self.take("near", self.plane_in.at[1])
        self.take("relay", self.plane_in.at[2])
        for s in range(seqs):
            add_rows_two(self.parts.at[0, at.p, s], self.plane_in.at[1, s], self.plane_in.at[2, s], rows)
        if give_credit:
            for device in (at.x_dev, at.y_dev):
                pl.semaphore_signal(self.credit, inc=1, device_id=device, device_id_type=MESH)

    def drain(self):
        for name, src, dst, device in self.posts:
            self.make(name, src, dst, device).wait_send()
        self.posts = []


def backward_kernel(dims, *refs):
    layers, seqs, rows, slots, width, ff, depth, per_layer = dims
    flat, wide = seqs * rows, pad_lanes(width)
    pairs = wide // LANES
    total = seqs * pairs
    refs = list(refs)

    def grab(n):
        out = refs[:n]
        del refs[:n]
        return out

    cot, lengths, vecs = grab(3)
    kept = [dict(zip(KEPT, grab(len(KEPT)))) for _ in range(layers)]
    wholes = [grab(4) for _ in range(layers)]
    grad_in, small_out = grab(2)
    outs = grab(layers * per_layer)
    kv_sib = grab(layers)
    (g_send, g_recv, g_local, g_credit, kv_send, kv_recv, kv_local, kv_credit) = grab(8)
    (pg_send, pg_recv, pg_local, pg_credit, sm_send, sm_recv, load_sem, w_sem, kvp_sem) = grab(9)
    acc, plane_in, z_in, rest_acc, fin = grab(5)
    g, hx, dn = grab(3)
    gm, gu, ga, gq, gk, gv = grab(6)
    pz, pc, po, pa = grab(4)
    dg, q, go, o, lse, bias, kvp = grab(7)
    parts, kv_stage, kv_plane = grab(3)
    wt_a, wt_u, wt_q, gm3 = grab(4)
    sm, sm_sum, sm_in, sm_z, up_row = grab(5)

    at = Place()
    core = at.core
    barrier = pltpu.get_barrier_semaphore()
    others = [{"fsdp": lax.rem(at.z + i, depth)} for i in range(1, depth)]
    for device in [at.sib, at.x_dev, at.y_dev] + others:
        pl.semaphore_signal(barrier, inc=1, device_id=device, device_id_type=MESH)
    pl.semaphore_wait(barrier, 3 + depth - 1)

    exchange = {
        "down": [("pz", pz), ("gm", gm)],
        "up": [("pc", pc), ("gu", gu)],
        "out": [("po", po), ("ga", ga)],
        "mix": [("pa", pa), ("gq", gq), ("gk", gk), ("gv", gv)],
    }
    slot_of = {}
    for kind in KINDS:
        for name, _ in exchange[kind]:
            slot_of[name] = len(slot_of)
    buffers = {name: buf for kind in KINDS for name, buf in exchange[kind]}
    posted = {}

    def pg_copy(name, src):
        i = slot_of[name]
        buf = buffers[name]
        dst = buf.at[1]
        return remote(src, dst, pg_send.at[i], pg_recv.at[i], at.sib)

    def pg_post(name, src):
        pg_copy(name, src).start()
        posted[name] = src

    def pg_sent(name):
        src = posted.pop(name, None)
        if src is not None:
            pg_copy(name, src).wait_send()

    def pg_take(name):
        buf = buffers[name].at[1]
        pg_copy(name, buf).wait_recv()

    def piece_load(l, name):
        return pltpu.make_async_copy(kept[l][name].at[core], buffers[name].at[0], pg_local.at[slot_of[name]])

    def free_kind(kind, l):
        if l < layers - 1:
            pl.semaphore_wait(pg_credit.at[KINDS.index(kind)], 1)

    def done_kind(kind, l):
        if l > 0:
            pl.semaphore_signal(
                pg_credit.at[KINDS.index(kind)], inc=1, device_id=at.sib, device_id_type=MESH
            )

    active, items = [], []
    line_up = layers * per_layer

    def pump(times=1):
        for _ in range(times):
            for entry in list(active):
                for do in entry[1].pop(0):
                    do()
                if not entry[1]:
                    active.remove(entry)

    def open_set():
        index = len(items)
        if index >= SETS:
            old = items[index - SETS]
            while any(entry[0] is old and len(entry[1]) > 2 for entry in active):
                pump()
        return index

    def launch(source):
        index = len(items)
        s = index % SETS
        item = Granule(
            at, index, source, plane_in.at[s], z_in.at[s], fin.at[index], outs[index],
            g_send.at[index], g_recv.at[index], g_local.at[index], g_credit.at[index],
            g_credit.at[index - SETS] if index >= SETS else None, index + SETS < line_up,
        )
        item.begin()
        items.append(item)
        active.append([item, item.stages()])

    def weight_grad(l, unit, piece, rhs, first):
        index = open_set()
        s = index % SETS
        home = 0 if unit < 8 else 1

        def do(off, size):
            cols = pl.ds(off, size)
            right = rhs[:, :, pl.ds(pl.multiple_of(first + off, LANES), size)].reshape(2 * flat, size)
            left = piece[:, :, pl.ds(0, depth * LANES)].reshape(2 * flat, depth * LANES)
            out = over_rows(left, right).astype(BF16)
            for t in range(depth):
                acc[s, t, :, cols] = out[t * LANES : (t + 1) * LANES]

            @pl.when(core == home)
            def _():
                last = piece[:, :, pl.ds(depth * LANES, LANES)].reshape(2 * flat, LANES)
                more = over_rows(last, right).astype(BF16)
                for t in range(depth):
                    rest_acc[t, pl.ds(16 * (unit - 8 * home), 16), cols] = more[t * 16 : (t + 1) * 16]

        by_tiles(wide, 384, do)
        launch(acc.at[s])

    def rest_grad():
        open_set()
        launch(rest_acc)

    def put_row(l, i, value):
        sm[pl.ds(l * 16 + i, 1), pl.ds(0, width)] = value

    def column_sums(l, i, src):
        put_row(l, i, jnp.sum(src[0, :, pl.ds(0, width)].astype(F32), axis=0, keepdims=True))

    def norm_back(l, i):
        gain = vecs[l, pl.ds(i, 1), pl.ds(0, width)]

        def do(step, carry):
            gain_sum, shift_sum = carry
            here = pl.ds(pl.multiple_of(step * 32, 32), 32)
            unit, scale = row_norm(hx[here, :])
            grad = dn[here, :]
            inner = grad * gain
            mean_inner = jnp.mean(inner, axis=-1, keepdims=True)
            mean_unit = jnp.mean(inner * unit, axis=-1, keepdims=True)
            g[here, :] = g[here, :] + scale * (inner - mean_inner - unit * mean_unit)
            return (
                gain_sum + jnp.sum(grad * unit, axis=0, keepdims=True),
                shift_sum + jnp.sum(grad, axis=0, keepdims=True),
            )

        zero = jnp.zeros((1, width), F32)
        gain_sum, shift_sum = lax.fori_loop(0, flat // 32, do, (zero, zero))
        put_row(l, i, gain_sum)
        put_row(l, 2 + i, shift_sum)

    def load(l, name, dst, index):
        return pltpu.make_async_copy(kept[l][name], dst, load_sem.at[index])

    def low_copy(src, dst):
        def do(first, size):
            here = pl.ds(first, size)
            dst[0, here, pl.ds(0, width)] = src[here, :].astype(BF16)

        by_tiles(flat, 64, do)

    def row_tile(whole, buf, slot, first, size, sem):
        return pltpu.make_async_copy(
            whole.at[pl.ds(first, size)], buf.at[slot, pl.ds(0, size)], sem.at[slot]
        )

    def ff_back(l):
        w_up, w_down = wholes[l][2], wholes[l][3]
        tile = 256
        count = ff // tile

        def copies(i, slot):
            first = pl.multiple_of(i * tile, tile)
            return (
                pltpu.make_async_copy(w_down.at[pl.ds(first, tile)], wt_a.at[slot], w_sem.at[0, slot]),
                pltpu.make_async_copy(w_up.at[:, pl.ds(first, tile)], wt_u.at[slot], w_sem.at[1, slot]),
            )

        dn[...] = jnp.zeros_like(dn)
        for copy in copies(0, 0):
            copy.start()

        def step(i, carry):
            slot = lax.rem(i, 2)
            for copy in copies(i, slot):
                copy.wait()

            @pl.when(i + 1 < count)
            def _():
                for copy in copies(i + 1, 1 - slot):
                    copy.start()

            cols = pl.ds(pl.multiple_of(i * tile, tile), tile)
            grad = across(gm[0, :, pl.ds(0, width)], wt_a[slot])
            low = (grad * dg[:, cols].astype(F32)).astype(BF16)
            gu[0, :, cols] = low
            up_row[pl.ds(0, 1), cols] = jnp.sum(low.astype(F32), axis=0, keepdims=True)
            dn[...] = dn[...] + across(low, wt_u[slot])
            return carry

        def part(first, size):
            lax.fori_loop(first, first + size, step, 0)

        half = count // 2
        part(0, half)
        pump()
        part(half, count - half)

    def tiles_back(whole, buf, sem, left, put):
        tile = buf.shape[1]
        spans = [(i, min(tile, width - i)) for i in range(0, width, tile)]
        row_tile(whole, buf, 0, *spans[0], sem).start()
        for n, (first, size) in enumerate(spans):
            row_tile(whole, buf, n % 2, first, size, sem).wait()
            if n + 1 < len(spans):
                row_tile(whole, buf, (n + 1) % 2, *spans[n + 1], sem).start()
            put(first, size, across(left(), buf[n % 2, pl.ds(0, size)]))

    def kv_copy(l, it, slot):
        s, j = it // pairs, lax.rem(it, pairs)
        return [
            pltpu.make_async_copy(
                kept[l]["kv"].at[s, :, pl.ds(pl.multiple_of(i * wide + j * LANES, LANES), LANES)],
                kvp.at[slot, i],
                kvp_sem.at[slot, i],
            )
            for i in range(2)
        ]

    def attend_back(l, first, count):
        def step(it, carry):
            slot = lax.rem(it, 2)
            for copy in kv_copy(l, it, slot):
                copy.wait()

            @pl.when(it + 1 < total)
            def _():
                for copy in kv_copy(l, it + 1, 1 - slot):
                    copy.start()

            s, j = it // pairs, lax.rem(it, pairs)
            here = pl.ds(pl.multiple_of(s * rows, rows), rows)
            col = pl.ds(pl.multiple_of(j * LANES, LANES), LANES)
            col_v = pl.ds(pl.multiple_of(wide + j * LANES, LANES), LANES)
            q2, go_block = two_heads(q[here, col]), go[here, col]
            go2 = two_heads(go_block)
            keys, values = kvp[slot, 0], kvp[slot, 1]
            product = go_block.astype(F32) * o[here, col].astype(F32)
            delta = jnp.sum(two_heads(product), axis=-1, keepdims=True)
            lane = lax.broadcasted_iota(jnp.int32, (2 * rows, LANES), 1)
            block = lse[pl.ds(pl.multiple_of(s * 2 * rows, rows), 2 * rows), :]
            log_total = jnp.sum(jnp.where(lane == it, block, 0.0), axis=-1, keepdims=True)
            seen = bias[s]
            scores = across(q2, keys) * (HEAD_DIM ** (-0.5)) + jnp.concatenate([seen, seen], axis=0)
            probs = jnp.exp(scores - log_total)
            grads = across(go2, values)
            low = (probs * (grads - delta)).astype(BF16)
            dq = jnp.dot(low, keys, preferred_element_type=F32) * (HEAD_DIM ** (-0.5))
            gq[0, here, col] = one_pair(dq, rows).astype(BF16)
            dk = (over_rows(low, q2) * (HEAD_DIM ** (-0.5))).astype(BF16)
            dv = over_rows(probs.astype(BF16), go2).astype(BF16)
            for b in range(slots // rows):
                mine = lax.rem(b + core, 2)
                span = slice(b * rows, (b + 1) * rows)
                parts[mine, b // 2, s, :, col] = dk[span]
                parts[mine, b // 2, s, :, col_v] = dv[span]
            return carry

        lax.fori_loop(first, first + count, step, 0)

    loads = {}

    def early(l):
        for i, (name, dst) in enumerate((("h1", hx), ("dg", dg), ("q", q), ("o", o), ("lse", lse))):
            loads[name] = load(l, name, dst, i)
            loads[name].start()
        for kind in KINDS:
            free_kind(kind, l)
            name = exchange[kind][0][0]
            piece_load(l, name).start()
            pg_sent(name)
            pg_post(name, kept[l][name].at[1 - core])

    rest_acc[...] = jnp.zeros_like(rest_acc)
    sm[...] = jnp.zeros_like(sm)
    for buf in (gm, gu, ga, gq, gk, gv):
        buf[0] = jnp.zeros(buf.shape[1:], BF16)
    go[...] = jnp.zeros_like(go)
    early(layers - 1)
    for s in range(seqs):

        def first_grad(first, size):
            here = pl.ds(s * rows + first, size)
            place = at.c8 * rows + first + lax.broadcasted_iota(jnp.int32, (size, width), 0)
            g[here, :] = jnp.where(place < lengths[s], cot[here, :].astype(F32), 0.0)

        by_tiles(rows, 32, first_grad)
    key_bias(bias, seqs, rows, slots, lengths, at.c8)

    for l in reversed(range(layers)):
        keys = KeyGrads(
            at, parts, kv_sib[l], kv_stage, kv_plane, kv_send.at[l], kv_recv.at[l], kv_local,
            kv_credit, None if l == layers - 1 else l,
        )
        if l < layers - 1:
            early(l)
        pg_sent("gm")
        low_copy(g, gm)
        pg_post("gm", gm.at[0])
        column_sums(l, 7, gm)
        piece_load(l, "pz").wait()
        pg_take("pz")
        pg_take("gm")
        for i in range(4):
            weight_grad(l, i, pz.at[:, i], gm, 0)
            pump()
        done_kind("down", l)
        loads["dg"].wait()
        pg_sent("gu")
        ff_back(l)
        pg_post("gu", gu.at[0])
        pump()
        for r in range(4):
            sm[pl.ds(l * 16 + 8 + r, 1), :] = up_row[pl.ds(0, 1), pl.ds(r * wide, wide)]
        loads["h1"].wait()
        norm_back(l, 1)
        loads["h"] = load(l, "h", hx, 5)
        loads["h"].start()
        pg_sent("ga")
        low_copy(g, ga)
        pg_post("ga", ga.at[0])
        column_sums(l, 6, ga)
        pump()

        def put_go(first, size, value):
            go[:, pl.ds(first, size)] = value.astype(BF16)

        tiles_back(wholes[l][1], wt_a, w_sem.at[0], lambda: ga[0, :, pl.ds(0, width)], put_go)
        for copy in kv_copy(l, 0, 0):
            copy.start()
        pump()
        piece_load(l, "pc").wait()
        pg_take("pc")
        pg_take("gu")
        for i in range(4):
            weight_grad(l, 4 + i, pc, gu, i * wide)
            pump()
        done_kind("up", l)
        piece_load(l, "po").wait()
        pg_take("po")
        pg_take("ga")
        weight_grad(l, 8, po, ga, 0)
        done_kind("out", l)
        pump()
        for name in ("q", "o", "lse"):
            loads[name].wait()
        pg_sent("gq")
        step = 3
        for first in range(0, total, step):
            attend_back(l, first, min(step, total - first))
            pump()
        keys.start()
        pg_post("gq", gq.at[0])
        column_sums(l, 4, gq)
        keys.first()
        pump()
        keys.relay()
        pump()
        keys.combine(l > 0)
        pg_sent("gk")
        pg_sent("gv")
        for s in range(seqs):
            here = pl.ds(s * rows, rows)
            gk[0, here, :] = parts[0, at.p, s, :, pl.ds(0, wide)]
            gv[0, here, :] = parts[0, at.p, s, :, pl.ds(wide, wide)]
        pg_post("gk", gk.at[0])
        pg_post("gv", gv.at[0])
        column_sums(l, 5, gv)
        for i, src in enumerate((gq, gk, gv)):

            def join(first, size):
                here = pl.ds(first, size)
                gm3[here, pl.ds(i * width, width)] = src[0, here, pl.ds(0, width)]

            by_tiles(flat, 64, join)

        def put_dn(first, size, value):
            dn[:, pl.ds(first, size)] = value

        piece_load(l, "pa").wait()
        pg_take("pa")
        pg_take("gq")
        weight_grad(l, 9, pa, gq, 0)
        pg_take("gk")
        weight_grad(l, 10, pa, gk, 0)
        pg_take("gv")
        weight_grad(l, 11, pa, gv, 0)
        done_kind("mix", l)
        rest_grad()
        rest_item = items[-1]
        pump()
        tiles_back(wholes[l][0], wt_q, w_sem.at[2], lambda: gm3[...], put_dn)
        loads["h"].wait()
        pump()
        norm_back(l, 0)
        keys.drain()
        while l and any(entry[0] is rest_item and len(entry[1]) > 2 for entry in active):
            pump()

    def do_out(first, size):
        here = pl.ds(first, size)
        grad_in[here, :] = g[here, :]

    by_tiles(flat, 64, do_out)

    def sm_copy(i, src, dst, device):
        return remote(src, dst, sm_send.at[i], sm_recv.at[i], device)

    current = sm
    for i, device in enumerate((at.sib, at.x_dev, at.y_dev)):
        copy = sm_copy(i, current, sm_in.at[i], device)
        copy.start()
        pump()
        copy.wait()
        sm_sum[i] = current[...] + sm_in[i]
        current = sm_sum.at[i]
    hops = []
    for i, device in enumerate(others):
        copy = sm_copy(3 + i, current, sm_z.at[i], device)
        copy.start()
        hops.append(copy)
    pump()
    for copy in hops:
        copy.wait()
    small_total = jnp.zeros(sm.shape, F32)
    for z in range(depth):
        slot = lax.rem(at.z - z - 1 + 2 * depth, depth)
        other = sm_z[jnp.minimum(slot, depth - 2)]
        small_total = small_total + jnp.where(slot == depth - 1, current[...], other)
    small_out[...] = small_total
    while active:
        pump()
    for item in items:
        item.drain()
    for name in list(posted):
        pg_sent(name)


def backward(cotangent, lengths, vecs, kept, wholes, layers, ff):
    seqs, rows, width = cotangent.shape
    depth = lax.axis_size("fsdp")
    slots = rows * lax.axis_size("ctx")
    flat, wide = seqs * rows, pad_lanes(width)
    per_layer = 13
    count = layers * per_layer
    dims = (layers, seqs, rows, slots, width, ff, depth, per_layer)
    any_spec = pl.BlockSpec(memory_space=pl.ANY)
    vmem = pl.BlockSpec(memory_space=pltpu.VMEM)
    struct = lambda shape, kind: jax.ShapeDtypeStruct(shape, kind)
    out_shape = [struct((flat, width), F32), struct((layers * 16, wide), F32)]
    out_shape += [struct((2 * LANES, wide), BF16) for _ in range(count)]
    out_shape += [struct((4, seqs, rows, 2 * wide), BF16) for _ in range(layers)]
    dma, regular = pltpu.SemaphoreType.DMA, pltpu.SemaphoreType.REGULAR
    low = lambda *shape: pltpu.VMEM(shape, BF16)
    full = lambda *shape: pltpu.VMEM(shape, F32)
    chunk = LANES // 4
    scratch = [
        dma((count, 24)), dma((count, 24)), dma((count,)), regular((count,)),
        dma((layers, 8)), dma((layers, 8)), dma, regular,
        dma((10,)), dma((10,)), dma((10,)), regular((4,)), dma((8,)), dma((8,)), dma((8,)), dma((3, 2)), dma((2, 2)),
        low(SETS, depth, LANES, wide), low(SETS, 3, depth, chunk, wide), low(SETS, depth + 1, chunk, wide),
        low(depth, LANES, wide), low(count, chunk, wide),
        full(flat, width), full(flat, width), full(flat, width),
        low(2, flat, wide), low(2, flat, 4 * wide), low(2, flat, wide),
        low(2, flat, wide), low(2, flat, wide), low(2, flat, wide),
        low(2, 4, flat, PIECE), low(2, flat, PIECE), low(2, flat, PIECE), low(2, flat, PIECE),
        low(flat, ff), low(flat, wide), low(flat, wide), low(flat, wide), full(2 * flat, LANES),
        full(seqs, rows, slots), low(2, 2, slots, LANES),
        low(2, 4, seqs, rows, 2 * wide), low(seqs, rows, 2 * wide), low(3, seqs, rows, 2 * wide),
        low(2, 256, width), low(2, width, 256), low(2, 256, 3 * width), low(flat, 3 * width),
        full(layers * 16, wide), full(3, layers * 16, wide), full(3, layers * 16, wide),
        full(depth - 1, layers * 16, wide), full(8, 4 * wide),
    ]
    flat_kept = [kept[l][name] for l in range(layers) for name in KEPT]
    flat_wholes = [item for layer in wholes for item in layer]
    outs = pl.pallas_call(
        functools.partial(backward_kernel, dims),
        out_shape=out_shape,
        in_specs=[vmem, pl.BlockSpec(memory_space=pltpu.SMEM), vmem]
        + [any_spec] * (len(flat_kept) + len(flat_wholes)),
        out_specs=[vmem, vmem] + [any_spec] * (len(out_shape) - 2),
        scratch_shapes=scratch,
        compiler_params=pltpu.CompilerParams(
            collective_id=1, has_side_effects=True, vmem_limit_bytes=63 * 1024 * 1024
        ),
    )(cotangent.reshape(flat, width), lengths, vecs, *flat_kept, *flat_wholes)
    sums = outs[2 : 2 + count]
    grads = [sums[(layers - 1 - l) * per_layer : (layers - l) * per_layer] for l in range(layers)]
    return outs[0], outs[1].reshape(layers, 16, wide), grads


def assemble(sums, width, ff):
    rest = sums[12]
    unit = lambda u: jnp.concatenate([sums[u], rest[16 * u : 16 * u + 16]], axis=0)
    down = jnp.concatenate([unit(i)[:, :width] for i in range(4)], axis=0)
    up = jnp.concatenate([unit(4 + i) for i in range(4)], axis=1)[:, :ff]
    out = unit(8)[:, :width]
    mix = jnp.concatenate([unit(9 + i)[:, :width] for i in range(3)], axis=1)
    return [item.astype(F32) for item in (down, up, out, mix)]


def normalize(values, scales, shifts):
    average = jnp.mean(values, axis=-1, keepdims=True)
    centred = values - average
    variance = jnp.mean(centred * centred, axis=-1, keepdims=True)
    return centred * lax.rsqrt(variance + 1e-05) * scales + shifts


def outer_sum(left_rows, right_rows):
    return lax.dot_general(
        left_rows, right_rows, (((0,), (0,)), ((), ())), preferred_element_type=jnp.float32
    )


def times_transpose(left_rows, weight_rows):
    return lax.dot_general(
        left_rows, weight_rows, (((1,), (1,)), ((), ())), preferred_element_type=jnp.float32
    )


def allowed_mask(positions, key_places, lengths):
    causal = (key_places[None, :] <= positions[:, None]) & (key_places[None, :] >= 0)
    inside = key_places[None, :] < lengths[:, None]
    return causal[None, None, :, :] & inside[:, None, None, :]


def attend_forward(queries, key_part, value_part, positions, lengths, score_scale):
    seq_count, row_count, head_count, head_width = queries.shape
    lowest = jnp.full((seq_count, head_count, row_count), -1e30, jnp.float32)
    key_places = jnp.arange(key_part.shape[1], dtype=jnp.int32)
    allowed = allowed_mask(positions, key_places, lengths)
    scores = (
        jnp.einsum("sqhe,skhe->shqk", queries, key_part, preferred_element_type=jnp.float32)
        * score_scale
    )
    scores = jnp.where(allowed, scores, -1e30)
    new_top = jnp.maximum(lowest, jnp.max(scores, axis=-1))
    exp_weights = jnp.where(allowed, jnp.exp(scores - new_top[..., None]), 0.0)
    running_total = jnp.sum(exp_weights, axis=-1)
    running_sum = jnp.einsum(
        "shqk,skhe->shqe",
        exp_weights.astype(jnp.bfloat16),
        value_part,
        preferred_element_type=jnp.float32,
    )
    output = jnp.transpose(running_sum / running_total[..., None], (0, 2, 1, 3))
    return (output, new_top + jnp.log(running_total))


def block_terms(
    queries,
    grad_out,
    log_total,
    delta_row,
    key_part,
    value_part,
    first_key,
    positions,
    lengths,
    score_scale,
):
    key_places = first_key + jnp.arange(key_part.shape[1], dtype=jnp.int32)
    allowed = allowed_mask(positions, key_places, lengths)
    scores = (
        jnp.einsum("sqhe,skhe->shqk", queries, key_part, preferred_element_type=jnp.float32)
        * score_scale
    )
    scores = jnp.where(allowed, scores, -1e30)
    probability = jnp.where(allowed, jnp.exp(scores - log_total[..., None]), 0.0)
    grad_probs = jnp.einsum(
        "sqhe,skhe->shqk", grad_out, value_part, preferred_element_type=jnp.float32
    )
    grad_scores = (probability * (grad_probs - delta_row[..., None])).astype(jnp.bfloat16)
    query_add = (
        jnp.einsum("shqk,skhe->sqhe", grad_scores, key_part, preferred_element_type=jnp.float32)
        * score_scale
    )
    key_add = (
        jnp.einsum("shqk,sqhe->skhe", grad_scores, queries, preferred_element_type=jnp.float32)
        * score_scale
    )
    value_add = jnp.einsum(
        "shqk,sqhe->skhe",
        probability.astype(jnp.bfloat16),
        grad_out,
        preferred_element_type=jnp.float32,
    )
    return (query_add, key_add, value_add)


def pack_small(ln_gain, ln_bias, b_qv, b_out, b_up, b_down):
    layers, _, part = ln_gain.shape
    return jnp.concatenate(
        [ln_gain, ln_bias, b_qv, b_out[:, None], b_down[:, None], b_up.reshape(layers, 4, part)],
        axis=1,
    )


def unpack_small(whole):
    depth, _, part = whole.shape
    flat = jnp.transpose(whole[:, :8], (1, 0, 2)).reshape(8, depth * part)
    up_bias = whole[:, 8:].reshape(depth * 4 * part)
    return flat[0:2], flat[2:4], flat[4:6], flat[6], flat[7], up_bias


def small_rows(gains, shifts, mix_bias, out_bias, down_bias, up_bias, depth):
    width = gains.shape[-1]
    flat = jnp.concatenate([gains, shifts, mix_bias, out_bias[None], down_bias[None]], axis=0)
    flat = jnp.transpose(flat.reshape(8, depth, width // depth), (1, 0, 2))
    return jnp.concatenate([flat, up_bias.reshape(depth, 4, width // depth)], axis=1)


def fast_mesh(rows):
    return lax.axis_size("ctx") == 8 and rows % 272 == 0


def gather_all(weights, small):
    flat = [item for layer in weights for item in layer]
    layers = len(weights)
    wholes = [lax.all_gather(item, "fsdp", axis=0, tiled=True) for item in flat]
    small_all = lax.all_gather(small, "fsdp", axis=0)
    return [wholes[4 * i : 4 * i + 4] for i in range(layers)], [small_all[:, i] for i in range(layers)]


def reduce_layer(grads):
    shards_now = [
        lax.psum_scatter(item, "fsdp", scatter_dimension=0, tiled=True) for item in grads
    ]
    return [lax.psum(item, "ctx") for item in shards_now]


def shards(
    tokens,
    lengths,
    cotangent,
    ln_gain,
    ln_bias,
    w_qkv,
    b_qv,
    w_out,
    b_out,
    w_up,
    b_up,
    w_down,
    b_down,
):
    seq_count, row_count, model_width = tokens.shape
    head_width = HEAD_DIM
    head_count = model_width // head_width
    score_scale = head_width ** (-0.5)
    ctx_index = lax.axis_index("ctx")
    depth = lax.axis_size("fsdp")
    positions = ctx_index * row_count + jnp.arange(row_count, dtype=jnp.int32)
    valid_rows = (positions[None, :] < lengths[:, None]).astype(jnp.float32)[..., None]
    flat_rows = seq_count * row_count
    split_shape = (seq_count, row_count, head_count, head_width)
    layer_total = ln_gain.shape[0]
    hidden = tokens.astype(jnp.float32).reshape(flat_rows, model_width)
    small = pack_small(ln_gain, ln_bias, b_qv, b_out, b_up, b_down)
    if fast_mesh(w_qkv.shape[1]):
        part = small.shape[2]
        ff = w_up.shape[2]
        padded = jnp.pad(small, ((0, 0), (0, 4), (0, pad_lanes(part) - part)))
        activations, vectors, weights, kept = forward(
            tokens, lengths, w_qkv, w_out, w_up, w_down, padded.reshape(layer_total * 16, -1)
        )
        grad_in, small_sums, sums = backward(
            cotangent, lengths, vectors, kept, weights, layer_total, ff
        )
        mine = lambda rows: lax.dynamic_slice_in_dim(
            rows[..., :model_width], lax.axis_index("fsdp") * part, part, axis=rows.ndim - 1
        )
        up_bias = small_sums[:, 8:12].reshape(layer_total, -1)[:, :ff]
        up_part = ff // depth
        shard_grads = [assemble(item, model_width, ff) for item in sums]
        whole = lambda member: jnp.stack([item[member] for item in shard_grads])
        return (
            activations.reshape(tokens.shape),
            grad_in.reshape(tokens.shape),
            mine(small_sums[:, 0:2]),
            mine(small_sums[:, 2:4]),
            whole(3),
            mine(small_sums[:, 4:6]),
            whole(2),
            mine(small_sums[:, 6]),
            whole(1),
            lax.dynamic_slice_in_dim(up_bias, lax.axis_index("fsdp") * up_part, up_part, axis=1),
            whole(0),
            mine(small_sums[:, 7]),
        )
    weights, smalls = gather_all(
        [(w_qkv[i], w_out[i], w_up[i], w_down[i]) for i in range(layer_total)], small
    )
    kept_layers = []
    for layer_index in range(layer_total):
        mix_weight, out_weight, up_weight, down_weight = weights[layer_index]
        gain_rows, shift_rows, mix_bias, out_bias, down_bias, up_bias = unpack_small(
            smalls[layer_index].astype(jnp.float32)
        )
        normed_first = normalize(hidden, gain_rows[0], shift_rows[0]).astype(jnp.bfloat16)
        mixed_rows = jnp.dot(normed_first, mix_weight, preferred_element_type=jnp.float32)
        queries = (
            (mixed_rows[:, :model_width] + mix_bias[0]).astype(jnp.bfloat16).reshape(split_shape)
        )
        key_rows = (
            mixed_rows[:, model_width : 2 * model_width].astype(jnp.bfloat16).reshape(split_shape)
        )
        value_rows = (
            (mixed_rows[:, 2 * model_width :] + mix_bias[1])
            .astype(jnp.bfloat16)
            .reshape(split_shape)
        )
        key_part = lax.all_gather(key_rows, "ctx", axis=1, tiled=True)
        value_part = lax.all_gather(value_rows, "ctx", axis=1, tiled=True)
        output, log_total = attend_forward(
            queries, key_part, value_part, positions, lengths, score_scale
        )
        output = output.reshape(flat_rows, model_width)
        attended = output.astype(jnp.bfloat16)
        middle = (
            hidden + jnp.dot(attended, out_weight, preferred_element_type=jnp.float32) + out_bias
        )
        normed_second = normalize(middle, gain_rows[1], shift_rows[1]).astype(jnp.bfloat16)
        upper_pre = (
            jnp.dot(normed_second, up_weight, preferred_element_type=jnp.float32) + up_bias
        )
        active = jax.nn.gelu(upper_pre).astype(jnp.bfloat16)
        kept_layers.append(
            (
                hidden,
                normed_first,
                queries,
                key_part,
                value_part,
                output,
                log_total,
                attended,
                middle,
                normed_second,
                upper_pre,
                active,
                gain_rows,
                shift_rows,
            )
        )
        hidden = (
            middle + jnp.dot(active, down_weight, preferred_element_type=jnp.float32) + down_bias
        )
    activations = (valid_rows * hidden.reshape(seq_count, row_count, model_width)).astype(
        jnp.bfloat16
    )
    grad_hidden = (cotangent.astype(jnp.float32) * valid_rows).reshape(flat_rows, model_width)
    big_grads = [None] * layer_total
    small_grads = [None] * layer_total
    for layer_index in reversed(range(layer_total)):
        (
            hidden_in,
            normed_first,
            queries,
            key_part,
            value_part,
            output,
            log_total,
            attended,
            middle,
            normed_second,
            upper_pre,
            active,
            gain_rows,
            shift_rows,
        ) = kept_layers[layer_index]
        mix_weight, out_weight, up_weight, down_weight = weights[layer_index]
        grad_branch = grad_hidden.astype(jnp.bfloat16)
        down_bias_grad = jnp.sum(grad_branch.astype(jnp.float32), axis=0)
        down_grad = outer_sum(active, grad_branch)
        grad_active = times_transpose(grad_branch, down_weight)
        unused_gelu, gelu_pull = jax.vjp(jax.nn.gelu, upper_pre)
        grad_upper = gelu_pull(grad_active)[0].astype(jnp.bfloat16)
        up_bias_grad = jnp.sum(grad_upper.astype(jnp.float32), axis=0)
        up_grad = outer_sum(normed_second, grad_upper)
        grad_normed = times_transpose(grad_upper, up_weight)
        unused_norm, norm_pull = jax.vjp(normalize, middle, gain_rows[1], shift_rows[1])
        grad_middle, gain_second, shift_second = norm_pull(grad_normed)
        grad_middle = grad_middle + grad_hidden
        grad_attn = grad_middle.astype(jnp.bfloat16)
        out_bias_grad = jnp.sum(grad_attn.astype(jnp.float32), axis=0)
        out_grad = outer_sum(attended, grad_attn)
        grad_output = times_transpose(grad_attn, out_weight).astype(jnp.bfloat16)
        delta_row = jnp.transpose(
            jnp.sum((grad_output.astype(jnp.float32) * output).reshape(split_shape), axis=-1),
            (0, 2, 1),
        )
        grad_heads = grad_output.reshape(split_shape)
        query_grad, key_add, value_add = block_terms(
            queries,
            grad_heads,
            log_total,
            delta_row,
            key_part,
            value_part,
            0,
            positions,
            lengths,
            score_scale,
        )
        key_low = lax.psum_scatter(
            key_add.astype(jnp.bfloat16), "ctx", scatter_dimension=1, tiled=True
        ).reshape(flat_rows, model_width)
        value_low = lax.psum_scatter(
            value_add.astype(jnp.bfloat16), "ctx", scatter_dimension=1, tiled=True
        ).reshape(flat_rows, model_width)
        query_low = query_grad.reshape(flat_rows, model_width).astype(jnp.bfloat16)
        grad_mixed = jnp.concatenate([query_low, key_low, value_low], axis=1)
        mix_bias_grad = jnp.stack(
            [
                jnp.sum(query_low.astype(jnp.float32), axis=0),
                jnp.sum(value_low.astype(jnp.float32), axis=0),
            ]
        )
        mix_grad = outer_sum(normed_first, grad_mixed)
        grad_normed_first = times_transpose(grad_mixed, mix_weight)
        unused_first, first_pull = jax.vjp(normalize, hidden_in, gain_rows[0], shift_rows[0])
        grad_input, gain_first, shift_first = first_pull(grad_normed_first)
        grad_hidden = grad_input + grad_middle
        big_grads[layer_index] = reduce_layer(
            [item.astype(jnp.bfloat16) for item in (up_grad, down_grad, mix_grad, out_grad)]
        )
        small_grads[layer_index] = small_rows(
            jnp.stack([gain_first, gain_second]),
            jnp.stack([shift_first, shift_second]),
            mix_bias_grad,
            out_bias_grad,
            down_bias_grad,
            up_bias_grad,
            depth,
        )
    input_grad = grad_hidden.reshape(seq_count, row_count, model_width)
    packed = jnp.stack(small_grads).astype(jnp.bfloat16)
    total = lax.psum(packed, ("fsdp", "ctx"))
    own = lax.dynamic_index_in_dim(total, lax.axis_index("fsdp"), 1, keepdims=False)
    own = own.astype(jnp.float32)

    def whole(member):
        return jnp.stack([big_grads[i][member].astype(jnp.float32) for i in range(layer_total)])

    return (
        activations,
        input_grad,
        own[:, 0:2],
        own[:, 2:4],
        whole(2),
        own[:, 4:6],
        whole(3),
        own[:, 6],
        whole(0),
        own[:, 8:].reshape(layer_total, -1),
        whole(1),
        own[:, 7],
    )


def solution(mesh):
    placed = (
        P("fsdp", "ctx", None),
        P("fsdp"),
        P("fsdp", "ctx", None),
        P(None, None, "fsdp"),
        P(None, None, "fsdp"),
        P(None, "fsdp", None),
        P(None, None, "fsdp"),
        P(None, "fsdp", None),
        P(None, "fsdp"),
        P(None, "fsdp", None),
        P(None, "fsdp"),
        P(None, "fsdp", None),
        P(None, "fsdp"),
    )
    return jax.shard_map(
        shards,
        mesh=mesh,
        in_specs=placed,
        out_specs=(
            P("fsdp", "ctx", None),
            P("fsdp", "ctx", None),
            P(None, None, "fsdp"),
            P(None, None, "fsdp"),
            P(None, "fsdp", None),
            P(None, None, "fsdp"),
            P(None, "fsdp", None),
            P(None, "fsdp"),
            P(None, "fsdp", None),
            P(None, "fsdp"),
            P(None, "fsdp", None),
            P(None, "fsdp"),
        ),
        check_vma=False,
    )
```

```python
import functools

import jax
import jax.numpy as jnp
from jax import lax
from jax.experimental import pallas as pl
from jax.experimental.pallas import tpu as pltpu
from jax.sharding import PartitionSpec as P

MESH = pl.DeviceIdType.MESH


class Place:
    def __init__(self):
        self.depth = lax.axis_size("fsdp")
        self.z = lax.axis_index("fsdp")
        self.c8 = lax.axis_index("ctx")
        self.core = lax.rem(self.c8, 2)
        self.p = self.c8 // 2
        self.px = lax.rem(self.p, 2)
        self.py = self.p // 2
        self.sib = {"ctx": self.c8 + 1 - 2 * self.core}
        self.x_dev = {"ctx": self.c8 + 2 - 4 * self.px}
        self.y_dev = {"ctx": self.c8 + 4 - 8 * self.py}
        self.p_x = self.p + 1 - 2 * self.px
        self.p_y = self.p + 2 - 4 * self.py
        self.p_d = 3 - self.p
        self.relay_from = self.p + (1 - self.core) * (1 - 2 * self.px) + self.core * (2 - 4 * self.py)
        self.relay_dev = {
            "ctx": self.c8 + (1 - self.core) * (4 - 8 * self.py) + self.core * (2 - 4 * self.px)
        }

    def up(self):
        return {"fsdp": self.z + 1}

    def down(self):
        return {"fsdp": self.z - 1}

    def greet(self):
        barrier = pltpu.get_barrier_semaphore()
        for device in (self.sib, self.x_dev, self.y_dev):
            pl.semaphore_signal(barrier, inc=1, device_id=device, device_id_type=MESH)

        @pl.when(self.z > 0)
        def _():
            pl.semaphore_signal(barrier, inc=1, device_id=self.down(), device_id_type=MESH)

        @pl.when(self.z < self.depth - 1)
        def _():
            pl.semaphore_signal(barrier, inc=1, device_id=self.up(), device_id_type=MESH)

        below = jnp.where(self.z > 0, 1, 0)
        above = jnp.where(self.z < self.depth - 1, 1, 0)
        pl.semaphore_wait(barrier, 3 + below + above)


def remote(src, dst, send_sem, recv_sem, device):
    return pltpu.make_async_remote_copy(
        src_ref=src, dst_ref=dst, send_sem=send_sem, recv_sem=recv_sem, device_id=device, device_id_type=MESH
    )


class Gather:
    def __init__(self, at, own, whole, left_core, send, recv, line=0):
        self.at, self.own, self.whole = at, own, whole
        self.send, self.recv = send, recv
        rows = own.shape[0]
        self.rows = rows
        unit = rows // 17
        self.block = 8 * unit
        self.t1 = 2 * unit - line
        self.line = pl.ds(pl.multiple_of(at.core * self.block + 4 * self.t1, 16), 4 * line) if line else None
        self.rest = pl.ds(16 * unit, unit)
        self.has_rest = at.core == left_core

    def t1_rows(self, p, core=None):
        core = self.at.core if core is None else core
        return pl.ds(pl.multiple_of(core * self.block + p * self.t1, 16), self.t1)

    def block_rows(self, core):
        return pl.ds(pl.multiple_of(core * self.block, 16), self.block)

    def copy(self, kind, shard, rows, device, src=None, second=False):
        depth = self.at.depth
        slot = kind * depth + shard
        place = self.place(shard, rows)
        src = place if src is None else src
        send = self.send.at[(8 * depth + kind) if second else slot]
        return remote(src, place, send, self.recv.at[slot], device)

    def place(self, shard, rows):
        first = pl.multiple_of(shard * self.rows + rows.start, 16)
        return self.whole.at[pl.ds(first, rows.size)]

    def start(self):
        at = self.at
        mine = self.t1_rows(at.p)

        @pl.when(at.z < at.depth - 1)
        def _():
            self.copy(0, at.z, mine, at.up(), self.own.at[mine]).start()
            if self.line:
                self.copy(7, at.z, self.line, at.up(), self.own.at[self.line]).start()

            @pl.when(self.has_rest)
            def _():
                self.copy(1, at.z, self.rest, at.up(), self.own.at[self.rest]).start()

        @pl.when(at.z > 0)
        def _():
            self.copy(0, at.z, mine, at.down(), self.own.at[mine], True).start()
            if self.line:
                self.copy(7, at.z, self.line, at.down(), self.own.at[self.line], True).start()

            @pl.when(self.has_rest)
            def _():
                self.copy(1, at.z, self.rest, at.down(), self.own.at[self.rest], True).start()

    def cases(self, step, do):
        at = self.at

        @pl.when(at.z - 1 - step >= 0)
        def _():
            do(at.z - 1 - step, at.z < at.depth - 1, at.up())

        @pl.when(at.z + 1 + step < at.depth)
        def _():
            do(at.z + 1 + step, at.z > 0, at.down())

    def arrive(self, step):
        at = self.at
        mine = self.t1_rows(at.p)

        def do(shard, onward, device):
            self.copy(0, shard, mine, at.sib).wait_recv()

            @pl.when(onward)
            def _():
                self.copy(0, shard, mine, device).start()

            self.copy(2, shard, mine, at.x_dev).start()
            self.copy(3, shard, mine, at.y_dev).start()
            if self.line:
                self.copy(7, shard, self.line, at.sib).wait_recv()

                @pl.when(onward)
                def _():
                    self.copy(7, shard, self.line, device).start()

            @pl.when(self.has_rest)
            def _():
                self.copy(1, shard, self.rest, at.sib).wait_recv()

                @pl.when(onward)
                def _():
                    self.copy(1, shard, self.rest, device).start()

                self.copy(5, shard, self.rest, at.sib).start()

        self.cases(step, do)

    def plane(self, step):
        at = self.at

        def do(shard, onward, device):
            self.copy(2, shard, self.t1_rows(at.p_x), at.sib).wait_recv()
            self.copy(3, shard, self.t1_rows(at.p_y), at.sib).wait_recv()
            self.copy(4, shard, self.t1_rows(at.relay_from), at.relay_dev).start()

        self.cases(step, do)

    def share(self, step):
        at = self.at

        def do(shard, onward, device):
            self.copy(4, shard, self.t1_rows(at.p_d), at.sib).wait_recv()
            self.copy(6, shard, self.block_rows(at.core), at.sib).start()

        self.cases(step, do)

    def finish(self):
        at = self.at
        mine = self.t1_rows(at.p)

        def do(shard, onward, device):
            self.copy(6, shard, self.block_rows(1 - at.core), at.sib).wait_recv()

            @pl.when(jnp.logical_not(self.has_rest))
            def _():
                self.copy(5, shard, self.rest, at.sib).wait_recv()

        for step in range(at.depth - 1):
            self.cases(step, do)

    def drain(self):
        at = self.at
        mine = self.t1_rows(at.p)

        @pl.when(at.z < at.depth - 1)
        def _():
            self.copy(0, at.z, mine, at.up(), self.own.at[mine]).wait_send()
            if self.line:
                self.copy(7, at.z, self.line, at.up(), self.own.at[self.line]).wait_send()

            @pl.when(self.has_rest)
            def _():
                self.copy(1, at.z, self.rest, at.up(), self.own.at[self.rest]).wait_send()

        @pl.when(at.z > 0)
        def _():
            self.copy(0, at.z, mine, at.down(), self.own.at[mine], True).wait_send()
            if self.line:
                self.copy(7, at.z, self.line, at.down(), self.own.at[self.line], True).wait_send()

            @pl.when(self.has_rest)
            def _():
                self.copy(1, at.z, self.rest, at.down(), self.own.at[self.rest], True).wait_send()

        def do(shard, onward, device):
            @pl.when(onward)
            def _():
                self.copy(0, shard, mine, device).wait_send()
                if self.line:
                    self.copy(7, shard, self.line, device).wait_send()

                @pl.when(self.has_rest)
                def _():
                    self.copy(1, shard, self.rest, device).wait_send()

            self.copy(2, shard, mine, at.x_dev).wait_send()
            self.copy(3, shard, mine, at.y_dev).wait_send()
            self.copy(4, shard, self.t1_rows(at.relay_from), at.relay_dev).wait_send()
            self.copy(6, shard, self.block_rows(at.core), at.sib).wait_send()

            @pl.when(self.has_rest)
            def _():
                self.copy(5, shard, self.rest, at.sib).wait_send()

        for step in range(at.depth - 1):
            self.cases(step, do)


def both(*conds):
    conds = [c for c in conds if c is not None]
    if not conds:
        return None
    total = conds[0]
    for c in conds[1:]:
        total = jnp.logical_and(total, c)
    return total


def under(cond, do):
    if cond is None:
        do()
    else:
        pl.when(cond)(do)


def add_rows(acc, extra, rows):
    def step(i, carry):
        piece = pl.ds(pl.multiple_of(i * 16, 16), 16)
        acc[piece, :] = acc[piece, :] + extra[piece, :]
        return carry

    lax.fori_loop(0, rows // 16, step, 0)


def add_rows_two(acc, one, two, rows):
    def step(i, carry):
        piece = pl.ds(pl.multiple_of(i * 16, 16), 16)
        total = acc[piece, :].astype(jnp.float32) + one[piece, :].astype(jnp.float32)
        acc[piece, :] = (total + two[piece, :].astype(jnp.float32)).astype(jnp.bfloat16)
        return carry

    lax.fori_loop(0, rows // 16, step, 0)


HEAD_DIM = 64
LANES = 128
F32, BF16 = jnp.float32, jnp.bfloat16


def pad_lanes(n):
    return (n + LANES - 1) // LANES * LANES


def by_tiles(total, tile, do):
    count = total // tile

    def step(i, carry):
        do(pl.multiple_of(i * tile, tile), tile)
        return carry

    if count:
        lax.fori_loop(0, count, step, 0)
    if total % tile:
        do(count * tile, total % tile)


def row_norm(values):
    average = jnp.mean(values, axis=-1, keepdims=True)
    centred = values - average
    variance = jnp.mean(centred * centred, axis=-1, keepdims=True)
    scale = lax.rsqrt(variance + 1e-05)
    return centred * scale, scale


GELU_A = 0.7978845608028654
GELU_B = 0.044715


def gelu_both(u):
    square = u * u
    bent = jnp.tanh(GELU_A * (u + GELU_B * u * square))
    half = 0.5 * (1.0 + bent)
    slope = half + 0.5 * u * (1.0 - bent * bent) * (GELU_A * (1.0 + 3.0 * GELU_B * square))
    return u * half, slope


def cut_pieces(src, dst, part, first):
    depth = 4

    def do(off, size):
        here = pl.ds(off, size)
        left = []
        for t in range(depth):
            start = (first + t * (src.shape[1] // part // depth)) * part
            block = src[here, pl.ds(start, part)]
            for core in range(2):
                dst[core, here, pl.ds(t * LANES, LANES)] = block[:, core * LANES : (core + 1) * LANES]
            left.append(block[:, 2 * LANES :])
        rest = jnp.concatenate(left + [jnp.zeros_like(left[0])] * 4, axis=1)
        for core in range(2):
            dst[core, here, pl.ds(depth * LANES, LANES)] = rest

    by_tiles(src.shape[0], 64, do)


class Context:
    def __init__(self, at, own, whole, rows, send, recv, local):
        self.at, self.own, self.whole, self.rows = at, own, whole, rows
        self.send, self.recv, self.local = send, recv, local
        core, p = at.core, at.p
        self.names, self.posts = {}, []

    def place(self, p, core):
        return self.whole.at[:, pl.ds(pl.multiple_of((2 * p + core) * self.rows, 16), self.rows)]

    def make(self, name, src, dst, device):
        i = self.names.setdefault(name, len(self.names))
        return remote(src, dst, self.send.at[i], self.recv.at[i], device)

    def post(self, name, src, dst, device):
        self.make(name, src, dst, device).start()
        self.posts.append((name, src, dst, device))

    def take(self, name, dst):
        self.make(name, dst, dst, self.at.sib).wait_recv()

    def start(self):
        at = self.at
        here = self.place(at.p, at.core)
        self.post("x", self.own, here, at.x_dev)
        self.post("y", self.own, here, at.y_dev)
        self.post("s", self.own, here, at.sib)
        self.keep = pltpu.make_async_copy(self.own, here, self.local)
        self.keep.start()

    def relay(self):
        at = self.at
        for name, p in (("x", at.p_x), ("y", at.p_y)):
            self.take(name, self.place(p, at.core))
        here = self.place(at.relay_from, at.core)
        self.post("d", here, here, at.relay_dev)
        for name, p in (("x", at.p_x), ("y", at.p_y)):
            here = self.place(p, at.core)
            self.post(name + "s", here, here, at.sib)

    def last(self):
        at = self.at
        here = self.place(at.p_d, at.core)
        self.take("d", here)
        self.post("ds", here, here, at.sib)

    def finish(self):
        at = self.at
        for name, p in (("s", at.p), ("xs", at.p_x), ("ys", at.p_y), ("ds", at.p_d)):
            self.take(name, self.place(p, 1 - at.core))
        self.keep.wait()

    def drain(self, own):
        for name, src, dst, device in self.posts:
            if (name in ("x", "y", "s")) == own:
                self.make(name, src, dst, device).wait_send()


KEPT = ("h", "pa", "q", "kv", "o", "po", "lse", "h1", "pc", "pz", "dg")
PIECE = 5 * LANES
LINE_ROWS = (0, 0, 16, 16)


def kept_shapes(seqs, slots, rows, width, ff):
    wide = pad_lanes(width)
    flat = seqs * rows
    return {
        "h": ((flat, width), F32),
        "pa": ((2, flat, PIECE), BF16),
        "q": ((flat, wide), BF16),
        "kv": ((seqs, slots, 2 * wide), BF16),
        "o": ((flat, wide), BF16),
        "po": ((2, flat, PIECE), BF16),
        "lse": ((flat * 2, LANES), F32),
        "h1": ((flat, width), F32),
        "pc": ((2, flat, PIECE), BF16),
        "pz": ((2, 4, flat, PIECE), BF16),
        "dg": ((flat, ff), BF16),
    }


def key_bias(out, seqs, rows, slots, lengths, ctx):
    for s in range(seqs):
        key = lax.broadcasted_iota(jnp.int32, (rows, slots), 1)
        row = ctx * rows + lax.broadcasted_iota(jnp.int32, (rows, slots), 0)
        seen = jnp.logical_and(key <= row, key < lengths[s])
        out[s] = jnp.where(seen, 0.0, -1e30)


def two_heads(block):
    lane = lax.broadcasted_iota(jnp.int32, block.shape, 1)
    zero = jnp.zeros_like(block)
    return jnp.concatenate(
        [jnp.where(lane < HEAD_DIM, block, zero), jnp.where(lane < HEAD_DIM, zero, block)], axis=0
    )


def one_pair(stacked, rows):
    lane = lax.broadcasted_iota(jnp.int32, (rows, LANES), 1)
    return jnp.where(lane < HEAD_DIM, stacked[:rows], stacked[rows:])


def across(a, b):
    return lax.dot_general(a, b, (((1,), (1,)), ((), ())), preferred_element_type=F32)


def attend(s, first, count, q_ref, kv_ref, bias_ref, o_ref, lse_ref, rows, pairs, wide):
    def step(i, carry):
        j = first + i
        col = pl.ds(pl.multiple_of(j * LANES, LANES), LANES)
        q2 = two_heads(q_ref[pl.ds(s * rows, rows), col])
        keys = kv_ref[s, :, col]
        values = kv_ref[s, :, pl.ds(pl.multiple_of(wide + j * LANES, LANES), LANES)]
        bias = bias_ref[s]
        scores = across(q2, keys) * (HEAD_DIM ** (-0.5))
        scores = scores + jnp.concatenate([bias, bias], axis=0)
        top = jnp.max(scores, axis=-1, keepdims=True)
        weights = jnp.exp(scores - top)
        total = jnp.sum(weights, axis=-1, keepdims=True)
        out = jnp.dot(weights.astype(BF16), values, preferred_element_type=F32) / total
        o_ref[pl.ds(s * rows, rows), col] = one_pair(out, rows).astype(BF16)
        mine = s * pairs + j
        here = pl.ds(s * 2 * rows, 2 * rows)
        lane = lax.broadcasted_iota(jnp.int32, (2 * rows, LANES), 1)
        lse_ref[here, :] = jnp.where(lane == mine, top + jnp.log(total), lse_ref[here, :])
        return carry

    lax.fori_loop(0, count, step, 0)


def forward_kernel(dims, *refs):
    layers, seqs, rows, slots, width, ff, depth = dims
    flat, wide = seqs * rows, pad_lanes(width)
    pairs = wide // LANES
    part = width // depth
    refs = list(refs)

    def grab(n):
        out = refs[:n]
        del refs[:n]
        return out

    tokens, lengths, w_qkv, w_out, w_up, w_down, small = grab(7)
    acts, vecs = grab(2)
    wholes = grab(4 * layers)
    kept = [dict(zip(KEPT, grab(len(KEPT)))) for _ in range(layers)]
    (send, recv, small_send, small_recv, kv_send, kv_recv, load_sem, keep_sem, stage_sem) = grab(9)
    (small_all, vec, up_bias, h, a, q, own_kv, kv, bias, o, lse, h1, c, u, z, dg, pa, pc, po, pz) = grab(20)
    w_bufs = grab(4)
    at = Place()
    at.greet()

    owns = [ref.at[l] for l in range(layers) for ref in (w_qkv, w_out, w_up, w_down)]
    items = [Gather(at, owns[k], wholes[k], k % 2, send.at[k], recv.at[k], LINE_ROWS[k % 4]) for k in range(4 * layers)]
    contexts = [
        Context(at, own_kv, kept[l]["kv"], rows, kv_send.at[l], kv_recv.at[l], keep_sem.at[l, len(KEPT)])
        for l in range(layers)
    ]
    pending = {}

    def keep(l, name, src):
        copy = pltpu.make_async_copy(src, kept[l][name], keep_sem.at[l, KEPT.index(name)])
        copy.start()
        pending[(l, name)] = copy

    def free(l, name):
        copy = pending.pop((l, name), None)
        if copy is not None:
            copy.wait()

    def buffer(k):
        return w_bufs[k % 4]

    def own_copy(k, load):
        r = owns[k].shape[0]
        shard = lax.rem(at.z + k // 4, depth)
        place = buffer(k).at[pl.ds(pl.multiple_of(shard * r, 16), r)]
        if load:
            return pltpu.make_async_copy(owns[k], place, stage_sem.at[0, k])
        return pltpu.make_async_copy(place, items[k].place(at.z, pl.ds(0, r)), stage_sem.at[1, k])

    def own_load(k):
        own_copy(k, True).start()

    def own_store(k):
        own_copy(k, True).wait()
        own_copy(k, False).start()

    def own_done(k):
        own_copy(k, False).wait()

    def fetch(k):
        pltpu.make_async_copy(wholes[k], buffer(k), load_sem.at[k]).start()

    def ready(k):
        pltpu.make_async_copy(wholes[k], buffer(k), load_sem.at[k]).wait()

    def small_copy(shard, device, src=None, second=False):
        return remote(
            small_all.at[shard] if src is None else src,
            small_all.at[shard],
            small_send.at[depth if second else shard],
            small_recv.at[shard],
            device,
        )

    def small_start():
        @pl.when(at.z < depth - 1)
        def _():
            small_copy(at.z, at.up(), small).start()

        @pl.when(at.z > 0)
        def _():
            small_copy(at.z, at.down(), small, True).start()

        pltpu.make_async_copy(small, small_all.at[at.z], stage_sem.at[2, 0]).start()

    def small_take():
        def do(shard, onward, device):
            small_copy(shard, at.sib).wait_recv()
            pl.when(onward)(lambda: small_copy(shard, device).start())

        for step in range(depth - 1):
            items[0].cases(step, do)
        pltpu.make_async_copy(small, small_all.at[at.z], stage_sem.at[2, 0]).wait()

    def small_drain():
        @pl.when(at.z < depth - 1)
        def _():
            small_copy(at.z, at.up(), small).wait_send()

        @pl.when(at.z > 0)
        def _():
            small_copy(at.z, at.down(), small, True).wait_send()

        def do(shard, onward, device):
            pl.when(onward)(lambda: small_copy(shard, device).wait_send())

        for step in range(depth - 1):
            items[0].cases(step, do)

    def small_spread():
        part = width // depth
        per_layer = small_all.shape[1] // layers
        total = jnp.zeros((small_all.shape[1], wide), F32)
        room = jnp.zeros((small_all.shape[1], wide - small_all.shape[2]), F32)
        pieces = [small_all[i].astype(F32) for i in range(depth)]
        for i in range(depth):
            piece = jnp.concatenate([pieces[i], room], axis=1)
            total = total + (pltpu.roll(piece, i * part, 1) if i else piece)
        for l in range(layers):
            vec[l] = total[l * per_layer : l * per_layer + 8]
            vecs[l] = total[l * per_layer : l * per_layer + 8]
            wide_up = jnp.zeros((1, ff), F32)
            up_room = jnp.zeros((1, ff - small_all.shape[2]), F32)
            for i in range(depth):
                for r in range(4):
                    at_row = l * per_layer + 8 + r
                    piece = jnp.concatenate([pieces[i][at_row : at_row + 1], up_room], axis=1)
                    shift = (i * 4 + r) * part
                    wide_up = wide_up + (pltpu.roll(piece, shift, 1) if shift else piece)
            up_bias[l] = jnp.broadcast_to(wide_up, (8, ff))

    def row(l, i):
        return vec[l, pl.ds(i, 1), pl.ds(0, width)]

    def norm(l, i, src, dst):
        def do(first, size):
            here = pl.ds(first, size)
            unit, _ = row_norm(src[here, :])
            dst[here, :] = (unit * row(l, i) + row(l, 2 + i)).astype(BF16)

        by_tiles(flat, 32, do)

    def load_tokens():
        def do(first, size):
            here = pl.ds(first, size)
            h[here, :] = tokens[here, :].astype(F32)

        by_tiles(flat, 32, do)

    def mix(l):
        def do(first, size):
            cols = pl.ds(first, size)
            u[:, cols] = jnp.dot(a[...], w_bufs[0][:, cols], preferred_element_type=F32)

        by_tiles(3 * width, 256, do)

        for s in range(seqs):

            def split(first, size):
                here, there = pl.ds(s * rows + first, size), pl.ds(first, size)
                queries = u[here, pl.ds(0, width)] + row(l, 4)
                keys = u[here, pl.ds(width, width)]
                values = u[here, pl.ds(2 * width, width)] + row(l, 5)
                q[here, pl.ds(0, width)] = queries.astype(BF16)
                own_kv[s, there, pl.ds(0, width)] = keys.astype(BF16)
                own_kv[s, there, pl.ds(wide, width)] = values.astype(BF16)

            by_tiles(rows, 32, split)

    def project(l):
        def do(first, size):
            cols = pl.ds(first, size)
            bias_row = vec[l, pl.ds(6, 1), cols]
            h1[:, cols] = (
                h[:, cols]
                + jnp.dot(o[:, pl.ds(0, width)], w_bufs[1][:, cols], preferred_element_type=F32)
                + bias_row
            )

        by_tiles(width, 256, do)

    def rise(l):
        def do(first, size):
            cols = pl.ds(first, size)
            pre = jnp.dot(c[...], w_bufs[2][:, cols], preferred_element_type=F32) + up_bias[l, pl.ds(0, 1), cols]
            value, slope = gelu_both(pre)
            z[:, cols] = value.astype(BF16)
            dg[:, cols] = slope.astype(BF16)

        by_tiles(ff, 256, do)

    def fall(l):
        def do(first, size):
            cols = pl.ds(first, size)
            h[:, cols] = (
                h1[:, cols]
                + jnp.dot(z[...], w_bufs[3][:, cols], preferred_element_type=F32)
                + vec[l, pl.ds(7, 1), cols]
            )

        by_tiles(width, 256, do)

    def finish_tokens():
        for s in range(seqs):
            def do(first, size):
                here = pl.ds(s * rows + first, size)
                place = at.c8 * rows + first + lax.broadcasted_iota(jnp.int32, (size, width), 0)
                acts[here, :] = jnp.where(place < lengths[s], h[here, :], 0.0).astype(BF16)

            by_tiles(rows, 32, do)

    steps = depth - 1
    ticks = []
    for k in range(4 * layers):
        if k == 0:
            ticks += [functools.partial(items[0].arrive, i) for i in range(steps)]
        if k + 2 < 4 * layers:
            ticks.append(items[k + 2].start)
        for i in range(steps):
            ticks.append(functools.partial(items[k].plane, i))
            if k + 1 < 4 * layers:
                ticks.append(functools.partial(items[k + 1].arrive, i))
            ticks.append(functools.partial(items[k].share, i))
        ticks.append(("end", k))

    def tick(n):
        for _ in range(n):
            if not ticks:
                return
            item = ticks.pop(0)
            if isinstance(item, tuple) and item[0] == "end":
                items[item[1]].finish()
            else:
                item()

    def reach(k):
        while ("end", k) in ticks:
            tick(1)

    small_start()
    items[0].start()
    items[1].start()
    for k in range(4 * layers):
        own_load(k)
    load_tokens()
    q[...] = jnp.zeros_like(q)
    o[...] = jnp.zeros_like(o)
    own_kv[...] = jnp.zeros_like(own_kv)
    lse[...] = jnp.zeros_like(lse)
    key_bias(bias, seqs, rows, slots, lengths, at.c8)
    for k in range(4 * layers):
        own_store(k)
    tick(steps)
    small_take()
    small_spread()
    for k in range(4 * layers):
        own_done(k)
    for l in range(layers):
        k = 4 * l
        norm(l, 0, h, a)
        keep(l, "h", h)
        free(l - 1, "pa")
        cut_pieces(a, pa, part, 0)
        keep(l, "pa", pa)
        reach(k)
        fetch(k)
        free(l - 1, "q")
        if l:
            contexts[l - 1].drain(True)
        ready(k)
        mix(l)
        contexts[l].start()
        keep(l, "q", q)
        tick(8)
        contexts[l].relay()
        reach(k + 1)
        fetch(k + 1)
        tick(4)
        contexts[l].last()
        tick(3)
        contexts[l].finish()
        seen = pltpu.make_async_copy(kept[l]["kv"], kv, load_sem.at[4 * layers])
        seen.start()
        free(l - 1, "o")
        free(l - 1, "lse")
        seen.wait()
        half = pairs // 2
        for s in range(seqs):
            attend(s, 0, half, q, kv, bias, o, lse, rows, pairs, wide)
            tick(2)
            attend(s, half, pairs - half, q, kv, bias, o, lse, rows, pairs, wide)
            tick(2)
        keep(l, "o", o)
        keep(l, "lse", lse)
        free(l - 1, "po")
        cut_pieces(o.at[:, pl.ds(0, wide)], po, part, 0)
        keep(l, "po", po)
        ready(k + 1)
        free(l - 1, "h1")
        project(l)
        keep(l, "h1", h1)
        norm(l, 1, h1, c)
        free(l - 1, "pc")
        cut_pieces(c, pc, part, 0)
        keep(l, "pc", pc)
        reach(k + 2)
        fetch(k + 2)
        ready(k + 2)
        free(l - 1, "dg")
        rise(l)
        keep(l, "dg", dg)
        free(l - 1, "pz")
        for i in range(4):
            cut_pieces(z, pz.at[:, i], part, i)
        keep(l, "pz", pz)
        reach(k + 3)
        fetch(k + 3)
        free(l, "h")
        ready(k + 3)
        fall(l)
    tick(len(ticks))
    finish_tokens()
    for key in list(pending):
        free(*key)
    small_drain()
    for item in items:
        item.drain()
    contexts[-1].drain(True)
    for context in contexts:
        context.drain(False)


def forward(tokens, lengths, w_qkv, w_out, w_up, w_down, small):
    seqs, rows, width = tokens.shape
    layers, part, _ = w_qkv.shape
    depth = lax.axis_size("fsdp")
    slots = rows * lax.axis_size("ctx")
    ff = w_up.shape[2]
    flat, wide = seqs * rows, pad_lanes(width)
    dims = (layers, seqs, rows, slots, width, ff, depth)
    any_spec = pl.BlockSpec(memory_space=pl.ANY)
    vmem = pl.BlockSpec(memory_space=pltpu.VMEM)
    struct = lambda shape, kind: jax.ShapeDtypeStruct(shape, kind)
    shapes = kept_shapes(seqs, slots, rows, width, ff)
    out_shape = [struct((flat, width), BF16), struct((layers, 8, wide), F32)]
    for l in range(layers):
        for ref in (w_qkv, w_out, w_up, w_down):
            out_shape.append(struct((depth * ref.shape[1], ref.shape[2]), BF16))
    for l in range(layers):
        out_shape += [struct(*shapes[name]) for name in KEPT]
    count = 4 * layers
    dma = pltpu.SemaphoreType.DMA
    scratch = [
        dma((count, 8 * depth + 8)),
        dma((count, 8 * depth)),
        dma((depth + 1,)),
        dma((depth,)),
        dma((layers, 8)),
        dma((layers, 8)),
        dma((count + 1,)),
        dma((layers, len(KEPT) + 1)),
        dma((3, count)),
        pltpu.VMEM((depth,) + small.shape, BF16),
        pltpu.VMEM((layers, 8, wide), F32),
        pltpu.VMEM((layers, 8, ff), F32),
        pltpu.VMEM((flat, width), F32),
        pltpu.VMEM((flat, width), BF16),
        pltpu.VMEM((flat, wide), BF16),
        pltpu.VMEM((seqs, rows, 2 * wide), BF16),
        pltpu.VMEM((seqs, slots, 2 * wide), BF16),
        pltpu.VMEM((seqs, rows, slots), F32),
        pltpu.VMEM((flat, wide), BF16),
        pltpu.VMEM((2 * flat, LANES), F32),
        pltpu.VMEM((flat, width), F32),
        pltpu.VMEM((flat, width), BF16),
        pltpu.VMEM((flat, 3 * width), F32),
        pltpu.VMEM((flat, ff), BF16),
        pltpu.VMEM((flat, ff), BF16),
        pltpu.VMEM((2, flat, PIECE), BF16),
        pltpu.VMEM((2, flat, PIECE), BF16),
        pltpu.VMEM((2, flat, PIECE), BF16),
        pltpu.VMEM((2, 4, flat, PIECE), BF16),
    ] + [pltpu.VMEM((depth * ref.shape[1], ref.shape[2]), BF16) for ref in (w_qkv, w_out, w_up, w_down)]
    outs = pl.pallas_call(
        functools.partial(forward_kernel, dims),
        out_shape=out_shape,
        in_specs=[vmem, pl.BlockSpec(memory_space=pltpu.SMEM)] + [any_spec] * 5,
        out_specs=[vmem, vmem] + [any_spec] * (len(out_shape) - 2),
        scratch_shapes=scratch,
        compiler_params=pltpu.CompilerParams(
            collective_id=0, has_side_effects=True, vmem_limit_bytes=63 * 1024 * 1024
        ),
    )(tokens.reshape(flat, width), lengths, w_qkv, w_out, w_up, w_down, small)
    acts, vecs = outs[:2]
    wholes = outs[2 : 2 + count]
    rest = outs[2 + count :]
    kept = [dict(zip(KEPT, rest[l * len(KEPT) : (l + 1) * len(KEPT)])) for l in range(layers)]
    return acts, vecs, [wholes[4 * l : 4 * l + 4] for l in range(layers)], kept


SETS = 5
FINS = 10
LINE_FIRST = ()
LINE_LAG = 0
TILES = 3
KINDS = ("down", "up", "out", "mix")


def over_rows(a, b):
    return lax.dot_general(a, b, (((0,), (0,)), ((), ())), preferred_element_type=F32)


class Granule:
    def __init__(self, at, others, line_first, acc, plane_in, z_in, fin, out, send, recv, local, credit, wait_credit, give_credit, before):
        self.before = before
        self.line_first = line_first
        self.at, self.others, self.acc, self.plane_in, self.z_in = at, others, acc, plane_in, z_in
        self.fin, self.out, self.send, self.recv, self.local = fin, out, send, recv, local
        self.credit, self.wait_credit, self.give_credit = credit, wait_credit, give_credit
        self.t1 = acc.shape[2]
        self.names, self.posts = {}, []
        core, p = at.core, at.p
        self.direct_p = p + (1 - core) * (2 - 4 * at.py) + core * (1 - 2 * at.px)
        self.owner_dev = {"ctx": at.c8 + (1 - core) * (2 - 4 * at.px) + core * (4 - 8 * at.py)}

    def make(self, name, src, dst, device):
        i = self.names.setdefault(name, len(self.names))
        return remote(src, dst, self.send.at[i], self.recv.at[i], device)

    def post(self, name, src, dst, device):
        self.make(name, src, dst, device).start()
        self.posts.append((name, src, dst, device))

    def take(self, name, dst):
        self.make(name, dst, dst, self.at.sib).wait_recv()

    def place(self, p, core):
        ref, first, col, cols = self.out
        row = pl.multiple_of(first + core * 4 * self.t1 + p * self.t1, 16)
        return ref.at[pl.ds(row, self.t1), pl.ds(col, cols)]

    def line_out(self, part, landing):
        for i, device in enumerate(self.others):
            goal = lax.rem(self.at.z + 1 + i, self.at.depth)
            self.post(f"z{i}", part(goal), landing.at[i], device)

    def line_in(self, landing):
        for i in range(len(self.others)):
            self.take(f"z{i}", landing.at[i])

    def plane_out(self, part, landing):
        self.post("diag", part(self.at.p_d), landing.at[0], self.at.relay_dev)
        self.post("near", part(self.direct_p), landing.at[1], self.at.relay_dev)

    def plane_relay(self, part, landing, add):
        self.take("diag", landing.at[0])
        add(part(self.at.relay_from), landing.at[0])
        self.post("relay", part(self.at.relay_from), landing.at[2], self.owner_dev)

    def plane_in_all(self, landing):
        self.take("near", landing.at[1])
        self.take("relay", landing.at[2])

    def over_shards(self, acc, extra):
        for t in range(self.at.depth):
            add_rows(acc.at[t], extra.at[t], self.t1)

    def total(self, own, extra, out):
        def step(i, carry):
            piece = pl.ds(pl.multiple_of(i * 16, 16), 16)
            value = own[piece, :].astype(F32)
            for j in range(3):
                value = value + extra(j)[piece, :].astype(F32)
            out[piece, :] = value.astype(BF16)
            return carry

        lax.fori_loop(0, self.t1 // 16, step, 0)

    def of_shard(self, p):
        return self.acc.at[self.at.z, p]

    def of_chip(self, p):
        return self.acc.at[:, p]

    def begin(self):
        if self.wait_credit is not None:
            pl.semaphore_wait(self.wait_credit, 2 + len(self.others))
        if self.line_first:
            self.line_out(lambda t: self.acc.at[t], self.plane_in)
        else:
            self.plane_out(self.of_chip, self.plane_in)

    def second(self):
        at = self.at
        if self.line_first:
            self.line_in(self.plane_in)
            for p in range(4):
                own = self.of_shard(p)
                self.total(own, lambda j: self.plane_in.at[j, p], own)
            self.plane_out(self.of_shard, self.z_in)
        else:
            self.plane_relay(self.of_chip, self.plane_in, self.over_shards)

    def third(self):
        at = self.at
        if self.line_first:
            self.plane_relay(self.of_shard, self.z_in, lambda a, b: add_rows(a, b, self.t1))
        else:
            self.plane_in_all(self.plane_in)
            mine = self.of_chip(at.p)
            for t in range(at.depth):
                add_rows_two(mine.at[t], self.plane_in.at[1, t], self.plane_in.at[2, t], self.t1)
            self.line_out(lambda t: self.acc.at[t, at.p], self.z_in)

    def fin_sent(self):
        for name, src, dst, device in self.posts:
            if name in ("sx", "sy", "ss"):
                self.make(name, src, dst, device).wait_send()
        self.posts = [post for post in self.posts if post[0] not in ("sx", "sy", "ss")]

    def end(self):
        at = self.at
        if self.before is not None:
            self.before.fin_sent()
        own = self.of_shard(at.p)
        if self.line_first:
            self.plane_in_all(self.z_in)

            def step(i, carry):
                piece = pl.ds(pl.multiple_of(i * 16, 16), 16)
                value = own[piece, :].astype(F32) + self.z_in[1, piece, :].astype(F32)
                self.fin[piece, :] = (value + self.z_in[2, piece, :].astype(F32)).astype(BF16)
                return carry

            lax.fori_loop(0, self.t1 // 16, step, 0)
        else:
            self.line_in(self.z_in)
            self.total(own, lambda j: self.z_in.at[j], self.fin)
        if self.give_credit:
            for device in [at.x_dev, at.y_dev] + self.others:
                pl.semaphore_signal(self.credit, inc=1, device_id=device, device_id_type=MESH)
        here = self.place(at.p, at.core)
        pltpu.make_async_copy(self.fin, here, self.local).start()
        self.post("sx", self.fin, here, at.x_dev)
        self.post("sy", self.fin, here, at.y_dev)
        self.post("ss", self.fin, here, at.sib)

    def release(self):
        keep = []
        for name, src, dst, device in self.posts:
            if name[0] == "s":
                keep.append((name, src, dst, device))
            else:
                self.make(name, src, dst, device).wait_send()
        self.posts = keep

    def spread_relay(self):
        at = self.at
        for far, p in (("sx", at.p_x), ("sy", at.p_y)):
            here = self.place(p, at.core)
            self.take(far, here)
            self.post(far + "s", here, here, at.sib)
        here = self.place(at.relay_from, at.core)
        self.post("sd", here, here, at.relay_dev)

    def spread_last(self):
        at = self.at
        here = self.place(at.p_d, at.core)
        self.take("sd", here)
        self.post("sds", here, here, at.sib)

    def finish(self):
        at = self.at
        for name, p in (("ss", at.p), ("sxs", at.p_x), ("sys", at.p_y), ("sds", at.p_d)):
            self.take(name, self.place(p, 1 - at.core))
        pltpu.make_async_copy(self.fin, self.place(at.p, at.core), self.local).wait()

    def drain(self):
        for name, src, dst, device in self.posts:
            self.make(name, src, dst, device).wait_send()

    def stages(self):
        wait = [[] for _ in range(LINE_LAG)] if self.line_first else []
        return wait + [
            [self.second], [self.third], [self.end], [self.release, self.spread_relay], [self.spread_last],
            [self.finish],
        ]


class KeyGrads:
    def __init__(self, at, parts, sib_in, stage, plane_in, send, recv, local, credit, layer):
        self.at, self.parts, self.sib_in, self.stage, self.plane_in = at, parts, sib_in, stage, plane_in
        self.send, self.recv, self.local, self.credit, self.layer = send, recv, local, credit, layer
        self.names, self.posts = {}, []
        core, p = at.core, at.p
        self.direct_p = p + (1 - core) * (2 - 4 * at.py) + core * (1 - 2 * at.px)
        self.owner_dev = {"ctx": at.c8 + (1 - core) * (2 - 4 * at.px) + core * (4 - 8 * at.py)}
        self.order = [at.p_d, self.direct_p, at.relay_from, at.p]

    def make(self, name, src, dst, device):
        i = self.names.setdefault(name, len(self.names))
        return remote(src, dst, self.send.at[i], self.recv.at[i], device)

    def post(self, name, src, dst, device):
        self.make(name, src, dst, device).start()
        self.posts.append((name, src, dst, device))

    def take(self, name, dst):
        self.make(name, dst, dst, self.at.sib).wait_recv()

    def start(self):
        for i, p in enumerate(self.other_order()):
            self.post(f"s{i}", self.parts.at[1, p], self.sib_in.at[p], self.at.sib)

    def other_order(self):
        at = self.at
        core = 1 - at.core
        direct = at.p + (1 - core) * (2 - 4 * at.py) + core * (1 - 2 * at.px)
        relay = at.p + (1 - core) * (1 - 2 * at.px) + core * (2 - 4 * at.py)
        return [at.p_d, direct, relay, at.p]

    def add(self, p, extra):
        seqs, rows = self.parts.shape[2], self.parts.shape[3]
        for s in range(seqs):
            add_rows(self.parts.at[0, p, s], extra.at[s], rows)

    def core_sum(self, i):
        p = self.order[i]
        self.take(f"s{i}", self.sib_in.at[p])
        for s in range(self.parts.shape[2]):
            copy = pltpu.make_async_copy(self.sib_in.at[p, s], self.stage, self.local)
            copy.start()
            copy.wait()
            add_rows(self.parts.at[0, p, s], self.stage, self.parts.shape[3])

    def first(self):
        at = self.at
        self.core_sum(0)
        if self.layer is not None:
            pl.semaphore_wait(self.credit, 2)
        self.post("diag", self.parts.at[0, at.p_d], self.plane_in.at[0], at.relay_dev)
        self.core_sum(1)
        self.post("near", self.parts.at[0, self.direct_p], self.plane_in.at[1], at.relay_dev)
        self.core_sum(2)
        self.core_sum(3)

    def relay(self):
        at = self.at
        self.take("diag", self.plane_in.at[0])
        self.add(at.relay_from, self.plane_in.at[0])
        self.post("relay", self.parts.at[0, at.relay_from], self.plane_in.at[2], self.owner_dev)

    def combine(self, give_credit):
        at = self.at
        seqs, rows = self.parts.shape[2], self.parts.shape[3]
        self.take("near", self.plane_in.at[1])
        self.take("relay", self.plane_in.at[2])
        for s in range(seqs):
            add_rows_two(self.parts.at[0, at.p, s], self.plane_in.at[1, s], self.plane_in.at[2, s], rows)
        if give_credit:
            for device in (at.x_dev, at.y_dev):
                pl.semaphore_signal(self.credit, inc=1, device_id=device, device_id_type=MESH)

    def drain(self):
        for name, src, dst, device in self.posts:
            self.make(name, src, dst, device).wait_send()
        self.posts = []


def backward_kernel(dims, *refs):
    layers, seqs, rows, slots, width, ff, depth, per_layer = dims
    flat, wide = seqs * rows, pad_lanes(width)
    pairs = wide // LANES
    total = seqs * pairs
    refs = list(refs)

    def grab(n):
        out = refs[:n]
        del refs[:n]
        return out

    cot, lengths, vecs = grab(3)
    kept = [dict(zip(KEPT, grab(len(KEPT)))) for _ in range(layers)]
    wholes = [grab(4) for _ in range(layers)]
    grad_in, small_out = grab(2)
    outs = [grab(5) for _ in range(layers)]
    kv_sib = grab(layers)
    (g_send, g_recv, g_local, g_credit, kv_send, kv_recv, kv_local, kv_credit) = grab(8)
    (pg_send, pg_recv, pg_local, pg_credit, sm_send, sm_recv, load_sem, w_sem, kvp_sem, rest_sem) = grab(10)
    acc, plane_in, z_in, rest_acc, fin = grab(5)
    hx, dn = grab(2)
    g = grad_in
    gm, gu, ga, gx = grab(4)
    pz, pc, po, pa = grab(4)
    dg, q, go, o, lse, bias, kvp = grab(7)
    parts, kv_stage, kv_plane = grab(3)
    wt_a, wt_u, wt_q, gq = grab(4)
    sm, sm_sum, sm_in, sm_z, up_row = grab(5)

    at = Place()
    core = at.core
    barrier = pltpu.get_barrier_semaphore()
    others = [{"fsdp": lax.rem(at.z + i, depth)} for i in range(1, depth)]
    for device in [at.sib, at.x_dev, at.y_dev] + others:
        pl.semaphore_signal(barrier, inc=1, device_id=device, device_id_type=MESH)
    pl.semaphore_wait(barrier, 3 + depth - 1)

    exchange = {
        "down": [("pz", pz), ("gm", gm)],
        "up": [("pc", pc), ("gu", gu)],
        "out": [("po", po), ("ga", ga)],
        "mix": [("pa", pa), ("gx", gx)],
    }
    slot_of = {}
    for kind in KINDS:
        for name, _ in exchange[kind]:
            slot_of[name] = len(slot_of)
    buffers = {name: buf for kind in KINDS for name, buf in exchange[kind]}
    posted = {}

    def pg_copy(name, src):
        i = slot_of[name]
        buf = buffers[name]
        dst = buf.at[1]
        return remote(src, dst, pg_send.at[i], pg_recv.at[i], at.sib)

    def pg_post(name, src):
        pg_copy(name, src).start()
        posted[name] = src

    def pg_sent(name):
        src = posted.pop(name, None)
        if src is not None:
            pg_copy(name, src).wait_send()

    def pg_take(name):
        buf = buffers[name].at[1]
        pg_copy(name, buf).wait_recv()

    def piece_load(l, name):
        return pltpu.make_async_copy(kept[l][name].at[core], buffers[name].at[0], pg_local.at[slot_of[name]])

    def free_kind(kind, l):
        if l < layers - 1:
            pl.semaphore_wait(pg_credit.at[KINDS.index(kind)], 1)

    def done_kind(kind, l):
        if l > 0:
            pl.semaphore_signal(
                pg_credit.at[KINDS.index(kind)], inc=1, device_id=at.sib, device_id_type=MESH
            )

    active, items = [], []
    line_up = layers * per_layer

    def pump(times=1):
        for _ in range(times):
            for entry in list(active):
                for do in entry[1].pop(0):
                    do()
                if not entry[1]:
                    active.remove(entry)

    def open_set():
        index = len(items)
        if index >= SETS:
            old = items[index - SETS]
            while any(entry[0] is old and len(entry[1]) > 2 for entry in active):
                pump()
        return index

    def goal(l, unit):
        down, up, out, mix, rest = outs[l]
        part = width // depth
        if unit < 4:
            return down, part * unit, 0, wide
        if unit < 8:
            return up, 0, (unit - 4) * wide, wide
        if unit == 8:
            return out, 0, 0, wide
        if unit < 12:
            return mix, 0, (unit - 9) * wide, wide
        return rest, 0, 0, wide

    def launch(l, unit, source):
        index = len(items)
        s = index % SETS
        item = Granule(
            at, others, unit in LINE_FIRST, source, plane_in.at[s], z_in.at[s], fin.at[index % FINS], goal(l, unit),
            g_send.at[index], g_recv.at[index], g_local.at[index], g_credit.at[index],
            g_credit.at[index - SETS] if index >= SETS else None, index + SETS < line_up,
            items[index - FINS] if index >= FINS else None,
        )
        if index >= FINS:
            assert all(entry[0] is not items[index - FINS] for entry in active)
        item.begin()
        items.append(item)
        active.append([item, item.stages()])

    def weight_grad(l, unit, piece, rhs, first):
        index = open_set()
        s = index % SETS
        home = 0 if unit < 8 else 1

        def do(off, size):
            cols = pl.ds(off, size)
            right = rhs[:, :, pl.ds(pl.multiple_of(first + off, LANES), size)].reshape(2 * flat, size)
            left = piece[:, :, pl.ds(0, depth * LANES)].reshape(2 * flat, depth * LANES)
            out = over_rows(left, right).astype(BF16)
            for t in range(depth):
                acc[s, t, :, :, cols] = out[t * LANES : (t + 1) * LANES].reshape(4, LANES // 4, size)

            @pl.when(core == home)
            def _():
                last = piece[:, :, pl.ds(depth * LANES, LANES)].reshape(2 * flat, LANES)
                more = over_rows(last, right).astype(BF16)
                for t in range(depth):
                    u = unit - 8 * home
                    rest_acc[t, u // 2, pl.ds(16 * (u % 2), 16), cols] = more[t * 16 : (t + 1) * 16]

        by_tiles(wide, 384, do)
        launch(l, unit, acc.at[s])

    def rest_grad(l):
        open_set()
        launch(l, 12, rest_acc)

    def rest_rows(l):
        part = width // depth
        rest_v = gq
        copy = pltpu.make_async_copy(outs[l][4], rest_v, rest_sem.at[0])
        copy.start()
        copy.wait()
        moves = []
        for unit in range(12):
            ref, first, col, cols = goal(l, unit)
            moves.append(
                pltpu.make_async_copy(
                    rest_v.at[pl.ds(16 * unit, 16)],
                    ref.at[pl.ds(first + 2 * LANES, part - 2 * LANES), pl.ds(col, cols)],
                    rest_sem.at[1 + unit],
                )
            )
        for move in moves:
            move.start()
        for move in moves:
            move.wait()

    def put_row(l, i, value):
        sm[pl.ds(l * 16 + i, 1), pl.ds(0, width)] = value

    def column_sums(l, i, src):
        put_row(l, i, jnp.sum(src[0, :, pl.ds(0, width)].astype(F32), axis=0, keepdims=True))

    def norm_back(l, i):
        gain = vecs[l, pl.ds(i, 1), pl.ds(0, width)]

        def do(step, carry):
            gain_sum, shift_sum = carry
            here = pl.ds(pl.multiple_of(step * 32, 32), 32)
            unit, scale = row_norm(hx[here, :])
            grad = dn[here, :]
            inner = grad * gain
            mean_inner = jnp.mean(inner, axis=-1, keepdims=True)
            mean_unit = jnp.mean(inner * unit, axis=-1, keepdims=True)
            g[here, :] = g[here, :] + scale * (inner - mean_inner - unit * mean_unit)
            return (
                gain_sum + jnp.sum(grad * unit, axis=0, keepdims=True),
                shift_sum + jnp.sum(grad, axis=0, keepdims=True),
            )

        zero = jnp.zeros((1, width), F32)
        gain_sum, shift_sum = lax.fori_loop(0, flat // 32, do, (zero, zero))
        put_row(l, i, gain_sum)
        put_row(l, 2 + i, shift_sum)

    def load(l, name, dst, index):
        return pltpu.make_async_copy(kept[l][name], dst, load_sem.at[index])

    def low_copy(src, dst):
        def do(first, size):
            here = pl.ds(first, size)
            dst[0, here, pl.ds(0, width)] = src[here, :].astype(BF16)

        by_tiles(flat, 64, do)

    def row_tile(whole, buf, slot, first, size, sem):
        return pltpu.make_async_copy(
            whole.at[pl.ds(first, size)], buf.at[slot, pl.ds(0, size)], sem.at[slot]
        )

    def ff_back(l):
        w_up, w_down = wholes[l][2], wholes[l][3]
        tile = 256
        count = ff // tile

        def copies(i, slot):
            first = pl.multiple_of(i * tile, tile)
            return (
                pltpu.make_async_copy(w_down.at[pl.ds(first, tile)], wt_a.at[slot], w_sem.at[0, slot]),
                pltpu.make_async_copy(w_up.at[:, pl.ds(first, tile)], wt_u.at[slot], w_sem.at[1, slot]),
            )

        dn[...] = jnp.zeros_like(dn)
        for i in range(TILES - 1):
            for copy in copies(i, i):
                copy.start()

        def step(i, carry):
            slot = lax.rem(i, TILES)
            for copy in copies(i, slot):
                copy.wait()

            @pl.when(i + TILES - 1 < count)
            def _():
                for copy in copies(i + TILES - 1, lax.rem(i + TILES - 1, TILES)):
                    copy.start()

            cols = pl.ds(pl.multiple_of(i * tile, tile), tile)
            grad = across(gm[0, :, pl.ds(0, width)], wt_a[slot])
            low = (grad * dg[:, cols].astype(F32)).astype(BF16)
            gu[0, :, cols] = low
            up_row[pl.ds(0, 1), cols] = jnp.sum(low.astype(F32), axis=0, keepdims=True)
            dn[...] = dn[...] + across(low, wt_u[slot])
            return carry

        def part(first, size):
            lax.fori_loop(first, first + size, step, 0)

        half = count // 2
        part(0, half)
        pump()
        part(half, count - half)

    def tiles_back(whole, buf, sem, left, put):
        tile = buf.shape[1]
        spans = [(i, min(tile, width - i)) for i in range(0, width, tile)]
        row_tile(whole, buf, 0, *spans[0], sem).start()
        for n, (first, size) in enumerate(spans):
            row_tile(whole, buf, n % 2, first, size, sem).wait()
            if n + 1 < len(spans):
                row_tile(whole, buf, (n + 1) % 2, *spans[n + 1], sem).start()
            put(first, size, across(left(), buf[n % 2, pl.ds(0, size)]))

    def kv_copy(l, it, slot):
        s, j = it // pairs, lax.rem(it, pairs)
        return [
            pltpu.make_async_copy(
                kept[l]["kv"].at[s, :, pl.ds(pl.multiple_of(i * wide + j * LANES, LANES), LANES)],
                kvp.at[slot, i],
                kvp_sem.at[slot, i],
            )
            for i in range(2)
        ]

    def attend_back(l, first, count):
        def step(it, carry):
            slot = lax.rem(it, 2)
            for copy in kv_copy(l, it, slot):
                copy.wait()

            @pl.when(it + 1 < total)
            def _():
                for copy in kv_copy(l, it + 1, 1 - slot):
                    copy.start()

            s, j = it // pairs, lax.rem(it, pairs)
            here = pl.ds(pl.multiple_of(s * rows, rows), rows)
            col = pl.ds(pl.multiple_of(j * LANES, LANES), LANES)
            col_v = pl.ds(pl.multiple_of(wide + j * LANES, LANES), LANES)
            q2, go_block = two_heads(q[here, col]), go[here, col]
            go2 = two_heads(go_block)
            keys, values = kvp[slot, 0], kvp[slot, 1]
            product = go_block.astype(F32) * o[here, col].astype(F32)
            delta = jnp.sum(two_heads(product), axis=-1, keepdims=True)
            lane = lax.broadcasted_iota(jnp.int32, (2 * rows, LANES), 1)
            block = lse[pl.ds(pl.multiple_of(s * 2 * rows, rows), 2 * rows), :]
            log_total = jnp.sum(jnp.where(lane == it, block, 0.0), axis=-1, keepdims=True)
            seen = bias[s]
            scores = across(q2, keys) * (HEAD_DIM ** (-0.5)) + jnp.concatenate([seen, seen], axis=0)
            probs = jnp.exp(scores - log_total)
            grads = across(go2, values)
            low = (probs * (grads - delta)).astype(BF16)
            dq = jnp.dot(low, keys, preferred_element_type=F32) * (HEAD_DIM ** (-0.5))
            gq[here, col] = one_pair(dq, rows).astype(BF16)
            dk = (over_rows(low, q2) * (HEAD_DIM ** (-0.5))).astype(BF16)
            dv = over_rows(probs.astype(BF16), go2).astype(BF16)
            for b in range(slots // rows):
                mine = lax.rem(b + core, 2)
                span = slice(b * rows, (b + 1) * rows)
                parts[mine, b // 2, s, :, col] = dk[span]
                parts[mine, b // 2, s, :, col_v] = dv[span]
            return carry

        lax.fori_loop(first, first + count, step, 0)

    loads = {}

    def early(l):
        for i, (name, dst) in enumerate((("h1", hx), ("dg", dg), ("q", q), ("o", o), ("lse", lse))):
            loads[name] = load(l, name, dst, i)
            loads[name].start()
        for kind in KINDS:
            free_kind(kind, l)
            name = exchange[kind][0][0]
            piece_load(l, name).start()
            pg_sent(name)
            pg_post(name, kept[l][name].at[1 - core])

    rest_acc[...] = jnp.zeros_like(rest_acc)
    sm[...] = jnp.zeros_like(sm)
    for buf in (gm, gu, ga, gx):
        buf[0] = jnp.zeros(buf.shape[1:], BF16)
    go[...] = jnp.zeros_like(go)
    early(layers - 1)
    for s in range(seqs):

        def first_grad(first, size):
            here = pl.ds(s * rows + first, size)
            place = at.c8 * rows + first + lax.broadcasted_iota(jnp.int32, (size, width), 0)
            g[here, :] = jnp.where(place < lengths[s], cot[here, :].astype(F32), 0.0)

        by_tiles(rows, 32, first_grad)
    key_bias(bias, seqs, rows, slots, lengths, at.c8)

    for l in reversed(range(layers)):
        keys = KeyGrads(
            at, parts, kv_sib[l], kv_stage, kv_plane, kv_send.at[l], kv_recv.at[l], kv_local,
            kv_credit, None if l == layers - 1 else l,
        )
        if l < layers - 1:
            early(l)
        pg_sent("gm")
        low_copy(g, gm)
        pg_post("gm", gm.at[0])
        column_sums(l, 7, gm)
        piece_load(l, "pz").wait()
        pg_take("pz")
        pg_take("gm")
        for i in range(4):
            weight_grad(l, i, pz.at[:, i], gm, 0)
            pump()
        done_kind("down", l)
        loads["dg"].wait()
        pg_sent("gu")
        ff_back(l)
        pg_post("gu", gu.at[0])
        pump()
        for r in range(4):
            sm[pl.ds(l * 16 + 8 + r, 1), :] = up_row[pl.ds(0, 1), pl.ds(r * wide, wide)]
        loads["h1"].wait()
        norm_back(l, 1)
        loads["h"] = load(l, "h", hx, 5)
        loads["h"].start()
        pg_sent("ga")
        low_copy(g, ga)
        pg_post("ga", ga.at[0])
        column_sums(l, 6, ga)
        pump()

        def put_go(first, size, value):
            go[:, pl.ds(first, size)] = value.astype(BF16)

        tiles_back(wholes[l][1], wt_a, w_sem.at[0], lambda: ga[0, :, pl.ds(0, width)], put_go)
        for copy in kv_copy(l, 0, 0):
            copy.start()
        pump()
        piece_load(l, "pc").wait()
        pg_take("pc")
        pg_take("gu")
        for i in range(4):
            weight_grad(l, 4 + i, pc, gu, i * wide)
            pump()
        done_kind("up", l)
        piece_load(l, "po").wait()
        pg_take("po")
        pg_take("ga")
        weight_grad(l, 8, po, ga, 0)
        done_kind("out", l)
        pump()
        for name in ("q", "o", "lse"):
            loads[name].wait()
        step = 3
        for first in range(0, total, step):
            attend_back(l, first, min(step, total - first))
            pump()
        keys.start()
        keys.first()
        pump()
        keys.relay()
        pump()
        keys.combine(l > 0)
        pg_sent("gx")
        for s in range(seqs):

            def join(first, size):
                here, there = pl.ds(s * rows + first, size), pl.ds(first, size)
                gx[0, here, pl.ds(0, width)] = gq[here, pl.ds(0, width)]
                gx[0, here, pl.ds(width, width)] = parts[0, at.p, s, there, pl.ds(0, width)]
                gx[0, here, pl.ds(2 * width, width)] = parts[0, at.p, s, there, pl.ds(wide, width)]

            by_tiles(rows, 64, join)
        pg_post("gx", gx.at[0])
        for i, col in ((4, 0), (5, 2 * width)):
            put_row(l, i, jnp.sum(gx[0, :, pl.ds(col, width)].astype(F32), axis=0, keepdims=True))

        def put_dn(first, size, value):
            dn[:, pl.ds(first, size)] = value

        piece_load(l, "pa").wait()
        pg_take("pa")
        pg_take("gx")
        for i in range(3):
            weight_grad(l, 9 + i, pa, gx, i * wide)
            pump()
        done_kind("mix", l)
        rest_grad(l)
        rest_item = items[-1]
        pump()
        tiles_back(wholes[l][0], wt_q, w_sem.at[2], lambda: gx[0, :, pl.ds(0, 3 * width)], put_dn)
        loads["h"].wait()
        pump()
        norm_back(l, 0)
        keys.drain()
        while l and any(entry[0] is rest_item and len(entry[1]) > 2 for entry in active):
            pump()

    def sm_copy(i, src, dst, device):
        return remote(src, dst, sm_send.at[i], sm_recv.at[i], device)

    current = sm
    for i, device in enumerate((at.sib, at.x_dev, at.y_dev)):
        copy = sm_copy(i, current, sm_in.at[i], device)
        copy.start()
        pump()
        copy.wait()
        sm_sum[i % 2] = current[...] + sm_in[i]
        current = sm_sum.at[i % 2]
    hops = []
    for i, device in enumerate(others):
        copy = sm_copy(3 + i, current, sm_z.at[i], device)
        copy.start()
        hops.append(copy)
    pump()
    for copy in hops:
        copy.wait()
    small_total = jnp.zeros(sm.shape, F32)
    for z in range(depth):
        slot = lax.rem(at.z - z - 1 + 2 * depth, depth)
        other = sm_z[jnp.minimum(slot, depth - 2)]
        small_total = small_total + jnp.where(slot == depth - 1, current[...], other)
    small_out[...] = small_total
    for l in range(layers):
        while any(entry[0] is items[(layers - l) * per_layer - 1] for entry in active):
            pump()
        rest_rows(l)
    while active:
        pump()
    for item in items:
        item.drain()
    for name in list(posted):
        pg_sent(name)


def backward(cotangent, lengths, vecs, kept, wholes, layers, ff):
    seqs, rows, width = cotangent.shape
    depth = lax.axis_size("fsdp")
    slots = rows * lax.axis_size("ctx")
    flat, wide = seqs * rows, pad_lanes(width)
    per_layer = 13
    count = layers * per_layer
    dims = (layers, seqs, rows, slots, width, ff, depth, per_layer)
    any_spec = pl.BlockSpec(memory_space=pl.ANY)
    vmem = pl.BlockSpec(memory_space=pltpu.VMEM)
    struct = lambda shape, kind: jax.ShapeDtypeStruct(shape, kind)
    out_shape = [struct((flat, width), F32), struct((layers * 16, wide), F32)]
    part = width // depth
    for _ in range(layers):
        out_shape += [
            struct((4 * part, wide), BF16),
            struct((part, 4 * wide), BF16),
            struct((part, wide), BF16),
            struct((part, 3 * wide), BF16),
            struct((2 * LANES, wide), BF16),
        ]
    out_shape += [struct((4, seqs, rows, 2 * wide), BF16) for _ in range(layers)]
    dma, regular = pltpu.SemaphoreType.DMA, pltpu.SemaphoreType.REGULAR
    low = lambda *shape: pltpu.VMEM(shape, BF16)
    full = lambda *shape: pltpu.VMEM(shape, F32)
    chunk = LANES // 4
    scratch = [
        dma((count, 24)), dma((count, 24)), dma((count,)), regular((count,)),
        dma((layers, 8)), dma((layers, 8)), dma, regular,
        dma((10,)), dma((10,)), dma((10,)), regular((4,)), dma((8,)), dma((8,)), dma((8,)), dma((3, TILES)), dma((2, 2)), dma((13,)),
        low(SETS, depth, 4, chunk, wide), low(SETS, 3, depth, chunk, wide), low(SETS, depth - 1, chunk, wide),
        low(depth, 4, chunk, wide), low(FINS, chunk, wide),
        full(flat, width), full(flat, width),
        low(2, flat, wide), low(2, flat, 4 * wide), low(2, flat, wide), low(2, flat, 3 * wide),
        low(2, 4, flat, PIECE), low(2, flat, PIECE), low(2, flat, PIECE), low(2, flat, PIECE),
        low(flat, ff), low(flat, wide), low(flat, wide), low(flat, wide), full(2 * flat, LANES),
        full(seqs, rows, slots), low(2, 2, slots, LANES),
        low(2, 4, seqs, rows, 2 * wide), low(rows, 2 * wide), low(3, seqs, rows, 2 * wide),
        low(TILES, 256, width), low(TILES, width, 256), low(2, 256, 3 * width), low(flat, wide),
        full(layers * 16, wide), full(2, layers * 16, wide), full(3, layers * 16, wide),
        full(depth - 1, layers * 16, wide), full(8, 4 * wide),
    ]
    flat_kept = [kept[l][name] for l in range(layers) for name in KEPT]
    flat_wholes = [item for layer in wholes for item in layer]
    outs = pl.pallas_call(
        functools.partial(backward_kernel, dims),
        out_shape=out_shape,
        in_specs=[vmem, pl.BlockSpec(memory_space=pltpu.SMEM), vmem]
        + [any_spec] * (len(flat_kept) + len(flat_wholes)),
        out_specs=[vmem, vmem] + [any_spec] * (len(out_shape) - 2),
        scratch_shapes=scratch,
        compiler_params=pltpu.CompilerParams(
            collective_id=1, has_side_effects=True, vmem_limit_bytes=63 * 1024 * 1024
        ),
    )(cotangent.reshape(flat, width), lengths, vecs, *flat_kept, *flat_wholes)
    grads = [outs[2 + 5 * l : 6 + 5 * l] for l in range(layers)]
    return outs[0], outs[1].reshape(layers, 16, wide), grads


def normalize(values, scales, shifts):
    average = jnp.mean(values, axis=-1, keepdims=True)
    centred = values - average
    variance = jnp.mean(centred * centred, axis=-1, keepdims=True)
    return centred * lax.rsqrt(variance + 1e-05) * scales + shifts


def outer_sum(left_rows, right_rows):
    return lax.dot_general(
        left_rows, right_rows, (((0,), (0,)), ((), ())), preferred_element_type=jnp.float32
    )


def times_transpose(left_rows, weight_rows):
    return lax.dot_general(
        left_rows, weight_rows, (((1,), (1,)), ((), ())), preferred_element_type=jnp.float32
    )


def allowed_mask(positions, key_places, lengths):
    causal = (key_places[None, :] <= positions[:, None]) & (key_places[None, :] >= 0)
    inside = key_places[None, :] < lengths[:, None]
    return causal[None, None, :, :] & inside[:, None, None, :]


def attend_forward(queries, key_part, value_part, positions, lengths, score_scale):
    seq_count, row_count, head_count, head_width = queries.shape
    lowest = jnp.full((seq_count, head_count, row_count), -1e30, jnp.float32)
    key_places = jnp.arange(key_part.shape[1], dtype=jnp.int32)
    allowed = allowed_mask(positions, key_places, lengths)
    scores = (
        jnp.einsum("sqhe,skhe->shqk", queries, key_part, preferred_element_type=jnp.float32)
        * score_scale
    )
    scores = jnp.where(allowed, scores, -1e30)
    new_top = jnp.maximum(lowest, jnp.max(scores, axis=-1))
    exp_weights = jnp.where(allowed, jnp.exp(scores - new_top[..., None]), 0.0)
    running_total = jnp.sum(exp_weights, axis=-1)
    running_sum = jnp.einsum(
        "shqk,skhe->shqe",
        exp_weights.astype(jnp.bfloat16),
        value_part,
        preferred_element_type=jnp.float32,
    )
    output = jnp.transpose(running_sum / running_total[..., None], (0, 2, 1, 3))
    return (output, new_top + jnp.log(running_total))


def block_terms(
    queries,
    grad_out,
    log_total,
    delta_row,
    key_part,
    value_part,
    first_key,
    positions,
    lengths,
    score_scale,
):
    key_places = first_key + jnp.arange(key_part.shape[1], dtype=jnp.int32)
    allowed = allowed_mask(positions, key_places, lengths)
    scores = (
        jnp.einsum("sqhe,skhe->shqk", queries, key_part, preferred_element_type=jnp.float32)
        * score_scale
    )
    scores = jnp.where(allowed, scores, -1e30)
    probability = jnp.where(allowed, jnp.exp(scores - log_total[..., None]), 0.0)
    grad_probs = jnp.einsum(
        "sqhe,skhe->shqk", grad_out, value_part, preferred_element_type=jnp.float32
    )
    grad_scores = (probability * (grad_probs - delta_row[..., None])).astype(jnp.bfloat16)
    query_add = (
        jnp.einsum("shqk,skhe->sqhe", grad_scores, key_part, preferred_element_type=jnp.float32)
        * score_scale
    )
    key_add = (
        jnp.einsum("shqk,sqhe->skhe", grad_scores, queries, preferred_element_type=jnp.float32)
        * score_scale
    )
    value_add = jnp.einsum(
        "shqk,sqhe->skhe",
        probability.astype(jnp.bfloat16),
        grad_out,
        preferred_element_type=jnp.float32,
    )
    return (query_add, key_add, value_add)


def pack_small(ln_gain, ln_bias, b_qv, b_out, b_up, b_down):
    layers, _, part = ln_gain.shape
    return jnp.concatenate(
        [ln_gain, ln_bias, b_qv, b_out[:, None], b_down[:, None], b_up.reshape(layers, 4, part)],
        axis=1,
    )


def unpack_small(whole):
    depth, _, part = whole.shape
    flat = jnp.transpose(whole[:, :8], (1, 0, 2)).reshape(8, depth * part)
    up_bias = whole[:, 8:].reshape(depth * 4 * part)
    return flat[0:2], flat[2:4], flat[4:6], flat[6], flat[7], up_bias


def small_rows(gains, shifts, mix_bias, out_bias, down_bias, up_bias, depth):
    width = gains.shape[-1]
    flat = jnp.concatenate([gains, shifts, mix_bias, out_bias[None], down_bias[None]], axis=0)
    flat = jnp.transpose(flat.reshape(8, depth, width // depth), (1, 0, 2))
    return jnp.concatenate([flat, up_bias.reshape(depth, 4, width // depth)], axis=1)


def fast_mesh(rows):
    return lax.axis_size("ctx") == 8 and rows % 272 == 0


def gather_all(weights, small):
    flat = [item for layer in weights for item in layer]
    layers = len(weights)
    wholes = [lax.all_gather(item, "fsdp", axis=0, tiled=True) for item in flat]
    small_all = lax.all_gather(small, "fsdp", axis=0)
    return [wholes[4 * i : 4 * i + 4] for i in range(layers)], [small_all[:, i] for i in range(layers)]


def reduce_layer(grads):
    shards_now = [
        lax.psum_scatter(item, "fsdp", scatter_dimension=0, tiled=True) for item in grads
    ]
    return [lax.psum(item, "ctx") for item in shards_now]


def shards(
    tokens,
    lengths,
    cotangent,
    ln_gain,
    ln_bias,
    w_qkv,
    b_qv,
    w_out,
    b_out,
    w_up,
    b_up,
    w_down,
    b_down,
):
    seq_count, row_count, model_width = tokens.shape
    head_width = HEAD_DIM
    head_count = model_width // head_width
    score_scale = head_width ** (-0.5)
    ctx_index = lax.axis_index("ctx")
    depth = lax.axis_size("fsdp")
    positions = ctx_index * row_count + jnp.arange(row_count, dtype=jnp.int32)
    valid_rows = (positions[None, :] < lengths[:, None]).astype(jnp.float32)[..., None]
    flat_rows = seq_count * row_count
    split_shape = (seq_count, row_count, head_count, head_width)
    layer_total = ln_gain.shape[0]
    hidden = tokens.astype(jnp.float32).reshape(flat_rows, model_width)
    small = pack_small(ln_gain, ln_bias, b_qv, b_out, b_up, b_down)
    if fast_mesh(w_qkv.shape[1]):
        part = small.shape[2]
        ff = w_up.shape[2]
        padded = jnp.pad(small, ((0, 0), (0, 4), (0, pad_lanes(part) - part)))
        activations, vectors, weights, kept = forward(
            tokens, lengths, w_qkv, w_out, w_up, w_down, padded.reshape(layer_total * 16, -1)
        )
        grad_in, small_sums, sums = backward(
            cotangent, lengths, vectors, kept, weights, layer_total, ff
        )
        mine = lambda rows: lax.dynamic_slice_in_dim(
            rows[..., :model_width], lax.axis_index("fsdp") * part, part, axis=rows.ndim - 1
        )
        up_bias = small_sums[:, 8:12].reshape(layer_total, -1)[:, :ff]
        up_part = ff // depth
        whole = lambda member, cols: jnp.stack(
            [item[member][:, :cols].astype(jnp.float32) for item in sums]
        )
        return (
            activations.reshape(tokens.shape),
            grad_in.reshape(tokens.shape),
            mine(small_sums[:, 0:2]),
            mine(small_sums[:, 2:4]),
            whole(3, 3 * model_width),
            mine(small_sums[:, 4:6]),
            whole(2, model_width),
            mine(small_sums[:, 6]),
            whole(1, ff),
            lax.dynamic_slice_in_dim(up_bias, lax.axis_index("fsdp") * up_part, up_part, axis=1),
            whole(0, model_width),
            mine(small_sums[:, 7]),
        )
    weights, smalls = gather_all(
        [(w_qkv[i], w_out[i], w_up[i], w_down[i]) for i in range(layer_total)], small
    )
    kept_layers = []
    for layer_index in range(layer_total):
        mix_weight, out_weight, up_weight, down_weight = weights[layer_index]
        gain_rows, shift_rows, mix_bias, out_bias, down_bias, up_bias = unpack_small(
            smalls[layer_index].astype(jnp.float32)
        )
        normed_first = normalize(hidden, gain_rows[0], shift_rows[0]).astype(jnp.bfloat16)
        mixed_rows = jnp.dot(normed_first, mix_weight, preferred_element_type=jnp.float32)
        queries = (
            (mixed_rows[:, :model_width] + mix_bias[0]).astype(jnp.bfloat16).reshape(split_shape)
        )
        key_rows = (
            mixed_rows[:, model_width : 2 * model_width].astype(jnp.bfloat16).reshape(split_shape)
        )
        value_rows = (
            (mixed_rows[:, 2 * model_width :] + mix_bias[1])
            .astype(jnp.bfloat16)
            .reshape(split_shape)
        )
        key_part = lax.all_gather(key_rows, "ctx", axis=1, tiled=True)
        value_part = lax.all_gather(value_rows, "ctx", axis=1, tiled=True)
        output, log_total = attend_forward(
            queries, key_part, value_part, positions, lengths, score_scale
        )
        output = output.reshape(flat_rows, model_width)
        attended = output.astype(jnp.bfloat16)
        middle = (
            hidden + jnp.dot(attended, out_weight, preferred_element_type=jnp.float32) + out_bias
        )
        normed_second = normalize(middle, gain_rows[1], shift_rows[1]).astype(jnp.bfloat16)
        upper_pre = (
            jnp.dot(normed_second, up_weight, preferred_element_type=jnp.float32) + up_bias
        )
        active = jax.nn.gelu(upper_pre).astype(jnp.bfloat16)
        kept_layers.append(
            (
                hidden,
                normed_first,
                queries,
                key_part,
                value_part,
                output,
                log_total,
                attended,
                middle,
                normed_second,
                upper_pre,
                active,
                gain_rows,
                shift_rows,
            )
        )
        hidden = (
            middle + jnp.dot(active, down_weight, preferred_element_type=jnp.float32) + down_bias
        )
    activations = (valid_rows * hidden.reshape(seq_count, row_count, model_width)).astype(
        jnp.bfloat16
    )
    grad_hidden = (cotangent.astype(jnp.float32) * valid_rows).reshape(flat_rows, model_width)
    big_grads = [None] * layer_total
    small_grads = [None] * layer_total
    for layer_index in reversed(range(layer_total)):
        (
            hidden_in,
            normed_first,
            queries,
            key_part,
            value_part,
            output,
            log_total,
            attended,
            middle,
            normed_second,
            upper_pre,
            active,
            gain_rows,
            shift_rows,
        ) = kept_layers[layer_index]
        mix_weight, out_weight, up_weight, down_weight = weights[layer_index]
        grad_branch = grad_hidden.astype(jnp.bfloat16)
        down_bias_grad = jnp.sum(grad_branch.astype(jnp.float32), axis=0)
        down_grad = outer_sum(active, grad_branch)
        grad_active = times_transpose(grad_branch, down_weight)
        unused_gelu, gelu_pull = jax.vjp(jax.nn.gelu, upper_pre)
        grad_upper = gelu_pull(grad_active)[0].astype(jnp.bfloat16)
        up_bias_grad = jnp.sum(grad_upper.astype(jnp.float32), axis=0)
        up_grad = outer_sum(normed_second, grad_upper)
        grad_normed = times_transpose(grad_upper, up_weight)
        unused_norm, norm_pull = jax.vjp(normalize, middle, gain_rows[1], shift_rows[1])
        grad_middle, gain_second, shift_second = norm_pull(grad_normed)
        grad_middle = grad_middle + grad_hidden
        grad_attn = grad_middle.astype(jnp.bfloat16)
        out_bias_grad = jnp.sum(grad_attn.astype(jnp.float32), axis=0)
        out_grad = outer_sum(attended, grad_attn)
        grad_output = times_transpose(grad_attn, out_weight).astype(jnp.bfloat16)
        delta_row = jnp.transpose(
            jnp.sum((grad_output.astype(jnp.float32) * output).reshape(split_shape), axis=-1),
            (0, 2, 1),
        )
        grad_heads = grad_output.reshape(split_shape)
        query_grad, key_add, value_add = block_terms(
            queries,
            grad_heads,
            log_total,
            delta_row,
            key_part,
            value_part,
            0,
            positions,
            lengths,
            score_scale,
        )
        key_low = lax.psum_scatter(
            key_add.astype(jnp.bfloat16), "ctx", scatter_dimension=1, tiled=True
        ).reshape(flat_rows, model_width)
        value_low = lax.psum_scatter(
            value_add.astype(jnp.bfloat16), "ctx", scatter_dimension=1, tiled=True
        ).reshape(flat_rows, model_width)
        query_low = query_grad.reshape(flat_rows, model_width).astype(jnp.bfloat16)
        grad_mixed = jnp.concatenate([query_low, key_low, value_low], axis=1)
        mix_bias_grad = jnp.stack(
            [
                jnp.sum(query_low.astype(jnp.float32), axis=0),
                jnp.sum(value_low.astype(jnp.float32), axis=0),
            ]
        )
        mix_grad = outer_sum(normed_first, grad_mixed)
        grad_normed_first = times_transpose(grad_mixed, mix_weight)
        unused_first, first_pull = jax.vjp(normalize, hidden_in, gain_rows[0], shift_rows[0])
        grad_input, gain_first, shift_first = first_pull(grad_normed_first)
        grad_hidden = grad_input + grad_middle
        big_grads[layer_index] = reduce_layer(
            [item.astype(jnp.bfloat16) for item in (up_grad, down_grad, mix_grad, out_grad)]
        )
        small_grads[layer_index] = small_rows(
            jnp.stack([gain_first, gain_second]),
            jnp.stack([shift_first, shift_second]),
            mix_bias_grad,
            out_bias_grad,
            down_bias_grad,
            up_bias_grad,
            depth,
        )
    input_grad = grad_hidden.reshape(seq_count, row_count, model_width)
    packed = jnp.stack(small_grads).astype(jnp.bfloat16)
    total = lax.psum(packed, ("fsdp", "ctx"))
    own = lax.dynamic_index_in_dim(total, lax.axis_index("fsdp"), 1, keepdims=False)
    own = own.astype(jnp.float32)

    def whole(member):
        return jnp.stack([big_grads[i][member].astype(jnp.float32) for i in range(layer_total)])

    return (
        activations,
        input_grad,
        own[:, 0:2],
        own[:, 2:4],
        whole(2),
        own[:, 4:6],
        whole(3),
        own[:, 6],
        whole(0),
        own[:, 8:].reshape(layer_total, -1),
        whole(1),
        own[:, 7],
    )


def solution(mesh):
    placed = (
        P("fsdp", "ctx", None),
        P("fsdp"),
        P("fsdp", "ctx", None),
        P(None, None, "fsdp"),
        P(None, None, "fsdp"),
        P(None, "fsdp", None),
        P(None, None, "fsdp"),
        P(None, "fsdp", None),
        P(None, "fsdp"),
        P(None, "fsdp", None),
        P(None, "fsdp"),
        P(None, "fsdp", None),
        P(None, "fsdp"),
    )
    return jax.shard_map(
        shards,
        mesh=mesh,
        in_specs=placed,
        out_specs=(
            P("fsdp", "ctx", None),
            P("fsdp", "ctx", None),
            P(None, None, "fsdp"),
            P(None, None, "fsdp"),
            P(None, "fsdp", None),
            P(None, None, "fsdp"),
            P(None, "fsdp", None),
            P(None, "fsdp"),
            P(None, "fsdp", None),
            P(None, "fsdp"),
            P(None, "fsdp", None),
            P(None, "fsdp"),
        ),
        check_vma=False,
    )
```

```python
import functools

import jax
import jax.numpy as jnp
from jax import lax
from jax.experimental import pallas as pl
from jax.experimental.pallas import tpu as pltpu
from jax.sharding import PartitionSpec as P

MESH = pl.DeviceIdType.MESH


class Place:
    def __init__(self):
        self.depth = lax.axis_size("fsdp")
        self.z = lax.axis_index("fsdp")
        self.c8 = lax.axis_index("ctx")
        self.core = lax.rem(self.c8, 2)
        self.p = self.c8 // 2
        self.px = lax.rem(self.p, 2)
        self.py = self.p // 2
        self.sib = {"ctx": self.c8 + 1 - 2 * self.core}
        self.x_dev = {"ctx": self.c8 + 2 - 4 * self.px}
        self.y_dev = {"ctx": self.c8 + 4 - 8 * self.py}
        self.p_x = self.p + 1 - 2 * self.px
        self.p_y = self.p + 2 - 4 * self.py
        self.p_d = 3 - self.p
        self.relay_from = self.p + (1 - self.core) * (1 - 2 * self.px) + self.core * (2 - 4 * self.py)
        self.relay_dev = {
            "ctx": self.c8 + (1 - self.core) * (4 - 8 * self.py) + self.core * (2 - 4 * self.px)
        }

    def up(self):
        return {"fsdp": self.z + 1}

    def down(self):
        return {"fsdp": self.z - 1}

    def greet(self):
        barrier = pltpu.get_barrier_semaphore()
        for device in (self.sib, self.x_dev, self.y_dev):
            pl.semaphore_signal(barrier, inc=1, device_id=device, device_id_type=MESH)

        @pl.when(self.z > 0)
        def _():
            pl.semaphore_signal(barrier, inc=1, device_id=self.down(), device_id_type=MESH)

        @pl.when(self.z < self.depth - 1)
        def _():
            pl.semaphore_signal(barrier, inc=1, device_id=self.up(), device_id_type=MESH)

        below = jnp.where(self.z > 0, 1, 0)
        above = jnp.where(self.z < self.depth - 1, 1, 0)
        pl.semaphore_wait(barrier, 3 + below + above)


def remote(src, dst, send_sem, recv_sem, device):
    return pltpu.make_async_remote_copy(
        src_ref=src, dst_ref=dst, send_sem=send_sem, recv_sem=recv_sem, device_id=device, device_id_type=MESH
    )


class Gather:
    def __init__(self, at, own, whole, left_core, send, recv, line=0):
        self.at, self.own, self.whole = at, own, whole
        self.send, self.recv = send, recv
        rows = own.shape[0]
        self.rows = rows
        unit = rows // 17
        self.block = 8 * unit
        self.t1 = 2 * unit - line
        self.line = pl.ds(pl.multiple_of(at.core * self.block + 4 * self.t1, 16), 4 * line) if line else None
        self.rest = pl.ds(16 * unit, unit)
        self.has_rest = at.core == left_core

    def t1_rows(self, p, core=None):
        core = self.at.core if core is None else core
        return pl.ds(pl.multiple_of(core * self.block + p * self.t1, 16), self.t1)

    def block_rows(self, core):
        return pl.ds(pl.multiple_of(core * self.block, 16), self.block)

    def copy(self, kind, shard, rows, device, src=None, second=False):
        depth = self.at.depth
        slot = kind * depth + shard
        place = self.place(shard, rows)
        src = place if src is None else src
        send = self.send.at[(8 * depth + kind) if second else slot]
        return remote(src, place, send, self.recv.at[slot], device)

    def place(self, shard, rows):
        first = pl.multiple_of(shard * self.rows + rows.start, 16)
        return self.whole.at[pl.ds(first, rows.size)]

    def start(self):
        at = self.at
        mine = self.t1_rows(at.p)

        @pl.when(at.z < at.depth - 1)
        def _():
            self.copy(0, at.z, mine, at.up(), self.own.at[mine]).start()
            if self.line:
                self.copy(7, at.z, self.line, at.up(), self.own.at[self.line]).start()

            @pl.when(self.has_rest)
            def _():
                self.copy(1, at.z, self.rest, at.up(), self.own.at[self.rest]).start()

        @pl.when(at.z > 0)
        def _():
            self.copy(0, at.z, mine, at.down(), self.own.at[mine], True).start()
            if self.line:
                self.copy(7, at.z, self.line, at.down(), self.own.at[self.line], True).start()

            @pl.when(self.has_rest)
            def _():
                self.copy(1, at.z, self.rest, at.down(), self.own.at[self.rest], True).start()

    def cases(self, step, do):
        at = self.at

        @pl.when(at.z - 1 - step >= 0)
        def _():
            do(at.z - 1 - step, at.z < at.depth - 1, at.up())

        @pl.when(at.z + 1 + step < at.depth)
        def _():
            do(at.z + 1 + step, at.z > 0, at.down())

    def arrive(self, step):
        at = self.at
        mine = self.t1_rows(at.p)

        def do(shard, onward, device):
            self.copy(0, shard, mine, at.sib).wait_recv()

            @pl.when(onward)
            def _():
                self.copy(0, shard, mine, device).start()

            self.copy(2, shard, mine, at.x_dev).start()
            self.copy(3, shard, mine, at.y_dev).start()
            if self.line:
                self.copy(7, shard, self.line, at.sib).wait_recv()

                @pl.when(onward)
                def _():
                    self.copy(7, shard, self.line, device).start()

            @pl.when(self.has_rest)
            def _():
                self.copy(1, shard, self.rest, at.sib).wait_recv()

                @pl.when(onward)
                def _():
                    self.copy(1, shard, self.rest, device).start()

                self.copy(5, shard, self.rest, at.sib).start()

        self.cases(step, do)

    def plane(self, step):
        at = self.at

        def do(shard, onward, device):
            self.copy(2, shard, self.t1_rows(at.p_x), at.sib).wait_recv()
            self.copy(3, shard, self.t1_rows(at.p_y), at.sib).wait_recv()
            self.copy(4, shard, self.t1_rows(at.relay_from), at.relay_dev).start()

        self.cases(step, do)

    def share(self, step):
        at = self.at

        def do(shard, onward, device):
            self.copy(4, shard, self.t1_rows(at.p_d), at.sib).wait_recv()
            self.copy(6, shard, self.block_rows(at.core), at.sib).start()

        self.cases(step, do)

    def finish(self, step, then):
        at = self.at

        def do(shard, onward, device):
            self.copy(6, shard, self.block_rows(1 - at.core), at.sib).wait_recv()

            @pl.when(jnp.logical_not(self.has_rest))
            def _():
                self.copy(5, shard, self.rest, at.sib).wait_recv()

            then(shard)

        self.cases(step, do)

    def drain(self):
        at = self.at
        mine = self.t1_rows(at.p)

        @pl.when(at.z < at.depth - 1)
        def _():
            self.copy(0, at.z, mine, at.up(), self.own.at[mine]).wait_send()
            if self.line:
                self.copy(7, at.z, self.line, at.up(), self.own.at[self.line]).wait_send()

            @pl.when(self.has_rest)
            def _():
                self.copy(1, at.z, self.rest, at.up(), self.own.at[self.rest]).wait_send()

        @pl.when(at.z > 0)
        def _():
            self.copy(0, at.z, mine, at.down(), self.own.at[mine], True).wait_send()
            if self.line:
                self.copy(7, at.z, self.line, at.down(), self.own.at[self.line], True).wait_send()

            @pl.when(self.has_rest)
            def _():
                self.copy(1, at.z, self.rest, at.down(), self.own.at[self.rest], True).wait_send()

        def do(shard, onward, device):
            @pl.when(onward)
            def _():
                self.copy(0, shard, mine, device).wait_send()
                if self.line:
                    self.copy(7, shard, self.line, device).wait_send()

                @pl.when(self.has_rest)
                def _():
                    self.copy(1, shard, self.rest, device).wait_send()

            self.copy(2, shard, mine, at.x_dev).wait_send()
            self.copy(3, shard, mine, at.y_dev).wait_send()
            self.copy(4, shard, self.t1_rows(at.relay_from), at.relay_dev).wait_send()
            self.copy(6, shard, self.block_rows(at.core), at.sib).wait_send()

            @pl.when(self.has_rest)
            def _():
                self.copy(5, shard, self.rest, at.sib).wait_send()

        for step in range(at.depth - 1):
            self.cases(step, do)


def both(*conds):
    conds = [c for c in conds if c is not None]
    if not conds:
        return None
    total = conds[0]
    for c in conds[1:]:
        total = jnp.logical_and(total, c)
    return total


def under(cond, do):
    if cond is None:
        do()
    else:
        pl.when(cond)(do)


def add_rows(acc, extra, rows):
    def step(i, carry):
        piece = pl.ds(pl.multiple_of(i * 16, 16), 16)
        acc[piece, :] = acc[piece, :] + extra[piece, :]
        return carry

    lax.fori_loop(0, rows // 16, step, 0)


def add_rows_two(acc, one, two, rows):
    def step(i, carry):
        piece = pl.ds(pl.multiple_of(i * 16, 16), 16)
        total = acc[piece, :].astype(jnp.float32) + one[piece, :].astype(jnp.float32)
        acc[piece, :] = (total + two[piece, :].astype(jnp.float32)).astype(jnp.bfloat16)
        return carry

    lax.fori_loop(0, rows // 16, step, 0)


HEAD_DIM = 64
LANES = 128
F32, BF16 = jnp.float32, jnp.bfloat16


def pad_lanes(n):
    return (n + LANES - 1) // LANES * LANES


def by_tiles(total, tile, do):
    count = total // tile

    def step(i, carry):
        do(pl.multiple_of(i * tile, tile), tile)
        return carry

    if count:
        lax.fori_loop(0, count, step, 0)
    if total % tile:
        do(count * tile, total % tile)


def row_norm(values):
    average = jnp.mean(values, axis=-1, keepdims=True)
    centred = values - average
    variance = jnp.mean(centred * centred, axis=-1, keepdims=True)
    scale = lax.rsqrt(variance + 1e-05)
    return centred * scale, scale


GELU_A = 0.7978845608028654
GELU_B = 0.044715


def gelu_both(u):
    square = u * u
    bent = jnp.tanh(GELU_A * (u + GELU_B * u * square))
    half = 0.5 * (1.0 + bent)
    slope = half + 0.5 * u * (1.0 - bent * bent) * (GELU_A * (1.0 + 3.0 * GELU_B * square))
    return u * half, slope


def cut_pieces(src, dst, part, first):
    depth = 4

    def do(off, size):
        here = pl.ds(off, size)
        left = []
        for t in range(depth):
            start = (first + t * (src.shape[1] // part // depth)) * part
            block = src[here, pl.ds(start, part)]
            for core in range(2):
                dst[core, here, pl.ds(t * LANES, LANES)] = block[:, core * LANES : (core + 1) * LANES]
            left.append(block[:, 2 * LANES :])
        rest = jnp.concatenate(left + [jnp.zeros_like(left[0])] * 4, axis=1)
        for core in range(2):
            dst[core, here, pl.ds(depth * LANES, LANES)] = rest

    by_tiles(src.shape[0], 64, do)


class Context:
    def __init__(self, at, own, whole, rows, send, recv, local):
        self.at, self.own, self.whole, self.rows = at, own, whole, rows
        self.send, self.recv, self.local = send, recv, local
        core, p = at.core, at.p
        self.names, self.posts = {}, []

    def place(self, p, core):
        return self.whole.at[pl.ds(pl.multiple_of((2 * p + core) * self.rows, 16), self.rows)]

    def make(self, name, src, dst, device):
        i = self.names.setdefault(name, len(self.names))
        return remote(src, dst, self.send.at[i], self.recv.at[i], device)

    def post(self, name, src, dst, device):
        self.make(name, src, dst, device).start()
        self.posts.append((name, src, dst, device))

    def take(self, name, dst):
        self.make(name, dst, dst, self.at.sib).wait_recv()

    def start(self):
        at = self.at
        here = self.place(at.p, at.core)
        self.post("x", self.own, here, at.x_dev)
        self.post("y", self.own, here, at.y_dev)
        self.post("s", self.own, here, at.sib)
        self.keep = pltpu.make_async_copy(self.own, here, self.local)
        self.keep.start()

    def relay(self):
        at = self.at
        for name, p in (("x", at.p_x), ("y", at.p_y)):
            self.take(name, self.place(p, at.core))
        here = self.place(at.relay_from, at.core)
        self.post("d", here, here, at.relay_dev)
        for name, p in (("x", at.p_x), ("y", at.p_y)):
            here = self.place(p, at.core)
            self.post(name + "s", here, here, at.sib)

    def last(self):
        at = self.at
        here = self.place(at.p_d, at.core)
        self.take("d", here)
        self.post("ds", here, here, at.sib)

    def finish(self):
        at = self.at
        for name, p in (("s", at.p), ("xs", at.p_x), ("ys", at.p_y), ("ds", at.p_d)):
            self.take(name, self.place(p, 1 - at.core))
        self.keep.wait()

    def drain(self, own):
        for name, src, dst, device in self.posts:
            if (name in ("x", "y", "s")) == own:
                self.make(name, src, dst, device).wait_send()


KEPT = ("h", "pa", "q", "kv", "o", "po", "lse", "h1", "pc", "pz", "dg")
PIECE = 5 * LANES
LINE_ROWS = (0, 0, 16, 16)
SHARE_LAG, FINISH_LAG = 0, 1
TICKS = (2, 2, 2, 2)


def kept_shapes(seqs, slots, rows, width, ff):
    wide = pad_lanes(width)
    flat = seqs * rows
    return {
        "h": ((flat, width), F32),
        "pa": ((2, flat, PIECE), BF16),
        "q": ((flat, wide), BF16),
        "kv": ((seqs, slots, 2 * wide), BF16),
        "o": ((flat, wide), BF16),
        "po": ((2, flat, PIECE), BF16),
        "lse": ((flat * 2, LANES), F32),
        "h1": ((flat, width), F32),
        "pc": ((2, flat, PIECE), BF16),
        "pz": ((2, 4, flat, PIECE), BF16),
        "dg": ((flat, ff), BF16),
    }


def key_bias(out, seqs, rows, slots, lengths, ctx):
    for s in range(seqs):
        key = lax.broadcasted_iota(jnp.int32, (rows, slots), 1)
        row = ctx * rows + lax.broadcasted_iota(jnp.int32, (rows, slots), 0)
        seen = jnp.logical_and(key <= row, key < lengths[s])
        out[s] = jnp.where(seen, 0.0, -1e30)


def two_heads(block):
    lane = lax.broadcasted_iota(jnp.int32, block.shape, 1)
    zero = jnp.zeros_like(block)
    return jnp.concatenate(
        [jnp.where(lane < HEAD_DIM, block, zero), jnp.where(lane < HEAD_DIM, zero, block)], axis=0
    )


def one_pair(stacked, rows):
    lane = lax.broadcasted_iota(jnp.int32, (rows, LANES), 1)
    return jnp.where(lane < HEAD_DIM, stacked[:rows], stacked[rows:])


def across(a, b):
    return lax.dot_general(a, b, (((1,), (1,)), ((), ())), preferred_element_type=F32)


def attend(s, first, count, q_ref, kv_ref, bias_ref, o_ref, lse_ref, rows, pairs, wide):
    def step(i, carry):
        j = first + i
        col = pl.ds(pl.multiple_of(j * LANES, LANES), LANES)
        q2 = two_heads(q_ref[pl.ds(s * rows, rows), col])
        keys = kv_ref[s, :, col]
        values = kv_ref[s, :, pl.ds(pl.multiple_of(wide + j * LANES, LANES), LANES)]
        bias = bias_ref[s]
        scores = across(q2, keys) * (HEAD_DIM ** (-0.5))
        scores = scores + jnp.concatenate([bias, bias], axis=0)
        top = jnp.max(scores, axis=-1, keepdims=True)
        weights = jnp.exp(scores - top)
        total = jnp.sum(weights, axis=-1, keepdims=True)
        out = jnp.dot(weights.astype(BF16), values, preferred_element_type=F32) / total
        o_ref[pl.ds(s * rows, rows), col] = one_pair(out, rows).astype(BF16)
        mine = s * pairs + j
        here = pl.ds(s * 2 * rows, 2 * rows)
        lane = lax.broadcasted_iota(jnp.int32, (2 * rows, LANES), 1)
        lse_ref[here, :] = jnp.where(lane == mine, top + jnp.log(total), lse_ref[here, :])
        return carry

    lax.fori_loop(0, count, step, 0)


def forward_kernel(dims, *refs):
    layers, seqs, rows, slots, width, ff, depth = dims
    flat, wide = seqs * rows, pad_lanes(width)
    pairs = wide // LANES
    part = width // depth
    refs = list(refs)

    def grab(n):
        out = refs[:n]
        del refs[:n]
        return out

    tokens, lengths, w_qkv, w_out, w_up, w_down, small = grab(7)
    acts, vecs = grab(2)
    wholes = grab(4 * layers)
    kept = [dict(zip(KEPT, grab(len(KEPT)))) for _ in range(layers)]
    (send, recv, small_send, small_recv, kv_send, kv_recv, load_sem, keep_sem, stage_sem) = grab(9)
    (small_all, vec, up_bias, h, a, q, own_kv, kv, bias, o, lse, h1, c, u, z, dg, pa, pc, po, pz) = grab(20)
    w_bufs = grab(4)
    at = Place()
    at.greet()

    owns = [ref.at[l] for l in range(layers) for ref in (w_qkv, w_out, w_up, w_down)]
    items = [Gather(at, owns[k], wholes[k], k % 2, send.at[k], recv.at[k], LINE_ROWS[k % 4]) for k in range(4 * layers)]
    contexts = [
        [
            Context(
                at, own_kv.at[s], kept[l]["kv"].at[s], rows, kv_send.at[l, s], kv_recv.at[l, s],
                keep_sem.at[l, len(KEPT) + s],
            )
            for s in range(seqs)
        ]
        for l in range(layers)
    ]
    pending = {}

    def keep(l, name, src):
        copy = pltpu.make_async_copy(src, kept[l][name], keep_sem.at[l, KEPT.index(name)])
        copy.start()
        pending[(l, name)] = copy

    def free(l, name):
        copy = pending.pop((l, name), None)
        if copy is not None:
            copy.wait()

    def buffer(k):
        return w_bufs[k % 4]

    def own_copy(k, load):
        r = owns[k].shape[0]
        shard = lax.rem(at.z + k // 4, depth)
        place = buffer(k).at[pl.ds(pl.multiple_of(shard * r, 16), r)]
        if load:
            return pltpu.make_async_copy(owns[k], place, stage_sem.at[0, k])
        return pltpu.make_async_copy(place, items[k].place(at.z, pl.ds(0, r)), stage_sem.at[1, k])

    def own_load(k):
        own_copy(k, True).start()

    def own_store(k):
        own_copy(k, True).wait()
        own_copy(k, False).start()

    def own_done(k):
        own_copy(k, False).wait()

    def fetch_copy(k, shard):
        r = owns[k].shape[0]
        here = pl.ds(pl.multiple_of(shard * r, 16), r)
        return pltpu.make_async_copy(wholes[k].at[here], buffer(k).at[here], load_sem.at[k, shard])

    def fetch(k, shard):
        fetch_copy(k, shard).start()

    def ready(k):
        for shard in range(depth):
            fetch_copy(k, shard).wait()

    def small_copy(shard, device, src=None, second=False):
        return remote(
            small_all.at[shard] if src is None else src,
            small_all.at[shard],
            small_send.at[depth if second else shard],
            small_recv.at[shard],
            device,
        )

    def small_start():
        @pl.when(at.z < depth - 1)
        def _():
            small_copy(at.z, at.up(), small).start()

        @pl.when(at.z > 0)
        def _():
            small_copy(at.z, at.down(), small, True).start()

        pltpu.make_async_copy(small, small_all.at[at.z], stage_sem.at[2, 0]).start()

    def small_take():
        def do(shard, onward, device):
            small_copy(shard, at.sib).wait_recv()
            pl.when(onward)(lambda: small_copy(shard, device).start())

        for step in range(depth - 1):
            items[0].cases(step, do)
        pltpu.make_async_copy(small, small_all.at[at.z], stage_sem.at[2, 0]).wait()

    def small_drain():
        @pl.when(at.z < depth - 1)
        def _():
            small_copy(at.z, at.up(), small).wait_send()

        @pl.when(at.z > 0)
        def _():
            small_copy(at.z, at.down(), small, True).wait_send()

        def do(shard, onward, device):
            pl.when(onward)(lambda: small_copy(shard, device).wait_send())

        for step in range(depth - 1):
            items[0].cases(step, do)

    def small_spread():
        part = width // depth
        per_layer = small_all.shape[1] // layers
        total = jnp.zeros((small_all.shape[1], wide), F32)
        room = jnp.zeros((small_all.shape[1], wide - small_all.shape[2]), F32)
        pieces = [small_all[i].astype(F32) for i in range(depth)]
        for i in range(depth):
            piece = jnp.concatenate([pieces[i], room], axis=1)
            total = total + (pltpu.roll(piece, i * part, 1) if i else piece)
        for l in range(layers):
            vec[l] = total[l * per_layer : l * per_layer + 8]
            vecs[l] = total[l * per_layer : l * per_layer + 8]
            wide_up = jnp.zeros((1, ff), F32)
            up_room = jnp.zeros((1, ff - small_all.shape[2]), F32)
            for i in range(depth):
                for r in range(4):
                    at_row = l * per_layer + 8 + r
                    piece = jnp.concatenate([pieces[i][at_row : at_row + 1], up_room], axis=1)
                    shift = (i * 4 + r) * part
                    wide_up = wide_up + (pltpu.roll(piece, shift, 1) if shift else piece)
            up_bias[l] = jnp.broadcast_to(wide_up, (8, ff))

    def row(l, i):
        return vec[l, pl.ds(i, 1), pl.ds(0, width)]

    def norm(l, i, src, dst):
        def do(first, size):
            here = pl.ds(first, size)
            unit, _ = row_norm(src[here, :])
            dst[here, :] = (unit * row(l, i) + row(l, 2 + i)).astype(BF16)

        by_tiles(flat, 32, do)

    def load_tokens():
        def do(first, size):
            here = pl.ds(first, size)
            h[here, :] = tokens[here, :].astype(F32)

        by_tiles(flat, 32, do)

    def mix(l):
        def do(first, size):
            cols = pl.ds(first, size)
            u[:, cols] = jnp.dot(a[...], w_bufs[0][:, cols], preferred_element_type=F32)

        by_tiles(3 * width, 256, do)

        for s in range(seqs):

            def split(first, size):
                here, there = pl.ds(s * rows + first, size), pl.ds(first, size)
                queries = u[here, pl.ds(0, width)] + row(l, 4)
                keys = u[here, pl.ds(width, width)]
                values = u[here, pl.ds(2 * width, width)] + row(l, 5)
                q[here, pl.ds(0, width)] = queries.astype(BF16)
                own_kv[s, there, pl.ds(0, width)] = keys.astype(BF16)
                own_kv[s, there, pl.ds(wide, width)] = values.astype(BF16)

            by_tiles(rows, 32, split)

    def project(l):
        def do(first, size):
            cols = pl.ds(first, size)
            bias_row = vec[l, pl.ds(6, 1), cols]
            h1[:, cols] = (
                h[:, cols]
                + jnp.dot(o[:, pl.ds(0, width)], w_bufs[1][:, cols], preferred_element_type=F32)
                + bias_row
            )

        by_tiles(width, 256, do)

    def rise(l):
        def do(first, size):
            cols = pl.ds(first, size)
            pre = jnp.dot(c[...], w_bufs[2][:, cols], preferred_element_type=F32) + up_bias[l, pl.ds(0, 1), cols]
            value, slope = gelu_both(pre)
            z[:, cols] = value.astype(BF16)
            dg[:, cols] = slope.astype(BF16)

        by_tiles(ff, 256, do)

    def fall(l):
        def do(first, size):
            cols = pl.ds(first, size)
            h[:, cols] = (
                h1[:, cols]
                + jnp.dot(z[...], w_bufs[3][:, cols], preferred_element_type=F32)
                + vec[l, pl.ds(7, 1), cols]
            )

        by_tiles(width, 256, do)

    def finish_tokens():
        for s in range(seqs):
            def do(first, size):
                here = pl.ds(s * rows + first, size)
                place = at.c8 * rows + first + lax.broadcasted_iota(jnp.int32, (size, width), 0)
                acts[here, :] = jnp.where(place < lengths[s], h[here, :], 0.0).astype(BF16)

            by_tiles(rows, 32, do)

    steps = depth - 1
    ticks = [functools.partial(items[0].arrive, i) for i in range(steps)]
    last = 4 * layers * steps
    for n in range(last + FINISH_LAG):
        k, i = divmod(n, steps)
        if n < last:
            if i == 0 and k + 2 < 4 * layers:
                ticks.append(items[k + 2].start)
            ticks.append(functools.partial(items[k].plane, i))
            if k + 1 < 4 * layers:
                ticks.append(functools.partial(items[k + 1].arrive, i))
        if 0 <= n - SHARE_LAG < last:
            k, i = divmod(n - SHARE_LAG, steps)
            ticks.append(functools.partial(items[k].share, i))
        if n >= FINISH_LAG:
            k, i = divmod(n - FINISH_LAG, steps)
            ticks.append(("shard", k, i))
            if i == steps - 1:
                ticks.append(("end", k))

    def tick(n):
        for _ in range(n):
            if not ticks:
                return
            item = ticks.pop(0)
            if isinstance(item, tuple) and item[0] == "end":
                fetch(item[1], at.z)
            elif isinstance(item, tuple):
                items[item[1]].finish(item[2], functools.partial(fetch, item[1]))
            else:
                item()

    def reach(k):
        while ("end", k) in ticks:
            tick(1)

    small_start()
    items[0].start()
    items[1].start()
    for k in range(4 * layers):
        own_load(k)
    load_tokens()
    q[...] = jnp.zeros_like(q)
    o[...] = jnp.zeros_like(o)
    own_kv[...] = jnp.zeros_like(own_kv)
    lse[...] = jnp.zeros_like(lse)
    key_bias(bias, seqs, rows, slots, lengths, at.c8)
    for k in range(4 * layers):
        own_store(k)
    tick(steps)
    small_take()
    small_spread()
    for k in range(4 * layers):
        own_done(k)
    for l in range(layers):
        k = 4 * l
        norm(l, 0, h, a)
        keep(l, "h", h)
        free(l - 1, "pa")
        cut_pieces(a, pa, part, 0)
        keep(l, "pa", pa)
        reach(k)
        free(l - 1, "q")
        if l:
            for context in contexts[l - 1]:
                context.drain(True)
        ready(k)
        mix(l)
        for context in contexts[l]:
            context.start()
        keep(l, "q", q)
        free(l - 1, "o")
        free(l - 1, "lse")
        for context in contexts[l]:
            tick(TICKS[0])
            context.relay()
        for s, context in enumerate(contexts[l]):
            tick(TICKS[1])
            context.last()
            tick(TICKS[2])
            context.finish()
            seen = pltpu.make_async_copy(kept[l]["kv"].at[s], kv.at[s], load_sem.at[4 * layers, s])
            seen.start()
            seen.wait()
            first = 0
            for count in (pairs // 3, pairs // 3, pairs - 2 * (pairs // 3)):
                attend(s, first, count, q, kv, bias, o, lse, rows, pairs, wide)
                first += count
                tick(TICKS[3])
        keep(l, "o", o)
        keep(l, "lse", lse)
        free(l - 1, "po")
        cut_pieces(o.at[:, pl.ds(0, wide)], po, part, 0)
        keep(l, "po", po)
        ready(k + 1)
        free(l - 1, "h1")
        project(l)
        keep(l, "h1", h1)
        norm(l, 1, h1, c)
        free(l - 1, "pc")
        cut_pieces(c, pc, part, 0)
        keep(l, "pc", pc)
        reach(k + 2)
        ready(k + 2)
        free(l - 1, "dg")
        rise(l)
        keep(l, "dg", dg)
        free(l - 1, "pz")
        for i in range(4):
            cut_pieces(z, pz.at[:, i], part, i)
        keep(l, "pz", pz)
        reach(k + 3)
        free(l, "h")
        ready(k + 3)
        fall(l)
    tick(len(ticks))
    finish_tokens()
    for key in list(pending):
        free(*key)
    small_drain()
    for item in items:
        item.drain()
    for context in contexts[-1]:
        context.drain(True)
    for of_layer in contexts:
        for context in of_layer:
            context.drain(False)


def forward(tokens, lengths, w_qkv, w_out, w_up, w_down, small):
    seqs, rows, width = tokens.shape
    layers, part, _ = w_qkv.shape
    depth = lax.axis_size("fsdp")
    slots = rows * lax.axis_size("ctx")
    ff = w_up.shape[2]
    flat, wide = seqs * rows, pad_lanes(width)
    dims = (layers, seqs, rows, slots, width, ff, depth)
    any_spec = pl.BlockSpec(memory_space=pl.ANY)
    vmem = pl.BlockSpec(memory_space=pltpu.VMEM)
    struct = lambda shape, kind: jax.ShapeDtypeStruct(shape, kind)
    shapes = kept_shapes(seqs, slots, rows, width, ff)
    out_shape = [struct((flat, width), BF16), struct((layers, 8, wide), F32)]
    for l in range(layers):
        for ref in (w_qkv, w_out, w_up, w_down):
            out_shape.append(struct((depth * ref.shape[1], ref.shape[2]), BF16))
    for l in range(layers):
        out_shape += [struct(*shapes[name]) for name in KEPT]
    count = 4 * layers
    dma = pltpu.SemaphoreType.DMA
    scratch = [
        dma((count, 8 * depth + 8)),
        dma((count, 8 * depth)),
        dma((depth + 1,)),
        dma((depth,)),
        dma((layers, seqs, 8)),
        dma((layers, seqs, 8)),
        dma((count + 1, depth)),
        dma((layers, len(KEPT) + seqs)),
        dma((3, count)),
        pltpu.VMEM((depth,) + small.shape, BF16),
        pltpu.VMEM((layers, 8, wide), F32),
        pltpu.VMEM((layers, 8, ff), F32),
        pltpu.VMEM((flat, width), F32),
        pltpu.VMEM((flat, width), BF16),
        pltpu.VMEM((flat, wide), BF16),
        pltpu.VMEM((seqs, rows, 2 * wide), BF16),
        pltpu.VMEM((seqs, slots, 2 * wide), BF16),
        pltpu.VMEM((seqs, rows, slots), F32),
        pltpu.VMEM((flat, wide), BF16),
        pltpu.VMEM((2 * flat, LANES), F32),
        pltpu.VMEM((flat, width), F32),
        pltpu.VMEM((flat, width), BF16),
        pltpu.VMEM((flat, 3 * width), F32),
        pltpu.VMEM((flat, ff), BF16),
        pltpu.VMEM((flat, ff), BF16),
        pltpu.VMEM((2, flat, PIECE), BF16),
        pltpu.VMEM((2, flat, PIECE), BF16),
        pltpu.VMEM((2, flat, PIECE), BF16),
        pltpu.VMEM((2, 4, flat, PIECE), BF16),
    ] + [pltpu.VMEM((depth * ref.shape[1], ref.shape[2]), BF16) for ref in (w_qkv, w_out, w_up, w_down)]
    outs = pl.pallas_call(
        functools.partial(forward_kernel, dims),
        out_shape=out_shape,
        in_specs=[vmem, pl.BlockSpec(memory_space=pltpu.SMEM)] + [any_spec] * 5,
        out_specs=[vmem, vmem] + [any_spec] * (len(out_shape) - 2),
        scratch_shapes=scratch,
        compiler_params=pltpu.CompilerParams(
            collective_id=0, has_side_effects=True, vmem_limit_bytes=63 * 1024 * 1024
        ),
    )(tokens.reshape(flat, width), lengths, w_qkv, w_out, w_up, w_down, small)
    acts, vecs = outs[:2]
    wholes = outs[2 : 2 + count]
    rest = outs[2 + count :]
    kept = [dict(zip(KEPT, rest[l * len(KEPT) : (l + 1) * len(KEPT)])) for l in range(layers)]
    return acts, vecs, [wholes[4 * l : 4 * l + 4] for l in range(layers)], kept


SETS = 5
FINS = 10
LINE_FIRST = ()
LINE_LAG = 0
TILES = 3
KINDS = ("down", "up", "out", "mix")


def over_rows(a, b):
    return lax.dot_general(a, b, (((0,), (0,)), ((), ())), preferred_element_type=F32)


class Granule:
    def __init__(self, at, others, line_first, acc, plane_in, z_in, fin, out, send, recv, local, credit, wait_credit, give_credit, before):
        self.before = before
        self.line_first = line_first
        self.at, self.others, self.acc, self.plane_in, self.z_in = at, others, acc, plane_in, z_in
        self.fin, self.out, self.send, self.recv, self.local = fin, out, send, recv, local
        self.credit, self.wait_credit, self.give_credit = credit, wait_credit, give_credit
        self.t1 = acc.shape[2]
        self.names, self.posts = {}, []
        core, p = at.core, at.p
        self.direct_p = p + (1 - core) * (2 - 4 * at.py) + core * (1 - 2 * at.px)
        self.owner_dev = {"ctx": at.c8 + (1 - core) * (2 - 4 * at.px) + core * (4 - 8 * at.py)}

    def make(self, name, src, dst, device):
        i = self.names.setdefault(name, len(self.names))
        return remote(src, dst, self.send.at[i], self.recv.at[i], device)

    def post(self, name, src, dst, device):
        self.make(name, src, dst, device).start()
        self.posts.append((name, src, dst, device))

    def take(self, name, dst):
        self.make(name, dst, dst, self.at.sib).wait_recv()

    def place(self, p, core):
        ref, first, col, cols = self.out
        row = pl.multiple_of(first + core * 4 * self.t1 + p * self.t1, 16)
        return ref.at[pl.ds(row, self.t1), pl.ds(col, cols)]

    def line_out(self, part, landing):
        for i, device in enumerate(self.others):
            goal = lax.rem(self.at.z + 1 + i, self.at.depth)
            self.post(f"z{i}", part(goal), landing.at[i], device)

    def line_in(self, landing):
        for i in range(len(self.others)):
            self.take(f"z{i}", landing.at[i])

    def plane_out(self, part, landing):
        self.post("diag", part(self.at.p_d), landing.at[0], self.at.relay_dev)
        self.post("near", part(self.direct_p), landing.at[1], self.at.relay_dev)

    def plane_relay(self, part, landing, add):
        self.take("diag", landing.at[0])
        add(part(self.at.relay_from), landing.at[0])
        self.post("relay", part(self.at.relay_from), landing.at[2], self.owner_dev)

    def plane_in_all(self, landing):
        self.take("near", landing.at[1])
        self.take("relay", landing.at[2])

    def over_shards(self, acc, extra):
        for t in range(self.at.depth):
            add_rows(acc.at[t], extra.at[t], self.t1)

    def total(self, own, extra, out):
        def step(i, carry):
            piece = pl.ds(pl.multiple_of(i * 16, 16), 16)
            value = own[piece, :].astype(F32)
            for j in range(3):
                value = value + extra(j)[piece, :].astype(F32)
            out[piece, :] = value.astype(BF16)
            return carry

        lax.fori_loop(0, self.t1 // 16, step, 0)

    def of_shard(self, p):
        return self.acc.at[self.at.z, p]

    def of_chip(self, p):
        return self.acc.at[:, p]

    def begin(self):
        if self.wait_credit is not None:
            pl.semaphore_wait(self.wait_credit, 2 + len(self.others))
        if self.line_first:
            self.line_out(lambda t: self.acc.at[t], self.plane_in)
        else:
            self.plane_out(self.of_chip, self.plane_in)

    def second(self):
        at = self.at
        if self.line_first:
            self.line_in(self.plane_in)
            for p in range(4):
                own = self.of_shard(p)
                self.total(own, lambda j: self.plane_in.at[j, p], own)
            self.plane_out(self.of_shard, self.z_in)
        else:
            self.plane_relay(self.of_chip, self.plane_in, self.over_shards)

    def third(self):
        at = self.at
        if self.line_first:
            self.plane_relay(self.of_shard, self.z_in, lambda a, b: add_rows(a, b, self.t1))
        else:
            self.plane_in_all(self.plane_in)
            mine = self.of_chip(at.p)
            for t in range(at.depth):
                add_rows_two(mine.at[t], self.plane_in.at[1, t], self.plane_in.at[2, t], self.t1)
            self.line_out(lambda t: self.acc.at[t, at.p], self.z_in)

    def fin_sent(self):
        for name, src, dst, device in self.posts:
            if name in ("sx", "sy", "ss"):
                self.make(name, src, dst, device).wait_send()
        self.posts = [post for post in self.posts if post[0] not in ("sx", "sy", "ss")]

    def end(self):
        at = self.at
        if self.before is not None:
            self.before.fin_sent()
        own = self.of_shard(at.p)
        if self.line_first:
            self.plane_in_all(self.z_in)

            def step(i, carry):
                piece = pl.ds(pl.multiple_of(i * 16, 16), 16)
                value = own[piece, :].astype(F32) + self.z_in[1, piece, :].astype(F32)
                self.fin[piece, :] = (value + self.z_in[2, piece, :].astype(F32)).astype(BF16)
                return carry

            lax.fori_loop(0, self.t1 // 16, step, 0)
        else:
            self.line_in(self.z_in)
            self.total(own, lambda j: self.z_in.at[j], self.fin)
        if self.give_credit:
            for device in [at.x_dev, at.y_dev] + self.others:
                pl.semaphore_signal(self.credit, inc=1, device_id=device, device_id_type=MESH)
        here = self.place(at.p, at.core)
        pltpu.make_async_copy(self.fin, here, self.local).start()
        self.post("sx", self.fin, here, at.x_dev)
        self.post("sy", self.fin, here, at.y_dev)
        self.post("ss", self.fin, here, at.sib)

    def release(self):
        keep = []
        for name, src, dst, device in self.posts:
            if name[0] == "s":
                keep.append((name, src, dst, device))
            else:
                self.make(name, src, dst, device).wait_send()
        self.posts = keep

    def spread_relay(self):
        at = self.at
        for far, p in (("sx", at.p_x), ("sy", at.p_y)):
            here = self.place(p, at.core)
            self.take(far, here)
            self.post(far + "s", here, here, at.sib)
        here = self.place(at.relay_from, at.core)
        self.post("sd", here, here, at.relay_dev)

    def spread_last(self):
        at = self.at
        here = self.place(at.p_d, at.core)
        self.take("sd", here)
        self.post("sds", here, here, at.sib)

    def finish(self):
        at = self.at
        for name, p in (("ss", at.p), ("sxs", at.p_x), ("sys", at.p_y), ("sds", at.p_d)):
            self.take(name, self.place(p, 1 - at.core))
        pltpu.make_async_copy(self.fin, self.place(at.p, at.core), self.local).wait()

    def drain(self):
        for name, src, dst, device in self.posts:
            self.make(name, src, dst, device).wait_send()

    def stages(self):
        wait = [[] for _ in range(LINE_LAG)] if self.line_first else []
        return wait + [
            [self.second], [self.third], [self.end], [self.release, self.spread_relay], [self.spread_last],
            [self.finish],
        ]


class KeyGrads:
    def __init__(self, at, parts, sib_in, stage, plane_in, send, recv, local, credit, layer):
        self.at, self.parts, self.sib_in, self.stage, self.plane_in = at, parts, sib_in, stage, plane_in
        self.send, self.recv, self.local, self.credit, self.layer = send, recv, local, credit, layer
        self.names, self.posts = {}, []
        core, p = at.core, at.p
        self.direct_p = p + (1 - core) * (2 - 4 * at.py) + core * (1 - 2 * at.px)
        self.owner_dev = {"ctx": at.c8 + (1 - core) * (2 - 4 * at.px) + core * (4 - 8 * at.py)}
        self.order = [at.p_d, self.direct_p, at.relay_from, at.p]

    def make(self, name, src, dst, device):
        i = self.names.setdefault(name, len(self.names))
        return remote(src, dst, self.send.at[i], self.recv.at[i], device)

    def post(self, name, src, dst, device):
        self.make(name, src, dst, device).start()
        self.posts.append((name, src, dst, device))

    def take(self, name, dst):
        self.make(name, dst, dst, self.at.sib).wait_recv()

    def start(self):
        for i, p in enumerate(self.other_order()):
            self.post(f"s{i}", self.parts.at[1, p], self.sib_in.at[p], self.at.sib)

    def other_order(self):
        at = self.at
        core = 1 - at.core
        direct = at.p + (1 - core) * (2 - 4 * at.py) + core * (1 - 2 * at.px)
        relay = at.p + (1 - core) * (1 - 2 * at.px) + core * (2 - 4 * at.py)
        return [at.p_d, direct, relay, at.p]

    def add(self, p, extra):
        add_rows(self.parts.at[0, p], extra, self.parts.shape[2])

    def core_sum(self, i):
        p = self.order[i]
        self.take(f"s{i}", self.sib_in.at[p])
        copy = pltpu.make_async_copy(self.sib_in.at[p], self.stage, self.local)
        copy.start()
        copy.wait()
        self.add(p, self.stage)

    def first(self):
        at = self.at
        self.core_sum(0)
        if self.layer is not None:
            pl.semaphore_wait(self.credit, 2)
        self.post("diag", self.parts.at[0, at.p_d], self.plane_in.at[0], at.relay_dev)
        self.core_sum(1)
        self.post("near", self.parts.at[0, self.direct_p], self.plane_in.at[1], at.relay_dev)
        self.core_sum(2)
        self.core_sum(3)

    def relay(self):
        at = self.at
        self.take("diag", self.plane_in.at[0])
        self.add(at.relay_from, self.plane_in.at[0])
        self.post("relay", self.parts.at[0, at.relay_from], self.plane_in.at[2], self.owner_dev)

    def combine(self, give_credit):
        at = self.at
        self.take("near", self.plane_in.at[1])
        self.take("relay", self.plane_in.at[2])
        add_rows_two(self.parts.at[0, at.p], self.plane_in.at[1], self.plane_in.at[2], self.parts.shape[2])
        if give_credit:
            for device in (at.x_dev, at.y_dev):
                pl.semaphore_signal(self.credit, inc=1, device_id=device, device_id_type=MESH)

    def drain(self):
        for name, src, dst, device in self.posts:
            self.make(name, src, dst, device).wait_send()
        self.posts = []


def backward_kernel(dims, *refs):
    layers, seqs, rows, slots, width, ff, depth, per_layer = dims
    flat, wide = seqs * rows, pad_lanes(width)
    pairs = wide // LANES
    total = seqs * pairs
    refs = list(refs)

    def grab(n):
        out = refs[:n]
        del refs[:n]
        return out

    cot, lengths, vecs = grab(3)
    kept = [dict(zip(KEPT, grab(len(KEPT)))) for _ in range(layers)]
    wholes = [grab(4) for _ in range(layers)]
    grad_in, small_out = grab(2)
    outs = [grab(5) for _ in range(layers)]
    kv_sib = grab(layers)
    (g_send, g_recv, g_local, g_credit, kv_send, kv_recv, kv_local, kv_credit) = grab(8)
    (pg_send, pg_recv, pg_local, pg_credit, sm_send, sm_recv, load_sem, w_sem, kvp_sem, rest_sem) = grab(10)
    acc, plane_in, z_in, rest_acc, fin = grab(5)
    hx, dn = grab(2)
    g = grad_in
    gm, gu, ga, gx = grab(4)
    pz, pc, po, pa = grab(4)
    dg, q, go, o, lse, bias, kvp = grab(7)
    parts, kv_stage, kv_plane = grab(3)
    wt_a, wt_u, wt_q, gq = grab(4)
    sm, sm_sum, sm_in, sm_z, up_row = grab(5)

    at = Place()
    core = at.core
    barrier = pltpu.get_barrier_semaphore()
    others = [{"fsdp": lax.rem(at.z + i, depth)} for i in range(1, depth)]
    for device in [at.sib, at.x_dev, at.y_dev] + others:
        pl.semaphore_signal(barrier, inc=1, device_id=device, device_id_type=MESH)
    pl.semaphore_wait(barrier, 3 + depth - 1)

    exchange = {
        "down": [("pz", pz), ("gm", gm)],
        "up": [("pc", pc), ("gu", gu)],
        "out": [("po", po), ("ga", ga)],
        "mix": [("pa", pa), ("gx", gx)],
    }
    slot_of = {}
    for kind in KINDS:
        for name, _ in exchange[kind]:
            slot_of[name] = len(slot_of)
    buffers = {name: buf for kind in KINDS for name, buf in exchange[kind]}
    posted = {}

    def pg_copy(name, src):
        i = slot_of[name]
        buf = buffers[name]
        dst = buf.at[1]
        return remote(src, dst, pg_send.at[i], pg_recv.at[i], at.sib)

    def pg_post(name, src):
        pg_copy(name, src).start()
        posted[name] = src

    def pg_sent(name):
        src = posted.pop(name, None)
        if src is not None:
            pg_copy(name, src).wait_send()

    def pg_take(name):
        buf = buffers[name].at[1]
        pg_copy(name, buf).wait_recv()

    def piece_load(l, name):
        return pltpu.make_async_copy(kept[l][name].at[core], buffers[name].at[0], pg_local.at[slot_of[name]])

    def free_kind(kind, l):
        if l < layers - 1:
            pl.semaphore_wait(pg_credit.at[KINDS.index(kind)], 1)

    def done_kind(kind, l):
        if l > 0:
            pl.semaphore_signal(
                pg_credit.at[KINDS.index(kind)], inc=1, device_id=at.sib, device_id_type=MESH
            )

    active, items, rest_done = [], [], []
    line_up = layers * per_layer

    def pump(times=1):
        for _ in range(times):
            for entry in list(active):
                for do in entry[1].pop(0):
                    do()
                if not entry[1]:
                    active.remove(entry)

    def open_set():
        index = len(items)
        if index >= SETS:
            old = items[index - SETS]
            while any(entry[0] is old and len(entry[1]) > 2 for entry in active):
                pump()
        return index

    def goal(l, unit):
        down, up, out, mix, rest = outs[l]
        part = width // depth
        if unit < 4:
            return down, part * unit, 0, wide
        if unit < 8:
            return up, 0, (unit - 4) * wide, min(wide, ff - (unit - 4) * wide)
        if unit == 8:
            return out, 0, 0, wide
        if unit < 12:
            return mix, 0, (unit - 9) * wide, min(wide, pad_lanes(3 * width) - (unit - 9) * wide)
        return rest, 0, 0, wide

    def launch(l, unit, source):
        index = len(items)
        s = index % SETS
        cols = pl.ds(0, goal(l, unit)[3])
        item = Granule(
            at, others, unit in LINE_FIRST, source.at[:, :, :, cols], plane_in.at[s, :, :, :, cols],
            z_in.at[s, :, :, cols], fin.at[index % FINS, :, cols], goal(l, unit),
            g_send.at[index], g_recv.at[index], g_local.at[index], g_credit.at[index],
            g_credit.at[index - SETS] if index >= SETS else None, index + SETS < line_up,
            items[index - FINS] if index >= FINS else None,
        )
        if index >= FINS:
            assert all(entry[0] is not items[index - FINS] for entry in active)
        item.begin()
        items.append(item)
        active.append([item, item.stages()])

    def weight_grad(l, unit, piece, rhs, first):
        index = open_set()
        s = index % SETS
        home = 0 if unit < 8 else 1

        def do(off, size):
            cols = pl.ds(off, size)
            right = rhs[:, :, pl.ds(pl.multiple_of(first + off, LANES), size)].reshape(2 * flat, size)
            left = piece[:, :, pl.ds(0, depth * LANES)].reshape(2 * flat, depth * LANES)
            out = over_rows(left, right).astype(BF16)
            for t in range(depth):
                acc[s, t, :, :, cols] = out[t * LANES : (t + 1) * LANES].reshape(4, LANES // 4, size)

            @pl.when(core == home)
            def _():
                last = piece[:, :, pl.ds(depth * LANES, LANES)].reshape(2 * flat, LANES)
                more = over_rows(last, right).astype(BF16)
                for t in range(depth):
                    u = unit - 8 * home
                    rest_acc[t, u // 2, pl.ds(16 * (u % 2), 16), cols] = more[t * 16 : (t + 1) * 16]

        by_tiles(wide, 384, do)
        launch(l, unit, acc.at[s])

    def rest_grad(l):
        open_set()
        launch(l, 12, rest_acc)

    def rest_rows(l):
        part = width // depth
        rest_v = gq
        copy = pltpu.make_async_copy(outs[l][4], rest_v, rest_sem.at[0])
        copy.start()
        copy.wait()
        moves = []
        for unit in range(12):
            ref, first, col, cols = goal(l, unit)
            moves.append(
                pltpu.make_async_copy(
                    rest_v.at[pl.ds(16 * unit, 16), pl.ds(0, cols)],
                    ref.at[pl.ds(first + 2 * LANES, part - 2 * LANES), pl.ds(col, cols)],
                    rest_sem.at[1 + unit],
                )
            )
        for move in moves:
            move.start()
        for move in moves:
            move.wait()

    def put_row(l, i, value):
        sm[pl.ds(l * 16 + i, 1), pl.ds(0, width)] = value

    def column_sums(l, i, src):
        put_row(l, i, jnp.sum(src[0, :, pl.ds(0, width)].astype(F32), axis=0, keepdims=True))

    def norm_back(l, i):
        gain = vecs[l, pl.ds(i, 1), pl.ds(0, width)]

        def do(step, carry):
            gain_sum, shift_sum = carry
            here = pl.ds(pl.multiple_of(step * 32, 32), 32)
            unit, scale = row_norm(hx[here, :])
            grad = dn[here, :]
            inner = grad * gain
            mean_inner = jnp.mean(inner, axis=-1, keepdims=True)
            mean_unit = jnp.mean(inner * unit, axis=-1, keepdims=True)
            g[here, :] = g[here, :] + scale * (inner - mean_inner - unit * mean_unit)
            return (
                gain_sum + jnp.sum(grad * unit, axis=0, keepdims=True),
                shift_sum + jnp.sum(grad, axis=0, keepdims=True),
            )

        zero = jnp.zeros((1, width), F32)
        gain_sum, shift_sum = lax.fori_loop(0, flat // 32, do, (zero, zero))
        put_row(l, i, gain_sum)
        put_row(l, 2 + i, shift_sum)

    def load(l, name, dst, index):
        return pltpu.make_async_copy(kept[l][name], dst, load_sem.at[index])

    def low_copy(src, dst):
        def do(first, size):
            here = pl.ds(first, size)
            dst[0, here, pl.ds(0, width)] = src[here, :].astype(BF16)

        by_tiles(flat, 64, do)

    def row_tile(whole, buf, slot, first, size, sem):
        return pltpu.make_async_copy(
            whole.at[pl.ds(first, size)], buf.at[slot, pl.ds(0, size)], sem.at[slot]
        )

    def ff_back(l):
        w_up, w_down = wholes[l][2], wholes[l][3]
        tile = 256
        count = ff // tile

        def copies(i, slot):
            first = pl.multiple_of(i * tile, tile)
            return (
                pltpu.make_async_copy(w_down.at[pl.ds(first, tile)], wt_a.at[slot], w_sem.at[0, slot]),
                pltpu.make_async_copy(w_up.at[:, pl.ds(first, tile)], wt_u.at[slot], w_sem.at[1, slot]),
            )

        dn[...] = jnp.zeros_like(dn)
        for i in range(TILES - 1):
            for copy in copies(i, i):
                copy.start()

        def step(i, carry):
            slot = lax.rem(i, TILES)
            for copy in copies(i, slot):
                copy.wait()

            @pl.when(i + TILES - 1 < count)
            def _():
                for copy in copies(i + TILES - 1, lax.rem(i + TILES - 1, TILES)):
                    copy.start()

            cols = pl.ds(pl.multiple_of(i * tile, tile), tile)
            grad = across(gm[0, :, pl.ds(0, width)], wt_a[slot])
            low = (grad * dg[:, cols].astype(F32)).astype(BF16)
            gu[0, :, cols] = low
            up_row[pl.ds(0, 1), cols] = jnp.sum(low.astype(F32), axis=0, keepdims=True)
            dn[...] = dn[...] + across(low, wt_u[slot])
            return carry

        def part(first, size):
            lax.fori_loop(first, first + size, step, 0)

        half = count // 2
        part(0, half)
        pump()
        part(half, count - half)

    def tiles_back(whole, buf, sem, left, put):
        tile = buf.shape[1]
        spans = [(i, min(tile, width - i)) for i in range(0, width, tile)]
        row_tile(whole, buf, 0, *spans[0], sem).start()
        for n, (first, size) in enumerate(spans):
            row_tile(whole, buf, n % 2, first, size, sem).wait()
            if n + 1 < len(spans):
                row_tile(whole, buf, (n + 1) % 2, *spans[n + 1], sem).start()
            put(first, size, across(left(), buf[n % 2, pl.ds(0, size)]))

    def kv_copy(l, it, slot):
        s, j = it // pairs, lax.rem(it, pairs)
        return [
            pltpu.make_async_copy(
                kept[l]["kv"].at[s, :, pl.ds(pl.multiple_of(i * wide + j * LANES, LANES), LANES)],
                kvp.at[slot, i],
                kvp_sem.at[slot, i],
            )
            for i in range(2)
        ]

    def attend_back(l, first, count):
        def step(it, carry):
            slot = lax.rem(it, 2)
            for copy in kv_copy(l, it, slot):
                copy.wait()

            @pl.when(it + 1 < total)
            def _():
                for copy in kv_copy(l, it + 1, 1 - slot):
                    copy.start()

            s, j = it // pairs, lax.rem(it, pairs)
            here = pl.ds(pl.multiple_of(s * rows, rows), rows)
            col = pl.ds(pl.multiple_of(j * LANES, LANES), LANES)
            col_v = pl.ds(pl.multiple_of(wide + j * LANES, LANES), LANES)
            q2, go_block = two_heads(q[here, col]), go[here, col]
            go2 = two_heads(go_block)
            keys, values = kvp[slot, 0], kvp[slot, 1]
            product = go_block.astype(F32) * o[here, col].astype(F32)
            delta = jnp.sum(two_heads(product), axis=-1, keepdims=True)
            lane = lax.broadcasted_iota(jnp.int32, (2 * rows, LANES), 1)
            block = lse[pl.ds(pl.multiple_of(s * 2 * rows, rows), 2 * rows), :]
            log_total = jnp.sum(jnp.where(lane == it, block, 0.0), axis=-1, keepdims=True)
            seen = bias[s]
            scores = across(q2, keys) * (HEAD_DIM ** (-0.5)) + jnp.concatenate([seen, seen], axis=0)
            probs = jnp.exp(scores - log_total)
            grads = across(go2, values)
            low = (probs * (grads - delta)).astype(BF16)
            dq = jnp.dot(low, keys, preferred_element_type=F32) * (HEAD_DIM ** (-0.5))
            gq[here, col] = one_pair(dq, rows).astype(BF16)
            dk = (over_rows(low, q2) * (HEAD_DIM ** (-0.5))).astype(BF16)
            dv = over_rows(probs.astype(BF16), go2).astype(BF16)
            for b in range(slots // rows):
                mine = lax.rem(b + core, 2)
                span = slice(b * rows, (b + 1) * rows)
                parts[s, mine, b // 2, :, col] = dk[span]
                parts[s, mine, b // 2, :, col_v] = dv[span]
            return carry

        lax.fori_loop(first, first + count, step, 0)

    loads = {}

    def early(l):
        for i, (name, dst) in enumerate((("h1", hx), ("dg", dg), ("q", q), ("o", o), ("lse", lse))):
            loads[name] = load(l, name, dst, i)
            loads[name].start()
        for kind in KINDS:
            free_kind(kind, l)
            name = exchange[kind][0][0]
            piece_load(l, name).start()
            pg_sent(name)
            pg_post(name, kept[l][name].at[1 - core])

    rest_acc[...] = jnp.zeros_like(rest_acc)
    sm[...] = jnp.zeros_like(sm)
    for buf, used in ((gm, width), (gu, ff), (ga, width), (gx, 3 * width)):
        first = used // LANES * LANES
        buf[0, :, pl.ds(first, buf.shape[2] - first)] = jnp.zeros((flat, buf.shape[2] - first), BF16)
    go[:, pl.ds(wide - LANES, LANES)] = jnp.zeros((flat, LANES), BF16)
    early(layers - 1)
    for s in range(seqs):

        def first_grad(first, size):
            here = pl.ds(s * rows + first, size)
            place = at.c8 * rows + first + lax.broadcasted_iota(jnp.int32, (size, width), 0)
            g[here, :] = jnp.where(place < lengths[s], cot[here, :].astype(F32), 0.0)

        by_tiles(rows, 32, first_grad)
    key_bias(bias, seqs, rows, slots, lengths, at.c8)

    for l in reversed(range(layers)):
        keys = [
            KeyGrads(
                at, parts.at[s], kv_sib[l].at[s], kv_stage, kv_plane.at[s], kv_send.at[l, s], kv_recv.at[l, s],
                kv_local, kv_credit.at[s], None if l == layers - 1 else l,
            )
            for s in range(seqs)
        ]
        if l < layers - 1:
            early(l)
        pg_sent("gm")
        low_copy(g, gm)
        pg_post("gm", gm.at[0])
        column_sums(l, 7, gm)
        piece_load(l, "pz").wait()
        pg_take("pz")
        pg_take("gm")
        for i in range(4):
            weight_grad(l, i, pz.at[:, i], gm, 0)
            pump()
        done_kind("down", l)
        loads["dg"].wait()
        pg_sent("gu")
        ff_back(l)
        pg_post("gu", gu.at[0])
        pump()
        for r in range(4):
            sm[pl.ds(l * 16 + 8 + r, 1), :] = up_row[pl.ds(0, 1), pl.ds(r * wide, wide)]
        loads["h1"].wait()
        norm_back(l, 1)
        loads["h"] = load(l, "h", hx, 5)
        loads["h"].start()
        pg_sent("ga")
        low_copy(g, ga)
        pg_post("ga", ga.at[0])
        column_sums(l, 6, ga)
        pump()

        def put_go(first, size, value):
            go[:, pl.ds(first, size)] = value.astype(BF16)

        tiles_back(wholes[l][1], wt_a, w_sem.at[0], lambda: ga[0, :, pl.ds(0, width)], put_go)
        for copy in kv_copy(l, 0, 0):
            copy.start()
        pump()
        piece_load(l, "pc").wait()
        pg_take("pc")
        pg_take("gu")
        for i in range(4):
            weight_grad(l, 4 + i, pc, gu, i * wide)
            pump()
        done_kind("up", l)
        piece_load(l, "po").wait()
        pg_take("po")
        pg_take("ga")
        weight_grad(l, 8, po, ga, 0)
        done_kind("out", l)
        pump()
        if l < layers - 1 and all(entry[0] is not items[per_layer * (layers - 1 - l) - 1] for entry in active):
            rest_rows(l + 1)
            rest_done.append(l + 1)
        for name in ("q", "o", "lse"):
            loads[name].wait()
        steps = []
        for s in range(seqs):
            third = pairs // 3
            pieces = [(s * pairs, third), (s * pairs + third, third), (s * pairs + 2 * third, pairs - 2 * third)]
            for piece in pieces:
                attend_back(l, *piece)
                pump()
                if steps:
                    steps.pop(0)()
            steps += [keys[s].start, keys[s].first, keys[s].relay, functools.partial(keys[s].combine, l > 0)]
            steps.pop(0)()
        while steps:
            steps.pop(0)()
            if steps:
                pump()
        pg_sent("gx")
        for s in range(seqs):

            def join(first, size):
                here, there = pl.ds(s * rows + first, size), pl.ds(first, size)
                gx[0, here, pl.ds(0, width)] = gq[here, pl.ds(0, width)]
                gx[0, here, pl.ds(width, width)] = parts[s, 0, at.p, there, pl.ds(0, width)]
                gx[0, here, pl.ds(2 * width, width)] = parts[s, 0, at.p, there, pl.ds(wide, width)]

            by_tiles(rows, 64, join)
        pg_post("gx", gx.at[0])
        for i, col in ((4, 0), (5, 2 * width)):
            put_row(l, i, jnp.sum(gx[0, :, pl.ds(col, width)].astype(F32), axis=0, keepdims=True))

        def put_dn(first, size, value):
            dn[:, pl.ds(first, size)] = value

        piece_load(l, "pa").wait()
        pg_take("pa")
        pg_take("gx")
        for i in range(3):
            weight_grad(l, 9 + i, pa, gx, i * wide)
            pump()
        done_kind("mix", l)
        rest_grad(l)
        rest_item = items[-1]
        pump()
        tiles_back(wholes[l][0], wt_q, w_sem.at[2], lambda: gx[0, :, pl.ds(0, 3 * width)], put_dn)
        loads["h"].wait()
        pump()
        norm_back(l, 0)
        for item in keys:
            item.drain()
        while l and any(entry[0] is rest_item and len(entry[1]) > 2 for entry in active):
            pump()

    def sm_copy(i, src, dst, device):
        return remote(src, dst, sm_send.at[i], sm_recv.at[i], device)

    current = sm
    for i, device in enumerate((at.sib, at.x_dev, at.y_dev)):
        copy = sm_copy(i, current, sm_in.at[i], device)
        copy.start()
        pump()
        copy.wait()
        sm_sum[i % 2] = current[...] + sm_in[i]
        current = sm_sum.at[i % 2]
    hops = []
    for i, device in enumerate(others):
        copy = sm_copy(3 + i, current, sm_z.at[i], device)
        copy.start()
        hops.append(copy)
    pump()
    for copy in hops:
        copy.wait()
    small_total = jnp.zeros(sm.shape, F32)
    for z in range(depth):
        slot = lax.rem(at.z - z - 1 + 2 * depth, depth)
        other = sm_z[jnp.minimum(slot, depth - 2)]
        small_total = small_total + jnp.where(slot == depth - 1, current[...], other)
    small_out[...] = small_total
    for l in range(layers):
        while any(entry[0] is items[(layers - l) * per_layer - 1] for entry in active):
            pump()
        if l not in rest_done:
            rest_rows(l)
    while active:
        pump()
    for item in items:
        item.drain()
    for name in list(posted):
        pg_sent(name)


def backward(cotangent, lengths, vecs, kept, wholes, layers, ff):
    seqs, rows, width = cotangent.shape
    depth = lax.axis_size("fsdp")
    slots = rows * lax.axis_size("ctx")
    flat, wide = seqs * rows, pad_lanes(width)
    per_layer = 13
    count = layers * per_layer
    dims = (layers, seqs, rows, slots, width, ff, depth, per_layer)
    any_spec = pl.BlockSpec(memory_space=pl.ANY)
    vmem = pl.BlockSpec(memory_space=pltpu.VMEM)
    struct = lambda shape, kind: jax.ShapeDtypeStruct(shape, kind)
    out_shape = [struct((flat, width), F32), struct((layers * 16, wide), F32)]
    part = width // depth
    for _ in range(layers):
        out_shape += [
            struct((4 * part, wide), BF16),
            struct((part, 4 * wide), BF16),
            struct((part, wide), BF16),
            struct((part, 3 * wide), BF16),
            struct((2 * LANES, wide), BF16),
        ]
    out_shape += [struct((seqs, 4, rows, 2 * wide), BF16) for _ in range(layers)]
    dma, regular = pltpu.SemaphoreType.DMA, pltpu.SemaphoreType.REGULAR
    low = lambda *shape: pltpu.VMEM(shape, BF16)
    full = lambda *shape: pltpu.VMEM(shape, F32)
    chunk = LANES // 4
    scratch = [
        dma((count, 24)), dma((count, 24)), dma((count,)), regular((count,)),
        dma((layers, seqs, 8)), dma((layers, seqs, 8)), dma, regular((seqs,)),
        dma((10,)), dma((10,)), dma((10,)), regular((4,)), dma((8,)), dma((8,)), dma((8,)), dma((3, TILES)), dma((2, 2)), dma((13,)),
        low(SETS, depth, 4, chunk, wide), low(SETS, 3, depth, chunk, wide), low(SETS, depth - 1, chunk, wide),
        low(depth, 4, chunk, wide), low(FINS, chunk, wide),
        full(flat, width), full(flat, width),
        low(2, flat, wide), low(2, flat, 4 * wide), low(2, flat, wide), low(2, flat, 3 * wide),
        low(2, 4, flat, PIECE), low(2, flat, PIECE), low(2, flat, PIECE), low(2, flat, PIECE),
        low(flat, ff), low(flat, wide), low(flat, wide), low(flat, wide), full(2 * flat, LANES),
        full(seqs, rows, slots), low(2, 2, slots, LANES),
        low(seqs, 2, 4, rows, 2 * wide), low(rows, 2 * wide), low(seqs, 3, rows, 2 * wide),
        low(TILES, 256, width), low(TILES, width, 256), low(2, 256, 3 * width), low(flat, wide),
        full(layers * 16, wide), full(2, layers * 16, wide), full(3, layers * 16, wide),
        full(depth - 1, layers * 16, wide), full(8, 4 * wide),
    ]
    flat_kept = [kept[l][name] for l in range(layers) for name in KEPT]
    flat_wholes = [item for layer in wholes for item in layer]
    outs = pl.pallas_call(
        functools.partial(backward_kernel, dims),
        out_shape=out_shape,
        in_specs=[vmem, pl.BlockSpec(memory_space=pltpu.SMEM), vmem]
        + [any_spec] * (len(flat_kept) + len(flat_wholes)),
        out_specs=[vmem, vmem] + [any_spec] * (len(out_shape) - 2),
        scratch_shapes=scratch,
        compiler_params=pltpu.CompilerParams(
            collective_id=1, has_side_effects=True, vmem_limit_bytes=63 * 1024 * 1024
        ),
    )(cotangent.reshape(flat, width), lengths, vecs, *flat_kept, *flat_wholes)
    grads = [outs[2 + 5 * l : 6 + 5 * l] for l in range(layers)]
    return outs[0], outs[1].reshape(layers, 16, wide), grads


def normalize(values, scales, shifts):
    average = jnp.mean(values, axis=-1, keepdims=True)
    centred = values - average
    variance = jnp.mean(centred * centred, axis=-1, keepdims=True)
    return centred * lax.rsqrt(variance + 1e-05) * scales + shifts


def outer_sum(left_rows, right_rows):
    return lax.dot_general(
        left_rows, right_rows, (((0,), (0,)), ((), ())), preferred_element_type=jnp.float32
    )


def times_transpose(left_rows, weight_rows):
    return lax.dot_general(
        left_rows, weight_rows, (((1,), (1,)), ((), ())), preferred_element_type=jnp.float32
    )


def allowed_mask(positions, key_places, lengths):
    causal = (key_places[None, :] <= positions[:, None]) & (key_places[None, :] >= 0)
    inside = key_places[None, :] < lengths[:, None]
    return causal[None, None, :, :] & inside[:, None, None, :]


def attend_forward(queries, key_part, value_part, positions, lengths, score_scale):
    seq_count, row_count, head_count, head_width = queries.shape
    lowest = jnp.full((seq_count, head_count, row_count), -1e30, jnp.float32)
    key_places = jnp.arange(key_part.shape[1], dtype=jnp.int32)
    allowed = allowed_mask(positions, key_places, lengths)
    scores = (
        jnp.einsum("sqhe,skhe->shqk", queries, key_part, preferred_element_type=jnp.float32)
        * score_scale
    )
    scores = jnp.where(allowed, scores, -1e30)
    new_top = jnp.maximum(lowest, jnp.max(scores, axis=-1))
    exp_weights = jnp.where(allowed, jnp.exp(scores - new_top[..., None]), 0.0)
    running_total = jnp.sum(exp_weights, axis=-1)
    running_sum = jnp.einsum(
        "shqk,skhe->shqe",
        exp_weights.astype(jnp.bfloat16),
        value_part,
        preferred_element_type=jnp.float32,
    )
    output = jnp.transpose(running_sum / running_total[..., None], (0, 2, 1, 3))
    return (output, new_top + jnp.log(running_total))


def block_terms(
    queries,
    grad_out,
    log_total,
    delta_row,
    key_part,
    value_part,
    first_key,
    positions,
    lengths,
    score_scale,
):
    key_places = first_key + jnp.arange(key_part.shape[1], dtype=jnp.int32)
    allowed = allowed_mask(positions, key_places, lengths)
    scores = (
        jnp.einsum("sqhe,skhe->shqk", queries, key_part, preferred_element_type=jnp.float32)
        * score_scale
    )
    scores = jnp.where(allowed, scores, -1e30)
    probability = jnp.where(allowed, jnp.exp(scores - log_total[..., None]), 0.0)
    grad_probs = jnp.einsum(
        "sqhe,skhe->shqk", grad_out, value_part, preferred_element_type=jnp.float32
    )
    grad_scores = (probability * (grad_probs - delta_row[..., None])).astype(jnp.bfloat16)
    query_add = (
        jnp.einsum("shqk,skhe->sqhe", grad_scores, key_part, preferred_element_type=jnp.float32)
        * score_scale
    )
    key_add = (
        jnp.einsum("shqk,sqhe->skhe", grad_scores, queries, preferred_element_type=jnp.float32)
        * score_scale
    )
    value_add = jnp.einsum(
        "shqk,sqhe->skhe",
        probability.astype(jnp.bfloat16),
        grad_out,
        preferred_element_type=jnp.float32,
    )
    return (query_add, key_add, value_add)


def pack_small(ln_gain, ln_bias, b_qv, b_out, b_up, b_down):
    layers, _, part = ln_gain.shape
    return jnp.concatenate(
        [ln_gain, ln_bias, b_qv, b_out[:, None], b_down[:, None], b_up.reshape(layers, 4, part)],
        axis=1,
    )


def unpack_small(whole):
    depth, _, part = whole.shape
    flat = jnp.transpose(whole[:, :8], (1, 0, 2)).reshape(8, depth * part)
    up_bias = whole[:, 8:].reshape(depth * 4 * part)
    return flat[0:2], flat[2:4], flat[4:6], flat[6], flat[7], up_bias


def small_rows(gains, shifts, mix_bias, out_bias, down_bias, up_bias, depth):
    width = gains.shape[-1]
    flat = jnp.concatenate([gains, shifts, mix_bias, out_bias[None], down_bias[None]], axis=0)
    flat = jnp.transpose(flat.reshape(8, depth, width // depth), (1, 0, 2))
    return jnp.concatenate([flat, up_bias.reshape(depth, 4, width // depth)], axis=1)


def fast_mesh(rows):
    return lax.axis_size("ctx") == 8 and rows % 272 == 0


def gather_all(weights, small):
    flat = [item for layer in weights for item in layer]
    layers = len(weights)
    wholes = [lax.all_gather(item, "fsdp", axis=0, tiled=True) for item in flat]
    small_all = lax.all_gather(small, "fsdp", axis=0)
    return [wholes[4 * i : 4 * i + 4] for i in range(layers)], [small_all[:, i] for i in range(layers)]


def reduce_layer(grads):
    shards_now = [
        lax.psum_scatter(item, "fsdp", scatter_dimension=0, tiled=True) for item in grads
    ]
    return [lax.psum(item, "ctx") for item in shards_now]


def shards(
    tokens,
    lengths,
    cotangent,
    ln_gain,
    ln_bias,
    w_qkv,
    b_qv,
    w_out,
    b_out,
    w_up,
    b_up,
    w_down,
    b_down,
):
    seq_count, row_count, model_width = tokens.shape
    head_width = HEAD_DIM
    head_count = model_width // head_width
    score_scale = head_width ** (-0.5)
    ctx_index = lax.axis_index("ctx")
    depth = lax.axis_size("fsdp")
    positions = ctx_index * row_count + jnp.arange(row_count, dtype=jnp.int32)
    valid_rows = (positions[None, :] < lengths[:, None]).astype(jnp.float32)[..., None]
    flat_rows = seq_count * row_count
    split_shape = (seq_count, row_count, head_count, head_width)
    layer_total = ln_gain.shape[0]
    hidden = tokens.astype(jnp.float32).reshape(flat_rows, model_width)
    small = pack_small(ln_gain, ln_bias, b_qv, b_out, b_up, b_down)
    if fast_mesh(w_qkv.shape[1]):
        part = small.shape[2]
        ff = w_up.shape[2]
        padded = jnp.pad(small, ((0, 0), (0, 4), (0, pad_lanes(part) - part)))
        activations, vectors, weights, kept = forward(
            tokens, lengths, w_qkv, w_out, w_up, w_down, padded.reshape(layer_total * 16, -1)
        )
        grad_in, small_sums, sums = backward(
            cotangent, lengths, vectors, kept, weights, layer_total, ff
        )
        mine = lambda rows: lax.dynamic_slice_in_dim(
            rows[..., :model_width], lax.axis_index("fsdp") * part, part, axis=rows.ndim - 1
        )
        up_bias = small_sums[:, 8:12].reshape(layer_total, -1)[:, :ff]
        up_part = ff // depth
        whole = lambda member, cols: jnp.stack(
            [item[member][:, :cols].astype(jnp.float32) for item in sums]
        )
        return (
            activations.reshape(tokens.shape),
            grad_in.reshape(tokens.shape),
            mine(small_sums[:, 0:2]),
            mine(small_sums[:, 2:4]),
            whole(3, 3 * model_width),
            mine(small_sums[:, 4:6]),
            whole(2, model_width),
            mine(small_sums[:, 6]),
            whole(1, ff),
            lax.dynamic_slice_in_dim(up_bias, lax.axis_index("fsdp") * up_part, up_part, axis=1),
            whole(0, model_width),
            mine(small_sums[:, 7]),
        )
    weights, smalls = gather_all(
        [(w_qkv[i], w_out[i], w_up[i], w_down[i]) for i in range(layer_total)], small
    )
    kept_layers = []
    for layer_index in range(layer_total):
        mix_weight, out_weight, up_weight, down_weight = weights[layer_index]
        gain_rows, shift_rows, mix_bias, out_bias, down_bias, up_bias = unpack_small(
            smalls[layer_index].astype(jnp.float32)
        )
        normed_first = normalize(hidden, gain_rows[0], shift_rows[0]).astype(jnp.bfloat16)
        mixed_rows = jnp.dot(normed_first, mix_weight, preferred_element_type=jnp.float32)
        queries = (
            (mixed_rows[:, :model_width] + mix_bias[0]).astype(jnp.bfloat16).reshape(split_shape)
        )
        key_rows = (
            mixed_rows[:, model_width : 2 * model_width].astype(jnp.bfloat16).reshape(split_shape)
        )
        value_rows = (
            (mixed_rows[:, 2 * model_width :] + mix_bias[1])
            .astype(jnp.bfloat16)
            .reshape(split_shape)
        )
        key_part = lax.all_gather(key_rows, "ctx", axis=1, tiled=True)
        value_part = lax.all_gather(value_rows, "ctx", axis=1, tiled=True)
        output, log_total = attend_forward(
            queries, key_part, value_part, positions, lengths, score_scale
        )
        output = output.reshape(flat_rows, model_width)
        attended = output.astype(jnp.bfloat16)
        middle = (
            hidden + jnp.dot(attended, out_weight, preferred_element_type=jnp.float32) + out_bias
        )
        normed_second = normalize(middle, gain_rows[1], shift_rows[1]).astype(jnp.bfloat16)
        upper_pre = (
            jnp.dot(normed_second, up_weight, preferred_element_type=jnp.float32) + up_bias
        )
        active = jax.nn.gelu(upper_pre).astype(jnp.bfloat16)
        kept_layers.append(
            (
                hidden,
                normed_first,
                queries,
                key_part,
                value_part,
                output,
                log_total,
                attended,
                middle,
                normed_second,
                upper_pre,
                active,
                gain_rows,
                shift_rows,
            )
        )
        hidden = (
            middle + jnp.dot(active, down_weight, preferred_element_type=jnp.float32) + down_bias
        )
    activations = (valid_rows * hidden.reshape(seq_count, row_count, model_width)).astype(
        jnp.bfloat16
    )
    grad_hidden = (cotangent.astype(jnp.float32) * valid_rows).reshape(flat_rows, model_width)
    big_grads = [None] * layer_total
    small_grads = [None] * layer_total
    for layer_index in reversed(range(layer_total)):
        (
            hidden_in,
            normed_first,
            queries,
            key_part,
            value_part,
            output,
            log_total,
            attended,
            middle,
            normed_second,
            upper_pre,
            active,
            gain_rows,
            shift_rows,
        ) = kept_layers[layer_index]
        mix_weight, out_weight, up_weight, down_weight = weights[layer_index]
        grad_branch = grad_hidden.astype(jnp.bfloat16)
        down_bias_grad = jnp.sum(grad_branch.astype(jnp.float32), axis=0)
        down_grad = outer_sum(active, grad_branch)
        grad_active = times_transpose(grad_branch, down_weight)
        unused_gelu, gelu_pull = jax.vjp(jax.nn.gelu, upper_pre)
        grad_upper = gelu_pull(grad_active)[0].astype(jnp.bfloat16)
        up_bias_grad = jnp.sum(grad_upper.astype(jnp.float32), axis=0)
        up_grad = outer_sum(normed_second, grad_upper)
        grad_normed = times_transpose(grad_upper, up_weight)
        unused_norm, norm_pull = jax.vjp(normalize, middle, gain_rows[1], shift_rows[1])
        grad_middle, gain_second, shift_second = norm_pull(grad_normed)
        grad_middle = grad_middle + grad_hidden
        grad_attn = grad_middle.astype(jnp.bfloat16)
        out_bias_grad = jnp.sum(grad_attn.astype(jnp.float32), axis=0)
        out_grad = outer_sum(attended, grad_attn)
        grad_output = times_transpose(grad_attn, out_weight).astype(jnp.bfloat16)
        delta_row = jnp.transpose(
            jnp.sum((grad_output.astype(jnp.float32) * output).reshape(split_shape), axis=-1),
            (0, 2, 1),
        )
        grad_heads = grad_output.reshape(split_shape)
        query_grad, key_add, value_add = block_terms(
            queries,
            grad_heads,
            log_total,
            delta_row,
            key_part,
            value_part,
            0,
            positions,
            lengths,
            score_scale,
        )
        key_low = lax.psum_scatter(
            key_add.astype(jnp.bfloat16), "ctx", scatter_dimension=1, tiled=True
        ).reshape(flat_rows, model_width)
        value_low = lax.psum_scatter(
            value_add.astype(jnp.bfloat16), "ctx", scatter_dimension=1, tiled=True
        ).reshape(flat_rows, model_width)
        query_low = query_grad.reshape(flat_rows, model_width).astype(jnp.bfloat16)
        grad_mixed = jnp.concatenate([query_low, key_low, value_low], axis=1)
        mix_bias_grad = jnp.stack(
            [
                jnp.sum(query_low.astype(jnp.float32), axis=0),
                jnp.sum(value_low.astype(jnp.float32), axis=0),
            ]
        )
        mix_grad = outer_sum(normed_first, grad_mixed)
        grad_normed_first = times_transpose(grad_mixed, mix_weight)
        unused_first, first_pull = jax.vjp(normalize, hidden_in, gain_rows[0], shift_rows[0])
        grad_input, gain_first, shift_first = first_pull(grad_normed_first)
        grad_hidden = grad_input + grad_middle
        big_grads[layer_index] = reduce_layer(
            [item.astype(jnp.bfloat16) for item in (up_grad, down_grad, mix_grad, out_grad)]
        )
        small_grads[layer_index] = small_rows(
            jnp.stack([gain_first, gain_second]),
            jnp.stack([shift_first, shift_second]),
            mix_bias_grad,
            out_bias_grad,
            down_bias_grad,
            up_bias_grad,
            depth,
        )
    input_grad = grad_hidden.reshape(seq_count, row_count, model_width)
    packed = jnp.stack(small_grads).astype(jnp.bfloat16)
    total = lax.psum(packed, ("fsdp", "ctx"))
    own = lax.dynamic_index_in_dim(total, lax.axis_index("fsdp"), 1, keepdims=False)
    own = own.astype(jnp.float32)

    def whole(member):
        return jnp.stack([big_grads[i][member].astype(jnp.float32) for i in range(layer_total)])

    return (
        activations,
        input_grad,
        own[:, 0:2],
        own[:, 2:4],
        whole(2),
        own[:, 4:6],
        whole(3),
        own[:, 6],
        whole(0),
        own[:, 8:].reshape(layer_total, -1),
        whole(1),
        own[:, 7],
    )


def solution(mesh):
    placed = (
        P("fsdp", "ctx", None),
        P("fsdp"),
        P("fsdp", "ctx", None),
        P(None, None, "fsdp"),
        P(None, None, "fsdp"),
        P(None, "fsdp", None),
        P(None, None, "fsdp"),
        P(None, "fsdp", None),
        P(None, "fsdp"),
        P(None, "fsdp", None),
        P(None, "fsdp"),
        P(None, "fsdp", None),
        P(None, "fsdp"),
    )
    return jax.shard_map(
        shards,
        mesh=mesh,
        in_specs=placed,
        out_specs=(
            P("fsdp", "ctx", None),
            P("fsdp", "ctx", None),
            P(None, None, "fsdp"),
            P(None, None, "fsdp"),
            P(None, "fsdp", None),
            P(None, None, "fsdp"),
            P(None, "fsdp", None),
            P(None, "fsdp"),
            P(None, "fsdp", None),
            P(None, "fsdp"),
            P(None, "fsdp", None),
            P(None, "fsdp"),
        ),
        check_vma=False,
    )
```

```python
import functools

import jax
import jax.numpy as jnp
from jax import lax
from jax.experimental import pallas as pl
from jax.experimental.pallas import tpu as pltpu
from jax.sharding import PartitionSpec as P

MESH = pl.DeviceIdType.MESH


class Place:
    def __init__(self):
        self.depth = lax.axis_size("fsdp")
        self.z = lax.axis_index("fsdp")
        self.c8 = lax.axis_index("ctx")
        self.core = lax.rem(self.c8, 2)
        self.p = self.c8 // 2
        self.px = lax.rem(self.p, 2)
        self.py = self.p // 2
        self.sib = {"ctx": self.c8 + 1 - 2 * self.core}
        self.x_dev = {"ctx": self.c8 + 2 - 4 * self.px}
        self.y_dev = {"ctx": self.c8 + 4 - 8 * self.py}
        self.p_x = self.p + 1 - 2 * self.px
        self.p_y = self.p + 2 - 4 * self.py
        self.p_d = 3 - self.p
        self.relay_from = self.p + (1 - self.core) * (1 - 2 * self.px) + self.core * (2 - 4 * self.py)
        self.relay_dev = {
            "ctx": self.c8 + (1 - self.core) * (4 - 8 * self.py) + self.core * (2 - 4 * self.px)
        }

    def up(self):
        return {"fsdp": self.z + 1}

    def down(self):
        return {"fsdp": self.z - 1}

    def greet(self):
        barrier = pltpu.get_barrier_semaphore()
        for device in (self.sib, self.x_dev, self.y_dev):
            pl.semaphore_signal(barrier, inc=1, device_id=device, device_id_type=MESH)

        @pl.when(self.z > 0)
        def _():
            pl.semaphore_signal(barrier, inc=1, device_id=self.down(), device_id_type=MESH)

        @pl.when(self.z < self.depth - 1)
        def _():
            pl.semaphore_signal(barrier, inc=1, device_id=self.up(), device_id_type=MESH)

        below = jnp.where(self.z > 0, 1, 0)
        above = jnp.where(self.z < self.depth - 1, 1, 0)
        pl.semaphore_wait(barrier, 3 + below + above)


def remote(src, dst, send_sem, recv_sem, device):
    return pltpu.make_async_remote_copy(
        src_ref=src, dst_ref=dst, send_sem=send_sem, recv_sem=recv_sem, device_id=device, device_id_type=MESH
    )


class Gather:
    def __init__(self, at, own, whole, left_core, send, recv, line=0):
        self.at, self.own, self.whole = at, own, whole
        self.send, self.recv = send, recv
        rows = own.shape[0]
        self.rows = rows
        unit = rows // 17
        self.block = 8 * unit
        self.t1 = 2 * unit - line
        self.line = pl.ds(pl.multiple_of(at.core * self.block + 4 * self.t1, 16), 4 * line) if line else None
        self.rest = pl.ds(16 * unit, unit)
        self.has_rest = at.core == left_core

    def t1_rows(self, p, core=None):
        core = self.at.core if core is None else core
        return pl.ds(pl.multiple_of(core * self.block + p * self.t1, 16), self.t1)

    def block_rows(self, core):
        return pl.ds(pl.multiple_of(core * self.block, 16), self.block)

    def copy(self, kind, shard, rows, device, src=None, second=False):
        depth = self.at.depth
        slot = kind * depth + shard
        place = self.place(shard, rows)
        src = place if src is None else src
        send = self.send.at[(8 * depth + kind) if second else slot]
        return remote(src, place, send, self.recv.at[slot], device)

    def place(self, shard, rows):
        first = pl.multiple_of(shard * self.rows + rows.start, 16)
        return self.whole.at[pl.ds(first, rows.size)]

    def start(self):
        at = self.at
        mine = self.t1_rows(at.p)

        @pl.when(at.z < at.depth - 1)
        def _():
            self.copy(0, at.z, mine, at.up(), self.own.at[mine]).start()
            if self.line:
                self.copy(7, at.z, self.line, at.up(), self.own.at[self.line]).start()

            @pl.when(self.has_rest)
            def _():
                self.copy(1, at.z, self.rest, at.up(), self.own.at[self.rest]).start()

        @pl.when(at.z > 0)
        def _():
            self.copy(0, at.z, mine, at.down(), self.own.at[mine], True).start()
            if self.line:
                self.copy(7, at.z, self.line, at.down(), self.own.at[self.line], True).start()

            @pl.when(self.has_rest)
            def _():
                self.copy(1, at.z, self.rest, at.down(), self.own.at[self.rest], True).start()

    def cases(self, step, do):
        at = self.at

        @pl.when(at.z - 1 - step >= 0)
        def _():
            do(at.z - 1 - step, at.z < at.depth - 1, at.up())

        @pl.when(at.z + 1 + step < at.depth)
        def _():
            do(at.z + 1 + step, at.z > 0, at.down())

    def arrive(self, step):
        at = self.at
        mine = self.t1_rows(at.p)

        def do(shard, onward, device):
            self.copy(0, shard, mine, at.sib).wait_recv()

            @pl.when(onward)
            def _():
                self.copy(0, shard, mine, device).start()

            self.copy(2, shard, mine, at.x_dev).start()
            self.copy(3, shard, mine, at.y_dev).start()
            if self.line:
                self.copy(7, shard, self.line, at.sib).wait_recv()

                @pl.when(onward)
                def _():
                    self.copy(7, shard, self.line, device).start()

            @pl.when(self.has_rest)
            def _():
                self.copy(1, shard, self.rest, at.sib).wait_recv()

                @pl.when(onward)
                def _():
                    self.copy(1, shard, self.rest, device).start()

                self.copy(5, shard, self.rest, at.sib).start()

        self.cases(step, do)

    def plane(self, step):
        at = self.at

        def do(shard, onward, device):
            self.copy(2, shard, self.t1_rows(at.p_x), at.sib).wait_recv()
            self.copy(3, shard, self.t1_rows(at.p_y), at.sib).wait_recv()
            self.copy(4, shard, self.t1_rows(at.relay_from), at.relay_dev).start()

        self.cases(step, do)

    def share(self, step):
        at = self.at

        def do(shard, onward, device):
            self.copy(4, shard, self.t1_rows(at.p_d), at.sib).wait_recv()
            self.copy(6, shard, self.block_rows(at.core), at.sib).start()

        self.cases(step, do)

    def finish(self, step, then):
        at = self.at

        def do(shard, onward, device):
            self.copy(6, shard, self.block_rows(1 - at.core), at.sib).wait_recv()

            @pl.when(jnp.logical_not(self.has_rest))
            def _():
                self.copy(5, shard, self.rest, at.sib).wait_recv()

            then(shard)

        self.cases(step, do)

    def drain(self):
        at = self.at
        mine = self.t1_rows(at.p)

        @pl.when(at.z < at.depth - 1)
        def _():
            self.copy(0, at.z, mine, at.up(), self.own.at[mine]).wait_send()
            if self.line:
                self.copy(7, at.z, self.line, at.up(), self.own.at[self.line]).wait_send()

            @pl.when(self.has_rest)
            def _():
                self.copy(1, at.z, self.rest, at.up(), self.own.at[self.rest]).wait_send()

        @pl.when(at.z > 0)
        def _():
            self.copy(0, at.z, mine, at.down(), self.own.at[mine], True).wait_send()
            if self.line:
                self.copy(7, at.z, self.line, at.down(), self.own.at[self.line], True).wait_send()

            @pl.when(self.has_rest)
            def _():
                self.copy(1, at.z, self.rest, at.down(), self.own.at[self.rest], True).wait_send()

        def do(shard, onward, device):
            @pl.when(onward)
            def _():
                self.copy(0, shard, mine, device).wait_send()
                if self.line:
                    self.copy(7, shard, self.line, device).wait_send()

                @pl.when(self.has_rest)
                def _():
                    self.copy(1, shard, self.rest, device).wait_send()

            self.copy(2, shard, mine, at.x_dev).wait_send()
            self.copy(3, shard, mine, at.y_dev).wait_send()
            self.copy(4, shard, self.t1_rows(at.relay_from), at.relay_dev).wait_send()
            self.copy(6, shard, self.block_rows(at.core), at.sib).wait_send()

            @pl.when(self.has_rest)
            def _():
                self.copy(5, shard, self.rest, at.sib).wait_send()

        for step in range(at.depth - 1):
            self.cases(step, do)


def both(*conds):
    conds = [c for c in conds if c is not None]
    if not conds:
        return None
    total = conds[0]
    for c in conds[1:]:
        total = jnp.logical_and(total, c)
    return total


def under(cond, do):
    if cond is None:
        do()
    else:
        pl.when(cond)(do)


def add_rows(acc, extra, rows):
    def step(i, carry):
        piece = pl.ds(pl.multiple_of(i * 16, 16), 16)
        acc[piece, :] = acc[piece, :] + extra[piece, :]
        return carry

    lax.fori_loop(0, rows // 16, step, 0)


def add_rows_two(acc, one, two, rows):
    def step(i, carry):
        piece = pl.ds(pl.multiple_of(i * 16, 16), 16)
        total = acc[piece, :].astype(jnp.float32) + one[piece, :].astype(jnp.float32)
        acc[piece, :] = (total + two[piece, :].astype(jnp.float32)).astype(jnp.bfloat16)
        return carry

    lax.fori_loop(0, rows // 16, step, 0)


HEAD_DIM = 64
LANES = 128
F32, BF16 = jnp.float32, jnp.bfloat16


def pad_lanes(n):
    return (n + LANES - 1) // LANES * LANES


def by_tiles(total, tile, do):
    count = total // tile

    def step(i, carry):
        do(pl.multiple_of(i * tile, tile), tile)
        return carry

    if count:
        lax.fori_loop(0, count, step, 0)
    if total % tile:
        do(count * tile, total % tile)


def row_norm(values):
    average = jnp.mean(values, axis=-1, keepdims=True)
    centred = values - average
    variance = jnp.mean(centred * centred, axis=-1, keepdims=True)
    scale = lax.rsqrt(variance + 1e-05)
    return centred * scale, scale


GELU_A = 0.7978845608028654
GELU_B = 0.044715


def gelu_both(u):
    square = u * u
    bent = jnp.tanh(GELU_A * (u + GELU_B * u * square))
    half = 0.5 * (1.0 + bent)
    slope = half + 0.5 * u * (1.0 - bent * bent) * (GELU_A * (1.0 + 3.0 * GELU_B * square))
    return u * half, slope


def cut_pieces(src, dst, part, first):
    depth = 4

    def do(off, size):
        here = pl.ds(off, size)
        left = []
        for t in range(depth):
            start = (first + t * (src.shape[1] // part // depth)) * part
            block = src[here, pl.ds(start, part)]
            for core in range(2):
                dst[core, here, pl.ds(t * LANES, LANES)] = block[:, core * LANES : (core + 1) * LANES]
            left.append(block[:, 2 * LANES :])
        rest = jnp.concatenate(left + [jnp.zeros_like(left[0])] * 4, axis=1)
        for core in range(2):
            dst[core, here, pl.ds(depth * LANES, LANES)] = rest

    by_tiles(src.shape[0], 64, do)


class Context:
    def __init__(self, at, own, whole, rows, send, recv, local):
        self.at, self.own, self.whole, self.rows = at, own, whole, rows
        self.send, self.recv, self.local = send, recv, local
        core, p = at.core, at.p
        self.names, self.posts = {}, []

    def place(self, p, core):
        return self.whole.at[pl.ds(pl.multiple_of((2 * p + core) * self.rows, 16), self.rows)]

    def make(self, name, src, dst, device):
        i = self.names.setdefault(name, len(self.names))
        return remote(src, dst, self.send.at[i], self.recv.at[i], device)

    def post(self, name, src, dst, device):
        self.make(name, src, dst, device).start()
        self.posts.append((name, src, dst, device))

    def take(self, name, dst):
        self.make(name, dst, dst, self.at.sib).wait_recv()

    def start(self):
        at = self.at
        here = self.place(at.p, at.core)
        self.post("x", self.own, here, at.x_dev)
        self.post("y", self.own, here, at.y_dev)
        self.post("s", self.own, here, at.sib)
        self.keep = pltpu.make_async_copy(self.own, here, self.local)
        self.keep.start()

    def relay(self):
        at = self.at
        for name, p in (("x", at.p_x), ("y", at.p_y)):
            self.take(name, self.place(p, at.core))
        here = self.place(at.relay_from, at.core)
        self.post("d", here, here, at.relay_dev)
        for name, p in (("x", at.p_x), ("y", at.p_y)):
            here = self.place(p, at.core)
            self.post(name + "s", here, here, at.sib)

    def last(self):
        at = self.at
        here = self.place(at.p_d, at.core)
        self.take("d", here)
        self.post("ds", here, here, at.sib)

    def finish(self):
        at = self.at
        for name, p in (("s", at.p), ("xs", at.p_x), ("ys", at.p_y), ("ds", at.p_d)):
            self.take(name, self.place(p, 1 - at.core))
        self.keep.wait()

    def drain(self, own):
        for name, src, dst, device in self.posts:
            if (name in ("x", "y", "s")) == own:
                self.make(name, src, dst, device).wait_send()


KEPT = ("h", "pa", "q", "kv", "o", "po", "lse", "h1", "pc", "pz", "dg")
PIECE = 5 * LANES
LINE_ROWS = (0, 0, 16, 0)
SHARE_LAG, FINISH_LAG = 0, 1
TICKS = (2, 2, 2, 2)


def kept_shapes(seqs, slots, rows, width, ff):
    wide = pad_lanes(width)
    flat = seqs * rows
    return {
        "h": ((flat, width), F32),
        "pa": ((2, flat, PIECE), BF16),
        "q": ((flat, wide), BF16),
        "kv": ((seqs, slots, 2 * wide), BF16),
        "o": ((flat, wide), BF16),
        "po": ((2, flat, PIECE), BF16),
        "lse": ((flat * 2, LANES), F32),
        "h1": ((flat, width), F32),
        "pc": ((2, flat, PIECE), BF16),
        "pz": ((2, 4, flat, PIECE), BF16),
        "dg": ((flat, ff), BF16),
    }


def key_bias(out, seqs, rows, slots, lengths, ctx):
    for s in range(seqs):
        key = lax.broadcasted_iota(jnp.int32, (rows, slots), 1)
        row = ctx * rows + lax.broadcasted_iota(jnp.int32, (rows, slots), 0)
        seen = jnp.logical_and(key <= row, key < lengths[s])
        out[s] = jnp.where(seen, 0.0, -1e30)


def two_heads(block):
    lane = lax.broadcasted_iota(jnp.int32, block.shape, 1)
    zero = jnp.zeros_like(block)
    return jnp.concatenate(
        [jnp.where(lane < HEAD_DIM, block, zero), jnp.where(lane < HEAD_DIM, zero, block)], axis=0
    )


def one_pair(stacked, rows):
    lane = lax.broadcasted_iota(jnp.int32, (rows, LANES), 1)
    return jnp.where(lane < HEAD_DIM, stacked[:rows], stacked[rows:])


def across(a, b):
    return lax.dot_general(a, b, (((1,), (1,)), ((), ())), preferred_element_type=F32)


def attend(s, first, count, q_ref, kv_ref, bias_ref, o_ref, lse_ref, rows, pairs, wide):
    def step(i, carry):
        j = first + i
        col = pl.ds(pl.multiple_of(j * LANES, LANES), LANES)
        q2 = two_heads(q_ref[pl.ds(s * rows, rows), col])
        keys = kv_ref[s, :, col]
        values = kv_ref[s, :, pl.ds(pl.multiple_of(wide + j * LANES, LANES), LANES)]
        bias = bias_ref[s]
        scores = across(q2, keys) * (HEAD_DIM ** (-0.5))
        scores = scores + jnp.concatenate([bias, bias], axis=0)
        top = jnp.max(scores, axis=-1, keepdims=True)
        weights = jnp.exp(scores - top)
        total = jnp.sum(weights, axis=-1, keepdims=True)
        out = jnp.dot(weights.astype(BF16), values, preferred_element_type=F32) / total
        o_ref[pl.ds(s * rows, rows), col] = one_pair(out, rows).astype(BF16)
        mine = s * pairs + j
        here = pl.ds(s * 2 * rows, 2 * rows)
        lane = lax.broadcasted_iota(jnp.int32, (2 * rows, LANES), 1)
        lse_ref[here, :] = jnp.where(lane == mine, top + jnp.log(total), lse_ref[here, :])
        return carry

    lax.fori_loop(0, count, step, 0)


def forward_kernel(dims, *refs):
    layers, seqs, rows, slots, width, ff, depth = dims
    flat, wide = seqs * rows, pad_lanes(width)
    pairs = wide // LANES
    part = width // depth
    refs = list(refs)

    def grab(n):
        out = refs[:n]
        del refs[:n]
        return out

    tokens, lengths, w_qkv, w_out, w_up, w_down, small = grab(7)
    acts, vecs = grab(2)
    wholes = grab(4 * layers)
    kept = [dict(zip(KEPT, grab(len(KEPT)))) for _ in range(layers)]
    (send, recv, small_send, small_recv, kv_send, kv_recv, load_sem, keep_sem, stage_sem) = grab(9)
    (small_all, vec, up_bias, h, a, q, own_kv, kv, bias, o, lse, h1, c, u, z, dg, pa, pc, po, pz) = grab(20)
    w_bufs = grab(4)
    at = Place()
    at.greet()

    owns = [ref.at[l] for l in range(layers) for ref in (w_qkv, w_out, w_up, w_down)]
    items = [Gather(at, owns[k], wholes[k], k % 2, send.at[k], recv.at[k], LINE_ROWS[k % 4]) for k in range(4 * layers)]
    contexts = [
        [
            Context(
                at, own_kv.at[s], kept[l]["kv"].at[s], rows, kv_send.at[l, s], kv_recv.at[l, s],
                keep_sem.at[l, len(KEPT) + s],
            )
            for s in range(seqs)
        ]
        for l in range(layers)
    ]
    pending = {}

    def keep(l, name, src):
        copy = pltpu.make_async_copy(src, kept[l][name], keep_sem.at[l, KEPT.index(name)])
        copy.start()
        pending[(l, name)] = copy

    def free(l, name):
        copy = pending.pop((l, name), None)
        if copy is not None:
            copy.wait()

    def buffer(k):
        return w_bufs[k % 4]

    def own_copy(k, load):
        r = owns[k].shape[0]
        shard = lax.rem(at.z + k // 4, depth)
        place = buffer(k).at[pl.ds(pl.multiple_of(shard * r, 16), r)]
        if load:
            return pltpu.make_async_copy(owns[k], place, stage_sem.at[0, k])
        return pltpu.make_async_copy(place, items[k].place(at.z, pl.ds(0, r)), stage_sem.at[1, k])

    def own_load(k):
        own_copy(k, True).start()

    def own_store(k):
        own_copy(k, True).wait()
        own_copy(k, False).start()

    def own_done(k):
        own_copy(k, False).wait()

    def fetch_copy(k, shard):
        r = owns[k].shape[0]
        here = pl.ds(pl.multiple_of(shard * r, 16), r)
        return pltpu.make_async_copy(wholes[k].at[here], buffer(k).at[here], load_sem.at[k, shard])

    def fetch(k, shard):
        fetch_copy(k, shard).start()

    def ready(k):
        for shard in range(depth):
            fetch_copy(k, shard).wait()

    def small_copy(shard, device, src=None, second=False):
        return remote(
            small_all.at[shard] if src is None else src,
            small_all.at[shard],
            small_send.at[depth if second else shard],
            small_recv.at[shard],
            device,
        )

    def small_start():
        @pl.when(at.z < depth - 1)
        def _():
            small_copy(at.z, at.up(), small).start()

        @pl.when(at.z > 0)
        def _():
            small_copy(at.z, at.down(), small, True).start()

        pltpu.make_async_copy(small, small_all.at[at.z], stage_sem.at[2, 0]).start()

    def small_take():
        def do(shard, onward, device):
            small_copy(shard, at.sib).wait_recv()
            pl.when(onward)(lambda: small_copy(shard, device).start())

        for step in range(depth - 1):
            items[0].cases(step, do)
        pltpu.make_async_copy(small, small_all.at[at.z], stage_sem.at[2, 0]).wait()

    def small_drain():
        @pl.when(at.z < depth - 1)
        def _():
            small_copy(at.z, at.up(), small).wait_send()

        @pl.when(at.z > 0)
        def _():
            small_copy(at.z, at.down(), small, True).wait_send()

        def do(shard, onward, device):
            pl.when(onward)(lambda: small_copy(shard, device).wait_send())

        for step in range(depth - 1):
            items[0].cases(step, do)

    def small_spread():
        part = width // depth
        per_layer = small_all.shape[1] // layers
        total = jnp.zeros((small_all.shape[1], wide), F32)
        room = jnp.zeros((small_all.shape[1], wide - small_all.shape[2]), F32)
        pieces = [small_all[i].astype(F32) for i in range(depth)]
        for i in range(depth):
            piece = jnp.concatenate([pieces[i], room], axis=1)
            total = total + (pltpu.roll(piece, i * part, 1) if i else piece)
        for l in range(layers):
            vec[l] = total[l * per_layer : l * per_layer + 8]
            vecs[l] = total[l * per_layer : l * per_layer + 8]
            wide_up = jnp.zeros((1, ff), F32)
            up_room = jnp.zeros((1, ff - small_all.shape[2]), F32)
            for i in range(depth):
                for r in range(4):
                    at_row = l * per_layer + 8 + r
                    piece = jnp.concatenate([pieces[i][at_row : at_row + 1], up_room], axis=1)
                    shift = (i * 4 + r) * part
                    wide_up = wide_up + (pltpu.roll(piece, shift, 1) if shift else piece)
            up_bias[l] = jnp.broadcast_to(wide_up, (8, ff))

    def row(l, i):
        return vec[l, pl.ds(i, 1), pl.ds(0, width)]

    def norm(l, i, src, dst):
        def do(first, size):
            here = pl.ds(first, size)
            unit, _ = row_norm(src[here, :])
            dst[here, :] = (unit * row(l, i) + row(l, 2 + i)).astype(BF16)

        by_tiles(flat, 32, do)

    def load_tokens():
        def do(first, size):
            here = pl.ds(first, size)
            h[here, :] = tokens[here, :].astype(F32)

        by_tiles(flat, 32, do)

    def mix(l):
        def do(first, size):
            cols = pl.ds(first, size)
            u[:, cols] = jnp.dot(a[...], w_bufs[0][:, cols], preferred_element_type=F32)

        by_tiles(3 * width, 256, do)

        for s in range(seqs):

            def split(first, size):
                here, there = pl.ds(s * rows + first, size), pl.ds(first, size)
                queries = u[here, pl.ds(0, width)] + row(l, 4)
                keys = u[here, pl.ds(width, width)]
                values = u[here, pl.ds(2 * width, width)] + row(l, 5)
                q[here, pl.ds(0, width)] = queries.astype(BF16)
                own_kv[s, there, pl.ds(0, width)] = keys.astype(BF16)
                own_kv[s, there, pl.ds(wide, width)] = values.astype(BF16)

            by_tiles(rows, 32, split)

    def project(l):
        def do(first, size):
            cols = pl.ds(first, size)
            bias_row = vec[l, pl.ds(6, 1), cols]
            h1[:, cols] = (
                h[:, cols]
                + jnp.dot(o[:, pl.ds(0, width)], w_bufs[1][:, cols], preferred_element_type=F32)
                + bias_row
            )

        by_tiles(width, 256, do)

    def rise(l):
        def do(first, size):
            cols = pl.ds(first, size)
            pre = jnp.dot(c[...], w_bufs[2][:, cols], preferred_element_type=F32) + up_bias[l, pl.ds(0, 1), cols]
            value, slope = gelu_both(pre)
            z[:, cols] = value.astype(BF16)
            dg[:, cols] = slope.astype(BF16)

        by_tiles(ff, 256, do)

    def fall(l):
        def do(first, size):
            cols = pl.ds(first, size)
            h[:, cols] = (
                h1[:, cols]
                + jnp.dot(z[...], w_bufs[3][:, cols], preferred_element_type=F32)
                + vec[l, pl.ds(7, 1), cols]
            )

        by_tiles(width, 256, do)

    def finish_tokens():
        for s in range(seqs):
            def do(first, size):
                here = pl.ds(s * rows + first, size)
                place = at.c8 * rows + first + lax.broadcasted_iota(jnp.int32, (size, width), 0)
                acts[here, :] = jnp.where(place < lengths[s], h[here, :], 0.0).astype(BF16)

            by_tiles(rows, 32, do)

    steps = depth - 1
    ticks = [functools.partial(items[0].arrive, i) for i in range(steps)]
    last = 4 * layers * steps
    for n in range(last + FINISH_LAG):
        k, i = divmod(n, steps)
        if n < last:
            if i == 0 and k + 2 < 4 * layers:
                ticks.append(items[k + 2].start)
            ticks.append(functools.partial(items[k].plane, i))
            if k + 1 < 4 * layers:
                ticks.append(functools.partial(items[k + 1].arrive, i))
        if 0 <= n - SHARE_LAG < last:
            k, i = divmod(n - SHARE_LAG, steps)
            ticks.append(functools.partial(items[k].share, i))
        if n >= FINISH_LAG:
            k, i = divmod(n - FINISH_LAG, steps)
            ticks.append(("shard", k, i))
            if i == steps - 1:
                ticks.append(("end", k))

    def tick(n):
        for _ in range(n):
            if not ticks:
                return
            item = ticks.pop(0)
            if isinstance(item, tuple) and item[0] == "end":
                fetch(item[1], at.z)
            elif isinstance(item, tuple):
                items[item[1]].finish(item[2], functools.partial(fetch, item[1]))
            else:
                item()

    def reach(k):
        while ("end", k) in ticks:
            tick(1)

    small_start()
    items[0].start()
    items[1].start()
    for k in range(4 * layers):
        own_load(k)
    load_tokens()
    q[...] = jnp.zeros_like(q)
    o[...] = jnp.zeros_like(o)
    own_kv[...] = jnp.zeros_like(own_kv)
    lse[...] = jnp.zeros_like(lse)
    key_bias(bias, seqs, rows, slots, lengths, at.c8)
    for k in range(4 * layers):
        own_store(k)
    tick(steps)
    small_take()
    small_spread()
    for k in range(4 * layers):
        own_done(k)
    for l in range(layers):
        k = 4 * l
        norm(l, 0, h, a)
        keep(l, "h", h)
        free(l - 1, "pa")
        cut_pieces(a, pa, part, 0)
        keep(l, "pa", pa)
        reach(k)
        free(l - 1, "q")
        if l:
            for context in contexts[l - 1]:
                context.drain(True)
        ready(k)
        mix(l)
        for context in contexts[l]:
            context.start()
        keep(l, "q", q)
        free(l - 1, "o")
        free(l - 1, "lse")
        for context in contexts[l]:
            tick(TICKS[0])
            context.relay()
        for s, context in enumerate(contexts[l]):
            tick(TICKS[1])
            context.last()
            tick(TICKS[2])
            context.finish()
            seen = pltpu.make_async_copy(kept[l]["kv"].at[s], kv.at[s], load_sem.at[4 * layers, s])
            seen.start()
            seen.wait()
            first = 0
            for count in (pairs // 3, pairs // 3, pairs - 2 * (pairs // 3)):
                attend(s, first, count, q, kv, bias, o, lse, rows, pairs, wide)
                first += count
                tick(TICKS[3])
        keep(l, "o", o)
        keep(l, "lse", lse)
        free(l - 1, "po")
        cut_pieces(o.at[:, pl.ds(0, wide)], po, part, 0)
        keep(l, "po", po)
        ready(k + 1)
        free(l - 1, "h1")
        project(l)
        keep(l, "h1", h1)
        norm(l, 1, h1, c)
        free(l - 1, "pc")
        cut_pieces(c, pc, part, 0)
        keep(l, "pc", pc)
        reach(k + 2)
        ready(k + 2)
        free(l - 1, "dg")
        rise(l)
        keep(l, "dg", dg)
        free(l - 1, "pz")
        for i in range(4):
            cut_pieces(z, pz.at[:, i], part, i)
        keep(l, "pz", pz)
        reach(k + 3)
        free(l, "h")
        ready(k + 3)
        fall(l)
    tick(len(ticks))
    finish_tokens()
    for key in list(pending):
        free(*key)
    small_drain()
    for item in items:
        item.drain()
    for context in contexts[-1]:
        context.drain(True)
    for of_layer in contexts:
        for context in of_layer:
            context.drain(False)


def forward(tokens, lengths, w_qkv, w_out, w_up, w_down, small):
    seqs, rows, width = tokens.shape
    layers, part, _ = w_qkv.shape
    depth = lax.axis_size("fsdp")
    slots = rows * lax.axis_size("ctx")
    ff = w_up.shape[2]
    flat, wide = seqs * rows, pad_lanes(width)
    dims = (layers, seqs, rows, slots, width, ff, depth)
    any_spec = pl.BlockSpec(memory_space=pl.ANY)
    vmem = pl.BlockSpec(memory_space=pltpu.VMEM)
    struct = lambda shape, kind: jax.ShapeDtypeStruct(shape, kind)
    shapes = kept_shapes(seqs, slots, rows, width, ff)
    out_shape = [struct((flat, width), BF16), struct((layers, 8, wide), F32)]
    for l in range(layers):
        for ref in (w_qkv, w_out, w_up, w_down):
            out_shape.append(struct((depth * ref.shape[1], ref.shape[2]), BF16))
    for l in range(layers):
        out_shape += [struct(*shapes[name]) for name in KEPT]
    count = 4 * layers
    dma = pltpu.SemaphoreType.DMA
    scratch = [
        dma((count, 8 * depth + 8)),
        dma((count, 8 * depth)),
        dma((depth + 1,)),
        dma((depth,)),
        dma((layers, seqs, 8)),
        dma((layers, seqs, 8)),
        dma((count + 1, depth)),
        dma((layers, len(KEPT) + seqs)),
        dma((3, count)),
        pltpu.VMEM((depth,) + small.shape, BF16),
        pltpu.VMEM((layers, 8, wide), F32),
        pltpu.VMEM((layers, 8, ff), F32),
        pltpu.VMEM((flat, width), F32),
        pltpu.VMEM((flat, width), BF16),
        pltpu.VMEM((flat, wide), BF16),
        pltpu.VMEM((seqs, rows, 2 * wide), BF16),
        pltpu.VMEM((seqs, slots, 2 * wide), BF16),
        pltpu.VMEM((seqs, rows, slots), F32),
        pltpu.VMEM((flat, wide), BF16),
        pltpu.VMEM((2 * flat, LANES), F32),
        pltpu.VMEM((flat, width), F32),
        pltpu.VMEM((flat, width), BF16),
        pltpu.VMEM((flat, 3 * width), F32),
        pltpu.VMEM((flat, ff), BF16),
        pltpu.VMEM((flat, ff), BF16),
        pltpu.VMEM((2, flat, PIECE), BF16),
        pltpu.VMEM((2, flat, PIECE), BF16),
        pltpu.VMEM((2, flat, PIECE), BF16),
        pltpu.VMEM((2, 4, flat, PIECE), BF16),
    ] + [pltpu.VMEM((depth * ref.shape[1], ref.shape[2]), BF16) for ref in (w_qkv, w_out, w_up, w_down)]
    outs = pl.pallas_call(
        functools.partial(forward_kernel, dims),
        out_shape=out_shape,
        in_specs=[vmem, pl.BlockSpec(memory_space=pltpu.SMEM)] + [any_spec] * 5,
        out_specs=[vmem, vmem] + [any_spec] * (len(out_shape) - 2),
        scratch_shapes=scratch,
        compiler_params=pltpu.CompilerParams(
            collective_id=0, has_side_effects=True, vmem_limit_bytes=63 * 1024 * 1024
        ),
    )(tokens.reshape(flat, width), lengths, w_qkv, w_out, w_up, w_down, small)
    acts, vecs = outs[:2]
    wholes = outs[2 : 2 + count]
    rest = outs[2 + count :]
    kept = [dict(zip(KEPT, rest[l * len(KEPT) : (l + 1) * len(KEPT)])) for l in range(layers)]
    return acts, vecs, [wholes[4 * l : 4 * l + 4] for l in range(layers)], kept


SETS = 5
FINS = 10
LINE_FIRST = ()
LINE_LAG = 0
TILES = 3
KINDS = ("down", "up", "out", "mix")


def over_rows(a, b):
    return lax.dot_general(a, b, (((0,), (0,)), ((), ())), preferred_element_type=F32)


class Granule:
    def __init__(self, at, others, line_first, acc, plane_in, z_in, fin, out, send, recv, local, credit, wait_credit, give_credit, before):
        self.before = before
        self.line_first = line_first
        self.at, self.others, self.acc, self.plane_in, self.z_in = at, others, acc, plane_in, z_in
        self.fin, self.out, self.send, self.recv, self.local = fin, out, send, recv, local
        self.credit, self.wait_credit, self.give_credit = credit, wait_credit, give_credit
        self.t1 = acc.shape[2]
        self.names, self.posts = {}, []
        core, p = at.core, at.p
        self.direct_p = p + (1 - core) * (2 - 4 * at.py) + core * (1 - 2 * at.px)
        self.owner_dev = {"ctx": at.c8 + (1 - core) * (2 - 4 * at.px) + core * (4 - 8 * at.py)}

    def make(self, name, src, dst, device):
        i = self.names.setdefault(name, len(self.names))
        return remote(src, dst, self.send.at[i], self.recv.at[i], device)

    def post(self, name, src, dst, device):
        self.make(name, src, dst, device).start()
        self.posts.append((name, src, dst, device))

    def take(self, name, dst):
        self.make(name, dst, dst, self.at.sib).wait_recv()

    def place(self, p, core):
        ref, first, col, cols = self.out
        row = pl.multiple_of(first + core * 4 * self.t1 + p * self.t1, 16)
        return ref.at[pl.ds(row, self.t1), pl.ds(col, cols)]

    def line_out(self, part, landing):
        for i, device in enumerate(self.others):
            goal = lax.rem(self.at.z + 1 + i, self.at.depth)
            self.post(f"z{i}", part(goal), landing.at[i], device)

    def line_in(self, landing):
        for i in range(len(self.others)):
            self.take(f"z{i}", landing.at[i])

    def plane_out(self, part, landing):
        self.post("diag", part(self.at.p_d), landing.at[0], self.at.relay_dev)
        self.post("near", part(self.direct_p), landing.at[1], self.at.relay_dev)

    def plane_relay(self, part, landing, add):
        self.take("diag", landing.at[0])
        add(part(self.at.relay_from), landing.at[0])
        self.post("relay", part(self.at.relay_from), landing.at[2], self.owner_dev)

    def plane_in_all(self, landing):
        self.take("near", landing.at[1])
        self.take("relay", landing.at[2])

    def over_shards(self, acc, extra):
        for t in range(self.at.depth):
            add_rows(acc.at[t], extra.at[t], self.t1)

    def total(self, own, extra, out):
        def step(i, carry):
            piece = pl.ds(pl.multiple_of(i * 16, 16), 16)
            value = own[piece, :].astype(F32)
            for j in range(3):
                value = value + extra(j)[piece, :].astype(F32)
            out[piece, :] = value.astype(BF16)
            return carry

        lax.fori_loop(0, self.t1 // 16, step, 0)

    def of_shard(self, p):
        return self.acc.at[self.at.z, p]

    def of_chip(self, p):
        return self.acc.at[:, p]

    def begin(self):
        if self.wait_credit is not None:
            pl.semaphore_wait(self.wait_credit, 2 + len(self.others))
        if self.line_first:
            self.line_out(lambda t: self.acc.at[t], self.plane_in)
        else:
            self.plane_out(self.of_chip, self.plane_in)

    def second(self):
        at = self.at
        if self.line_first:
            self.line_in(self.plane_in)
            for p in range(4):
                own = self.of_shard(p)
                self.total(own, lambda j: self.plane_in.at[j, p], own)
            self.plane_out(self.of_shard, self.z_in)
        else:
            self.plane_relay(self.of_chip, self.plane_in, self.over_shards)

    def third(self):
        at = self.at
        if self.line_first:
            self.plane_relay(self.of_shard, self.z_in, lambda a, b: add_rows(a, b, self.t1))
        else:
            self.plane_in_all(self.plane_in)
            mine = self.of_chip(at.p)
            for t in range(at.depth):
                add_rows_two(mine.at[t], self.plane_in.at[1, t], self.plane_in.at[2, t], self.t1)
            self.line_out(lambda t: self.acc.at[t, at.p], self.z_in)

    def fin_sent(self):
        for name, src, dst, device in self.posts:
            if name in ("sx", "sy", "ss"):
                self.make(name, src, dst, device).wait_send()
        self.posts = [post for post in self.posts if post[0] not in ("sx", "sy", "ss")]

    def end(self):
        at = self.at
        if self.before is not None:
            self.before.fin_sent()
        own = self.of_shard(at.p)
        if self.line_first:
            self.plane_in_all(self.z_in)

            def step(i, carry):
                piece = pl.ds(pl.multiple_of(i * 16, 16), 16)
                value = own[piece, :].astype(F32) + self.z_in[1, piece, :].astype(F32)
                self.fin[piece, :] = (value + self.z_in[2, piece, :].astype(F32)).astype(BF16)
                return carry

            lax.fori_loop(0, self.t1 // 16, step, 0)
        else:
            self.line_in(self.z_in)
            self.total(own, lambda j: self.z_in.at[j], self.fin)
        if self.give_credit:
            for device in [at.x_dev, at.y_dev] + self.others:
                pl.semaphore_signal(self.credit, inc=1, device_id=device, device_id_type=MESH)
        here = self.place(at.p, at.core)
        pltpu.make_async_copy(self.fin, here, self.local).start()
        self.post("sx", self.fin, here, at.x_dev)
        self.post("sy", self.fin, here, at.y_dev)
        self.post("ss", self.fin, here, at.sib)

    def release(self):
        keep = []
        for name, src, dst, device in self.posts:
            if name[0] == "s":
                keep.append((name, src, dst, device))
            else:
                self.make(name, src, dst, device).wait_send()
        self.posts = keep

    def spread_relay(self):
        at = self.at
        for far, p in (("sx", at.p_x), ("sy", at.p_y)):
            here = self.place(p, at.core)
            self.take(far, here)
            self.post(far + "s", here, here, at.sib)
        here = self.place(at.relay_from, at.core)
        self.post("sd", here, here, at.relay_dev)

    def spread_last(self):
        at = self.at
        here = self.place(at.p_d, at.core)
        self.take("sd", here)
        self.post("sds", here, here, at.sib)

    def finish(self):
        at = self.at
        for name, p in (("ss", at.p), ("sxs", at.p_x), ("sys", at.p_y), ("sds", at.p_d)):
            self.take(name, self.place(p, 1 - at.core))
        pltpu.make_async_copy(self.fin, self.place(at.p, at.core), self.local).wait()

    def drain(self):
        for name, src, dst, device in self.posts:
            self.make(name, src, dst, device).wait_send()

    def stages(self):
        wait = [[] for _ in range(LINE_LAG)] if self.line_first else []
        return wait + [
            [self.second], [self.third], [self.end], [self.release, self.spread_relay], [self.spread_last],
            [self.finish],
        ]


class KeyGrads:
    def __init__(self, at, parts, sib_in, stage, plane_in, send, recv, local, credit, layer):
        self.at, self.parts, self.sib_in, self.stage, self.plane_in = at, parts, sib_in, stage, plane_in
        self.send, self.recv, self.local, self.credit, self.layer = send, recv, local, credit, layer
        self.names, self.posts = {}, []
        core, p = at.core, at.p
        self.direct_p = p + (1 - core) * (2 - 4 * at.py) + core * (1 - 2 * at.px)
        self.owner_dev = {"ctx": at.c8 + (1 - core) * (2 - 4 * at.px) + core * (4 - 8 * at.py)}
        self.order = [at.p_d, self.direct_p, at.relay_from, at.p]

    def make(self, name, src, dst, device):
        i = self.names.setdefault(name, len(self.names))
        return remote(src, dst, self.send.at[i], self.recv.at[i], device)

    def post(self, name, src, dst, device):
        self.make(name, src, dst, device).start()
        self.posts.append((name, src, dst, device))

    def take(self, name, dst):
        self.make(name, dst, dst, self.at.sib).wait_recv()

    def start(self):
        for i, p in enumerate(self.other_order()):
            self.post(f"s{i}", self.parts.at[1, p], self.sib_in.at[p], self.at.sib)

    def other_order(self):
        at = self.at
        core = 1 - at.core
        direct = at.p + (1 - core) * (2 - 4 * at.py) + core * (1 - 2 * at.px)
        relay = at.p + (1 - core) * (1 - 2 * at.px) + core * (2 - 4 * at.py)
        return [at.p_d, direct, relay, at.p]

    def add(self, p, extra):
        add_rows(self.parts.at[0, p], extra, self.parts.shape[2])

    def core_sum(self, i):
        p = self.order[i]
        self.take(f"s{i}", self.sib_in.at[p])
        copy = pltpu.make_async_copy(self.sib_in.at[p], self.stage, self.local)
        copy.start()
        copy.wait()
        self.add(p, self.stage)

    def first(self):
        at = self.at
        self.core_sum(0)
        if self.layer is not None:
            pl.semaphore_wait(self.credit, 2)
        self.post("diag", self.parts.at[0, at.p_d], self.plane_in.at[0], at.relay_dev)
        self.core_sum(1)
        self.post("near", self.parts.at[0, self.direct_p], self.plane_in.at[1], at.relay_dev)
        self.core_sum(2)
        self.core_sum(3)

    def relay(self):
        at = self.at
        self.take("diag", self.plane_in.at[0])
        self.add(at.relay_from, self.plane_in.at[0])
        self.post("relay", self.parts.at[0, at.relay_from], self.plane_in.at[2], self.owner_dev)

    def combine(self, give_credit):
        at = self.at
        self.take("near", self.plane_in.at[1])
        self.take("relay", self.plane_in.at[2])
        add_rows_two(self.parts.at[0, at.p], self.plane_in.at[1], self.plane_in.at[2], self.parts.shape[2])
        if give_credit:
            for device in (at.x_dev, at.y_dev):
                pl.semaphore_signal(self.credit, inc=1, device_id=device, device_id_type=MESH)

    def drain(self):
        for name, src, dst, device in self.posts:
            self.make(name, src, dst, device).wait_send()
        self.posts = []


def backward_kernel(dims, *refs):
    layers, seqs, rows, slots, width, ff, depth, per_layer = dims
    flat, wide = seqs * rows, pad_lanes(width)
    pairs = wide // LANES
    total = seqs * pairs
    refs = list(refs)

    def grab(n):
        out = refs[:n]
        del refs[:n]
        return out

    cot, lengths, vecs = grab(3)
    kept = [dict(zip(KEPT, grab(len(KEPT)))) for _ in range(layers)]
    wholes = [grab(4) for _ in range(layers)]
    grad_in, small_out = grab(2)
    outs = [grab(5) for _ in range(layers)]
    kv_sib = grab(layers)
    (g_send, g_recv, g_local, g_credit, kv_send, kv_recv, kv_local, kv_credit) = grab(8)
    (pg_send, pg_recv, pg_local, pg_credit, sm_send, sm_recv, load_sem, w_sem, kvp_sem, rest_sem) = grab(10)
    acc, plane_in, z_in, rest_acc, fin = grab(5)
    hx, dn = grab(2)
    g = grad_in
    gm, gu, ga, gx = grab(4)
    pz, pc, po, pa = grab(4)
    dg, q, go, o, lse, bias, kvp = grab(7)
    parts, kv_stage, kv_plane = grab(3)
    wt_a, wt_u, wt_q, gq = grab(4)
    sm, sm_sum, sm_in, sm_z, up_row = grab(5)

    at = Place()
    core = at.core
    barrier = pltpu.get_barrier_semaphore()
    others = [{"fsdp": lax.rem(at.z + i, depth)} for i in range(1, depth)]
    for device in [at.sib, at.x_dev, at.y_dev] + others:
        pl.semaphore_signal(barrier, inc=1, device_id=device, device_id_type=MESH)
    pl.semaphore_wait(barrier, 3 + depth - 1)

    exchange = {
        "down": [("pz", pz), ("gm", gm)],
        "up": [("pc", pc), ("gu", gu)],
        "out": [("po", po), ("ga", ga)],
        "mix": [("pa", pa), ("gx", gx)],
    }
    slot_of = {}
    for kind in KINDS:
        for name, _ in exchange[kind]:
            slot_of[name] = len(slot_of)
    buffers = {name: buf for kind in KINDS for name, buf in exchange[kind]}
    posted = {}

    def pg_copy(name, src):
        i = slot_of[name]
        buf = buffers[name]
        dst = buf.at[1]
        return remote(src, dst, pg_send.at[i], pg_recv.at[i], at.sib)

    def pg_post(name, src):
        pg_copy(name, src).start()
        posted[name] = src

    def pg_sent(name):
        src = posted.pop(name, None)
        if src is not None:
            pg_copy(name, src).wait_send()

    def pg_take(name):
        buf = buffers[name].at[1]
        pg_copy(name, buf).wait_recv()

    def piece_load(l, name):
        return pltpu.make_async_copy(kept[l][name].at[core], buffers[name].at[0], pg_local.at[slot_of[name]])

    def free_kind(kind, l):
        if l < layers - 1:
            pl.semaphore_wait(pg_credit.at[KINDS.index(kind)], 1)

    def done_kind(kind, l):
        if l > 0:
            pl.semaphore_signal(
                pg_credit.at[KINDS.index(kind)], inc=1, device_id=at.sib, device_id_type=MESH
            )

    active, items, rest_done = [], [], []
    line_up = layers * per_layer

    def pump(times=1):
        for _ in range(times):
            for entry in list(active):
                for do in entry[1].pop(0):
                    do()
                if not entry[1]:
                    active.remove(entry)

    def open_set():
        index = len(items)
        if index >= SETS:
            old = items[index - SETS]
            while any(entry[0] is old and len(entry[1]) > 2 for entry in active):
                pump()
        return index

    def goal(l, unit):
        down, up, out, mix, rest = outs[l]
        part = width // depth
        if unit < 4:
            return down, part * unit, 0, wide
        if unit < 8:
            return up, 0, (unit - 4) * wide, min(wide, ff - (unit - 4) * wide)
        if unit == 8:
            return out, 0, 0, wide
        if unit < 12:
            return mix, 0, (unit - 9) * wide, min(wide, pad_lanes(3 * width) - (unit - 9) * wide)
        return rest, 0, 0, wide

    def launch(l, unit, source):
        index = len(items)
        s = index % SETS
        cols = pl.ds(0, goal(l, unit)[3])
        item = Granule(
            at, others, unit in LINE_FIRST, source.at[:, :, :, cols], plane_in.at[s, :, :, :, cols],
            z_in.at[s, :, :, cols], fin.at[index % FINS, :, cols], goal(l, unit),
            g_send.at[index], g_recv.at[index], g_local.at[index], g_credit.at[index],
            g_credit.at[index - SETS] if index >= SETS else None, index + SETS < line_up,
            items[index - FINS] if index >= FINS else None,
        )
        if index >= FINS:
            assert all(entry[0] is not items[index - FINS] for entry in active)
        item.begin()
        items.append(item)
        active.append([item, item.stages()])

    def weight_grad(l, unit, piece, rhs, first):
        index = open_set()
        s = index % SETS
        home = 0 if unit < 8 else 1

        def do(off, size):
            cols = pl.ds(off, size)
            right = rhs[:, :, pl.ds(pl.multiple_of(first + off, LANES), size)].reshape(2 * flat, size)
            left = piece[:, :, pl.ds(0, depth * LANES)].reshape(2 * flat, depth * LANES)
            out = over_rows(left, right).astype(BF16)
            for t in range(depth):
                acc[s, t, :, :, cols] = out[t * LANES : (t + 1) * LANES].reshape(4, LANES // 4, size)

            @pl.when(core == home)
            def _():
                last = piece[:, :, pl.ds(depth * LANES, LANES)].reshape(2 * flat, LANES)
                more = over_rows(last, right).astype(BF16)
                for t in range(depth):
                    u = unit - 8 * home
                    rest_acc[t, u // 2, pl.ds(16 * (u % 2), 16), cols] = more[t * 16 : (t + 1) * 16]

        by_tiles(wide, 384, do)
        launch(l, unit, acc.at[s])

    def rest_grad(l):
        open_set()
        launch(l, 12, rest_acc)

    def rest_rows(l):
        part = width // depth
        rest_v = gq
        copy = pltpu.make_async_copy(outs[l][4], rest_v, rest_sem.at[0])
        copy.start()
        copy.wait()
        moves = []
        for unit in range(12):
            ref, first, col, cols = goal(l, unit)
            moves.append(
                pltpu.make_async_copy(
                    rest_v.at[pl.ds(16 * unit, 16), pl.ds(0, cols)],
                    ref.at[pl.ds(first + 2 * LANES, part - 2 * LANES), pl.ds(col, cols)],
                    rest_sem.at[1 + unit],
                )
            )
        for move in moves:
            move.start()
        for move in moves:
            move.wait()

    def put_row(l, i, value):
        sm[pl.ds(l * 16 + i, 1), pl.ds(0, width)] = value

    def column_sums(l, i, src):
        put_row(l, i, jnp.sum(src[0, :, pl.ds(0, width)].astype(F32), axis=0, keepdims=True))

    def norm_back(l, i):
        gain = vecs[l, pl.ds(i, 1), pl.ds(0, width)]

        def do(step, carry):
            gain_sum, shift_sum = carry
            here = pl.ds(pl.multiple_of(step * 32, 32), 32)
            unit, scale = row_norm(hx[here, :])
            grad = dn[here, :]
            inner = grad * gain
            mean_inner = jnp.mean(inner, axis=-1, keepdims=True)
            mean_unit = jnp.mean(inner * unit, axis=-1, keepdims=True)
            g[here, :] = g[here, :] + scale * (inner - mean_inner - unit * mean_unit)
            return (
                gain_sum + jnp.sum(grad * unit, axis=0, keepdims=True),
                shift_sum + jnp.sum(grad, axis=0, keepdims=True),
            )

        zero = jnp.zeros((1, width), F32)
        gain_sum, shift_sum = lax.fori_loop(0, flat // 32, do, (zero, zero))
        put_row(l, i, gain_sum)
        put_row(l, 2 + i, shift_sum)

    def load(l, name, dst, index):
        return pltpu.make_async_copy(kept[l][name], dst, load_sem.at[index])

    def low_copy(src, dst):
        def do(first, size):
            here = pl.ds(first, size)
            dst[0, here, pl.ds(0, width)] = src[here, :].astype(BF16)

        by_tiles(flat, 64, do)

    def row_tile(whole, buf, slot, first, size, sem):
        return pltpu.make_async_copy(
            whole.at[pl.ds(first, size)], buf.at[slot, pl.ds(0, size)], sem.at[slot]
        )

    def ff_back(l):
        w_up, w_down = wholes[l][2], wholes[l][3]
        tile = 256
        count = ff // tile

        def copies(i, slot):
            first = pl.multiple_of(i * tile, tile)
            return (
                pltpu.make_async_copy(w_down.at[pl.ds(first, tile)], wt_a.at[slot], w_sem.at[0, slot]),
                pltpu.make_async_copy(w_up.at[:, pl.ds(first, tile)], wt_u.at[slot], w_sem.at[1, slot]),
            )

        dn[...] = jnp.zeros_like(dn)
        for i in range(TILES - 1):
            for copy in copies(i, i):
                copy.start()

        def step(i, carry):
            slot = lax.rem(i, TILES)
            for copy in copies(i, slot):
                copy.wait()

            @pl.when(i + TILES - 1 < count)
            def _():
                for copy in copies(i + TILES - 1, lax.rem(i + TILES - 1, TILES)):
                    copy.start()

            cols = pl.ds(pl.multiple_of(i * tile, tile), tile)
            grad = across(gm[0, :, pl.ds(0, width)], wt_a[slot])
            low = (grad * dg[:, cols].astype(F32)).astype(BF16)
            gu[0, :, cols] = low
            up_row[pl.ds(0, 1), cols] = jnp.sum(low.astype(F32), axis=0, keepdims=True)
            dn[...] = dn[...] + across(low, wt_u[slot])
            return carry

        def part(first, size):
            lax.fori_loop(first, first + size, step, 0)

        half = count // 2
        part(0, half)
        pump()
        part(half, count - half)

    def tiles_back(whole, buf, sem, left, put):
        tile = buf.shape[1]
        spans = [(i, min(tile, width - i)) for i in range(0, width, tile)]
        row_tile(whole, buf, 0, *spans[0], sem).start()
        for n, (first, size) in enumerate(spans):
            row_tile(whole, buf, n % 2, first, size, sem).wait()
            if n + 1 < len(spans):
                row_tile(whole, buf, (n + 1) % 2, *spans[n + 1], sem).start()
            put(first, size, across(left(), buf[n % 2, pl.ds(0, size)]))

    def kv_copy(l, it, slot):
        s, j = it // pairs, lax.rem(it, pairs)
        return [
            pltpu.make_async_copy(
                kept[l]["kv"].at[s, :, pl.ds(pl.multiple_of(i * wide + j * LANES, LANES), LANES)],
                kvp.at[slot, i],
                kvp_sem.at[slot, i],
            )
            for i in range(2)
        ]

    def attend_back(l, first, count):
        def step(it, carry):
            slot = lax.rem(it, 2)
            for copy in kv_copy(l, it, slot):
                copy.wait()

            @pl.when(it + 1 < total)
            def _():
                for copy in kv_copy(l, it + 1, 1 - slot):
                    copy.start()

            s, j = it // pairs, lax.rem(it, pairs)
            here = pl.ds(pl.multiple_of(s * rows, rows), rows)
            col = pl.ds(pl.multiple_of(j * LANES, LANES), LANES)
            col_v = pl.ds(pl.multiple_of(wide + j * LANES, LANES), LANES)
            q2, go_block = two_heads(q[here, col]), go[here, col]
            go2 = two_heads(go_block)
            keys, values = kvp[slot, 0], kvp[slot, 1]
            product = go_block.astype(F32) * o[here, col].astype(F32)
            delta = jnp.sum(two_heads(product), axis=-1, keepdims=True)
            lane = lax.broadcasted_iota(jnp.int32, (2 * rows, LANES), 1)
            block = lse[pl.ds(pl.multiple_of(s * 2 * rows, rows), 2 * rows), :]
            log_total = jnp.sum(jnp.where(lane == it, block, 0.0), axis=-1, keepdims=True)
            seen = bias[s]
            scores = across(q2, keys) * (HEAD_DIM ** (-0.5)) + jnp.concatenate([seen, seen], axis=0)
            probs = jnp.exp(scores - log_total)
            grads = across(go2, values)
            low = (probs * (grads - delta)).astype(BF16)
            dq = jnp.dot(low, keys, preferred_element_type=F32) * (HEAD_DIM ** (-0.5))
            gq[here, col] = one_pair(dq, rows).astype(BF16)
            dk = (over_rows(low, q2) * (HEAD_DIM ** (-0.5))).astype(BF16)
            dv = over_rows(probs.astype(BF16), go2).astype(BF16)
            for b in range(slots // rows):
                mine = lax.rem(b + core, 2)
                span = slice(b * rows, (b + 1) * rows)
                parts[s, mine, b // 2, :, col] = dk[span]
                parts[s, mine, b // 2, :, col_v] = dv[span]
            return carry

        lax.fori_loop(first, first + count, step, 0)

    loads = {}

    def early(l):
        for i, (name, dst) in enumerate((("h1", hx), ("dg", dg), ("q", q), ("o", o), ("lse", lse))):
            loads[name] = load(l, name, dst, i)
            loads[name].start()
        for kind in KINDS:
            free_kind(kind, l)
            name = exchange[kind][0][0]
            piece_load(l, name).start()
            pg_sent(name)
            pg_post(name, kept[l][name].at[1 - core])

    rest_acc[...] = jnp.zeros_like(rest_acc)
    sm[...] = jnp.zeros_like(sm)
    for buf, used in ((gm, width), (gu, ff), (ga, width), (gx, 3 * width)):
        first = used // LANES * LANES
        buf[0, :, pl.ds(first, buf.shape[2] - first)] = jnp.zeros((flat, buf.shape[2] - first), BF16)
    go[:, pl.ds(wide - LANES, LANES)] = jnp.zeros((flat, LANES), BF16)
    early(layers - 1)
    for s in range(seqs):

        def first_grad(first, size):
            here = pl.ds(s * rows + first, size)
            place = at.c8 * rows + first + lax.broadcasted_iota(jnp.int32, (size, width), 0)
            g[here, :] = jnp.where(place < lengths[s], cot[here, :].astype(F32), 0.0)

        by_tiles(rows, 32, first_grad)
    key_bias(bias, seqs, rows, slots, lengths, at.c8)

    for l in reversed(range(layers)):
        keys = [
            KeyGrads(
                at, parts.at[s], kv_sib[l].at[s], kv_stage, kv_plane.at[s], kv_send.at[l, s], kv_recv.at[l, s],
                kv_local, kv_credit.at[s], None if l == layers - 1 else l,
            )
            for s in range(seqs)
        ]
        if l < layers - 1:
            early(l)
        pg_sent("gm")
        low_copy(g, gm)
        pg_post("gm", gm.at[0])
        column_sums(l, 7, gm)
        piece_load(l, "pz").wait()
        pg_take("pz")
        pg_take("gm")
        for i in range(4):
            weight_grad(l, i, pz.at[:, i], gm, 0)
            pump()
        done_kind("down", l)
        loads["dg"].wait()
        pg_sent("gu")
        ff_back(l)
        pg_post("gu", gu.at[0])
        pump()
        for r in range(4):
            sm[pl.ds(l * 16 + 8 + r, 1), :] = up_row[pl.ds(0, 1), pl.ds(r * wide, wide)]
        loads["h1"].wait()
        norm_back(l, 1)
        loads["h"] = load(l, "h", hx, 5)
        loads["h"].start()
        pg_sent("ga")
        low_copy(g, ga)
        pg_post("ga", ga.at[0])
        column_sums(l, 6, ga)
        pump()

        def put_go(first, size, value):
            go[:, pl.ds(first, size)] = value.astype(BF16)

        tiles_back(wholes[l][1], wt_a, w_sem.at[0], lambda: ga[0, :, pl.ds(0, width)], put_go)
        for copy in kv_copy(l, 0, 0):
            copy.start()
        pump()
        piece_load(l, "pc").wait()
        pg_take("pc")
        pg_take("gu")
        for i in range(4):
            weight_grad(l, 4 + i, pc, gu, i * wide)
            pump()
        done_kind("up", l)
        piece_load(l, "po").wait()
        pg_take("po")
        pg_take("ga")
        weight_grad(l, 8, po, ga, 0)
        done_kind("out", l)
        pump()
        if l < layers - 1 and all(entry[0] is not items[per_layer * (layers - 1 - l) - 1] for entry in active):
            rest_rows(l + 1)
            rest_done.append(l + 1)
        for name in ("q", "o", "lse"):
            loads[name].wait()
        steps = []
        for s in range(seqs):
            third = pairs // 3
            pieces = [(s * pairs, third), (s * pairs + third, third), (s * pairs + 2 * third, pairs - 2 * third)]
            for piece in pieces:
                attend_back(l, *piece)
                pump()
                if steps:
                    steps.pop(0)()
            steps += [keys[s].start, keys[s].first, keys[s].relay, functools.partial(keys[s].combine, l > 0)]
            steps.pop(0)()
        while steps:
            steps.pop(0)()
            if steps:
                pump()
        pg_sent("gx")
        for s in range(seqs):

            def join(first, size):
                here, there = pl.ds(s * rows + first, size), pl.ds(first, size)
                gx[0, here, pl.ds(0, width)] = gq[here, pl.ds(0, width)]
                gx[0, here, pl.ds(width, width)] = parts[s, 0, at.p, there, pl.ds(0, width)]
                gx[0, here, pl.ds(2 * width, width)] = parts[s, 0, at.p, there, pl.ds(wide, width)]

            by_tiles(rows, 64, join)
        pg_post("gx", gx.at[0])
        for i, col in ((4, 0), (5, 2 * width)):
            put_row(l, i, jnp.sum(gx[0, :, pl.ds(col, width)].astype(F32), axis=0, keepdims=True))

        def put_dn(first, size, value):
            dn[:, pl.ds(first, size)] = value

        piece_load(l, "pa").wait()
        pg_take("pa")
        pg_take("gx")
        for i in range(3):
            weight_grad(l, 9 + i, pa, gx, i * wide)
            pump()
        done_kind("mix", l)
        rest_grad(l)
        rest_item = items[-1]
        pump()
        tiles_back(wholes[l][0], wt_q, w_sem.at[2], lambda: gx[0, :, pl.ds(0, 3 * width)], put_dn)
        loads["h"].wait()
        pump()
        norm_back(l, 0)
        for item in keys:
            item.drain()
        while l and any(entry[0] is rest_item and len(entry[1]) > 2 for entry in active):
            pump()

    def sm_copy(i, src, dst, device):
        return remote(src, dst, sm_send.at[i], sm_recv.at[i], device)

    current = sm
    for i, device in enumerate((at.sib, at.x_dev, at.y_dev)):
        copy = sm_copy(i, current, sm_in.at[i], device)
        copy.start()
        pump()
        copy.wait()
        sm_sum[i % 2] = current[...] + sm_in[i]
        current = sm_sum.at[i % 2]
    hops = []
    for i, device in enumerate(others):
        copy = sm_copy(3 + i, current, sm_z.at[i], device)
        copy.start()
        hops.append(copy)
    pump()
    for copy in hops:
        copy.wait()
    small_total = jnp.zeros(sm.shape, F32)
    for z in range(depth):
        slot = lax.rem(at.z - z - 1 + 2 * depth, depth)
        other = sm_z[jnp.minimum(slot, depth - 2)]
        small_total = small_total + jnp.where(slot == depth - 1, current[...], other)
    small_out[...] = small_total
    for l in range(layers):
        while any(entry[0] is items[(layers - l) * per_layer - 1] for entry in active):
            pump()
        if l not in rest_done:
            rest_rows(l)
    while active:
        pump()
    for item in items:
        item.drain()
    for name in list(posted):
        pg_sent(name)


def backward(cotangent, lengths, vecs, kept, wholes, layers, ff):
    seqs, rows, width = cotangent.shape
    depth = lax.axis_size("fsdp")
    slots = rows * lax.axis_size("ctx")
    flat, wide = seqs * rows, pad_lanes(width)
    per_layer = 13
    count = layers * per_layer
    dims = (layers, seqs, rows, slots, width, ff, depth, per_layer)
    any_spec = pl.BlockSpec(memory_space=pl.ANY)
    vmem = pl.BlockSpec(memory_space=pltpu.VMEM)
    struct = lambda shape, kind: jax.ShapeDtypeStruct(shape, kind)
    out_shape = [struct((flat, width), F32), struct((layers * 16, wide), F32)]
    part = width // depth
    for _ in range(layers):
        out_shape += [
            struct((4 * part, wide), BF16),
            struct((part, 4 * wide), BF16),
            struct((part, wide), BF16),
            struct((part, 3 * wide), BF16),
            struct((2 * LANES, wide), BF16),
        ]
    out_shape += [struct((seqs, 4, rows, 2 * wide), BF16) for _ in range(layers)]
    dma, regular = pltpu.SemaphoreType.DMA, pltpu.SemaphoreType.REGULAR
    low = lambda *shape: pltpu.VMEM(shape, BF16)
    full = lambda *shape: pltpu.VMEM(shape, F32)
    chunk = LANES // 4
    scratch = [
        dma((count, 24)), dma((count, 24)), dma((count,)), regular((count,)),
        dma((layers, seqs, 8)), dma((layers, seqs, 8)), dma, regular((seqs,)),
        dma((10,)), dma((10,)), dma((10,)), regular((4,)), dma((8,)), dma((8,)), dma((8,)), dma((3, TILES)), dma((2, 2)), dma((13,)),
        low(SETS, depth, 4, chunk, wide), low(SETS, 3, depth, chunk, wide), low(SETS, depth - 1, chunk, wide),
        low(depth, 4, chunk, wide), low(FINS, chunk, wide),
        full(flat, width), full(flat, width),
        low(2, flat, wide), low(2, flat, 4 * wide), low(2, flat, wide), low(2, flat, 3 * wide),
        low(2, 4, flat, PIECE), low(2, flat, PIECE), low(2, flat, PIECE), low(2, flat, PIECE),
        low(flat, ff), low(flat, wide), low(flat, wide), low(flat, wide), full(2 * flat, LANES),
        full(seqs, rows, slots), low(2, 2, slots, LANES),
        low(seqs, 2, 4, rows, 2 * wide), low(rows, 2 * wide), low(seqs, 3, rows, 2 * wide),
        low(TILES, 256, width), low(TILES, width, 256), low(2, 256, 3 * width), low(flat, wide),
        full(layers * 16, wide), full(2, layers * 16, wide), full(3, layers * 16, wide),
        full(depth - 1, layers * 16, wide), full(8, 4 * wide),
    ]
    flat_kept = [kept[l][name] for l in range(layers) for name in KEPT]
    flat_wholes = [item for layer in wholes for item in layer]
    outs = pl.pallas_call(
        functools.partial(backward_kernel, dims),
        out_shape=out_shape,
        in_specs=[vmem, pl.BlockSpec(memory_space=pltpu.SMEM), vmem]
        + [any_spec] * (len(flat_kept) + len(flat_wholes)),
        out_specs=[vmem, vmem] + [any_spec] * (len(out_shape) - 2),
        scratch_shapes=scratch,
        compiler_params=pltpu.CompilerParams(
            collective_id=1, has_side_effects=True, vmem_limit_bytes=63 * 1024 * 1024
        ),
    )(cotangent.reshape(flat, width), lengths, vecs, *flat_kept, *flat_wholes)
    grads = [outs[2 + 5 * l : 6 + 5 * l] for l in range(layers)]
    return outs[0], outs[1].reshape(layers, 16, wide), grads


def normalize(values, scales, shifts):
    average = jnp.mean(values, axis=-1, keepdims=True)
    centred = values - average
    variance = jnp.mean(centred * centred, axis=-1, keepdims=True)
    return centred * lax.rsqrt(variance + 1e-05) * scales + shifts


def outer_sum(left_rows, right_rows):
    return lax.dot_general(
        left_rows, right_rows, (((0,), (0,)), ((), ())), preferred_element_type=jnp.float32
    )


def times_transpose(left_rows, weight_rows):
    return lax.dot_general(
        left_rows, weight_rows, (((1,), (1,)), ((), ())), preferred_element_type=jnp.float32
    )


def allowed_mask(positions, key_places, lengths):
    causal = (key_places[None, :] <= positions[:, None]) & (key_places[None, :] >= 0)
    inside = key_places[None, :] < lengths[:, None]
    return causal[None, None, :, :] & inside[:, None, None, :]


def attend_forward(queries, key_part, value_part, positions, lengths, score_scale):
    seq_count, row_count, head_count, head_width = queries.shape
    lowest = jnp.full((seq_count, head_count, row_count), -1e30, jnp.float32)
    key_places = jnp.arange(key_part.shape[1], dtype=jnp.int32)
    allowed = allowed_mask(positions, key_places, lengths)
    scores = (
        jnp.einsum("sqhe,skhe->shqk", queries, key_part, preferred_element_type=jnp.float32)
        * score_scale
    )
    scores = jnp.where(allowed, scores, -1e30)
    new_top = jnp.maximum(lowest, jnp.max(scores, axis=-1))
    exp_weights = jnp.where(allowed, jnp.exp(scores - new_top[..., None]), 0.0)
    running_total = jnp.sum(exp_weights, axis=-1)
    running_sum = jnp.einsum(
        "shqk,skhe->shqe",
        exp_weights.astype(jnp.bfloat16),
        value_part,
        preferred_element_type=jnp.float32,
    )
    output = jnp.transpose(running_sum / running_total[..., None], (0, 2, 1, 3))
    return (output, new_top + jnp.log(running_total))


def block_terms(
    queries,
    grad_out,
    log_total,
    delta_row,
    key_part,
    value_part,
    first_key,
    positions,
    lengths,
    score_scale,
):
    key_places = first_key + jnp.arange(key_part.shape[1], dtype=jnp.int32)
    allowed = allowed_mask(positions, key_places, lengths)
    scores = (
        jnp.einsum("sqhe,skhe->shqk", queries, key_part, preferred_element_type=jnp.float32)
        * score_scale
    )
    scores = jnp.where(allowed, scores, -1e30)
    probability = jnp.where(allowed, jnp.exp(scores - log_total[..., None]), 0.0)
    grad_probs = jnp.einsum(
        "sqhe,skhe->shqk", grad_out, value_part, preferred_element_type=jnp.float32
    )
    grad_scores = (probability * (grad_probs - delta_row[..., None])).astype(jnp.bfloat16)
    query_add = (
        jnp.einsum("shqk,skhe->sqhe", grad_scores, key_part, preferred_element_type=jnp.float32)
        * score_scale
    )
    key_add = (
        jnp.einsum("shqk,sqhe->skhe", grad_scores, queries, preferred_element_type=jnp.float32)
        * score_scale
    )
    value_add = jnp.einsum(
        "shqk,sqhe->skhe",
        probability.astype(jnp.bfloat16),
        grad_out,
        preferred_element_type=jnp.float32,
    )
    return (query_add, key_add, value_add)


def pack_small(ln_gain, ln_bias, b_qv, b_out, b_up, b_down):
    layers, _, part = ln_gain.shape
    return jnp.concatenate(
        [ln_gain, ln_bias, b_qv, b_out[:, None], b_down[:, None], b_up.reshape(layers, 4, part)],
        axis=1,
    )


def unpack_small(whole):
    depth, _, part = whole.shape
    flat = jnp.transpose(whole[:, :8], (1, 0, 2)).reshape(8, depth * part)
    up_bias = whole[:, 8:].reshape(depth * 4 * part)
    return flat[0:2], flat[2:4], flat[4:6], flat[6], flat[7], up_bias


def small_rows(gains, shifts, mix_bias, out_bias, down_bias, up_bias, depth):
    width = gains.shape[-1]
    flat = jnp.concatenate([gains, shifts, mix_bias, out_bias[None], down_bias[None]], axis=0)
    flat = jnp.transpose(flat.reshape(8, depth, width // depth), (1, 0, 2))
    return jnp.concatenate([flat, up_bias.reshape(depth, 4, width // depth)], axis=1)


def fast_mesh(rows):
    return lax.axis_size("ctx") == 8 and rows % 272 == 0


def gather_all(weights, small):
    flat = [item for layer in weights for item in layer]
    layers = len(weights)
    wholes = [lax.all_gather(item, "fsdp", axis=0, tiled=True) for item in flat]
    small_all = lax.all_gather(small, "fsdp", axis=0)
    return [wholes[4 * i : 4 * i + 4] for i in range(layers)], [small_all[:, i] for i in range(layers)]


def reduce_layer(grads):
    shards_now = [
        lax.psum_scatter(item, "fsdp", scatter_dimension=0, tiled=True) for item in grads
    ]
    return [lax.psum(item, "ctx") for item in shards_now]


def shards(
    tokens,
    lengths,
    cotangent,
    ln_gain,
    ln_bias,
    w_qkv,
    b_qv,
    w_out,
    b_out,
    w_up,
    b_up,
    w_down,
    b_down,
):
    seq_count, row_count, model_width = tokens.shape
    head_width = HEAD_DIM
    head_count = model_width // head_width
    score_scale = head_width ** (-0.5)
    ctx_index = lax.axis_index("ctx")
    depth = lax.axis_size("fsdp")
    positions = ctx_index * row_count + jnp.arange(row_count, dtype=jnp.int32)
    valid_rows = (positions[None, :] < lengths[:, None]).astype(jnp.float32)[..., None]
    flat_rows = seq_count * row_count
    split_shape = (seq_count, row_count, head_count, head_width)
    layer_total = ln_gain.shape[0]
    hidden = tokens.astype(jnp.float32).reshape(flat_rows, model_width)
    small = pack_small(ln_gain, ln_bias, b_qv, b_out, b_up, b_down)
    if fast_mesh(w_qkv.shape[1]):
        part = small.shape[2]
        ff = w_up.shape[2]
        padded = jnp.pad(small, ((0, 0), (0, 4), (0, pad_lanes(part) - part)))
        activations, vectors, weights, kept = forward(
            tokens, lengths, w_qkv, w_out, w_up, w_down, padded.reshape(layer_total * 16, -1)
        )
        grad_in, small_sums, sums = backward(
            cotangent, lengths, vectors, kept, weights, layer_total, ff
        )
        mine = lambda rows: lax.dynamic_slice_in_dim(
            rows[..., :model_width], lax.axis_index("fsdp") * part, part, axis=rows.ndim - 1
        )
        up_bias = small_sums[:, 8:12].reshape(layer_total, -1)[:, :ff]
        up_part = ff // depth
        whole = lambda member, cols: jnp.stack(
            [item[member][:, :cols].astype(jnp.float32) for item in sums]
        )
        return (
            activations.reshape(tokens.shape),
            grad_in.reshape(tokens.shape),
            mine(small_sums[:, 0:2]),
            mine(small_sums[:, 2:4]),
            whole(3, 3 * model_width),
            mine(small_sums[:, 4:6]),
            whole(2, model_width),
            mine(small_sums[:, 6]),
            whole(1, ff),
            lax.dynamic_slice_in_dim(up_bias, lax.axis_index("fsdp") * up_part, up_part, axis=1),
            whole(0, model_width),
            mine(small_sums[:, 7]),
        )
    weights, smalls = gather_all(
        [(w_qkv[i], w_out[i], w_up[i], w_down[i]) for i in range(layer_total)], small
    )
    kept_layers = []
    for layer_index in range(layer_total):
        mix_weight, out_weight, up_weight, down_weight = weights[layer_index]
        gain_rows, shift_rows, mix_bias, out_bias, down_bias, up_bias = unpack_small(
            smalls[layer_index].astype(jnp.float32)
        )
        normed_first = normalize(hidden, gain_rows[0], shift_rows[0]).astype(jnp.bfloat16)
        mixed_rows = jnp.dot(normed_first, mix_weight, preferred_element_type=jnp.float32)
        queries = (
            (mixed_rows[:, :model_width] + mix_bias[0]).astype(jnp.bfloat16).reshape(split_shape)
        )
        key_rows = (
            mixed_rows[:, model_width : 2 * model_width].astype(jnp.bfloat16).reshape(split_shape)
        )
        value_rows = (
            (mixed_rows[:, 2 * model_width :] + mix_bias[1])
            .astype(jnp.bfloat16)
            .reshape(split_shape)
        )
        key_part = lax.all_gather(key_rows, "ctx", axis=1, tiled=True)
        value_part = lax.all_gather(value_rows, "ctx", axis=1, tiled=True)
        output, log_total = attend_forward(
            queries, key_part, value_part, positions, lengths, score_scale
        )
        output = output.reshape(flat_rows, model_width)
        attended = output.astype(jnp.bfloat16)
        middle = (
            hidden + jnp.dot(attended, out_weight, preferred_element_type=jnp.float32) + out_bias
        )
        normed_second = normalize(middle, gain_rows[1], shift_rows[1]).astype(jnp.bfloat16)
        upper_pre = (
            jnp.dot(normed_second, up_weight, preferred_element_type=jnp.float32) + up_bias
        )
        active = jax.nn.gelu(upper_pre).astype(jnp.bfloat16)
        kept_layers.append(
            (
                hidden,
                normed_first,
                queries,
                key_part,
                value_part,
                output,
                log_total,
                attended,
                middle,
                normed_second,
                upper_pre,
                active,
                gain_rows,
                shift_rows,
            )
        )
        hidden = (
            middle + jnp.dot(active, down_weight, preferred_element_type=jnp.float32) + down_bias
        )
    activations = (valid_rows * hidden.reshape(seq_count, row_count, model_width)).astype(
        jnp.bfloat16
    )
    grad_hidden = (cotangent.astype(jnp.float32) * valid_rows).reshape(flat_rows, model_width)
    big_grads = [None] * layer_total
    small_grads = [None] * layer_total
    for layer_index in reversed(range(layer_total)):
        (
            hidden_in,
            normed_first,
            queries,
            key_part,
            value_part,
            output,
            log_total,
            attended,
            middle,
            normed_second,
            upper_pre,
            active,
            gain_rows,
            shift_rows,
        ) = kept_layers[layer_index]
        mix_weight, out_weight, up_weight, down_weight = weights[layer_index]
        grad_branch = grad_hidden.astype(jnp.bfloat16)
        down_bias_grad = jnp.sum(grad_branch.astype(jnp.float32), axis=0)
        down_grad = outer_sum(active, grad_branch)
        grad_active = times_transpose(grad_branch, down_weight)
        unused_gelu, gelu_pull = jax.vjp(jax.nn.gelu, upper_pre)
        grad_upper = gelu_pull(grad_active)[0].astype(jnp.bfloat16)
        up_bias_grad = jnp.sum(grad_upper.astype(jnp.float32), axis=0)
        up_grad = outer_sum(normed_second, grad_upper)
        grad_normed = times_transpose(grad_upper, up_weight)
        unused_norm, norm_pull = jax.vjp(normalize, middle, gain_rows[1], shift_rows[1])
        grad_middle, gain_second, shift_second = norm_pull(grad_normed)
        grad_middle = grad_middle + grad_hidden
        grad_attn = grad_middle.astype(jnp.bfloat16)
        out_bias_grad = jnp.sum(grad_attn.astype(jnp.float32), axis=0)
        out_grad = outer_sum(attended, grad_attn)
        grad_output = times_transpose(grad_attn, out_weight).astype(jnp.bfloat16)
        delta_row = jnp.transpose(
            jnp.sum((grad_output.astype(jnp.float32) * output).reshape(split_shape), axis=-1),
            (0, 2, 1),
        )
        grad_heads = grad_output.reshape(split_shape)
        query_grad, key_add, value_add = block_terms(
            queries,
            grad_heads,
            log_total,
            delta_row,
            key_part,
            value_part,
            0,
            positions,
            lengths,
            score_scale,
        )
        key_low = lax.psum_scatter(
            key_add.astype(jnp.bfloat16), "ctx", scatter_dimension=1, tiled=True
        ).reshape(flat_rows, model_width)
        value_low = lax.psum_scatter(
            value_add.astype(jnp.bfloat16), "ctx", scatter_dimension=1, tiled=True
        ).reshape(flat_rows, model_width)
        query_low = query_grad.reshape(flat_rows, model_width).astype(jnp.bfloat16)
        grad_mixed = jnp.concatenate([query_low, key_low, value_low], axis=1)
        mix_bias_grad = jnp.stack(
            [
                jnp.sum(query_low.astype(jnp.float32), axis=0),
                jnp.sum(value_low.astype(jnp.float32), axis=0),
            ]
        )
        mix_grad = outer_sum(normed_first, grad_mixed)
        grad_normed_first = times_transpose(grad_mixed, mix_weight)
        unused_first, first_pull = jax.vjp(normalize, hidden_in, gain_rows[0], shift_rows[0])
        grad_input, gain_first, shift_first = first_pull(grad_normed_first)
        grad_hidden = grad_input + grad_middle
        big_grads[layer_index] = reduce_layer(
            [item.astype(jnp.bfloat16) for item in (up_grad, down_grad, mix_grad, out_grad)]
        )
        small_grads[layer_index] = small_rows(
            jnp.stack([gain_first, gain_second]),
            jnp.stack([shift_first, shift_second]),
            mix_bias_grad,
            out_bias_grad,
            down_bias_grad,
            up_bias_grad,
            depth,
        )
    input_grad = grad_hidden.reshape(seq_count, row_count, model_width)
    packed = jnp.stack(small_grads).astype(jnp.bfloat16)
    total = lax.psum(packed, ("fsdp", "ctx"))
    own = lax.dynamic_index_in_dim(total, lax.axis_index("fsdp"), 1, keepdims=False)
    own = own.astype(jnp.float32)

    def whole(member):
        return jnp.stack([big_grads[i][member].astype(jnp.float32) for i in range(layer_total)])

    return (
        activations,
        input_grad,
        own[:, 0:2],
        own[:, 2:4],
        whole(2),
        own[:, 4:6],
        whole(3),
        own[:, 6],
        whole(0),
        own[:, 8:].reshape(layer_total, -1),
        whole(1),
        own[:, 7],
    )


def solution(mesh):
    placed = (
        P("fsdp", "ctx", None),
        P("fsdp"),
        P("fsdp", "ctx", None),
        P(None, None, "fsdp"),
        P(None, None, "fsdp"),
        P(None, "fsdp", None),
        P(None, None, "fsdp"),
        P(None, "fsdp", None),
        P(None, "fsdp"),
        P(None, "fsdp", None),
        P(None, "fsdp"),
        P(None, "fsdp", None),
        P(None, "fsdp"),
    )
    return jax.shard_map(
        shards,
        mesh=mesh,
        in_specs=placed,
        out_specs=(
            P("fsdp", "ctx", None),
            P("fsdp", "ctx", None),
            P(None, None, "fsdp"),
            P(None, None, "fsdp"),
            P(None, "fsdp", None),
            P(None, None, "fsdp"),
            P(None, "fsdp", None),
            P(None, "fsdp"),
            P(None, "fsdp", None),
            P(None, "fsdp"),
            P(None, "fsdp", None),
            P(None, "fsdp"),
        ),
        check_vma=False,
    )
```
